32 devices in a mesh: gx: 8 (over z, y), yz: 4 (over x, core).
Axes of the slice: x: 2, y: 2, z: 4, core: 2. Of those that a mesh axis runs over, the one named last changes fastest.
Arguments:
- cell_matrix: bfloat16 [16, 128, 256, 256], P('gx', 'yz'), as said below
- x_coupling: bfloat16 [16, 128, 128], P('gx', 'yz'), may hold values from 0.5 to 2
- y_coupling: bfloat16 [16, 128, 128], P('gx', 'yz'), may hold values from 0.5 to 2
- cell_interp: bfloat16 [16, 128, 256, 128], P('gx', 'yz'), may hold values from -0.375 to 0.375
- cell_skel: int32 [16, 128, 128], P('gx', 'yz'), may hold values from 0 to 255, as said below
- cell_rank: int32 [16, 128], P('gx', 'yz'), may hold values from 64 to 128, as said below
- x_face_interp: bfloat16 [16, 128, 256, 128], P('gx', 'yz'), may hold values from -0.375 to 0.375
- x_face_skel: int32 [16, 128, 128], P('gx', 'yz'), may hold values from 0 to 255, as said below
- x_face_rank: int32 [16, 128], P('gx', 'yz'), may hold values from 64 to 128, as said below
- y_face_interp: bfloat16 [16, 128, 256, 128], P('gx', 'yz'), may hold values from -0.375 to 0.375
- y_face_skel: int32 [16, 128, 128], P('gx', 'yz'), may hold values from 0 to 255, as said below
- y_face_rank: int32 [16, 128], P('gx', 'yz'), may hold values from 64 to 128, as said below
Outputs:
- x_face_block: bfloat16 [16, 128, 128, 128], P('gx', 'yz')
- y_face_block: bfloat16 [16, 128, 128, 128], P('gx', 'yz')
The draws below stay inside these ranges and needn't reach their ends.
Inputs may be any that keep to these rules, and one draw needn't show every extreme that they name: `cell_skel`: each row names 128 distinct unknowns of a cell block. `cell_rank`: the slots of cell_skel below a cell's rank are its live skeleton. `x_face_skel`: each row names 128 distinct unknowns of the face's two cells. `x_face_rank`: the slots of x_face_skel below a face's rank are its live skeleton. `y_face_skel`: each row names 128 distinct unknowns of the face's two cells. `y_face_rank`: the slots of y_face_skel below a face's rank are its live skeleton. `cell_matrix`: symmetric.
All inputs are finite; a program needn't handle non-finite values.
Results may differ from the reference program's by a relative error of at most 0.0053.
Values may be sent and summed in bfloat16 or wider, within the bound.
No kernel may reach another device: no remote copies, remote signals or barrier semaphores. Data moves between devices by JAX's collectives and lax.ppermute only.
A program may use at most 128 MiB of HBM per device.

```python
import math
import jax
import jax.numpy as jnp
from jax import lax

B = 256
K = 128
KF = 128
NXC = 16
NYZ = 128


def draw_cell_matrix(key, part):
    first_key, second_key = jax.random.split(jax.random.fold_in(key, 7))
    noise = jax.random.normal(first_key, (NXC, NYZ, B, B), jnp.float32)
    diagonal = jax.random.uniform(second_key, (NXC, NYZ, B), jnp.float32, 1.0, 2.0)
    symmetric = (noise + jnp.swapaxes(noise, -1, -2)) * (0.35 / math.sqrt(B))
    return (symmetric + diagonal[..., None] * jnp.eye(B, dtype=jnp.float32)).astype(jnp.bfloat16)


def skeleton_lists(key, slot_total, pool_size):
    keys = jax.random.split(key, NXC * NYZ)

    def choose_slots(single_key):
        return jax.random.permutation(single_key, pool_size)[:slot_total]
    chosen = jax.vmap(choose_slots)(keys)
    return chosen.reshape(NXC, NYZ, slot_total).astype(jnp.int32)


def rank_values(key, slot_total):
    ranks = jax.random.randint(key, (NXC, NYZ), slot_total // 2, slot_total + 1, dtype=jnp.int32)
    return ranks.at[0, 0].set(slot_total).at[NXC - 1, NYZ - 1].set(slot_total // 2)


def draw_cell_skel(key, part):
    return skeleton_lists(jax.random.fold_in(key, 11), K, B)


def draw_cell_rank(key, part):
    return rank_values(jax.random.fold_in(key, 13), K)


def draw_x_face_skel(key, part):
    return skeleton_lists(jax.random.fold_in(key, 17), KF, 2 * K)


def draw_x_face_rank(key, part):
    return rank_values(jax.random.fold_in(key, 19), KF)


def draw_y_face_skel(key, part):
    return skeleton_lists(jax.random.fold_in(key, 23), KF, 2 * K)


def draw_y_face_rank(key, part):
    return rank_values(jax.random.fold_in(key, 29), KF)


def level_of(stream_key, shape, pieces, smallest, high):
    loudness, own = 1.0, jax.random.fold_in(stream_key, 6)
    for position, parts in pieces:
        heights = jnp.exp(jax.random.uniform(jax.random.fold_in(own, position), (parts,), jnp.float32, smallest / len(pieces), high / len(pieces)))
        loudness = loudness * jnp.repeat(heights, shape[position] // parts).reshape([-1 if axis == position else 1 for axis in range(len(shape))])
    return loudness


def normal_values(key, shape, deviation, most, shards=(), kind=jnp.bfloat16):
    factor_of = level_of(key, shape, shards, -0.22, 0.18) if shards else 1.0
    array = jax.random.normal(key, shape, jnp.float32) * deviation * factor_of
    return jnp.minimum(jnp.maximum(array, -most), most).astype(kind)


def setup_inputs(seed: int = 0) -> dict:
    splits = jax.random.split(jax.random.key(seed), 13)
    cell_matrix = draw_cell_matrix(jax.random.fold_in(splits[12], 71), 0)
    x_coupling = jnp.clip(jnp.exp(math.log(2.0) - 1.3862944 * jax.random.uniform(splits[1], (NXC, NYZ, B // 2), jnp.float32) ** level_of(splits[1], (NXC, NYZ, B // 2), ((0, 8), (1, 4)), -0.2, 0.2)), 0.5, 2.0).astype(jnp.bfloat16)
    y_coupling = jnp.clip(jnp.exp(math.log(2.0) - 1.3862944 * jax.random.uniform(splits[2], (NXC, NYZ, B // 2), jnp.float32) ** level_of(splits[2], (NXC, NYZ, B // 2), ((0, 8), (1, 4)), -0.2, 0.2)), 0.5, 2.0).astype(jnp.bfloat16)
    cell_interp = normal_values(splits[3], (NXC, NYZ, B, K), B ** -0.5, 0.375, ((0, 8), (1, 4)))
    cell_skel = draw_cell_skel(jax.random.fold_in(splits[12], 71), 0)
    cell_rank = draw_cell_rank(jax.random.fold_in(splits[12], 71), 0)
    x_face_interp = normal_values(splits[6], (NXC, NYZ, 2 * K, KF), (2 * K) ** -0.5, 0.375, ((0, 8), (1, 4)))
    x_face_skel = draw_x_face_skel(jax.random.fold_in(splits[12], 71), 0)
    x_face_rank = draw_x_face_rank(jax.random.fold_in(splits[12], 71), 0)
    y_face_interp = normal_values(splits[9], (NXC, NYZ, 2 * K, KF), (2 * K) ** -0.5, 0.375, ((0, 8), (1, 4)))
    y_face_skel = draw_y_face_skel(jax.random.fold_in(splits[12], 71), 0)
    y_face_rank = draw_y_face_rank(jax.random.fold_in(splits[12], 71), 0)
    return dict(cell_matrix=cell_matrix, x_coupling=x_coupling, y_coupling=y_coupling, cell_interp=cell_interp, cell_skel=cell_skel, cell_rank=cell_rank, x_face_interp=x_face_interp, x_face_skel=x_face_skel, x_face_rank=x_face_rank, y_face_interp=y_face_interp, y_face_skel=y_face_skel, y_face_rank=y_face_rank)


def make_basis(skel_list, rank_list, interp):
    row_count = interp.shape[-2]
    slot_count = skel_list.shape[-1]
    slot_index = lax.broadcasted_iota(jnp.int32, skel_list.shape, skel_list.ndim - 1)
    live_slots = slot_index < rank_list[..., None]
    row_index = lax.broadcasted_iota(jnp.int32, skel_list.shape[:-1] + (row_count, slot_count), skel_list.ndim - 1)
    picked_rows = (row_index == skel_list[..., None, :]) & live_slots[..., None, :]
    kept_rows = jnp.any(picked_rows, axis=-1, keepdims=True)
    interp_part = jnp.where(live_slots[..., None, :], interp.astype(jnp.float32), jnp.float32(0.0))
    return jnp.where(picked_rows, jnp.float32(1.0), jnp.where(kept_rows, jnp.float32(0.0), interp_part)).astype(jnp.bfloat16)


def project(matrix, left_basis, right_basis):
    inner_prod = jnp.einsum('...ij,...jk->...ik', matrix.astype(jnp.float32), right_basis.astype(jnp.float32)).astype(jnp.bfloat16)
    inner_prod = lax.optimization_barrier(inner_prod)
    return jnp.einsum('...ji,...jk->...ik', left_basis.astype(jnp.float32), inner_prod.astype(jnp.float32))


def coupling_link(conduct, own_basis, right_basis):
    half_rows = own_basis.shape[-2] // 2
    scaled = (-conduct.astype(jnp.float32)[..., None] * right_basis[..., :half_rows, :].astype(jnp.float32)).astype(jnp.bfloat16)
    scaled = lax.optimization_barrier(scaled)
    return jnp.einsum('...ji,...jk->...ik', own_basis[..., half_rows:, :].astype(jnp.float32), scaled.astype(jnp.float32))


def face_matrix(left_block, link_block, right_block):
    upper_half = jnp.concatenate([left_block, link_block], axis=-1)
    lower_half = jnp.concatenate([jnp.swapaxes(link_block, -1, -2), right_block], axis=-1)
    return jnp.concatenate([upper_half, lower_half], axis=-2)


def cell_row(packed):
    matrix, x_edge, y_edge, own_basis, right_x, right_y = packed
    schur_block = project(matrix, own_basis, own_basis).astype(jnp.bfloat16)
    x_link = coupling_link(x_edge, own_basis, right_x).astype(jnp.bfloat16)
    y_link = coupling_link(y_edge, own_basis, right_y).astype(jnp.bfloat16)
    return schur_block, x_link, y_link


def face_row(packed):
    left_block, link_block, right_block, face_basis = packed
    return project(face_matrix(left_block, link_block, right_block), face_basis, face_basis).astype(jnp.bfloat16)


def reference(cell_matrix, x_coupling, y_coupling, cell_interp, cell_skel, cell_rank, x_face_interp, x_face_skel, x_face_rank, y_face_interp, y_face_skel, y_face_rank):
    cell_basis = make_basis(cell_skel, cell_rank, cell_interp)
    next_x = jnp.concatenate([cell_basis[1:], jnp.zeros_like(cell_basis[:1])], axis=0)
    next_y = jnp.concatenate([cell_basis[:, 1:], jnp.zeros_like(cell_basis[:, :1])], axis=1)
    schur_block, x_link, y_link = lax.map(cell_row, (cell_matrix, x_coupling, y_coupling, cell_basis, next_x, next_y))
    schur_x = jnp.concatenate([schur_block[1:], jnp.zeros_like(schur_block[:1])], axis=0)
    schur_y = jnp.concatenate([schur_block[:, 1:], jnp.zeros_like(schur_block[:, :1])], axis=1)
    x_basis = make_basis(x_face_skel, x_face_rank, x_face_interp)
    y_basis = make_basis(y_face_skel, y_face_rank, y_face_interp)
    x_face_block = lax.map(face_row, (schur_block, x_link, schur_x, x_basis))
    y_face_block = lax.map(face_row, (schur_block, y_link, schur_y, y_basis))
    return x_face_block, y_face_block
```

```python
import functools

import jax
import jax.numpy as jnp
from jax import lax
from jax.experimental import pallas as pl
from jax.experimental.pallas import tpu as pltpu
from jax.sharding import PartitionSpec as P

BF = jnp.bfloat16
F32 = jnp.float32
VMEM_LIMIT = 56 * 1024 * 1024


def passed_along(x, axis, by):
    devices = lax.axis_size(axis)
    pairs = [(i, i + by) for i in range(devices) if 0 <= i + by < devices]
    return lax.ppermute(x, axis, pairs)


def dot(a, b):
    return lax.dot_general(a, b, (((1,), (0,)), ((), ())), preferred_element_type=F32)


def dot_nt(a, b):
    return lax.dot_general(a, b, (((1,), (1,)), ((), ())), preferred_element_type=F32)


def basis_t(skel_row, rank, interp):
    rows, slots = interp.shape
    live = lax.broadcasted_iota(jnp.int32, (1, slots), 1) < rank
    picked_row = jnp.where(live, skel_row, -1)
    row = lax.broadcasted_iota(jnp.int32, (rows, slots), 0)
    marked = jnp.where(
        row == picked_row, F32(1.0), jnp.where(live, interp.astype(F32), F32(0.0))
    ).astype(BF)
    turned = jnp.transpose(marked).astype(F32)
    most = jnp.max(turned, axis=0, keepdims=True)
    least = jnp.where(most == 1.0, F32(1.0), F32(-2.0))
    return jnp.where(turned >= least, turned, F32(0.0)).astype(BF)


def project_t(basis, matrix):
    return dot_nt(dot(basis, matrix).astype(BF), basis)


def links(own, conduct, right_top):
    half = own.shape[-1] // 2
    scaled = (right_top.astype(F32) * -conduct.astype(F32)).astype(BF)
    lower = own[:, half:]
    return dot_nt(lower, scaled).astype(BF), dot_nt(scaled, lower).astype(BF)


def face_t(basis, left, link, link_t, right):
    upper = jnp.concatenate([left, link], axis=1)
    lower = jnp.concatenate([link_t, right], axis=1)
    return project_t(basis, jnp.concatenate([upper, lower], axis=0))


def top_kernel(cells, rank_ref, skel_ref, interp_ref, out_ref):
    first = pl.program_id(0) * cells
    for k in range(cells):
        out_ref[k] = basis_t(skel_ref[0, k : k + 1], rank_ref[0, first + k], interp_ref[0, k])


def pack_masks(size):
    half = size // 2
    row = lax.broadcasted_iota(jnp.int32, (half, size), 0)
    lane = lax.broadcasted_iota(jnp.int32, (half, size), 1)
    ahead = lane - row
    upper = (ahead >= 0) & (ahead < half)
    return upper, ahead == 0, ahead == half


def cells_kernel(cells, rank_ref, skel_ref, interp_ref, matrix_ref, basis_ref, schur_ref, edge_ref, packed_ref):
    layer, chunk = pl.program_id(0), pl.program_id(1)
    first = chunk * cells
    slots = skel_ref.shape[-1]
    half = slots // 2
    upper, _, opposite = pack_masks(slots)
    packs, extras = [], []
    for k in range(cells):
        basis = basis_t(skel_ref[0, k : k + 1], rank_ref[layer, first + k], interp_ref[0, k])
        schur = project_t(basis, matrix_ref[0, k]).astype(BF)
        basis_ref[0, k] = basis
        schur_ref[0, k] = schur
        wide = schur.astype(F32)
        packs.append(jnp.where(upper, wide[:half], wide[half:]).astype(BF))
        extras.append(
            jnp.sum(jnp.where(opposite, wide[:half], F32(0.0)), axis=0, keepdims=True)
        )

    @pl.when(layer == 0)
    def _():
        pad = packed_ref.shape[1] - cells * half - cells
        for k in range(cells):
            packed_ref[chunk, k * half : (k + 1) * half] = packs[k]
        rows = extras + [jnp.zeros((pad, slots), F32)]
        packed_ref[chunk, cells * half :] = jnp.concatenate(rows, axis=0).astype(BF)

    @pl.when(chunk == 0)
    def _():
        edge_ref[layer, 0] = basis_ref[0, 0, :, : basis_ref.shape[-1] // 2]
        edge_ref[layer, 1] = schur_ref[0, 0]


def y_faces_kernel(cells, rank_ref, skel_ref, interp_ref, coup_ref, basis_ref, schur_ref, nbasis_ref, nschur_ref, out_ref):
    layer, chunk = pl.program_id(0), pl.program_id(1)
    first = chunk * cells
    half = nbasis_ref.shape[-1]
    for k in range(cells):
        face = basis_t(skel_ref[0, k : k + 1], rank_ref[layer, first + k], interp_ref[0, k])
        if k + 1 < cells:
            right_top, right = basis_ref[0, k + 1, :, :half], schur_ref[0, k + 1]
        else:
            right_top, right = nbasis_ref[0, 0], nschur_ref[0, 0]
        link, link_t = links(basis_ref[0, k], coup_ref[0, k : k + 1], right_top)
        out_ref[0, k] = face_t(face, schur_ref[0, k], link, link_t, right).astype(BF)


def y_edge_kernel(place, rank_ref, skel_ref, interp_ref, coup_ref, basis_ref, schur_ref, edge_ref, _, out_ref):
    layer = pl.program_id(0)
    row = place % skel_ref.shape[1]
    face = basis_t(skel_ref[0, row : row + 1], rank_ref[layer, place], interp_ref[0, 0])
    link, link_t = links(basis_ref[0, 0], coup_ref[0, row : row + 1], edge_ref[0, 0])
    out_ref[0, 0] = face_t(face, schur_ref[0, 0], link, link_t, edge_ref[0, 1]).astype(BF)


def x_faces_kernel(cells, rank_ref, skel_ref, interp_ref, coup_ref, basis_ref, schur_ref, nbasis_ref, nschur_ref, out_ref):
    layer, chunk = pl.program_id(0), pl.program_id(1)
    first = chunk * cells
    for k in range(cells):
        face = basis_t(skel_ref[0, k : k + 1], rank_ref[layer, first + k], interp_ref[0, k])
        link, link_t = links(basis_ref[0, k], coup_ref[0, k : k + 1], nbasis_ref[0, k])
        out_ref[0, k] = face_t(face, schur_ref[0, k], link, link_t, nschur_ref[0, k]).astype(BF)


def x_part_kernel(cells, layer, rank_ref, skel_ref, interp_ref, coup_ref, basis_ref, schur_ref, top_ref, part_ref, lower_ref):
    first = pl.program_id(0) * cells
    half = top_ref.shape[-1]
    for k in range(cells):
        face = basis_t(skel_ref[0, k : k + 1], rank_ref[layer, first + k], interp_ref[0, k])
        link, link_t = links(basis_ref[0, k], coup_ref[0, k : k + 1], top_ref[k])
        part_ref[k] = face_t(face, schur_ref[0, k], link, link_t, jnp.zeros_like(link))
        lower_ref[k] = face[:, half:]


def x_last_kernel(cells, part_ref, lower_ref, packed_ref, _, out_ref):
    slots = part_ref.shape[-1]
    half = slots // 2
    upper, same, opposite = pack_masks(slots)
    one, zero, mid = F32(1.0), F32(0.0), F32(0.5)
    top_scale = jnp.where(same, mid, jnp.where(upper, one, zero))
    low_scale = jnp.where(opposite, mid, jnp.where(upper, zero, one))
    opp_scale = jnp.where(opposite, one, zero)
    extras = packed_ref[0, cells * half :].astype(F32)
    for k in range(cells):
        packed = packed_ref[0, k * half : (k + 1) * half].astype(F32)
        top = packed * top_scale + extras[k : k + 1] * opp_scale
        low = packed * low_scale
        tri = jnp.concatenate([top, low], axis=0).astype(BF)
        lower = lower_ref[k]
        inner = (dot(lower, tri) + dot_nt(lower, tri)).astype(BF)
        out_ref[0, k] = (part_ref[k] + dot_nt(inner, lower)).astype(BF)


def call(kernel, grid, in_specs, out_specs, out_shape, flops, moved, aliases=None):
    return pl.pallas_call(
        kernel,
        grid=grid,
        in_specs=in_specs,
        out_specs=out_specs,
        out_shape=out_shape,
        input_output_aliases=aliases or {},
        compiler_params=pltpu.CompilerParams(vmem_limit_bytes=VMEM_LIMIT),
        cost_estimate=pl.CostEstimate(flops=flops, bytes_accessed=moved, transcendentals=0),
    )


def body(
    cell_matrix,
    x_coupling,
    y_coupling,
    cell_interp,
    cell_skel,
    cell_rank,
    x_face_interp,
    x_face_skel,
    x_face_rank,
    y_face_interp,
    y_face_skel,
    y_face_rank,
):
    nx, nj, rows, slots = cell_interp.shape
    half = rows // 2
    fslots = x_face_interp.shape[-1]
    cells = 8 if nj % 8 == 0 else nj
    chunks = nj // cells
    unit = 2 * nx * nj * slots * slots * slots
    smem = pl.BlockSpec(memory_space=pltpu.SMEM)
    shape = jax.ShapeDtypeStruct

    def block(*dims):
        return pl.BlockSpec((1, cells) + dims, lambda i, c: (i, c) + (0,) * len(dims))

    top = call(
        functools.partial(top_kernel, cells),
        (chunks,),
        [
            smem,
            pl.BlockSpec((1, cells, slots), lambda c: (0, c, 0)),
            pl.BlockSpec((1, cells, half, slots), lambda c: (0, c, 0, 0)),
        ],
        pl.BlockSpec((cells, slots, half), lambda c: (c, 0, 0)),
        shape((nj, slots, half), BF),
        0,
        4 * nj * half * slots,
    )(cell_rank, cell_skel, cell_interp)
    top_in = passed_along(top, "gx", -1)

    pack_rows = cells * slots // 2 + -(-cells // 16) * 16
    basis, schur, edge, packed = call(
        functools.partial(cells_kernel, cells),
        (nx, chunks),
        [smem, block(slots), block(rows, slots), block(rows, rows)],
        [
            block(slots, rows),
            block(slots, slots),
            pl.BlockSpec((nx, 2, slots, slots), lambda i, c: (0, 0, 0, 0)),
            pl.BlockSpec((chunks, pack_rows, slots), lambda i, c: (0, 0, 0)),
        ],
        [
            shape((nx, nj, slots, rows), BF),
            shape((nx, nj, slots, slots), BF),
            shape((nx, 2, slots, slots), BF),
            shape((chunks, pack_rows, slots), BF),
        ],
        6 * unit,
        nx * nj * (rows * rows + 2 * rows * slots + slots * slots) * 2,
    )(cell_rank, cell_skel, cell_interp, cell_matrix)
    edge_in = passed_along(edge, "yz", -1)
    packed_in = passed_along(packed, "gx", -1)

    face_bytes = nj * (2 * rows * slots + 4 * slots * slots) * 2
    y_out = call(
        functools.partial(y_faces_kernel, cells),
        (nx, chunks),
        [
            smem,
            block(fslots),
            block(rows, fslots),
            block(half),
            block(slots, rows),
            block(slots, slots),
            pl.BlockSpec((1, 1, slots, half), lambda i, c: (i, jnp.minimum((c + 1) * cells, nj - 1), 0, 0)),
            pl.BlockSpec((1, 1, slots, slots), lambda i, c: (i, jnp.minimum((c + 1) * cells, nj - 1), 0, 0)),
        ],
        block(fslots, fslots),
        shape((nx, nj, fslots, fslots), BF),
        8 * unit,
        nx * face_bytes,
    )(y_face_rank, y_face_skel, y_face_interp, y_coupling, basis, schur, basis, schur)

    if nx > 1:
        x_out = call(
            functools.partial(x_faces_kernel, cells),
            (nx - 1, chunks),
            [
                smem,
                block(fslots),
                block(rows, fslots),
                block(half),
                block(slots, rows),
                block(slots, slots),
                pl.BlockSpec((1, cells, slots, half), lambda i, c: (i + 1, c, 0, 0)),
                pl.BlockSpec((1, cells, slots, slots), lambda i, c: (i + 1, c, 0, 0)),
            ],
            block(fslots, fslots),
            shape((nx, nj, fslots, fslots), BF),
            8 * unit // nx * (nx - 1),
            (nx - 1) * face_bytes,
        )(x_face_rank, x_face_skel, x_face_interp, x_coupling, basis, schur, basis, schur)
    else:
        x_out = jnp.zeros((nx, nj, fslots, fslots), BF)

    last = nx - 1
    tail = nj - 1
    group = tail // cells

    def last_block(*dims):
        return pl.BlockSpec((1, cells) + dims, lambda c: (last, c) + (0,) * len(dims))

    def plain(*dims):
        return pl.BlockSpec((cells,) + dims, lambda c: (c,) + (0,) * len(dims))

    part, lower = call(
        functools.partial(x_part_kernel, cells, last),
        (chunks,),
        [
            smem,
            last_block(fslots),
            last_block(rows, fslots),
            last_block(half),
            last_block(slots, rows),
            last_block(slots, slots),
            plain(slots, half),
        ],
        [plain(fslots, fslots), plain(fslots, slots)],
        [shape((nj, fslots, fslots), F32), shape((nj, fslots, slots), BF)],
        8 * unit // nx,
        face_bytes,
    )(x_face_rank, x_face_skel, x_face_interp, x_coupling, basis, schur, top_in)

    y_out = call(
        functools.partial(y_edge_kernel, tail),
        (nx,),
        [
            smem,
            pl.BlockSpec((1, cells, fslots), lambda i: (i, group, 0)),
            pl.BlockSpec((1, 1, rows, fslots), lambda i: (i, tail, 0, 0)),
            pl.BlockSpec((1, cells, half), lambda i: (i, group, 0)),
            pl.BlockSpec((1, 1, slots, rows), lambda i: (i, tail, 0, 0)),
            pl.BlockSpec((1, 1, slots, slots), lambda i: (i, tail, 0, 0)),
            pl.BlockSpec((1, 2, slots, slots), lambda i: (i, 0, 0, 0)),
            pl.BlockSpec(memory_space=pl.ANY),
        ],
        pl.BlockSpec((1, 1, fslots, fslots), lambda i: (i, tail, 0, 0)),
        shape((nx, nj, fslots, fslots), BF),
        8 * unit // nj,
        nx * face_bytes // nj,
        {7: 0},
    )(y_face_rank, y_face_skel, y_face_interp, y_coupling, basis, schur, edge_in, y_out)

    x_out = call(
        functools.partial(x_last_kernel, cells),
        (chunks,),
        [
            plain(fslots, fslots),
            plain(fslots, slots),
            pl.BlockSpec((1, pack_rows, slots), lambda c: (c, 0, 0)),
            pl.BlockSpec(memory_space=pl.ANY),
        ],
        last_block(fslots, fslots),
        shape((nx, nj, fslots, fslots), BF),
        3 * unit // nx,
        nj * slots * slots * 9,
        {3: 0},
    )(part, lower, packed_in, x_out)
    return (x_out, y_out)


def solution(mesh):
    return jax.shard_map(
        body,
        mesh=mesh,
        in_specs=(
            P("gx", "yz", None, None),
            P("gx", "yz", None),
            P("gx", "yz", None),
            P("gx", "yz", None, None),
            P("gx", "yz", None),
            P("gx", "yz"),
            P("gx", "yz", None, None),
            P("gx", "yz", None),
            P("gx", "yz"),
            P("gx", "yz", None, None),
            P("gx", "yz", None),
            P("gx", "yz"),
        ),
        out_specs=(P("gx", "yz", None, None), P("gx", "yz", None, None)),
        check_vma=False,
    )
```

```python
import functools

import jax
import jax.numpy as jnp
from jax import lax
from jax.experimental import pallas as pl
from jax.experimental.pallas import tpu as pltpu
from jax.sharding import PartitionSpec as P

BF = jnp.bfloat16
F32 = jnp.float32
MIB = 1024 * 1024


def passed_along(x, axis, by):
    devices = lax.axis_size(axis)
    pairs = [(i, i + by) for i in range(devices) if 0 <= i + by < devices]
    return lax.ppermute(x, axis, pairs)


def dot(a, b):
    return lax.dot_general(a, b, (((1,), (0,)), ((), ())), preferred_element_type=F32)


def basis_of(skel_row, rank, interp):
    rows, slots = interp.shape
    live = lax.broadcasted_iota(jnp.int32, (1, slots), 1) < rank
    picked_row = jnp.where(live, skel_row, -1)
    row = lax.broadcasted_iota(jnp.int32, (rows, slots), 0)
    hit = jnp.where(row == picked_row, F32(1.0), F32(0.0))
    free = F32(1.0) - jnp.max(hit, axis=1, keepdims=True)
    live_row = jnp.where(live, F32(1.0), F32(0.0))
    return (hit + interp.astype(F32) * (free * live_row)).astype(BF)


def scaled(turned, conduct):
    return (turned.astype(F32) * -conduct.astype(F32)).astype(BF)


def face_of(left, link, link_t, right):
    upper = jnp.concatenate([left, link], axis=1)
    lower = jnp.concatenate([link_t, right], axis=1)
    return jnp.concatenate([upper, lower], axis=0)


def project(turned, matrices, bases):
    inner = [dot(t, m).astype(BF) for t, m in zip(turned, matrices)]
    return [dot(i, b) for i, b in zip(inner, bases)]


def bases_of(cells, layer, first, rank_ref, skel_ref, interp_ref):
    return [
        basis_of(skel_ref[0, k : k + 1], rank_ref[layer, first + k], interp_ref[0, k])
        for k in range(cells)
    ]


def top_kernel(cells, rank_ref, skel_ref, interp_ref, out_ref):
    first = pl.program_id(0) * cells
    for k in range(cells):
        out_ref[k] = basis_of(skel_ref[0, k : k + 1], rank_ref[0, first + k], interp_ref[0, k])


def pack_masks(size):
    half = size // 2
    row = lax.broadcasted_iota(jnp.int32, (half, size), 0)
    lane = lax.broadcasted_iota(jnp.int32, (half, size), 1)
    ahead = lane - row
    upper = (ahead >= 0) & (ahead < half)
    return upper, ahead == 0, ahead == half


def cells_kernel(cells, rank_ref, skel_ref, interp_ref, matrix_ref, basis_ref, turned_ref, schur_ref, edge_ref, packed_ref):
    layer, chunk = pl.program_id(0), pl.program_id(1)
    slots = skel_ref.shape[-1]
    half = slots // 2
    top = basis_ref.shape[2] // 2
    bases = bases_of(cells, layer, chunk * cells, rank_ref, skel_ref, interp_ref)
    turned = [jnp.transpose(b) for b in bases]
    for k in range(cells):
        basis_ref[0, k] = bases[k]
        turned_ref[0, k] = turned[k]
    schurs = project(turned, [matrix_ref[0, k] for k in range(cells)], bases)
    for k in range(cells):
        schur_ref[0, k] = schurs[k].astype(BF)

    @pl.when(layer == 0)
    def _():
        upper, _, opposite = pack_masks(slots)
        pad = packed_ref.shape[1] - cells * half - cells
        extras = []
        for k in range(cells):
            above = schur_ref[0, k, :half].astype(F32)
            below = schur_ref[0, k, half:].astype(F32)
            packed_ref[chunk, k * half : (k + 1) * half] = jnp.where(upper, above, below).astype(BF)
            extras.append(jnp.sum(jnp.where(opposite, above, F32(0.0)), axis=0, keepdims=True))
        rows = extras + [jnp.zeros((pad, slots), F32)]
        packed_ref[chunk, cells * half :] = jnp.concatenate(rows, axis=0).astype(BF)

    @pl.when(chunk == 0)
    def _():
        edge_ref[layer, 0] = basis_ref[0, 0, :top]
        edge_ref[layer, 1] = schur_ref[0, 0]


def y_faces_kernel(
    cells, rank_ref, skel_ref, interp_ref, coup_ref, basis_ref, turned_ref, schur_ref,
    next_basis_ref, next_turned_ref, next_schur_ref, out_ref,
):
    layer, chunk = pl.program_id(0), pl.program_id(1)
    half = next_turned_ref.shape[-1]
    faces = bases_of(cells, layer, chunk * cells, rank_ref, skel_ref, interp_ref)
    turned = [jnp.transpose(f) for f in faces]
    matrices = []
    for k in range(cells):
        if k + 1 < cells:
            right_top, right_turned = basis_ref[0, k + 1, :half], turned_ref[0, k + 1, :, :half]
            right = schur_ref[0, k + 1]
        else:
            right_top, right_turned = next_basis_ref[0, 0], next_turned_ref[0, 0]
            right = next_schur_ref[0, 0]
        conduct = coup_ref[0, k : k + 1]
        link = dot(scaled(turned_ref[0, k, :, half:], conduct), right_top).astype(BF)
        link_t = dot(scaled(right_turned, conduct), basis_ref[0, k, half:]).astype(BF)
        matrices.append(face_of(schur_ref[0, k], link, link_t, right))
    results = project(turned, matrices, faces)
    for k in range(cells):
        out_ref[0, k] = results[k].astype(BF)


def y_edge_kernel(place, rank_ref, skel_ref, interp_ref, coup_ref, turned_ref, schur_ref, edge_ref, _, out_ref):
    layer = pl.program_id(0)
    row = place % skel_ref.shape[1]
    face = basis_of(skel_ref[0, row : row + 1], rank_ref[layer, place], interp_ref[0, 0])
    link = dot(scaled(turned_ref[0, 0], coup_ref[0, row : row + 1]), edge_ref[0, 0]).astype(BF)
    matrix = face_of(schur_ref[0, 0], link, jnp.transpose(link), edge_ref[0, 1])
    out_ref[0, 0] = project([jnp.transpose(face)], [matrix], [face])[0].astype(BF)


def x_faces_kernel(
    cells, rank_ref, skel_ref, interp_ref, coup_ref, basis_ref, turned_ref, schur_ref,
    next_basis_ref, next_turned_ref, next_schur_ref, out_ref,
):
    layer, chunk = pl.program_id(0), pl.program_id(1)
    faces = bases_of(cells, layer, chunk * cells, rank_ref, skel_ref, interp_ref)
    turned = [jnp.transpose(f) for f in faces]
    matrices = []
    for k in range(cells):
        conduct = coup_ref[0, k : k + 1]
        link = dot(scaled(turned_ref[0, k], conduct), next_basis_ref[0, k]).astype(BF)
        link_t = dot(scaled(next_turned_ref[0, k], conduct), basis_ref[0, k]).astype(BF)
        matrices.append(face_of(schur_ref[0, k], link, link_t, next_schur_ref[0, k]))
    results = project(turned, matrices, faces)
    for k in range(cells):
        out_ref[0, k] = results[k].astype(BF)


def x_part_kernel(
    cells, layer, rank_ref, skel_ref, interp_ref, coup_ref, turned_ref, schur_ref, top_ref,
    part_ref, lower_ref, lower_turned_ref,
):
    half = top_ref.shape[-2]
    faces = bases_of(cells, layer, pl.program_id(0) * cells, rank_ref, skel_ref, interp_ref)
    turned = [jnp.transpose(f) for f in faces]
    for k in range(cells):
        lower_ref[k] = faces[k][half:]
        lower_turned_ref[k] = turned[k][:, half:]
    found = [
        dot(scaled(turned_ref[0, k], coup_ref[0, k : k + 1]), top_ref[k]).astype(BF)
        for k in range(cells)
    ]
    matrices = [
        face_of(schur_ref[0, k], found[k], jnp.transpose(found[k]), jnp.zeros_like(found[k]))
        for k in range(cells)
    ]
    results = project(turned, matrices, faces)
    for k in range(cells):
        part_ref[k] = results[k]


def x_last_kernel(cells, part_ref, lower_ref, lower_turned_ref, packed_ref, _, out_ref):
    slots = part_ref.shape[-1]
    half = slots // 2
    upper, same, opposite = pack_masks(slots)
    one, zero, mid = F32(1.0), F32(0.0), F32(0.5)
    top_scale = jnp.where(same, mid, jnp.where(upper, one, zero))
    low_scale = jnp.where(opposite, mid, jnp.where(upper, zero, one))
    opp_scale = jnp.where(opposite, one, zero)
    extras = packed_ref[0, cells * half :].astype(F32)
    schurs = []
    for k in range(cells):
        packed = packed_ref[0, k * half : (k + 1) * half].astype(F32)
        top = packed * top_scale + extras[k : k + 1] * opp_scale
        low = packed * low_scale
        tri = jnp.concatenate([top, low], axis=0).astype(BF)
        schurs.append(tri + jnp.transpose(tri))
    results = project(
        [lower_turned_ref[k] for k in range(cells)], schurs, [lower_ref[k] for k in range(cells)]
    )
    for k in range(cells):
        out_ref[0, k] = (part_ref[k] + results[k]).astype(BF)


def call(kernel, grid, in_specs, out_specs, out_shape, flops, moved, aliases=None, vmem=24):
    return pl.pallas_call(
        kernel,
        grid=grid,
        in_specs=in_specs,
        out_specs=out_specs,
        out_shape=out_shape,
        input_output_aliases=aliases or {},
        compiler_params=pltpu.CompilerParams(vmem_limit_bytes=vmem * MIB),
        cost_estimate=pl.CostEstimate(flops=flops, bytes_accessed=moved, transcendentals=0),
    )


def body(
    cell_matrix,
    x_coupling,
    y_coupling,
    cell_interp,
    cell_skel,
    cell_rank,
    x_face_interp,
    x_face_skel,
    x_face_rank,
    y_face_interp,
    y_face_skel,
    y_face_rank,
):
    nx, nj, rows, slots = cell_interp.shape
    half = rows // 2
    fslots = x_face_interp.shape[-1]
    cells = 8 if nj % 8 == 0 else nj
    chunks = nj // cells
    unit = 2 * nx * nj * slots * slots * slots
    smem = pl.BlockSpec(memory_space=pltpu.SMEM)
    shape = jax.ShapeDtypeStruct

    def block(*dims):
        return pl.BlockSpec((1, cells) + dims, lambda i, c: (i, c) + (0,) * len(dims))

    top = call(
        functools.partial(top_kernel, cells),
        (chunks,),
        [
            smem,
            pl.BlockSpec((1, cells, slots), lambda c: (0, c, 0)),
            pl.BlockSpec((1, cells, half, slots), lambda c: (0, c, 0, 0)),
        ],
        pl.BlockSpec((cells, half, slots), lambda c: (c, 0, 0)),
        shape((nj, half, slots), BF),
        0,
        4 * nj * half * slots,
        vmem=56,
    )(cell_rank, cell_skel, cell_interp)
    top_in = passed_along(top, "gx", -1)

    pack_rows = cells * slots // 2 + -(-cells // 16) * 16
    basis, turned, schur, edge, packed = call(
        functools.partial(cells_kernel, cells),
        (nx, chunks),
        [smem, block(slots), block(rows, slots), block(rows, rows)],
        [
            block(rows, slots),
            block(slots, rows),
            block(slots, slots),
            pl.BlockSpec((nx, 2, half, slots), lambda i, c: (0, 0, 0, 0)),
            pl.BlockSpec((chunks, pack_rows, slots), lambda i, c: (0, 0, 0)),
        ],
        [
            shape((nx, nj, rows, slots), BF),
            shape((nx, nj, slots, rows), BF),
            shape((nx, nj, slots, slots), BF),
            shape((nx, 2, half, slots), BF),
            shape((chunks, pack_rows, slots), BF),
        ],
        6 * unit,
        nx * nj * (rows * rows + 3 * rows * slots + slots * slots) * 2,
        vmem=56,
    )(cell_rank, cell_skel, cell_interp, cell_matrix)
    edge_in = passed_along(edge, "yz", -1)
    packed_in = passed_along(packed, "gx", -1)

    face_bytes = nj * (4 * rows * slots + 4 * slots * slots) * 2

    def after(c):
        return jnp.minimum((c + 1) * cells, nj - 1)

    y_out = call(
        functools.partial(y_faces_kernel, cells),
        (nx, chunks),
        [
            smem,
            block(fslots),
            block(rows, fslots),
            block(half),
            block(rows, slots),
            block(slots, rows),
            block(slots, slots),
            pl.BlockSpec((1, 1, half, slots), lambda i, c: (i, after(c), 0, 0)),
            pl.BlockSpec((1, 1, slots, half), lambda i, c: (i, after(c), 0, 0)),
            pl.BlockSpec((1, 1, slots, slots), lambda i, c: (i, after(c), 0, 0)),
        ],
        block(fslots, fslots),
        shape((nx, nj, fslots, fslots), BF),
        8 * unit,
        nx * face_bytes,
    )(y_face_rank, y_face_skel, y_face_interp, y_coupling, basis, turned, schur, basis, turned, schur)

    if nx > 1:
        x_out = call(
            functools.partial(x_faces_kernel, cells),
            (nx - 1, chunks),
            [
                smem,
                block(fslots),
                block(rows, fslots),
                block(half),
                pl.BlockSpec((1, cells, half, slots), lambda i, c: (i, c, 1, 0)),
                pl.BlockSpec((1, cells, slots, half), lambda i, c: (i, c, 0, 1)),
                block(slots, slots),
                pl.BlockSpec((1, cells, half, slots), lambda i, c: (i + 1, c, 0, 0)),
                pl.BlockSpec((1, cells, slots, half), lambda i, c: (i + 1, c, 0, 0)),
                pl.BlockSpec((1, cells, slots, slots), lambda i, c: (i + 1, c, 0, 0)),
            ],
            block(fslots, fslots),
            shape((nx, nj, fslots, fslots), BF),
            8 * unit // nx * (nx - 1),
            (nx - 1) * face_bytes,
        )(x_face_rank, x_face_skel, x_face_interp, x_coupling, basis, turned, schur, basis, turned, schur)
    else:
        x_out = jnp.zeros((nx, nj, fslots, fslots), BF)

    last = nx - 1
    tail = nj - 1
    group = tail // cells

    def last_block(*dims):
        return pl.BlockSpec((1, cells) + dims, lambda c: (last, c) + (0,) * len(dims))

    def plain(*dims):
        return pl.BlockSpec((cells,) + dims, lambda c: (c,) + (0,) * len(dims))

    part, lower, lower_turned = call(
        functools.partial(x_part_kernel, cells, last),
        (chunks,),
        [
            smem,
            last_block(fslots),
            last_block(rows, fslots),
            last_block(half),
            pl.BlockSpec((1, cells, slots, half), lambda c: (last, c, 0, 1)),
            last_block(slots, slots),
            plain(half, slots),
        ],
        [plain(fslots, fslots), plain(slots, fslots), plain(fslots, slots)],
        [
            shape((nj, fslots, fslots), F32),
            shape((nj, slots, fslots), BF),
            shape((nj, fslots, slots), BF),
        ],
        8 * unit // nx,
        face_bytes,
    )(x_face_rank, x_face_skel, x_face_interp, x_coupling, turned, schur, top_in)

    y_out = call(
        functools.partial(y_edge_kernel, tail),
        (nx,),
        [
            smem,
            pl.BlockSpec((1, cells, fslots), lambda i: (i, group, 0)),
            pl.BlockSpec((1, 1, rows, fslots), lambda i: (i, tail, 0, 0)),
            pl.BlockSpec((1, cells, half), lambda i: (i, group, 0)),
            pl.BlockSpec((1, 1, slots, half), lambda i: (i, tail, 0, 1)),
            pl.BlockSpec((1, 1, slots, slots), lambda i: (i, tail, 0, 0)),
            pl.BlockSpec((1, 2, half, slots), lambda i: (i, 0, 0, 0)),
            pl.BlockSpec(memory_space=pl.ANY),
        ],
        pl.BlockSpec((1, 1, fslots, fslots), lambda i: (i, tail, 0, 0)),
        shape((nx, nj, fslots, fslots), BF),
        8 * unit // nj,
        nx * face_bytes // nj,
        {7: 0},
    )(y_face_rank, y_face_skel, y_face_interp, y_coupling, turned, schur, edge_in, y_out)

    x_out = call(
        functools.partial(x_last_kernel, cells),
        (chunks,),
        [
            plain(fslots, fslots),
            plain(slots, fslots),
            plain(fslots, slots),
            pl.BlockSpec((1, pack_rows, slots), lambda c: (c, 0, 0)),
            pl.BlockSpec(memory_space=pl.ANY),
        ],
        last_block(fslots, fslots),
        shape((nx, nj, fslots, fslots), BF),
        3 * unit // nx,
        nj * slots * slots * 11,
        {4: 0},
    )(part, lower, lower_turned, packed_in, x_out)
    return (x_out, y_out)


def solution(mesh):
    return jax.shard_map(
        body,
        mesh=mesh,
        in_specs=(
            P("gx", "yz", None, None),
            P("gx", "yz", None),
            P("gx", "yz", None),
            P("gx", "yz", None, None),
            P("gx", "yz", None),
            P("gx", "yz"),
            P("gx", "yz", None, None),
            P("gx", "yz", None),
            P("gx", "yz"),
            P("gx", "yz", None, None),
            P("gx", "yz", None),
            P("gx", "yz"),
        ),
        out_specs=(P("gx", "yz", None, None), P("gx", "yz", None, None)),
        check_vma=False,
    )
```

```python
import functools

import jax
import jax.numpy as jnp
from jax import lax
from jax.experimental import pallas as pl
from jax.experimental.pallas import tpu as pltpu
from jax.sharding import PartitionSpec as P

BF = jnp.bfloat16
F32 = jnp.float32
MIB = 1024 * 1024


def passed_along(x, axis, by):
    devices = lax.axis_size(axis)
    pairs = [(i, i + by) for i in range(devices) if 0 <= i + by < devices]
    return lax.ppermute(x, axis, pairs)


def dot(a, b):
    return lax.dot_general(a, b, (((1,), (0,)), ((), ())), preferred_element_type=F32)


def marks_of(skel_row, rank, interp):
    rows, slots = interp.shape
    live = lax.broadcasted_iota(jnp.int32, (1, slots), 1) < rank
    picked_row = jnp.where(live, skel_row, -1).astype(F32).astype(BF)
    row = lax.broadcasted_iota(jnp.int32, (rows, slots), 0).astype(F32).astype(BF)
    live_row = jnp.where(live, F32(1.0), F32(0.0)).astype(BF)
    hit = jnp.where(row == picked_row, BF(1.0), BF(0.0))
    return hit, interp * live_row


def kept_cleared(hits, interps):
    slots = hits[0].shape[-1]
    ones = jnp.ones((slots, slots), BF)
    counts = [dot(hit, ones).astype(BF) for hit in hits]
    return [h + z * (BF(1.0) - n) for h, z, n in zip(hits, interps, counts)]


def bases_of(cells, layer, first, rank_ref, skel_ref, interp_ref):
    pairs = [
        marks_of(skel_ref[0, k : k + 1], rank_ref[layer, first + k], interp_ref[0, k])
        for k in range(cells)
    ]
    return kept_cleared([p[0] for p in pairs], [p[1] for p in pairs])


def scaled(turned, conduct):
    return turned * -conduct


def face_of(left, link, link_t, right):
    upper = jnp.concatenate([left, link], axis=1)
    lower = jnp.concatenate([link_t, right], axis=1)
    return jnp.concatenate([upper, lower], axis=0)


def project(turned, matrices, bases):
    inner = [dot(t, m).astype(BF) for t, m in zip(turned, matrices)]
    return [dot(i, b) for i, b in zip(inner, bases)]


def top_kernel(cells, rank_ref, skel_ref, interp_ref, out_ref):
    first = pl.program_id(0) * cells
    for k in range(cells):
        hit, interp = marks_of(skel_ref[0, k : k + 1], rank_ref[0, first + k], interp_ref[0, k])
        out_ref[k] = hit + interp * (BF(1.0) - hit)


def pack_masks(size):
    half = size // 2
    row = lax.broadcasted_iota(jnp.int32, (half, size), 0)
    lane = lax.broadcasted_iota(jnp.int32, (half, size), 1)
    ahead = lane - row
    upper = (ahead >= 0) & (ahead < half)
    return upper, ahead == 0, ahead == half


def main_kernel(
    cells, layers, chunks,
    rank_ref, skel_ref, interp_ref, matrix_ref,
    x_rank_ref, x_skel_ref, x_interp_ref, x_coup_ref,
    y_rank_ref, y_skel_ref, y_interp_ref, y_coup_ref,
    x_out_ref, y_out_ref, packed_ref, edge_ref, corner_ref, last_turned_ref, last_schur_ref,
    store_top, store_turned, store_schur,
):
    layer = layers - 1 - pl.program_id(0)
    chunk = chunks - 1 - pl.program_id(1)
    first = chunk * cells
    slots = skel_ref.shape[-1]
    half = slots // 2
    top = interp_ref.shape[2] // 2

    bases = bases_of(cells, layer, first, rank_ref, skel_ref, interp_ref)
    turned = [jnp.transpose(b) for b in bases]
    schurs = project(turned, [matrix_ref[0, k] for k in range(cells)], bases)
    schurs = [s.astype(BF) for s in schurs]

    def faces(out_ref, f_rank_ref, f_skel_ref, f_interp_ref, coup_ref, rights):
        found = bases_of(cells, layer, first, f_rank_ref, f_skel_ref, f_interp_ref)
        found_turned = [jnp.transpose(f) for f in found]
        matrices = []
        for k in range(cells):
            right_top, right_turned, right = rights[k]
            conduct = coup_ref[0, k : k + 1]
            link = dot(scaled(turned[k][:, top:], conduct), right_top).astype(BF)
            link_t = dot(scaled(right_turned, conduct), bases[k][top:]).astype(BF)
            matrices.append(face_of(schurs[k], link, link_t, right))
        results = project(found_turned, matrices, found)
        for k in range(cells):
            out_ref[0, k] = results[k].astype(BF)

    def stored(place):
        return store_top[place], store_turned[place], store_schur[place]

    after = jnp.minimum(first + cells, store_schur.shape[0] - 1)
    rights = [(bases[k][:top], turned[k][:, :top], schurs[k]) for k in range(1, cells)]
    faces(y_out_ref, y_rank_ref, y_skel_ref, y_interp_ref, y_coup_ref, rights + [stored(after)])

    @pl.when(layer < layers - 1)
    def _():
        rights = [stored(first + k) for k in range(cells)]
        faces(x_out_ref, x_rank_ref, x_skel_ref, x_interp_ref, x_coup_ref, rights)

    for k in range(cells):
        store_top[first + k] = bases[k][:top]
        store_turned[first + k] = turned[k][:, :top]
        store_schur[first + k] = schurs[k]

    @pl.when(layer == layers - 1)
    def _():
        for k in range(cells):
            last_turned_ref[k] = turned[k][:, top:]
            last_schur_ref[k] = schurs[k]

    @pl.when(layer == 0)
    def _():
        upper, _, opposite = pack_masks(slots)
        pad = packed_ref.shape[1] - cells * half - cells
        extras = []
        for k in range(cells):
            above = schurs[k][:half].astype(F32)
            below = schurs[k][half:].astype(F32)
            packed_ref[chunk, k * half : (k + 1) * half] = jnp.where(upper, above, below).astype(BF)
            extras.append(jnp.sum(jnp.where(opposite, above, F32(0.0)), axis=0, keepdims=True))
        rows = extras + [jnp.zeros((pad, slots), F32)]
        packed_ref[chunk, cells * half :] = jnp.concatenate(rows, axis=0).astype(BF)

    @pl.when(chunk == 0)
    def _():
        edge_ref[layer, 0] = bases[0][:top]
        edge_ref[layer, 1] = schurs[0]

    @pl.when(chunk == chunks - 1)
    def _():
        corner_ref[layer, 0] = turned[cells - 1][:, top:]
        corner_ref[layer, 1] = schurs[cells - 1]


def y_edge_kernel(layers, place, rank_ref, skel_ref, interp_ref, coup_ref, corner_ref, edge_ref, _, out_ref):
    row = place % skel_ref.shape[1]
    pairs = [
        marks_of(skel_ref[i, row : row + 1], rank_ref[i, place], interp_ref[i, 0])
        for i in range(layers)
    ]
    found = kept_cleared([p[0] for p in pairs], [p[1] for p in pairs])
    matrices = []
    for i in range(layers):
        link = dot(scaled(corner_ref[i, 0], coup_ref[i, row : row + 1]), edge_ref[i, 0]).astype(BF)
        matrices.append(face_of(corner_ref[i, 1], link, jnp.transpose(link), edge_ref[i, 1]))
    results = project([jnp.transpose(f) for f in found], matrices, found)
    for i in range(layers):
        out_ref[i, 0] = results[i].astype(BF)


def x_part_kernel(
    cells, layer, rank_ref, skel_ref, interp_ref, coup_ref, turned_ref, schur_ref, top_ref,
    part_ref, lower_ref, lower_turned_ref,
):
    half = top_ref.shape[-2]
    faces = bases_of(cells, layer, pl.program_id(0) * cells, rank_ref, skel_ref, interp_ref)
    turned = [jnp.transpose(f) for f in faces]
    for k in range(cells):
        lower_ref[k] = faces[k][half:]
        lower_turned_ref[k] = turned[k][:, half:]
    marked = [top_ref[k] for k in range(cells)]
    hits = [jnp.where(m == BF(1.0), BF(1.0), BF(0.0)) for m in marked]
    tops = kept_cleared(hits, marked)
    found = [
        dot(scaled(turned_ref[k], coup_ref[0, k : k + 1]), tops[k]).astype(BF)
        for k in range(cells)
    ]
    matrices = [
        face_of(schur_ref[k], found[k], jnp.transpose(found[k]), jnp.zeros_like(found[k]))
        for k in range(cells)
    ]
    results = project(turned, matrices, faces)
    for k in range(cells):
        part_ref[k] = results[k]


def x_last_kernel(cells, part_ref, lower_ref, lower_turned_ref, packed_ref, _, out_ref):
    slots = part_ref.shape[-1]
    half = slots // 2
    upper, same, opposite = pack_masks(slots)
    one, zero, mid = F32(1.0), F32(0.0), F32(0.5)
    top_scale = jnp.where(same, mid, jnp.where(upper, one, zero))
    low_scale = jnp.where(opposite, mid, jnp.where(upper, zero, one))
    opp_scale = jnp.where(opposite, one, zero)
    extras = packed_ref[0, cells * half :].astype(F32)
    schurs = []
    for k in range(cells):
        packed = packed_ref[0, k * half : (k + 1) * half].astype(F32)
        top = packed * top_scale + extras[k : k + 1] * opp_scale
        low = packed * low_scale
        tri = jnp.concatenate([top, low], axis=0).astype(BF)
        schurs.append(tri + jnp.transpose(tri))
    results = project(
        [lower_turned_ref[k] for k in range(cells)], schurs, [lower_ref[k] for k in range(cells)]
    )
    for k in range(cells):
        out_ref[0, k] = (part_ref[k] + results[k]).astype(BF)


def call(kernel, grid, in_specs, out_specs, out_shape, flops, moved, aliases=None, vmem=24, scratch=()):
    return pl.pallas_call(
        kernel,
        grid=grid,
        in_specs=in_specs,
        out_specs=out_specs,
        out_shape=out_shape,
        scratch_shapes=scratch,
        input_output_aliases=aliases or {},
        compiler_params=pltpu.CompilerParams(vmem_limit_bytes=vmem * MIB),
        cost_estimate=pl.CostEstimate(flops=flops, bytes_accessed=moved, transcendentals=0),
    )


def body(
    cell_matrix,
    x_coupling,
    y_coupling,
    cell_interp,
    cell_skel,
    cell_rank,
    x_face_interp,
    x_face_skel,
    x_face_rank,
    y_face_interp,
    y_face_skel,
    y_face_rank,
):
    nx, nj, rows, slots = cell_interp.shape
    half = rows // 2
    fslots = x_face_interp.shape[-1]
    cells = 8 if nj % 8 == 0 else nj
    chunks = nj // cells
    unit = 2 * nx * nj * slots * slots * slots
    smem = pl.BlockSpec(memory_space=pltpu.SMEM)
    shape = jax.ShapeDtypeStruct

    top = call(
        functools.partial(top_kernel, cells),
        (chunks,),
        [
            smem,
            pl.BlockSpec((1, cells, slots), lambda c: (0, c, 0)),
            pl.BlockSpec((1, cells, half, slots), lambda c: (0, c, 0, 0)),
        ],
        pl.BlockSpec((cells, half, slots), lambda c: (c, 0, 0)),
        shape((nj, half, slots), BF),
        0,
        4 * nj * half * slots,
        vmem=56,
    )(cell_rank, cell_skel, cell_interp)
    top_in = passed_along(top, "gx", -1)

    pack_rows = cells * slots // 2 + -(-cells // 16) * 16
    near = max(nx - 2, 0)

    def down(*dims):
        zeros = (0,) * len(dims)
        return pl.BlockSpec((1, cells) + dims, lambda i, c: (nx - 1 - i, chunks - 1 - c) + zeros)

    def down_x(*dims):
        zeros = (0,) * len(dims)

        def place(i, c):
            return (jnp.minimum(nx - 1 - i, near), jnp.where(i == 0, chunks - 1, chunks - 1 - c)) + zeros

        return pl.BlockSpec((1, cells) + dims, place)

    def whole(*dims):
        return pl.BlockSpec(dims, lambda i, c: (0,) * len(dims))

    def from_last(*dims):
        return pl.BlockSpec(
            (cells,) + dims, lambda i, c: (jnp.where(i == 0, chunks - 1 - c, 0),) + (0,) * len(dims)
        )

    x_out, y_out, packed, edge, corner, last_turned, last_schur = call(
        functools.partial(main_kernel, cells, nx, chunks),
        (nx, chunks),
        [
            smem, down(slots), down(rows, slots), down(rows, rows),
            smem, down_x(fslots), down_x(rows, fslots), down_x(half),
            smem, down(fslots), down(rows, fslots), down(half),
        ],
        [
            down_x(fslots, fslots),
            down(fslots, fslots),
            whole(chunks, pack_rows, slots),
            whole(nx, 2, half, slots),
            whole(nx, 2, slots, half),
            from_last(slots, half),
            from_last(slots, slots),
        ],
        [
            shape((nx, nj, fslots, fslots), BF),
            shape((nx, nj, fslots, fslots), BF),
            shape((chunks, pack_rows, slots), BF),
            shape((nx, 2, half, slots), BF),
            shape((nx, 2, slots, half), BF),
            shape((nj, slots, half), BF),
            shape((nj, slots, slots), BF),
        ],
        20 * unit,
        nx * nj * (rows * rows + 3 * rows * slots + 3 * slots * slots) * 2,
        vmem=56,
        scratch=[
            pltpu.VMEM((nj, half, slots), BF),
            pltpu.VMEM((nj, slots, half), BF),
            pltpu.VMEM((nj, slots, slots), BF),
        ],
    )(
        cell_rank, cell_skel, cell_interp, cell_matrix,
        x_face_rank, x_face_skel, x_face_interp, x_coupling,
        y_face_rank, y_face_skel, y_face_interp, y_coupling,
    )
    edge_in = passed_along(edge, "yz", -1)
    packed_in = passed_along(packed, "gx", -1)
    face_bytes = nj * (4 * rows * slots + 4 * slots * slots) * 2

    last = nx - 1
    tail = nj - 1
    group = tail // cells

    def last_block(*dims):
        return pl.BlockSpec((1, cells) + dims, lambda c: (last, c) + (0,) * len(dims))

    def plain(*dims):
        return pl.BlockSpec((cells,) + dims, lambda c: (c,) + (0,) * len(dims))

    part, lower, lower_turned = call(
        functools.partial(x_part_kernel, cells, last),
        (chunks,),
        [
            smem,
            last_block(fslots),
            last_block(rows, fslots),
            last_block(half),
            plain(slots, half),
            plain(slots, slots),
            plain(half, slots),
        ],
        [plain(fslots, fslots), plain(slots, fslots), plain(fslots, slots)],
        [
            shape((nj, fslots, fslots), F32),
            shape((nj, slots, fslots), BF),
            shape((nj, fslots, slots), BF),
        ],
        8 * unit // nx,
        face_bytes,
    )(x_face_rank, x_face_skel, x_face_interp, x_coupling, last_turned, last_schur, top_in)

    y_out = call(
        functools.partial(y_edge_kernel, nx, tail),
        (1,),
        [
            smem,
            pl.BlockSpec((nx, cells, fslots), lambda i: (0, group, 0)),
            pl.BlockSpec((nx, 1, rows, fslots), lambda i: (0, tail, 0, 0)),
            pl.BlockSpec((nx, cells, half), lambda i: (0, group, 0)),
            pl.BlockSpec((nx, 2, slots, half), lambda i: (0, 0, 0, 0)),
            pl.BlockSpec((nx, 2, half, slots), lambda i: (0, 0, 0, 0)),
            pl.BlockSpec(memory_space=pl.ANY),
        ],
        pl.BlockSpec((nx, 1, fslots, fslots), lambda i: (0, tail, 0, 0)),
        shape((nx, nj, fslots, fslots), BF),
        8 * unit // nj,
        nx * face_bytes // nj,
        {6: 0},
    )(y_face_rank, y_face_skel, y_face_interp, y_coupling, corner, edge_in, y_out)

    x_out = call(
        functools.partial(x_last_kernel, cells),
        (chunks,),
        [
            plain(fslots, fslots),
            plain(slots, fslots),
            plain(fslots, slots),
            pl.BlockSpec((1, pack_rows, slots), lambda c: (c, 0, 0)),
            pl.BlockSpec(memory_space=pl.ANY),
        ],
        last_block(fslots, fslots),
        shape((nx, nj, fslots, fslots), BF),
        3 * unit // nx,
        nj * slots * slots * 11,
        {4: 0},
    )(part, lower, lower_turned, packed_in, x_out)
    return (x_out, y_out)


def solution(mesh):
    return jax.shard_map(
        body,
        mesh=mesh,
        in_specs=(
            P("gx", "yz", None, None),
            P("gx", "yz", None),
            P("gx", "yz", None),
            P("gx", "yz", None, None),
            P("gx", "yz", None),
            P("gx", "yz"),
            P("gx", "yz", None, None),
            P("gx", "yz", None),
            P("gx", "yz"),
            P("gx", "yz", None, None),
            P("gx", "yz", None),
            P("gx", "yz"),
        ),
        out_specs=(P("gx", "yz", None, None), P("gx", "yz", None, None)),
        check_vma=False,
    )
```

```python
import functools

import jax
import jax.numpy as jnp
from jax import lax
from jax.experimental import pallas as pl
from jax.experimental.pallas import tpu as pltpu
from jax.sharding import PartitionSpec as P

BF = jnp.bfloat16
F32 = jnp.float32
MIB = 1024 * 1024


def passed_along(x, axis, by):
    devices = lax.axis_size(axis)
    pairs = [(i, i + by) for i in range(devices) if 0 <= i + by < devices]
    return lax.ppermute(x, axis, pairs)


def dot(a, b):
    return lax.dot_general(a, b, (((1,), (0,)), ((), ())), preferred_element_type=F32)


def marks_of(skel_row, rank, interp):
    rows, slots = interp.shape
    live = lax.broadcasted_iota(jnp.int32, (1, slots), 1) < rank
    picked_row = jnp.where(live, skel_row, -1).astype(F32).astype(BF)
    row = lax.broadcasted_iota(jnp.int32, (rows, slots), 0).astype(F32).astype(BF)
    live_row = jnp.where(live, F32(1.0), F32(0.0)).astype(BF)
    hit = jnp.where(row == picked_row, BF(1.0), BF(0.0))
    return hit, interp * live_row


def kept_cleared(hits, interps):
    slots = hits[0].shape[-1]
    ones = jnp.ones((slots, slots), BF)
    counts = [dot(hit, ones).astype(BF) for hit in hits]
    return [h + z * (BF(1.0) - n) for h, z, n in zip(hits, interps, counts)]


def bases_of(cells, layer, first, rank_ref, skel_ref, interp_ref):
    pairs = [
        marks_of(skel_ref[0, k : k + 1], rank_ref[layer, first + k], interp_ref[0, k])
        for k in range(cells)
    ]
    return kept_cleared([p[0] for p in pairs], [p[1] for p in pairs])


def scaled(turned, conduct):
    return turned * -conduct


def face_of(left, link, link_t, right):
    upper = jnp.concatenate([left, link], axis=1)
    lower = jnp.concatenate([link_t, right], axis=1)
    return jnp.concatenate([upper, lower], axis=0)


def project(turned, matrices, bases):
    inner = [dot(t, m).astype(BF) for t, m in zip(turned, matrices)]
    return [dot(i, b) for i, b in zip(inner, bases)]


def top_kernel(cells, rank_hbm, skel_hbm, interp_hbm, out_ref, rank_ref, skel_ref, held, small_sems, sems):
    count, half, _ = out_ref.shape
    small = [
        pltpu.make_async_copy(rank_hbm, rank_ref, small_sems.at[0]),
        pltpu.make_async_copy(skel_hbm.at[0], skel_ref, small_sems.at[1]),
    ]
    copies = []
    for c in range(count // cells):
        group = pl.ds(c * cells, cells)
        copies.append(
            pltpu.make_async_copy(
                interp_hbm.at[0, group, pl.ds(0, half)], held.at[group], sems.at[c]
            )
        )
    for copy in small + copies:
        copy.start()
    for copy in small:
        copy.wait()
    for c in range(count // cells):
        copies[c].wait()
        for k in range(c * cells, (c + 1) * cells):
            hit, interp = marks_of(skel_ref[k : k + 1], rank_ref[0, k], held[k])
            out_ref[k] = hit + interp * (BF(1.0) - hit)


def pack_masks(size):
    half = size // 2
    row = lax.broadcasted_iota(jnp.int32, (half, size), 0)
    lane = lax.broadcasted_iota(jnp.int32, (half, size), 1)
    ahead = lane - row
    upper = (ahead >= 0) & (ahead < half)
    return upper, ahead == 0, ahead == half


def main_kernel(
    cells, layers, chunks,
    rank_ref, skel_ref, interp_ref, matrix_ref,
    x_rank_ref, x_skel_ref, x_interp_ref, x_coup_ref,
    y_rank_ref, y_skel_ref, y_interp_ref, y_coup_ref,
    x_out_ref, y_out_ref, packed_ref, edge_ref, corner_ref, last_turned_ref, last_schur_ref,
    store_top, store_turned, store_schur,
):
    layer = layers - 1 - pl.program_id(0)
    chunk = chunks - 1 - pl.program_id(1)
    first = chunk * cells
    slots = skel_ref.shape[-1]
    half = slots // 2
    top = interp_ref.shape[2] // 2

    bases = bases_of(cells, layer, first, rank_ref, skel_ref, interp_ref)
    turned = [jnp.transpose(b) for b in bases]
    schurs = project(turned, [matrix_ref[0, k] for k in range(cells)], bases)
    schurs = [s.astype(BF) for s in schurs]

    def faces(out_ref, f_rank_ref, f_skel_ref, f_interp_ref, coup_ref, rights):
        found = bases_of(cells, layer, first, f_rank_ref, f_skel_ref, f_interp_ref)
        found_turned = [jnp.transpose(f) for f in found]
        matrices = []
        for k in range(cells):
            right_top, right_turned, right = rights[k]
            conduct = coup_ref[0, k : k + 1]
            link = dot(scaled(turned[k][:, top:], conduct), right_top).astype(BF)
            link_t = dot(scaled(right_turned, conduct), bases[k][top:]).astype(BF)
            matrices.append(face_of(schurs[k], link, link_t, right))
        results = project(found_turned, matrices, found)
        for k in range(cells):
            out_ref[0, k] = results[k].astype(BF)

    def stored(place):
        return store_top[place], store_turned[place], store_schur[place]

    after = jnp.minimum(first + cells, store_schur.shape[0] - 1)
    rights = [(bases[k][:top], turned[k][:, :top], schurs[k]) for k in range(1, cells)]
    faces(y_out_ref, y_rank_ref, y_skel_ref, y_interp_ref, y_coup_ref, rights + [stored(after)])

    @pl.when(layer < layers - 1)
    def _():
        rights = [stored(first + k) for k in range(cells)]
        faces(x_out_ref, x_rank_ref, x_skel_ref, x_interp_ref, x_coup_ref, rights)

    for k in range(cells):
        store_top[first + k] = bases[k][:top]
        store_turned[first + k] = turned[k][:, :top]
        store_schur[first + k] = schurs[k]

    @pl.when(layer == layers - 1)
    def _():
        for k in range(cells):
            last_turned_ref[k] = turned[k][:, top:]
            last_schur_ref[k] = schurs[k]

    @pl.when(layer == 0)
    def _():
        upper, _, opposite = pack_masks(slots)
        pad = packed_ref.shape[1] - cells * half - cells
        extras = []
        for k in range(cells):
            above = schurs[k][:half].astype(F32)
            below = schurs[k][half:].astype(F32)
            packed_ref[chunk, k * half : (k + 1) * half] = jnp.where(upper, above, below).astype(BF)
            extras.append(jnp.sum(jnp.where(opposite, above, F32(0.0)), axis=0, keepdims=True))
        rows = extras + [jnp.zeros((pad, slots), F32)]
        packed_ref[chunk, cells * half :] = jnp.concatenate(rows, axis=0).astype(BF)

    @pl.when(chunk == 0)
    def _():
        edge_ref[layer, 0] = bases[0][:top]
        edge_ref[layer, 1] = schurs[0]

    @pl.when(chunk == chunks - 1)
    def _():
        corner_ref[layer, 0] = turned[cells - 1][:, top:]
        corner_ref[layer, 1] = schurs[cells - 1]


def y_edge_kernel(layers, place, rank_ref, skel_ref, interp_ref, coup_ref, corner_ref, edge_ref, _, out_ref):
    row = place % skel_ref.shape[1]
    pairs = [
        marks_of(skel_ref[i, row : row + 1], rank_ref[i, place], interp_ref[i, 0])
        for i in range(layers)
    ]
    found = kept_cleared([p[0] for p in pairs], [p[1] for p in pairs])
    matrices = []
    for i in range(layers):
        link = dot(scaled(corner_ref[i, 0], coup_ref[i, row : row + 1]), edge_ref[i, 0]).astype(BF)
        matrices.append(face_of(corner_ref[i, 1], link, jnp.transpose(link), edge_ref[i, 1]))
    results = project([jnp.transpose(f) for f in found], matrices, found)
    for i in range(layers):
        out_ref[i, 0] = results[i].astype(BF)


def x_part_kernel(
    cells, layer, rank_ref, skel_ref, interp_ref, coup_ref, turned_ref, schur_ref, top_ref,
    part_ref, lower_ref, lower_turned_ref,
):
    half = top_ref.shape[-2]
    faces = bases_of(cells, layer, pl.program_id(0) * cells, rank_ref, skel_ref, interp_ref)
    turned = [jnp.transpose(f) for f in faces]
    for k in range(cells):
        lower_ref[k] = faces[k][half:]
        lower_turned_ref[k] = turned[k][:, half:]
    marked = [top_ref[k] for k in range(cells)]
    hits = [jnp.where(m == BF(1.0), BF(1.0), BF(0.0)) for m in marked]
    tops = kept_cleared(hits, marked)
    found = [
        dot(scaled(turned_ref[k], coup_ref[0, k : k + 1]), tops[k]).astype(BF)
        for k in range(cells)
    ]
    matrices = [
        face_of(schur_ref[k], found[k], jnp.transpose(found[k]), jnp.zeros_like(found[k]))
        for k in range(cells)
    ]
    results = project(turned, matrices, faces)
    for k in range(cells):
        part_ref[k] = results[k]


def x_last_kernel(
    cells, layer, part_ref, lower_ref, lower_turned_ref, packed_ref, _, out_ref, held, sems
):
    count, _, slots = part_ref.shape
    half = slots // 2
    upper, same, opposite = pack_masks(slots)
    one, zero, mid = F32(1.0), F32(0.0), F32(0.5)
    top_scale = jnp.where(same, mid, jnp.where(upper, one, zero))
    low_scale = jnp.where(opposite, mid, jnp.where(upper, zero, one))
    opp_scale = jnp.where(opposite, one, zero)
    copies = []
    for c in range(count // cells):
        extras = packed_ref[c, cells * half :].astype(F32)
        places = range(c * cells, (c + 1) * cells)
        schurs = []
        for k in range(cells):
            packed = packed_ref[c, k * half : (k + 1) * half].astype(F32)
            top = packed * top_scale + extras[k : k + 1] * opp_scale
            low = packed * low_scale
            tri = jnp.concatenate([top, low], axis=0).astype(BF)
            schurs.append(tri + jnp.transpose(tri))
        results = project(
            [lower_turned_ref[k] for k in places], schurs, [lower_ref[k] for k in places]
        )
        for k, result in zip(places, results):
            held[k] = (part_ref[k] + result).astype(BF)
        group = pl.ds(c * cells, cells)
        copies.append(
            pltpu.make_async_copy(held.at[group], out_ref.at[layer, group], sems.at[c])
        )
        copies[c].start()
    for copy in copies:
        copy.wait()


def call(kernel, grid, in_specs, out_specs, out_shape, flops, moved, aliases=None, vmem=24, scratch=()):
    return pl.pallas_call(
        kernel,
        grid=grid,
        in_specs=in_specs,
        out_specs=out_specs,
        out_shape=out_shape,
        scratch_shapes=scratch,
        input_output_aliases=aliases or {},
        compiler_params=pltpu.CompilerParams(vmem_limit_bytes=vmem * MIB),
        cost_estimate=pl.CostEstimate(flops=flops, bytes_accessed=moved, transcendentals=0),
    )


def in_hbm(x):
    return pltpu.with_memory_space_constraint(x, pltpu.HBM)


def body(
    cell_matrix,
    x_coupling,
    y_coupling,
    cell_interp,
    cell_skel,
    cell_rank,
    x_face_interp,
    x_face_skel,
    x_face_rank,
    y_face_interp,
    y_face_skel,
    y_face_rank,
):
    nx, nj, rows, slots = cell_interp.shape
    half = rows // 2
    fslots = x_face_interp.shape[-1]
    cells = 8 if nj % 8 == 0 else nj
    chunks = nj // cells
    unit = 2 * nx * nj * slots * slots * slots
    smem = pl.BlockSpec(memory_space=pltpu.SMEM)
    shape = jax.ShapeDtypeStruct

    hbm = pl.BlockSpec(memory_space=pltpu.HBM)
    vmem = pl.BlockSpec(memory_space=pltpu.VMEM)
    top = call(
        functools.partial(top_kernel, cells),
        (),
        [hbm, hbm, hbm],
        vmem,
        shape((nj, half, slots), BF),
        0,
        4 * nj * half * slots,
        vmem=8,
        scratch=[
            pltpu.SMEM((nx, nj), jnp.int32),
            pltpu.VMEM((nj, slots), jnp.int32),
            pltpu.VMEM((nj, half, slots), BF),
            pltpu.SemaphoreType.DMA((2,)),
            pltpu.SemaphoreType.DMA((chunks,)),
        ],
    )(in_hbm(cell_rank), in_hbm(cell_skel), in_hbm(cell_interp))
    top_in = passed_along(top, "gx", -1)

    pack_rows = cells * slots // 2 + -(-cells // 16) * 16
    near = max(nx - 2, 0)

    def down(*dims):
        zeros = (0,) * len(dims)
        return pl.BlockSpec((1, cells) + dims, lambda i, c: (nx - 1 - i, chunks - 1 - c) + zeros)

    def down_x(*dims):
        zeros = (0,) * len(dims)

        def place(i, c):
            return (jnp.minimum(nx - 1 - i, near), jnp.where(i == 0, chunks - 1, chunks - 1 - c)) + zeros

        return pl.BlockSpec((1, cells) + dims, place)

    def whole(*dims):
        return pl.BlockSpec(dims, lambda i, c: (0,) * len(dims))

    def from_last(*dims):
        return pl.BlockSpec(
            (cells,) + dims, lambda i, c: (jnp.where(i == 0, chunks - 1 - c, 0),) + (0,) * len(dims)
        )

    x_out, y_out, packed, edge, corner, last_turned, last_schur = call(
        functools.partial(main_kernel, cells, nx, chunks),
        (nx, chunks),
        [
            smem, down(slots), down(rows, slots), down(rows, rows),
            smem, down_x(fslots), down_x(rows, fslots), down_x(half),
            smem, down(fslots), down(rows, fslots), down(half),
        ],
        [
            down_x(fslots, fslots),
            down(fslots, fslots),
            whole(chunks, pack_rows, slots),
            whole(nx, 2, half, slots),
            whole(nx, 2, slots, half),
            from_last(slots, half),
            from_last(slots, slots),
        ],
        [
            shape((nx, nj, fslots, fslots), BF),
            shape((nx, nj, fslots, fslots), BF),
            shape((chunks, pack_rows, slots), BF),
            shape((nx, 2, half, slots), BF),
            shape((nx, 2, slots, half), BF),
            shape((nj, slots, half), BF),
            shape((nj, slots, slots), BF),
        ],
        20 * unit,
        nx * nj * (rows * rows + 3 * rows * slots + 3 * slots * slots) * 2,
        vmem=32,
        scratch=[
            pltpu.VMEM((nj, half, slots), BF),
            pltpu.VMEM((nj, slots, half), BF),
            pltpu.VMEM((nj, slots, slots), BF),
        ],
    )(
        cell_rank, in_hbm(cell_skel), in_hbm(cell_interp), in_hbm(cell_matrix),
        x_face_rank, in_hbm(x_face_skel), in_hbm(x_face_interp), in_hbm(x_coupling),
        y_face_rank, in_hbm(y_face_skel), in_hbm(y_face_interp), in_hbm(y_coupling),
    )
    edge_in = passed_along(edge, "yz", -1)
    packed_in = passed_along(packed, "gx", -1)
    face_bytes = nj * (4 * rows * slots + 4 * slots * slots) * 2

    last = nx - 1
    tail = nj - 1
    group = tail // cells

    def last_block(*dims):
        return pl.BlockSpec((1, cells) + dims, lambda c: (last, c) + (0,) * len(dims))

    def plain(*dims):
        return pl.BlockSpec((cells,) + dims, lambda c: (c,) + (0,) * len(dims))

    part, lower, lower_turned = call(
        functools.partial(x_part_kernel, cells, last),
        (chunks,),
        [
            smem,
            last_block(fslots),
            last_block(rows, fslots),
            last_block(half),
            plain(slots, half),
            plain(slots, slots),
            plain(half, slots),
        ],
        [plain(fslots, fslots), plain(slots, fslots), plain(fslots, slots)],
        [
            shape((nj, fslots, fslots), F32),
            shape((nj, slots, fslots), BF),
            shape((nj, fslots, slots), BF),
        ],
        8 * unit // nx,
        face_bytes,
    )(x_face_rank, x_face_skel, x_face_interp, x_coupling, last_turned, last_schur, top_in)

    edge_in, part = lax.optimization_barrier((edge_in, part))
    y_out = call(
        functools.partial(y_edge_kernel, nx, tail),
        (1,),
        [
            smem,
            pl.BlockSpec((nx, cells, fslots), lambda i: (0, group, 0)),
            pl.BlockSpec((nx, 1, rows, fslots), lambda i: (0, tail, 0, 0)),
            pl.BlockSpec((nx, cells, half), lambda i: (0, group, 0)),
            pl.BlockSpec((nx, 2, slots, half), lambda i: (0, 0, 0, 0)),
            pl.BlockSpec((nx, 2, half, slots), lambda i: (0, 0, 0, 0)),
            pl.BlockSpec(memory_space=pl.ANY),
        ],
        pl.BlockSpec((nx, 1, fslots, fslots), lambda i: (0, tail, 0, 0)),
        shape((nx, nj, fslots, fslots), BF),
        8 * unit // nj,
        nx * face_bytes // nj,
        {6: 0},
    )(y_face_rank, y_face_skel, in_hbm(y_face_interp), y_coupling, corner, edge_in, y_out)

    x_out = call(
        functools.partial(x_last_kernel, cells, last),
        (),
        [vmem, vmem, vmem, vmem, hbm],
        hbm,
        shape((nx, nj, fslots, fslots), BF),
        3 * unit // nx,
        nj * slots * slots * 11,
        {4: 0},
        scratch=[pltpu.VMEM((nj, fslots, fslots), BF), pltpu.SemaphoreType.DMA((chunks,))],
    )(part, lower, lower_turned, packed_in, x_out)
    return (x_out, y_out)


def solution(mesh):
    return jax.shard_map(
        body,
        mesh=mesh,
        in_specs=(
            P("gx", "yz", None, None),
            P("gx", "yz", None),
            P("gx", "yz", None),
            P("gx", "yz", None, None),
            P("gx", "yz", None),
            P("gx", "yz"),
            P("gx", "yz", None, None),
            P("gx", "yz", None),
            P("gx", "yz"),
            P("gx", "yz", None, None),
            P("gx", "yz", None),
            P("gx", "yz"),
        ),
        out_specs=(P("gx", "yz", None, None), P("gx", "yz", None, None)),
        check_vma=False,
    )
```

```python
import functools

import jax
import jax.numpy as jnp
from jax import lax
from jax.experimental import pallas as pl
from jax.experimental.pallas import tpu as pltpu
from jax.sharding import PartitionSpec as P

BF = jnp.bfloat16
F32 = jnp.float32
MIB = 1024 * 1024


def passed_along(x, axis, by):
    devices = lax.axis_size(axis)
    pairs = [(i, i + by) for i in range(devices) if 0 <= i + by < devices]
    return lax.ppermute(x, axis, pairs)


def dot(a, b):
    return lax.dot_general(a, b, (((1,), (0,)), ((), ())), preferred_element_type=F32)


def marks_of(skel_row, rank, interp):
    rows, slots = interp.shape
    live = lax.broadcasted_iota(jnp.int32, (1, slots), 1) < rank
    picked_row = jnp.where(live, skel_row, -1).astype(F32).astype(BF)
    row = lax.broadcasted_iota(jnp.int32, (rows, slots), 0).astype(F32).astype(BF)
    live_row = jnp.where(live, F32(1.0), F32(0.0)).astype(BF)
    return row == picked_row, interp * live_row


def kept_cleared(hits, interps):
    slots = hits[0].shape[-1]
    ones = jnp.ones((slots, slots), BF)
    hits = [jnp.where(hit, BF(1.0), BF(0.0)) for hit in hits]
    counts = [dot(hit, ones).astype(BF) for hit in hits]
    return [h + z * (BF(1.0) - n) for h, z, n in zip(hits, interps, counts)]


def bases_of(cells, layer, first, rank_ref, skel_ref, interp_ref):
    pairs = [
        marks_of(skel_ref[0, k : k + 1], rank_ref[layer, first + k], interp_ref[0, k])
        for k in range(cells)
    ]
    return kept_cleared([p[0] for p in pairs], [p[1] for p in pairs])


def scaled(turned, conduct):
    return turned * -conduct


def face_of(left, link, link_t, right):
    upper = jnp.concatenate([left, link], axis=1)
    lower = jnp.concatenate([link_t, right], axis=1)
    return jnp.concatenate([upper, lower], axis=0)


def project(turned, matrices, bases):
    inner = [dot(t, m).astype(BF) for t, m in zip(turned, matrices)]
    return [dot(i, b) for i, b in zip(inner, bases)]


def top_kernel(cells, rank_hbm, skel_hbm, interp_hbm, out_ref, rank_ref, skel_ref, held, small_sems, sems):
    count, half, _ = out_ref.shape
    small = [
        pltpu.make_async_copy(rank_hbm, rank_ref, small_sems.at[0]),
        pltpu.make_async_copy(skel_hbm.at[0], skel_ref, small_sems.at[1]),
    ]
    copies = []
    for c in range(count // cells):
        group = pl.ds(c * cells, cells)
        copies.append(
            pltpu.make_async_copy(
                interp_hbm.at[0, group, pl.ds(0, half)], held.at[group], sems.at[c]
            )
        )
    for copy in small + copies:
        copy.start()
    for copy in small:
        copy.wait()
    for c in range(count // cells):
        copies[c].wait()
        for k in range(c * cells, (c + 1) * cells):
            hit, interp = marks_of(skel_ref[k : k + 1], rank_ref[0, k], held[k])
            out_ref[k] = jnp.where(hit, BF(1.0), interp)


def pack_masks(size):
    half = size // 2
    row = lax.broadcasted_iota(jnp.int32, (half, size), 0)
    lane = lax.broadcasted_iota(jnp.int32, (half, size), 1)
    ahead = lane - row
    upper = (ahead >= 0) & (ahead < half)
    return upper, ahead == 0, ahead == half


def main_kernel(
    cells, layers, chunks,
    rank_ref, skel_ref, interp_ref, matrix_ref,
    x_rank_ref, x_skel_ref, x_interp_ref, x_coup_ref,
    y_rank_ref, y_skel_ref, y_interp_ref, y_coup_ref,
    x_out_ref, y_out_ref, packed_ref, packed_last_ref, edge_ref, corner_ref, last_turned_ref, last_schur_ref,
    store_top, store_turned, store_schur, store_extra,
):
    layer = layers - 1 - pl.program_id(0)
    chunk = chunks - 1 - pl.program_id(1)
    first = chunk * cells
    slots = skel_ref.shape[-1]
    half = slots // 2
    top = interp_ref.shape[2] // 2

    bases = bases_of(cells, layer, first, rank_ref, skel_ref, interp_ref)
    turned = [jnp.transpose(b) for b in bases]
    schurs = project(turned, [matrix_ref[0, k] for k in range(cells)], bases)
    schurs = [s.astype(BF) for s in schurs]

    def faces(out_ref, f_rank_ref, f_skel_ref, f_interp_ref, coup_ref, rights):
        found = bases_of(cells, layer, first, f_rank_ref, f_skel_ref, f_interp_ref)
        found_turned = [jnp.transpose(f) for f in found]
        matrices = []
        for k in range(cells):
            right_top, right_turned, right = rights[k]
            conduct = coup_ref[0, k : k + 1]
            link = dot(scaled(turned[k][:, top:], conduct), right_top).astype(BF)
            link_t = dot(scaled(right_turned, conduct), bases[k][top:]).astype(BF)
            matrices.append(face_of(schurs[k], link, link_t, right))
        results = project(found_turned, matrices, found)
        for k in range(cells):
            out_ref[0, k] = results[k].astype(BF)

    def stored(place):
        return store_top[place], store_turned[place], store_schur[place]

    after = jnp.minimum(first + cells, store_schur.shape[0] - 1)
    rights = [(bases[k][:top], turned[k][:, :top], schurs[k]) for k in range(1, cells)]
    faces(y_out_ref, y_rank_ref, y_skel_ref, y_interp_ref, y_coup_ref, rights + [stored(after)])

    @pl.when(layer < layers - 1)
    def _():
        rights = [stored(first + k) for k in range(cells)]
        faces(x_out_ref, x_rank_ref, x_skel_ref, x_interp_ref, x_coup_ref, rights)

    for k in range(cells):
        store_top[first + k] = bases[k][:top]
        store_turned[first + k] = turned[k][:, :top]
        store_schur[first + k] = schurs[k]

    @pl.when(layer == layers - 1)
    def _():
        for k in range(cells):
            last_turned_ref[k] = turned[k][:, top:]
            last_schur_ref[k] = schurs[k]

    @pl.when(layer == 0)
    def _():
        upper, same, opposite = pack_masks(slots)

        def put(packed_ref, start):
            for k in range(cells):
                above, below = schurs[k][:half].astype(F32), schurs[k][half:].astype(F32)
                place = pl.ds(pl.multiple_of(start + k * half, half), half)
                packed_ref[place] = jnp.where(upper, above, below).astype(BF)

        @pl.when(chunk < chunks - 1)
        def _():
            put(packed_ref, chunk * (cells * half))

        @pl.when(chunk == chunks - 1)
        def _():
            put(packed_last_ref, 0)

        for p in range(0, cells, 2):
            extra = jnp.where(opposite, schurs[p][:half].astype(F32), F32(0.0))
            if p + 1 < cells:
                extra += jnp.where(same, schurs[p + 1][half:].astype(F32), F32(0.0))
            store_extra[chunk, p // 2 : p // 2 + 1] = jnp.sum(extra, axis=0, keepdims=True)

        @pl.when(chunk == 0)
        def _():
            pairs = -(-cells // 2)
            for ref, places in ((packed_ref, range(chunks - 1)), (packed_last_ref, [chunks - 1])):
                start = len(places) * cells * half
                rows = [store_extra[c, :pairs] for c in places]
                pad = ref.shape[0] - start - pairs * len(places)
                if pad:
                    rows.append(jnp.zeros((pad, slots), F32))
                ref[start:] = jnp.concatenate(rows, axis=0).astype(BF)

    @pl.when(chunk == 0)
    def _():
        edge_ref[layer, 0] = bases[0][:top]
        edge_ref[layer, 1] = schurs[0]

    @pl.when(chunk == chunks - 1)
    def _():
        corner_ref[layer, 0] = turned[cells - 1][:, top:]
        corner_ref[layer, 1] = schurs[cells - 1]


def y_edge_kernel(layers, place, rank_ref, skel_ref, interp_ref, coup_ref, corner_ref, edge_ref, _, out_ref):
    row = place % skel_ref.shape[1]
    pairs = [
        marks_of(skel_ref[i, row : row + 1], rank_ref[i, place], interp_ref[i, 0])
        for i in range(layers)
    ]
    found = kept_cleared([p[0] for p in pairs], [p[1] for p in pairs])
    matrices = []
    for i in range(layers):
        link = dot(scaled(corner_ref[i, 0], coup_ref[i, row : row + 1]), edge_ref[i, 0]).astype(BF)
        matrices.append(face_of(corner_ref[i, 1], link, jnp.transpose(link), edge_ref[i, 1]))
    results = project([jnp.transpose(f) for f in found], matrices, found)
    for i in range(layers):
        out_ref[i, 0] = results[i].astype(BF)


def x_part_kernel(
    cells, layer, rank_ref, skel_ref, interp_ref, coup_ref, turned_ref, schur_ref, top_ref,
    part_ref, lower_ref, lower_turned_ref,
):
    half = top_ref.shape[-2]
    faces = bases_of(cells, layer, pl.program_id(0) * cells, rank_ref, skel_ref, interp_ref)
    turned = [jnp.transpose(f) for f in faces]
    for k in range(cells):
        lower_ref[k] = faces[k][half:]
        lower_turned_ref[k] = turned[k][:, half:]
    marked = [top_ref[k] for k in range(cells)]
    tops = kept_cleared([m == BF(1.0) for m in marked], marked)
    found = [
        dot(scaled(turned_ref[k], coup_ref[0, k : k + 1]), tops[k]).astype(BF)
        for k in range(cells)
    ]
    matrices = [
        face_of(schur_ref[k], found[k], jnp.transpose(found[k]), jnp.zeros_like(found[k]))
        for k in range(cells)
    ]
    results = project(turned, matrices, faces)
    for k in range(cells):
        part_ref[k] = results[k]


def x_last_kernel(
    cells, layer, places, part_ref, lower_ref, lower_turned_ref, packed_ref, _, out_ref, held, sems
):
    slots = part_ref.shape[-1]
    half = slots // 2
    upper, same, opposite = pack_masks(slots)
    one, zero, mid = F32(1.0), F32(0.0), F32(0.5)
    top_scale = jnp.where(same, mid, jnp.where(upper, one, zero))
    low_scale = jnp.where(opposite, mid, jnp.where(upper, zero, one))
    same_scale = jnp.where(same, one, zero)
    opposite_scale = jnp.where(opposite, one, zero)
    extras = packed_ref[len(places) * cells * half :].astype(F32)
    pairs = -(-cells // 2)
    copies = []
    for n, c in enumerate(places):
        group = range(c * cells, (c + 1) * cells)
        schurs = []
        for k in range(cells):
            start = (n * cells + k) * half
            packed = packed_ref[start : start + half].astype(F32)
            extra = extras[n * pairs + k // 2 : n * pairs + k // 2 + 1]
            top, low = packed * top_scale, packed * low_scale
            if k % 2 == 0:
                top += extra * opposite_scale
            else:
                low += extra * same_scale
            tri = jnp.concatenate([top, low], axis=0).astype(BF)
            schurs.append(tri + jnp.transpose(tri))
        results = project(
            [lower_turned_ref[k] for k in group], schurs, [lower_ref[k] for k in group]
        )
        for k, result in enumerate(results):
            held[n * cells + k] = (part_ref[c * cells + k] + result).astype(BF)
        copies.append(
            pltpu.make_async_copy(
                held.at[pl.ds(n * cells, cells)],
                out_ref.at[layer, pl.ds(c * cells, cells)],
                sems.at[n],
            )
        )
        copies[n].start()
    for copy in copies:
        copy.wait()


def call(kernel, grid, in_specs, out_specs, out_shape, flops, moved, aliases=None, vmem=24, scratch=()):
    return pl.pallas_call(
        kernel,
        grid=grid,
        in_specs=in_specs,
        out_specs=out_specs,
        out_shape=out_shape,
        scratch_shapes=scratch,
        input_output_aliases=aliases or {},
        compiler_params=pltpu.CompilerParams(vmem_limit_bytes=vmem * MIB),
        cost_estimate=pl.CostEstimate(flops=flops, bytes_accessed=moved, transcendentals=0),
    )


def in_hbm(x):
    return pltpu.with_memory_space_constraint(x, pltpu.HBM)


def body(
    cell_matrix,
    x_coupling,
    y_coupling,
    cell_interp,
    cell_skel,
    cell_rank,
    x_face_interp,
    x_face_skel,
    x_face_rank,
    y_face_interp,
    y_face_skel,
    y_face_rank,
):
    nx, nj, rows, slots = cell_interp.shape
    half = rows // 2
    fslots = x_face_interp.shape[-1]
    cells = next(n for n in (8, 4, 2, 1) if nj % n == 0 and nj > n)
    chunks = nj // cells
    unit = 2 * nx * nj * slots * slots * slots
    smem = pl.BlockSpec(memory_space=pltpu.SMEM)
    shape = jax.ShapeDtypeStruct

    hbm = pl.BlockSpec(memory_space=pltpu.HBM)
    vmem = pl.BlockSpec(memory_space=pltpu.VMEM)
    top = call(
        functools.partial(top_kernel, cells),
        (),
        [hbm, hbm, hbm],
        vmem,
        shape((nj, half, slots), BF),
        0,
        4 * nj * half * slots,
        vmem=8,
        scratch=[
            pltpu.SMEM((nx, nj), jnp.int32),
            pltpu.VMEM((nj, slots), jnp.int32),
            pltpu.VMEM((nj, half, slots), BF),
            pltpu.SemaphoreType.DMA((2,)),
            pltpu.SemaphoreType.DMA((chunks,)),
        ],
    )(in_hbm(cell_rank), in_hbm(cell_skel), in_hbm(cell_interp))
    top_in = passed_along(top, "gx", -1)


    def pack_rows(count):
        extra = count * -(-cells // 2)
        return count * cells * slots // 2 + -(-extra // 16) * 16

    near = max(nx - 2, 0)

    def down(*dims):
        zeros = (0,) * len(dims)
        return pl.BlockSpec((1, cells) + dims, lambda i, c: (nx - 1 - i, chunks - 1 - c) + zeros)

    def down_x(*dims):
        zeros = (0,) * len(dims)

        def place(i, c):
            return (jnp.minimum(nx - 1 - i, near), jnp.where(i == 0, chunks - 1, chunks - 1 - c)) + zeros

        return pl.BlockSpec((1, cells) + dims, place)

    def whole(*dims):
        return pl.BlockSpec(dims, lambda i, c: (0,) * len(dims))

    def from_last(*dims):
        return pl.BlockSpec(
            (cells,) + dims, lambda i, c: (jnp.where(i == 0, chunks - 1 - c, 0),) + (0,) * len(dims)
        )

    x_out, y_out, packed, packed_last, edge, corner, last_turned, last_schur = call(
        functools.partial(main_kernel, cells, nx, chunks),
        (nx, chunks),
        [
            smem, down(slots), down(rows, slots), down(rows, rows),
            smem, down_x(fslots), down_x(rows, fslots), down_x(half),
            smem, down(fslots), down(rows, fslots), down(half),
        ],
        [
            down_x(fslots, fslots),
            down(fslots, fslots),
            whole(pack_rows(chunks - 1), slots),
            whole(pack_rows(1), slots),
            whole(nx, 2, half, slots),
            whole(nx, 2, slots, half),
            from_last(slots, half),
            from_last(slots, slots),
        ],
        [
            shape((nx, nj, fslots, fslots), BF),
            shape((nx, nj, fslots, fslots), BF),
            shape((pack_rows(chunks - 1), slots), BF),
            shape((pack_rows(1), slots), BF),
            shape((nx, 2, half, slots), BF),
            shape((nx, 2, slots, half), BF),
            shape((nj, slots, half), BF),
            shape((nj, slots, slots), BF),
        ],
        20 * unit,
        nx * nj * (rows * rows + 3 * rows * slots + 3 * slots * slots) * 2,
        vmem=32,
        scratch=[
            pltpu.VMEM((nj, half, slots), BF),
            pltpu.VMEM((nj, slots, half), BF),
            pltpu.VMEM((nj, slots, slots), BF),
            pltpu.VMEM((chunks, cells, slots), F32),
        ],
    )(
        cell_rank, in_hbm(cell_skel), in_hbm(cell_interp), in_hbm(cell_matrix),
        x_face_rank, in_hbm(x_face_skel), in_hbm(x_face_interp), in_hbm(x_coupling),
        y_face_rank, in_hbm(y_face_skel), in_hbm(y_face_interp), in_hbm(y_coupling),
    )
    edge_in = passed_along(edge, "yz", -1)
    packed_in = passed_along(packed, "gx", -1)
    face_bytes = nj * (4 * rows * slots + 4 * slots * slots) * 2

    last = nx - 1
    tail = nj - 1
    group = tail // cells

    def last_block(*dims):
        return pl.BlockSpec((1, cells) + dims, lambda c: (last, c) + (0,) * len(dims))

    def plain(*dims):
        return pl.BlockSpec((cells,) + dims, lambda c: (c,) + (0,) * len(dims))

    part, lower, lower_turned = call(
        functools.partial(x_part_kernel, cells, last),
        (chunks,),
        [
            smem,
            last_block(fslots),
            last_block(rows, fslots),
            last_block(half),
            plain(slots, half),
            plain(slots, slots),
            plain(half, slots),
        ],
        [plain(fslots, fslots), plain(slots, fslots), plain(fslots, slots)],
        [
            shape((nj, fslots, fslots), F32),
            shape((nj, slots, fslots), BF),
            shape((nj, fslots, slots), BF),
        ],
        8 * unit // nx,
        face_bytes,
    )(x_face_rank, x_face_skel, x_face_interp, x_coupling, last_turned, last_schur, top_in)

    packed_last, part = lax.optimization_barrier((packed_last, part))
    packed_last_in = passed_along(packed_last, "gx", -1)
    edge_in, part = lax.optimization_barrier((edge_in, part))
    y_out = call(
        functools.partial(y_edge_kernel, nx, tail),
        (1,),
        [
            smem,
            pl.BlockSpec((nx, cells, fslots), lambda i: (0, group, 0)),
            pl.BlockSpec((nx, 1, rows, fslots), lambda i: (0, tail, 0, 0)),
            pl.BlockSpec((nx, cells, half), lambda i: (0, group, 0)),
            pl.BlockSpec((nx, 2, slots, half), lambda i: (0, 0, 0, 0)),
            pl.BlockSpec((nx, 2, half, slots), lambda i: (0, 0, 0, 0)),
            pl.BlockSpec(memory_space=pl.ANY),
        ],
        pl.BlockSpec((nx, 1, fslots, fslots), lambda i: (0, tail, 0, 0)),
        shape((nx, nj, fslots, fslots), BF),
        8 * unit // nj,
        nx * face_bytes // nj,
        {6: 0},
    )(y_face_rank, y_face_skel, in_hbm(y_face_interp), y_coupling, corner, edge_in, y_out)

    for places, arrived in (
        (range(chunks - 1), packed_in),
        (range(chunks - 1, chunks), packed_last_in),
    ):
        count = len(places)
        x_out = call(
            functools.partial(x_last_kernel, cells, last, places),
            (),
            [vmem, vmem, vmem, vmem, hbm],
            hbm,
            shape((nx, nj, fslots, fslots), BF),
            3 * unit // nx * count // chunks,
            nj * slots * slots * 11 * count // chunks,
            {4: 0},
            scratch=[
                pltpu.VMEM((count * cells, fslots, fslots), BF),
                pltpu.SemaphoreType.DMA((count,)),
            ],
        )(part, lower, lower_turned, arrived, x_out)
    return (x_out, y_out)


def solution(mesh):
    return jax.shard_map(
        body,
        mesh=mesh,
        in_specs=(
            P("gx", "yz", None, None),
            P("gx", "yz", None),
            P("gx", "yz", None),
            P("gx", "yz", None, None),
            P("gx", "yz", None),
            P("gx", "yz"),
            P("gx", "yz", None, None),
            P("gx", "yz", None),
            P("gx", "yz"),
            P("gx", "yz", None, None),
            P("gx", "yz", None),
            P("gx", "yz"),
        ),
        out_specs=(P("gx", "yz", None, None), P("gx", "yz", None, None)),
        check_vma=False,
    )
```

```python
import functools

import jax
import jax.numpy as jnp
from jax import lax
from jax.experimental import pallas as pl
from jax.experimental.pallas import tpu as pltpu
from jax.sharding import PartitionSpec as P

BF = jnp.bfloat16
F32 = jnp.float32
MIB = 1024 * 1024


def passed_along(x, axis, by):
    devices = lax.axis_size(axis)
    pairs = [(i, i + by) for i in range(devices) if 0 <= i + by < devices]
    return lax.ppermute(x, axis, pairs)


def dot(a, b):
    return lax.dot_general(a, b, (((1,), (0,)), ((), ())), preferred_element_type=F32)


def marks_of(skel_row, rank, interp):
    rows, slots = interp.shape
    live = lax.broadcasted_iota(jnp.int32, (1, slots), 1) < rank
    picked_row = jnp.where(live, skel_row, -1).astype(F32).astype(BF)
    row = lax.broadcasted_iota(jnp.int32, (rows, slots), 0).astype(F32).astype(BF)
    live_row = jnp.where(live, F32(1.0), F32(0.0)).astype(BF)
    return row == picked_row, interp * live_row


def kept_cleared(hits, interps):
    slots = hits[0].shape[-1]
    ones = jnp.ones((slots, slots), BF)
    hits = [jnp.where(hit, BF(1.0), BF(0.0)) for hit in hits]
    counts = [dot(hit, ones).astype(BF) for hit in hits]
    return [h + z * (BF(1.0) - n) for h, z, n in zip(hits, interps, counts)]


def bases_of(cells, layer, first, rank_ref, skel_ref, interp_ref):
    pairs = [
        marks_of(skel_ref[0, k : k + 1], rank_ref[layer, first + k], interp_ref[0, k])
        for k in range(cells)
    ]
    return kept_cleared([p[0] for p in pairs], [p[1] for p in pairs])


def scaled(turned, conduct):
    return turned * -conduct


def face_of(left, link, link_t, right):
    upper = jnp.concatenate([left, link], axis=1)
    lower = jnp.concatenate([link_t, right], axis=1)
    return jnp.concatenate([upper, lower], axis=0)


def project(turned, matrices, bases):
    inner = [dot(t, m).astype(BF) for t, m in zip(turned, matrices)]
    return [dot(i, b) for i, b in zip(inner, bases)]


def top_kernel(cells, rank_hbm, skel_hbm, interp_hbm, out_ref, rank_ref, skel_ref, held, small_sems, sems):
    count, half, _ = out_ref.shape
    small = [
        pltpu.make_async_copy(rank_hbm, rank_ref, small_sems.at[0]),
        pltpu.make_async_copy(skel_hbm.at[0], skel_ref, small_sems.at[1]),
    ]
    copies = []
    for c in range(count // cells):
        group = pl.ds(c * cells, cells)
        copies.append(
            pltpu.make_async_copy(
                interp_hbm.at[0, group, pl.ds(0, half)], held.at[group], sems.at[c]
            )
        )
    for copy in small + copies:
        copy.start()
    for copy in small:
        copy.wait()
    for c in range(count // cells):
        copies[c].wait()
        for k in range(c * cells, (c + 1) * cells):
            hit, interp = marks_of(skel_ref[k : k + 1], rank_ref[0, k], held[k])
            out_ref[k] = jnp.where(hit, BF(1.0), interp)


def pack_masks(size):
    half = size // 2
    row = lax.broadcasted_iota(jnp.int32, (half, size), 0)
    lane = lax.broadcasted_iota(jnp.int32, (half, size), 1)
    ahead = lane - row
    upper = (ahead >= 0) & (ahead < half)
    return upper, ahead == 0, ahead == half


def main_kernel(
    cells, layers, chunks,
    rank_ref, skel_ref, interp_ref, matrix_ref,
    x_rank_ref, x_skel_ref, x_interp_ref, x_coup_ref,
    y_rank_ref, y_skel_ref, y_interp_ref, y_coup_ref,
    x_out_ref, y_out_ref, packed_ref, packed_last_ref, edge_ref, corner_ref, last_turned_ref, last_schur_ref,
    store_top, store_turned, store_schur, store_extra,
):
    layer = layers - 1 - pl.program_id(0)
    chunk = chunks - 1 - pl.program_id(1)
    first = chunk * cells
    slots = skel_ref.shape[-1]
    half = slots // 2
    top = interp_ref.shape[2] // 2

    bases = bases_of(cells, layer, first, rank_ref, skel_ref, interp_ref)
    turned = [jnp.transpose(b) for b in bases]
    schurs = project(turned, [matrix_ref[0, k] for k in range(cells)], bases)
    schurs = [s.astype(BF) for s in schurs]

    def faces(out_ref, f_rank_ref, f_skel_ref, f_interp_ref, coup_ref, rights):
        found = bases_of(cells, layer, first, f_rank_ref, f_skel_ref, f_interp_ref)
        found_turned = [jnp.transpose(f) for f in found]
        matrices = []
        for k in range(cells):
            right_top, right_turned, right = rights[k]
            conduct = coup_ref[0, k : k + 1]
            link = dot(scaled(turned[k][:, top:], conduct), right_top).astype(BF)
            link_t = dot(scaled(right_turned, conduct), bases[k][top:]).astype(BF)
            matrices.append(face_of(schurs[k], link, link_t, right))
        results = project(found_turned, matrices, found)
        for k in range(cells):
            out_ref[0, k] = results[k].astype(BF)

    def stored(place):
        return store_top[place], store_turned[place], store_schur[place]

    after = jnp.minimum(first + cells, store_schur.shape[0] - 1)
    rights = [(bases[k][:top], turned[k][:, :top], schurs[k]) for k in range(1, cells)]
    faces(y_out_ref, y_rank_ref, y_skel_ref, y_interp_ref, y_coup_ref, rights + [stored(after)])

    @pl.when(layer < layers - 1)
    def _():
        rights = [stored(first + k) for k in range(cells)]
        faces(x_out_ref, x_rank_ref, x_skel_ref, x_interp_ref, x_coup_ref, rights)

    for k in range(cells):
        store_top[first + k] = bases[k][:top]
        store_turned[first + k] = turned[k][:, :top]
        store_schur[first + k] = schurs[k]

    @pl.when(layer == layers - 1)
    def _():
        for k in range(cells):
            last_turned_ref[k] = turned[k][:, top:]
            last_schur_ref[k] = schurs[k]

    @pl.when(layer == 0)
    def _():
        upper, same, opposite = pack_masks(slots)

        def put(packed_ref, start):
            for k in range(cells):
                above, below = schurs[k][:half].astype(F32), schurs[k][half:].astype(F32)
                place = pl.ds(pl.multiple_of(start + k * half, half), half)
                packed_ref[place] = jnp.where(upper, above, below).astype(BF)

        @pl.when(chunk < chunks - 1)
        def _():
            put(packed_ref, chunk * (cells * half))

        @pl.when(chunk == chunks - 1)
        def _():
            put(packed_last_ref, 0)

        for p in range(0, cells, 2):
            extra = jnp.where(opposite, schurs[p][:half].astype(F32), F32(0.0))
            if p + 1 < cells:
                extra += jnp.where(same, schurs[p + 1][half:].astype(F32), F32(0.0))
            store_extra[chunk, p // 2 : p // 2 + 1] = jnp.sum(extra, axis=0, keepdims=True)

        @pl.when(chunk == 0)
        def _():
            pairs = -(-cells // 2)
            for ref, places in ((packed_ref, range(chunks - 1)), (packed_last_ref, [chunks - 1])):
                start = len(places) * cells * half
                rows = [store_extra[c, :pairs] for c in places]
                pad = ref.shape[0] - start - pairs * len(places)
                if pad:
                    rows.append(jnp.zeros((pad, slots), F32))
                ref[start:] = jnp.concatenate(rows, axis=0).astype(BF)

    @pl.when(chunk == 0)
    def _():
        edge_ref[layer, 0] = bases[0][:top]
        edge_ref[layer, 1] = schurs[0]

    @pl.when(chunk == chunks - 1)
    def _():
        corner_ref[layer, 0] = turned[cells - 1][:, top:]
        corner_ref[layer, 1] = schurs[cells - 1]


def y_edge_kernel(layers, place, rank_ref, skel_ref, interp_ref, coup_ref, corner_ref, edge_ref, _, out_ref):
    row = place % skel_ref.shape[1]
    pairs = [
        marks_of(skel_ref[i, row : row + 1], rank_ref[i, place], interp_ref[i, 0])
        for i in range(layers)
    ]
    found = kept_cleared([p[0] for p in pairs], [p[1] for p in pairs])
    matrices = []
    for i in range(layers):
        link = dot(scaled(corner_ref[i, 0], coup_ref[i, row : row + 1]), edge_ref[i, 0]).astype(BF)
        matrices.append(face_of(corner_ref[i, 1], link, jnp.transpose(link), edge_ref[i, 1]))
    results = project([jnp.transpose(f) for f in found], matrices, found)
    for i in range(layers):
        out_ref[i, 0] = results[i].astype(BF)


def x_part_kernel(
    cells, layer, rank_ref, skel_ref, interp_ref, coup_ref, turned_ref, schur_ref, top_ref,
    part_ref, lower_ref, lower_turned_ref,
):
    half = top_ref.shape[-2]
    faces = bases_of(cells, layer, pl.program_id(0) * cells, rank_ref, skel_ref, interp_ref)
    turned = [jnp.transpose(f) for f in faces]
    for k in range(cells):
        lower_ref[k] = faces[k][half:]
        lower_turned_ref[k] = turned[k][:, half:]
    marked = [top_ref[k] for k in range(cells)]
    tops = kept_cleared([m == BF(1.0) for m in marked], marked)
    found = [
        dot(scaled(turned_ref[k], coup_ref[0, k : k + 1]), tops[k]).astype(BF)
        for k in range(cells)
    ]
    matrices = [
        face_of(schur_ref[k], found[k], jnp.transpose(found[k]), jnp.zeros_like(found[k]))
        for k in range(cells)
    ]
    results = project(turned, matrices, faces)
    for k in range(cells):
        part_ref[k] = results[k]


def x_last_kernel(
    cells, layer, places, part_ref, lower_ref, lower_turned_ref, packed_ref, _, out_ref, held, sems
):
    slots = part_ref.shape[-1]
    half = slots // 2
    upper, same, opposite = pack_masks(slots)
    one, zero, mid = F32(1.0), F32(0.0), F32(0.5)
    top_scale = jnp.where(same, mid, jnp.where(upper, one, zero))
    low_scale = jnp.where(opposite, mid, jnp.where(upper, zero, one))
    same_scale = jnp.where(same, one, zero)
    opposite_scale = jnp.where(opposite, one, zero)
    extras = packed_ref[len(places) * cells * half :].astype(F32)
    pairs = -(-cells // 2)
    copies = []
    for n, c in enumerate(places):
        group = range(c * cells, (c + 1) * cells)
        schurs = []
        for k in range(cells):
            start = (n * cells + k) * half
            packed = packed_ref[start : start + half].astype(F32)
            extra = extras[n * pairs + k // 2 : n * pairs + k // 2 + 1]
            top, low = packed * top_scale, packed * low_scale
            if k % 2 == 0:
                top += extra * opposite_scale
            else:
                low += extra * same_scale
            tri = jnp.concatenate([top, low], axis=0).astype(BF)
            schurs.append(tri + jnp.transpose(tri))
        results = project(
            [lower_turned_ref[k] for k in group], schurs, [lower_ref[k] for k in group]
        )
        for k, result in enumerate(results):
            held[n * cells + k] = (part_ref[c * cells + k] + result).astype(BF)
        copies.append(
            pltpu.make_async_copy(
                held.at[pl.ds(n * cells, cells)],
                out_ref.at[layer, pl.ds(c * cells, cells)],
                sems.at[n],
            )
        )
        copies[n].start()
    for copy in copies:
        copy.wait()


def call(kernel, grid, in_specs, out_specs, out_shape, flops, moved, aliases=None, vmem=24, scratch=()):
    return pl.pallas_call(
        kernel,
        grid=grid,
        in_specs=in_specs,
        out_specs=out_specs,
        out_shape=out_shape,
        scratch_shapes=scratch,
        input_output_aliases=aliases or {},
        compiler_params=pltpu.CompilerParams(vmem_limit_bytes=vmem * MIB),
        cost_estimate=pl.CostEstimate(flops=flops, bytes_accessed=moved, transcendentals=0),
    )


def in_hbm(x):
    return pltpu.with_memory_space_constraint(x, pltpu.HBM)


def body(
    cell_matrix,
    x_coupling,
    y_coupling,
    cell_interp,
    cell_skel,
    cell_rank,
    x_face_interp,
    x_face_skel,
    x_face_rank,
    y_face_interp,
    y_face_skel,
    y_face_rank,
):
    nx, nj, rows, slots = cell_interp.shape
    half = rows // 2
    fslots = x_face_interp.shape[-1]
    cells = next(n for n in (8, 4, 2, 1) if nj % n == 0 and nj > n)
    chunks = nj // cells
    unit = 2 * nx * nj * slots * slots * slots
    smem = pl.BlockSpec(memory_space=pltpu.SMEM)
    shape = jax.ShapeDtypeStruct

    hbm = pl.BlockSpec(memory_space=pltpu.HBM)
    vmem = pl.BlockSpec(memory_space=pltpu.VMEM)
    top = call(
        functools.partial(top_kernel, cells),
        (),
        [hbm, hbm, hbm],
        vmem,
        shape((nj, half, slots), BF),
        0,
        4 * nj * half * slots,
        vmem=8,
        scratch=[
            pltpu.SMEM((nx, nj), jnp.int32),
            pltpu.VMEM((nj, slots), jnp.int32),
            pltpu.VMEM((nj, half, slots), BF),
            pltpu.SemaphoreType.DMA((2,)),
            pltpu.SemaphoreType.DMA((chunks,)),
        ],
    )(in_hbm(cell_rank), in_hbm(cell_skel), in_hbm(cell_interp))
    top_in = passed_along(top, "gx", -1)


    def pack_rows(count):
        extra = count * -(-cells // 2)
        return count * cells * slots // 2 + -(-extra // 16) * 16

    near = max(nx - 2, 0)

    def down(*dims):
        zeros = (0,) * len(dims)
        return pl.BlockSpec((1, cells) + dims, lambda i, c: (nx - 1 - i, chunks - 1 - c) + zeros)

    def down_x(*dims):
        zeros = (0,) * len(dims)

        def place(i, c):
            return (jnp.minimum(nx - 1 - i, near), jnp.where(i == 0, chunks - 1, chunks - 1 - c)) + zeros

        return pl.BlockSpec((1, cells) + dims, place)

    def whole(*dims):
        return pl.BlockSpec(dims, lambda i, c: (0,) * len(dims))

    def from_last(*dims):
        return pl.BlockSpec(
            (cells,) + dims, lambda i, c: (jnp.where(i == 0, chunks - 1 - c, 0),) + (0,) * len(dims)
        )

    x_out, y_out, packed, packed_last, edge, corner, last_turned, last_schur = call(
        functools.partial(main_kernel, cells, nx, chunks),
        (nx, chunks),
        [
            smem, down(slots), down(rows, slots), down(rows, rows),
            smem, down_x(fslots), down_x(rows, fslots), down_x(half),
            smem, down(fslots), down(rows, fslots), down(half),
        ],
        [
            down_x(fslots, fslots),
            down(fslots, fslots),
            whole(pack_rows(chunks - 1), slots),
            whole(pack_rows(1), slots),
            whole(nx, 2, half, slots),
            whole(nx, 2, slots, half),
            from_last(slots, half),
            from_last(slots, slots),
        ],
        [
            shape((nx, nj, fslots, fslots), BF),
            shape((nx, nj, fslots, fslots), BF),
            shape((pack_rows(chunks - 1), slots), BF),
            shape((pack_rows(1), slots), BF),
            shape((nx, 2, half, slots), BF),
            shape((nx, 2, slots, half), BF),
            shape((nj, slots, half), BF),
            shape((nj, slots, slots), BF),
        ],
        20 * unit,
        nx * nj * (rows * rows + 3 * rows * slots + 3 * slots * slots) * 2,
        vmem=32,
        scratch=[
            pltpu.VMEM((nj, half, slots), BF),
            pltpu.VMEM((nj, slots, half), BF),
            pltpu.VMEM((nj, slots, slots), BF),
            pltpu.VMEM((chunks, cells, slots), F32),
        ],
    )(
        cell_rank, in_hbm(cell_skel), in_hbm(cell_interp), in_hbm(cell_matrix),
        x_face_rank, in_hbm(x_face_skel), in_hbm(x_face_interp), in_hbm(x_coupling),
        y_face_rank, in_hbm(y_face_skel), in_hbm(y_face_interp), in_hbm(y_coupling),
    )
    edge_in = passed_along(edge, "yz", -1)
    packed_in = passed_along(packed, "gx", -1)
    packed_last_in = passed_along(packed_last, "gx", -1)
    face_bytes = nj * (4 * rows * slots + 4 * slots * slots) * 2

    last = nx - 1
    tail = nj - 1
    group = tail // cells

    def last_block(*dims):
        return pl.BlockSpec((1, cells) + dims, lambda c: (last, c) + (0,) * len(dims))

    def plain(*dims):
        return pl.BlockSpec((cells,) + dims, lambda c: (c,) + (0,) * len(dims))

    part, lower, lower_turned = call(
        functools.partial(x_part_kernel, cells, last),
        (chunks,),
        [
            smem,
            last_block(fslots),
            last_block(rows, fslots),
            last_block(half),
            plain(slots, half),
            plain(slots, slots),
            plain(half, slots),
        ],
        [plain(fslots, fslots), plain(slots, fslots), plain(fslots, slots)],
        [
            shape((nj, fslots, fslots), F32),
            shape((nj, slots, fslots), BF),
            shape((nj, fslots, slots), BF),
        ],
        8 * unit // nx,
        face_bytes,
    )(x_face_rank, x_face_skel, x_face_interp, x_coupling, last_turned, last_schur, top_in)

    edge_in, part = lax.optimization_barrier((edge_in, part))
    y_out = call(
        functools.partial(y_edge_kernel, nx, tail),
        (1,),
        [
            smem,
            pl.BlockSpec((nx, cells, fslots), lambda i: (0, group, 0)),
            pl.BlockSpec((nx, 1, rows, fslots), lambda i: (0, tail, 0, 0)),
            pl.BlockSpec((nx, cells, half), lambda i: (0, group, 0)),
            pl.BlockSpec((nx, 2, slots, half), lambda i: (0, 0, 0, 0)),
            pl.BlockSpec((nx, 2, half, slots), lambda i: (0, 0, 0, 0)),
            pl.BlockSpec(memory_space=pl.ANY),
        ],
        pl.BlockSpec((nx, 1, fslots, fslots), lambda i: (0, tail, 0, 0)),
        shape((nx, nj, fslots, fslots), BF),
        8 * unit // nj,
        nx * face_bytes // nj,
        {6: 0},
    )(y_face_rank, y_face_skel, in_hbm(y_face_interp), y_coupling, corner, edge_in, y_out)

    for places, arrived in (
        (range(chunks - 1), packed_in),
        (range(chunks - 1, chunks), packed_last_in),
    ):
        count = len(places)
        x_out = call(
            functools.partial(x_last_kernel, cells, last, places),
            (),
            [vmem, vmem, vmem, vmem, hbm],
            hbm,
            shape((nx, nj, fslots, fslots), BF),
            3 * unit // nx * count // chunks,
            nj * slots * slots * 11 * count // chunks,
            {4: 0},
            scratch=[
                pltpu.VMEM((count * cells, fslots, fslots), BF),
                pltpu.SemaphoreType.DMA((count,)),
            ],
        )(part, lower, lower_turned, arrived, x_out)
    return (x_out, y_out)


def solution(mesh):
    return jax.shard_map(
        body,
        mesh=mesh,
        in_specs=(
            P("gx", "yz", None, None),
            P("gx", "yz", None),
            P("gx", "yz", None),
            P("gx", "yz", None, None),
            P("gx", "yz", None),
            P("gx", "yz"),
            P("gx", "yz", None, None),
            P("gx", "yz", None),
            P("gx", "yz"),
            P("gx", "yz", None, None),
            P("gx", "yz", None),
            P("gx", "yz"),
        ),
        out_specs=(P("gx", "yz", None, None), P("gx", "yz", None, None)),
        check_vma=False,
    )
```

```python
import functools

import jax
import jax.numpy as jnp
from jax import lax
from jax.experimental import pallas as pl
from jax.experimental.pallas import tpu as pltpu
from jax.sharding import PartitionSpec as P

BF = jnp.bfloat16
F32 = jnp.float32
MIB = 1024 * 1024


def passed_along(x, axis, by):
    devices = lax.axis_size(axis)
    pairs = [(i, i + by) for i in range(devices) if 0 <= i + by < devices]
    return lax.ppermute(x, axis, pairs)


def dot(a, b):
    return lax.dot_general(a, b, (((1,), (0,)), ((), ())), preferred_element_type=F32)


def marks_of(skel_row, rank, interp):
    rows, slots = interp.shape
    live = lax.broadcasted_iota(jnp.int32, (1, slots), 1) < rank
    picked_row = jnp.where(live, skel_row, -1).astype(F32).astype(BF)
    row = lax.broadcasted_iota(jnp.int32, (rows, slots), 0).astype(F32).astype(BF)
    live_row = jnp.where(live, F32(1.0), F32(0.0)).astype(BF)
    return row == picked_row, interp * live_row


def pair_ones(slots):
    row = lax.broadcasted_iota(jnp.int32, (2 * slots, 2 * slots), 0) < slots
    lane = lax.broadcasted_iota(jnp.int32, (2 * slots, 2 * slots), 1) < slots
    return jnp.where(row == lane, F32(1.0), F32(0.0)).astype(BF)


def kept_cleared(hits, interps):
    slots = hits[0].shape[-1]
    ones = pair_ones(slots)
    hits = [jnp.where(hit, BF(1.0), BF(0.0)) for hit in hits]
    counts = []
    for k in range(0, len(hits) - 1, 2):
        both = dot(jnp.concatenate(hits[k : k + 2], axis=1), ones).astype(BF)
        counts += [both[:, :slots], both[:, slots:]]
    if len(hits) % 2:
        counts.append(dot(hits[-1], ones[:slots, :slots]).astype(BF))
    return [h + z * (BF(1.0) - n) for h, z, n in zip(hits, interps, counts)]


def bases_of(cells, layer, first, rank_ref, skel_ref, interp_ref):
    pairs = [
        marks_of(skel_ref[0, k : k + 1], rank_ref[layer, first + k], interp_ref[0, k])
        for k in range(cells)
    ]
    return kept_cleared([p[0] for p in pairs], [p[1] for p in pairs])


def scaled(turned, conduct):
    return turned * -conduct


def face_of(left, link, link_t, right):
    upper = jnp.concatenate([left, link], axis=1)
    lower = jnp.concatenate([link_t, right], axis=1)
    return jnp.concatenate([upper, lower], axis=0)


def project(turned, matrices, bases):
    inner = [dot(t, m).astype(BF) for t, m in zip(turned, matrices)]
    return [dot(i, b) for i, b in zip(inner, bases)]


def top_kernel(cells, rank_hbm, skel_hbm, interp_hbm, out_ref, rank_ref, skel_ref, held, small_sems, sems):
    count, half, _ = out_ref.shape
    small = [
        pltpu.make_async_copy(rank_hbm, rank_ref, small_sems.at[0]),
        pltpu.make_async_copy(skel_hbm.at[0], skel_ref, small_sems.at[1]),
    ]
    copies = []
    for c in range(count // cells):
        group = pl.ds(c * cells, cells)
        copies.append(
            pltpu.make_async_copy(
                interp_hbm.at[0, group, pl.ds(0, half)], held.at[group], sems.at[c]
            )
        )
    for copy in small + copies:
        copy.start()
    for copy in small:
        copy.wait()
    for c in range(count // cells):
        copies[c].wait()
        for k in range(c * cells, (c + 1) * cells):
            hit, interp = marks_of(skel_ref[k : k + 1], rank_ref[0, k], held[k])
            out_ref[k] = jnp.where(hit, BF(1.0), interp)


def pack_masks(size):
    half = size // 2
    row = lax.broadcasted_iota(jnp.int32, (half, size), 0)
    lane = lax.broadcasted_iota(jnp.int32, (half, size), 1)
    ahead = lane - row
    upper = (ahead >= 0) & (ahead < half)
    return upper, ahead == 0, ahead == half


def main_kernel(
    cells, layers, chunks,
    rank_ref, skel_ref, interp_ref, matrix_ref,
    x_rank_ref, x_skel_ref, x_interp_ref, x_coup_ref,
    y_rank_ref, y_skel_ref, y_interp_ref, y_coup_ref,
    x_out_ref, y_out_ref, packed_ref, packed_last_ref, edge_ref, corner_ref, last_turned_ref, last_schur_ref,
    store_top, store_turned, store_schur, store_extra,
):
    layer = layers - 1 - pl.program_id(0)
    chunk = chunks - 1 - pl.program_id(1)
    first = chunk * cells
    slots = skel_ref.shape[-1]
    half = slots // 2
    top = interp_ref.shape[2] // 2

    bases = bases_of(cells, layer, first, rank_ref, skel_ref, interp_ref)
    turned = [jnp.transpose(b) for b in bases]
    schurs = project(turned, [matrix_ref[0, k] for k in range(cells)], bases)
    schurs = [s.astype(BF) for s in schurs]

    def faces(out_ref, f_rank_ref, f_skel_ref, f_interp_ref, coup_ref, rights):
        found = bases_of(cells, layer, first, f_rank_ref, f_skel_ref, f_interp_ref)
        found_turned = [jnp.transpose(f) for f in found]
        matrices = []
        for k in range(cells):
            right_top, right_turned, right = rights[k]
            conduct = coup_ref[0, k : k + 1]
            link = dot(scaled(turned[k][:, top:], conduct), right_top).astype(BF)
            link_t = dot(scaled(right_turned, conduct), bases[k][top:]).astype(BF)
            matrices.append(face_of(schurs[k], link, link_t, right))
        results = project(found_turned, matrices, found)
        for k in range(cells):
            out_ref[0, k] = results[k].astype(BF)

    def stored(place):
        return store_top[place], store_turned[place], store_schur[place]

    after = jnp.minimum(first + cells, store_schur.shape[0] - 1)
    rights = [(bases[k][:top], turned[k][:, :top], schurs[k]) for k in range(1, cells)]
    faces(y_out_ref, y_rank_ref, y_skel_ref, y_interp_ref, y_coup_ref, rights + [stored(after)])

    @pl.when(layer < layers - 1)
    def _():
        rights = [stored(first + k) for k in range(cells)]
        faces(x_out_ref, x_rank_ref, x_skel_ref, x_interp_ref, x_coup_ref, rights)

    for k in range(cells):
        store_top[first + k] = bases[k][:top]
        store_turned[first + k] = turned[k][:, :top]
        store_schur[first + k] = schurs[k]

    @pl.when(layer == layers - 1)
    def _():
        for k in range(cells):
            last_turned_ref[k] = turned[k][:, top:]
            last_schur_ref[k] = schurs[k]

    @pl.when(layer == 0)
    def _():
        upper, same, opposite = pack_masks(slots)

        def put(packed_ref, start):
            for k in range(cells):
                above, below = schurs[k][:half].astype(F32), schurs[k][half:].astype(F32)
                place = pl.ds(pl.multiple_of(start + k * half, half), half)
                packed_ref[place] = jnp.where(upper, above, below).astype(BF)

        @pl.when(chunk < chunks - 1)
        def _():
            put(packed_ref, chunk * (cells * half))

        @pl.when(chunk == chunks - 1)
        def _():
            put(packed_last_ref, 0)

        for p in range(0, cells, 2):
            extra = jnp.where(opposite, schurs[p][:half].astype(F32), F32(0.0))
            if p + 1 < cells:
                extra += jnp.where(same, schurs[p + 1][half:].astype(F32), F32(0.0))
            store_extra[chunk, p // 2 : p // 2 + 1] = jnp.sum(extra, axis=0, keepdims=True)

        @pl.when(chunk == 0)
        def _():
            pairs = -(-cells // 2)
            for ref, places in ((packed_ref, range(chunks - 1)), (packed_last_ref, [chunks - 1])):
                start = len(places) * cells * half
                rows = [store_extra[c, :pairs] for c in places]
                pad = ref.shape[0] - start - pairs * len(places)
                if pad:
                    rows.append(jnp.zeros((pad, slots), F32))
                ref[start:] = jnp.concatenate(rows, axis=0).astype(BF)

    @pl.when(chunk == 0)
    def _():
        edge_ref[layer, 0] = bases[0][:top]
        edge_ref[layer, 1] = schurs[0]

    @pl.when(chunk == chunks - 1)
    def _():
        corner_ref[layer, 0] = turned[cells - 1][:, top:]
        corner_ref[layer, 1] = schurs[cells - 1]


def y_edge_parts(place, rank_ref, skel_ref, interps, coup_ref, corner_ref, edge_ref):
    layers = skel_ref.shape[0]
    pairs = [
        marks_of(skel_ref[i, place : place + 1], rank_ref[i, place], interps[i])
        for i in range(layers)
    ]
    found = kept_cleared([p[0] for p in pairs], [p[1] for p in pairs])
    matrices = []
    for i in range(layers):
        conduct = coup_ref[i, place : place + 1]
        link = dot(scaled(corner_ref[i, 0], conduct), edge_ref[i, 0]).astype(BF)
        matrices.append(face_of(corner_ref[i, 1], link, jnp.transpose(link), edge_ref[i, 1]))
    return [jnp.transpose(f) for f in found], matrices, found


def x_part_kernel(
    cells, layer, rank_ref, skel_ref, interp_ref, coup_ref, turned_ref, schur_ref, top_ref,
    part_ref, lower_ref, lower_turned_ref,
):
    half = top_ref.shape[-2]
    faces = bases_of(cells, layer, pl.program_id(0) * cells, rank_ref, skel_ref, interp_ref)
    turned = [jnp.transpose(f) for f in faces]
    for k in range(cells):
        lower_ref[k] = faces[k][half:]
        lower_turned_ref[k] = turned[k][:, half:]
    marked = [top_ref[k] for k in range(cells)]
    tops = kept_cleared([m == BF(1.0) for m in marked], marked)
    found = [
        dot(scaled(turned_ref[k], coup_ref[0, k : k + 1]), tops[k]).astype(BF)
        for k in range(cells)
    ]
    matrices = [
        face_of(schur_ref[k], found[k], jnp.transpose(found[k]), jnp.zeros_like(found[k]))
        for k in range(cells)
    ]
    results = project(turned, matrices, faces)
    for k in range(cells):
        part_ref[k] = results[k]


def x_last_chunk(cells, layer, n, places, part_ref, lower_ref, lower_turned_ref, packed_ref, out_ref, held, sems, more):
    slots = part_ref.shape[-1]
    half = slots // 2
    upper, same, opposite = pack_masks(slots)
    one, zero, mid = F32(1.0), F32(0.0), F32(0.5)
    top_scale = jnp.where(same, mid, jnp.where(upper, one, zero))
    low_scale = jnp.where(opposite, mid, jnp.where(upper, zero, one))
    same_scale = jnp.where(same, one, zero)
    opposite_scale = jnp.where(opposite, one, zero)
    extras = packed_ref[len(places) * cells * half :].astype(F32)
    pairs = -(-cells // 2)
    c = places[n]
    group = range(c * cells, (c + 1) * cells)
    schurs = []
    for k in range(cells):
        start = (n * cells + k) * half
        packed = packed_ref[start : start + half].astype(F32)
        extra = extras[n * pairs + k // 2 : n * pairs + k // 2 + 1]
        top, low = packed * top_scale, packed * low_scale
        if k % 2 == 0:
            top += extra * opposite_scale
        else:
            low += extra * same_scale
        tri = jnp.concatenate([top, low], axis=0).astype(BF)
        schurs.append(tri + jnp.transpose(tri))
    results = project(
        [lower_turned_ref[k] for k in group] + more[0],
        schurs + more[1],
        [lower_ref[k] for k in group] + more[2],
    )
    for k in range(cells):
        held[n * cells + k] = (part_ref[c * cells + k] + results[k]).astype(BF)
    copy = pltpu.make_async_copy(
        held.at[pl.ds(n * cells, cells)], out_ref.at[layer, pl.ds(c * cells, cells)], sems.at[n]
    )
    copy.start()
    return copy, results[cells:]


def x_last_kernel(
    cells, layer, places, part_ref, lower_ref, lower_turned_ref, packed_ref, _, out_ref, held, sems
):
    copies = []
    for n in range(len(places)):
        copy, _ = x_last_chunk(
            cells, layer, n, places, part_ref, lower_ref, lower_turned_ref, packed_ref, out_ref, held, sems,
            ([], [], []),
        )
        copies.append(copy)
    for copy in copies:
        copy.wait()


def x_last_y_edge_kernel(
    cells, layer, places, place, part_ref, lower_ref, lower_turned_ref, packed_ref, _,
    rank_ref, skel_ref, interp_hbm, coup_ref, corner_ref, edge_ref, __,
    out_ref, y_out_ref, held, sems, interp_ref, y_held, y_sems,
):
    layers = skel_ref.shape[0]
    fetches = [
        pltpu.make_async_copy(interp_hbm.at[i, place], interp_ref.at[i], y_sems.at[i])
        for i in range(layers)
    ]
    for fetch in fetches:
        fetch.start()
    copies = []
    for n in range(len(places)):
        more = ([], [], [])
        if n == len(places) - 1:
            for fetch in fetches:
                fetch.wait()
            more = y_edge_parts(
                place, rank_ref, skel_ref, [interp_ref[i] for i in range(layers)], coup_ref, corner_ref, edge_ref
            )
        copy, results = x_last_chunk(
            cells, layer, n, places, part_ref, lower_ref, lower_turned_ref, packed_ref, out_ref, held, sems, more
        )
        copies.append(copy)
    for i in range(layers):
        y_held[i] = results[i].astype(BF)
        copies.append(
            pltpu.make_async_copy(y_held.at[i], y_out_ref.at[i, place], y_sems.at[layers + i])
        )
        copies[-1].start()
    for copy in copies:
        copy.wait()


def call(kernel, grid, in_specs, out_specs, out_shape, flops, moved, aliases=None, vmem=24, scratch=()):
    return pl.pallas_call(
        kernel,
        grid=grid,
        in_specs=in_specs,
        out_specs=out_specs,
        out_shape=out_shape,
        scratch_shapes=scratch,
        input_output_aliases=aliases or {},
        compiler_params=pltpu.CompilerParams(vmem_limit_bytes=vmem * MIB),
        cost_estimate=pl.CostEstimate(flops=flops, bytes_accessed=moved, transcendentals=0),
    )


def in_hbm(x):
    return pltpu.with_memory_space_constraint(x, pltpu.HBM)


def body(
    cell_matrix,
    x_coupling,
    y_coupling,
    cell_interp,
    cell_skel,
    cell_rank,
    x_face_interp,
    x_face_skel,
    x_face_rank,
    y_face_interp,
    y_face_skel,
    y_face_rank,
):
    nx, nj, rows, slots = cell_interp.shape
    half = rows // 2
    fslots = x_face_interp.shape[-1]
    cells = next(n for n in (8, 4, 2, 1) if nj % n == 0 and nj > n)
    chunks = nj // cells
    unit = 2 * nx * nj * slots * slots * slots
    smem = pl.BlockSpec(memory_space=pltpu.SMEM)
    shape = jax.ShapeDtypeStruct

    hbm = pl.BlockSpec(memory_space=pltpu.HBM)
    vmem = pl.BlockSpec(memory_space=pltpu.VMEM)
    top = call(
        functools.partial(top_kernel, cells),
        (),
        [hbm, hbm, hbm],
        vmem,
        shape((nj, half, slots), BF),
        0,
        4 * nj * half * slots,
        vmem=8,
        scratch=[
            pltpu.SMEM((nx, nj), jnp.int32),
            pltpu.VMEM((nj, slots), jnp.int32),
            pltpu.VMEM((nj, half, slots), BF),
            pltpu.SemaphoreType.DMA((2,)),
            pltpu.SemaphoreType.DMA((chunks,)),
        ],
    )(in_hbm(cell_rank), in_hbm(cell_skel), in_hbm(cell_interp))
    top_in = passed_along(top, "gx", -1)


    def pack_rows(count):
        extra = count * -(-cells // 2)
        return count * cells * slots // 2 + -(-extra // 16) * 16

    near = max(nx - 2, 0)

    def down(*dims):
        zeros = (0,) * len(dims)
        return pl.BlockSpec((1, cells) + dims, lambda i, c: (nx - 1 - i, chunks - 1 - c) + zeros)

    def down_x(*dims):
        zeros = (0,) * len(dims)

        def place(i, c):
            return (jnp.minimum(nx - 1 - i, near), jnp.where(i == 0, chunks - 1, chunks - 1 - c)) + zeros

        return pl.BlockSpec((1, cells) + dims, place)

    def whole(*dims):
        return pl.BlockSpec(dims, lambda i, c: (0,) * len(dims))

    def from_last(*dims):
        return pl.BlockSpec(
            (cells,) + dims, lambda i, c: (jnp.where(i == 0, chunks - 1 - c, 0),) + (0,) * len(dims)
        )

    x_out, y_out, packed, packed_last, edge, corner, last_turned, last_schur = call(
        functools.partial(main_kernel, cells, nx, chunks),
        (nx, chunks),
        [
            smem, down(slots), down(rows, slots), down(rows, rows),
            smem, down_x(fslots), down_x(rows, fslots), down_x(half),
            smem, down(fslots), down(rows, fslots), down(half),
        ],
        [
            down_x(fslots, fslots),
            down(fslots, fslots),
            whole(pack_rows(chunks - 1), slots),
            whole(pack_rows(1), slots),
            whole(nx, 2, half, slots),
            whole(nx, 2, slots, half),
            from_last(slots, half),
            from_last(slots, slots),
        ],
        [
            shape((nx, nj, fslots, fslots), BF),
            shape((nx, nj, fslots, fslots), BF),
            shape((pack_rows(chunks - 1), slots), BF),
            shape((pack_rows(1), slots), BF),
            shape((nx, 2, half, slots), BF),
            shape((nx, 2, slots, half), BF),
            shape((nj, slots, half), BF),
            shape((nj, slots, slots), BF),
        ],
        20 * unit,
        nx * nj * (rows * rows + 3 * rows * slots + 3 * slots * slots) * 2,
        vmem=32,
        scratch=[
            pltpu.VMEM((nj, half, slots), BF),
            pltpu.VMEM((nj, slots, half), BF),
            pltpu.VMEM((nj, slots, slots), BF),
            pltpu.VMEM((chunks, cells, slots), F32),
        ],
    )(
        cell_rank, in_hbm(cell_skel), in_hbm(cell_interp), in_hbm(cell_matrix),
        x_face_rank, in_hbm(x_face_skel), in_hbm(x_face_interp), in_hbm(x_coupling),
        y_face_rank, in_hbm(y_face_skel), in_hbm(y_face_interp), in_hbm(y_coupling),
    )
    edge_in = passed_along(edge, "yz", -1)
    packed_in = passed_along(packed, "gx", -1)
    packed_last_in = passed_along(packed_last, "gx", -1)
    face_bytes = nj * (4 * rows * slots + 4 * slots * slots) * 2

    last = nx - 1
    tail = nj - 1

    def last_block(*dims):
        return pl.BlockSpec((1, cells) + dims, lambda c: (last, c) + (0,) * len(dims))

    def plain(*dims):
        return pl.BlockSpec((cells,) + dims, lambda c: (c,) + (0,) * len(dims))

    part, lower, lower_turned = call(
        functools.partial(x_part_kernel, cells, last),
        (chunks,),
        [
            smem,
            last_block(fslots),
            last_block(rows, fslots),
            last_block(half),
            plain(slots, half),
            plain(slots, slots),
            plain(half, slots),
        ],
        [plain(fslots, fslots), plain(slots, fslots), plain(fslots, slots)],
        [
            shape((nj, fslots, fslots), F32),
            shape((nj, slots, fslots), BF),
            shape((nj, fslots, slots), BF),
        ],
        8 * unit // nx,
        face_bytes,
    )(x_face_rank, x_face_skel, x_face_interp, x_coupling, last_turned, last_schur, top_in)

    count = chunks - 1
    out_shape = shape((nx, nj, fslots, fslots), BF)
    x_out, y_out = call(
        functools.partial(x_last_y_edge_kernel, cells, last, range(count), tail),
        (),
        [vmem, vmem, vmem, vmem, hbm, smem, vmem, hbm, vmem, vmem, vmem, hbm],
        [hbm, hbm],
        [out_shape, out_shape],
        3 * unit // nx,
        nj * slots * slots * 11,
        {4: 0, 11: 1},
        scratch=[
            pltpu.VMEM((count * cells, fslots, fslots), BF),
            pltpu.SemaphoreType.DMA((count,)),
            pltpu.VMEM((nx, rows, fslots), BF),
            pltpu.VMEM((nx, fslots, fslots), BF),
            pltpu.SemaphoreType.DMA((2 * nx,)),
        ],
    )(
        part, lower, lower_turned, packed_in, x_out,
        y_face_rank, y_face_skel, in_hbm(y_face_interp), y_coupling, corner, edge_in, y_out,
    )
    x_out = call(
        functools.partial(x_last_kernel, cells, last, range(count, chunks)),
        (),
        [vmem, vmem, vmem, vmem, hbm],
        hbm,
        out_shape,
        3 * unit // nx // chunks,
        nj * slots * slots * 11 // chunks,
        {4: 0},
        scratch=[pltpu.VMEM((cells, fslots, fslots), BF), pltpu.SemaphoreType.DMA((1,))],
    )(part, lower, lower_turned, packed_last_in, x_out)
    return (x_out, y_out)


def solution(mesh):
    return jax.shard_map(
        body,
        mesh=mesh,
        in_specs=(
            P("gx", "yz", None, None),
            P("gx", "yz", None),
            P("gx", "yz", None),
            P("gx", "yz", None, None),
            P("gx", "yz", None),
            P("gx", "yz"),
            P("gx", "yz", None, None),
            P("gx", "yz", None),
            P("gx", "yz"),
            P("gx", "yz", None, None),
            P("gx", "yz", None),
            P("gx", "yz"),
        ),
        out_specs=(P("gx", "yz", None, None), P("gx", "yz", None, None)),
        check_vma=False,
    )
```

```python
import functools

import jax
import jax.numpy as jnp
from jax import lax
from jax.experimental import pallas as pl
from jax.experimental.pallas import tpu as pltpu
from jax.sharding import PartitionSpec as P

BF = jnp.bfloat16
F32 = jnp.float32
MIB = 1024 * 1024


def passed_along(x, axis, by):
    devices = lax.axis_size(axis)
    pairs = [(i, i + by) for i in range(devices) if 0 <= i + by < devices]
    return lax.ppermute(x, axis, pairs)


def dot_nt(a, b):
    return lax.dot_general(a, b, (((1,), (1,)), ((), ())), preferred_element_type=F32)


def dot(a, b):
    return lax.dot_general(a, b, (((1,), (0,)), ((), ())), preferred_element_type=F32)


def marks_of(skel_row, rank, interp):
    rows, slots = interp.shape
    live = lax.broadcasted_iota(jnp.int32, (1, slots), 1) < rank
    picked_row = jnp.where(live, skel_row, -1).astype(F32).astype(BF)
    row = lax.broadcasted_iota(jnp.int32, (rows, slots), 0).astype(F32).astype(BF)
    live_row = jnp.where(live, F32(1.0), F32(0.0)).astype(BF)
    return row == picked_row, interp * live_row


def kept_cleared(turned):
    most = jnp.max(turned, axis=0, keepdims=True)
    least = jnp.where(most.astype(F32) == 1.0, F32(1.0), F32(-2.0)).astype(BF)
    return jnp.where(turned >= least, turned, BF(0.0))


def marked_of(skel_row, rank, interp):
    hit, live = marks_of(skel_row, rank, interp)
    return jnp.where(hit, BF(1.0), live)


def bases_of(cells, layer, first, rank_ref, skel_ref, interp_ref):
    marked = [
        marked_of(skel_ref[0, k : k + 1], rank_ref[layer, first + k], interp_ref[0, k])
        for k in range(cells)
    ]
    return [kept_cleared(t) for t in [jnp.transpose(m) for m in marked]]


def scaled(turned, conduct):
    return turned * -conduct


def face_of(left, link, link_t, right):
    upper = jnp.concatenate([left, link], axis=1)
    lower = jnp.concatenate([link_t, right], axis=1)
    return jnp.concatenate([upper, lower], axis=0)


def project(turned, matrices):
    inner = [dot(t, m).astype(BF) for t, m in zip(turned, matrices)]
    return [dot_nt(i, t) for i, t in zip(inner, turned)]


def top_kernel(cells, rank_hbm, skel_hbm, interp_hbm, out_ref, rank_ref, skel_ref, held, small_sems, sems):
    count, half, _ = out_ref.shape
    small = [
        pltpu.make_async_copy(rank_hbm, rank_ref, small_sems.at[0]),
        pltpu.make_async_copy(skel_hbm.at[0], skel_ref, small_sems.at[1]),
    ]
    copies = []
    for c in range(count // cells):
        group = pl.ds(c * cells, cells)
        copies.append(
            pltpu.make_async_copy(
                interp_hbm.at[0, group, pl.ds(0, half)], held.at[group], sems.at[c]
            )
        )
    for copy in small + copies:
        copy.start()
    for copy in small:
        copy.wait()
    for c in range(count // cells):
        copies[c].wait()
        for k in range(c * cells, (c + 1) * cells):
            out_ref[k] = marked_of(skel_ref[k : k + 1], rank_ref[0, k], held[k])


def pack_masks(size):
    half = size // 2
    row = lax.broadcasted_iota(jnp.int32, (half, size), 0)
    lane = lax.broadcasted_iota(jnp.int32, (half, size), 1)
    ahead = lane - row
    upper = (ahead >= 0) & (ahead < half)
    return upper, ahead == 0, ahead == half


def main_kernel(
    cells, layers, chunks,
    rank_ref, skel_ref, interp_ref, matrix_ref,
    x_rank_ref, x_skel_ref, x_interp_ref, x_coup_ref,
    y_rank_ref, y_skel_ref, y_interp_ref, y_coup_ref,
    x_out_ref, y_out_ref, packed_ref, packed_last_ref, edge_ref, corner_ref, last_turned_ref, last_schur_ref,
    store_turned, store_schur, store_extra,
):
    layer = layers - 1 - pl.program_id(0)
    chunk = chunks - 1 - pl.program_id(1)
    first = chunk * cells
    slots = skel_ref.shape[-1]
    half = slots // 2
    top = interp_ref.shape[2] // 2

    turned = bases_of(cells, layer, first, rank_ref, skel_ref, interp_ref)
    schurs = project(turned, [matrix_ref[0, k] for k in range(cells)])
    schurs = [s.astype(BF) for s in schurs]

    def faces(out_ref, f_rank_ref, f_skel_ref, f_interp_ref, coup_ref, rights):
        found = bases_of(cells, layer, first, f_rank_ref, f_skel_ref, f_interp_ref)
        matrices = []
        for k in range(cells):
            right_turned, right = rights[k]
            conduct = coup_ref[0, k : k + 1]
            lower = turned[k][:, top:]
            link = dot_nt(scaled(lower, conduct), right_turned).astype(BF)
            link_t = dot_nt(scaled(right_turned, conduct), lower).astype(BF)
            matrices.append(face_of(schurs[k], link, link_t, right))
        results = project(found, matrices)
        for k in range(cells):
            out_ref[0, k] = results[k].astype(BF)

    def stored(place):
        return store_turned[place], store_schur[place]

    after = jnp.minimum(first + cells, store_schur.shape[0] - 1)
    rights = [(turned[k][:, :top], schurs[k]) for k in range(1, cells)]
    faces(y_out_ref, y_rank_ref, y_skel_ref, y_interp_ref, y_coup_ref, rights + [stored(after)])

    @pl.when(layer < layers - 1)
    def _():
        rights = [stored(first + k) for k in range(cells)]
        faces(x_out_ref, x_rank_ref, x_skel_ref, x_interp_ref, x_coup_ref, rights)

    for k in range(cells):
        store_turned[first + k] = turned[k][:, :top]
        store_schur[first + k] = schurs[k]

    @pl.when(layer == layers - 1)
    def _():
        for k in range(cells):
            last_turned_ref[k] = turned[k][:, top:]
            last_schur_ref[k] = schurs[k]

    @pl.when(layer == 0)
    def _():
        upper, same, opposite = pack_masks(slots)

        def put(packed_ref, start):
            for k in range(cells):
                above, below = schurs[k][:half].astype(F32), schurs[k][half:].astype(F32)
                place = pl.ds(pl.multiple_of(start + k * half, half), half)
                packed_ref[place] = jnp.where(upper, above, below).astype(BF)

        @pl.when(chunk < chunks - 1)
        def _():
            put(packed_ref, chunk * (cells * half))

        @pl.when(chunk == chunks - 1)
        def _():
            put(packed_last_ref, 0)

        for p in range(0, cells, 2):
            extra = jnp.where(opposite, schurs[p][:half].astype(F32), F32(0.0))
            if p + 1 < cells:
                extra += jnp.where(same, schurs[p + 1][half:].astype(F32), F32(0.0))
            store_extra[chunk, p // 2 : p // 2 + 1] = jnp.sum(extra, axis=0, keepdims=True)

        @pl.when(chunk == 0)
        def _():
            pairs = -(-cells // 2)
            for ref, places in ((packed_ref, range(chunks - 1)), (packed_last_ref, [chunks - 1])):
                start = len(places) * cells * half
                rows = [store_extra[c, :pairs] for c in places]
                pad = ref.shape[0] - start - pairs * len(places)
                if pad:
                    rows.append(jnp.zeros((pad, slots), F32))
                ref[start:] = jnp.concatenate(rows, axis=0).astype(BF)

    @pl.when(chunk == 0)
    def _():
        edge_ref[layer, 0] = turned[0][:, :top]
        edge_ref[layer, 1] = schurs[0]

    @pl.when(chunk == chunks - 1)
    def _():
        corner_ref[layer, 0] = turned[cells - 1][:, top:]
        corner_ref[layer, 1] = schurs[cells - 1]


def y_edge_kernel(layers, place, rank_ref, skel_ref, interp_ref, coup_ref, corner_ref, edge_ref, _, out_ref):
    row = place % skel_ref.shape[1]
    marked = [
        marked_of(skel_ref[i, row : row + 1], rank_ref[i, place], interp_ref[i, 0])
        for i in range(layers)
    ]
    found = [kept_cleared(jnp.transpose(m)) for m in marked]
    matrices = []
    for i in range(layers):
        conduct = coup_ref[i, row : row + 1]
        link = dot_nt(scaled(corner_ref[i, 0], conduct), edge_ref[i, 0]).astype(BF)
        link_t = dot_nt(scaled(edge_ref[i, 0], conduct), corner_ref[i, 0]).astype(BF)
        matrices.append(face_of(corner_ref[i, 1], link, link_t, edge_ref[i, 1]))
    results = project(found, matrices)
    for i in range(layers):
        out_ref[i, 0] = results[i].astype(BF)


def x_part_kernel(
    cells, layer, rank_ref, skel_ref, interp_ref, coup_ref, turned_ref, schur_ref, top_ref,
    part_ref, lower_turned_ref,
):
    half = top_ref.shape[-2]
    faces = bases_of(cells, layer, pl.program_id(0) * cells, rank_ref, skel_ref, interp_ref)
    for k in range(cells):
        lower_turned_ref[k] = faces[k][:, half:]
    tops = [kept_cleared(t) for t in [jnp.transpose(top_ref[k]) for k in range(cells)]]
    matrices = []
    for k in range(cells):
        conduct = coup_ref[0, k : k + 1]
        link = dot_nt(scaled(turned_ref[k], conduct), tops[k]).astype(BF)
        link_t = dot_nt(scaled(tops[k], conduct), turned_ref[k]).astype(BF)
        matrices.append(face_of(schur_ref[k], link, link_t, jnp.zeros_like(link)))
    results = project(faces, matrices)
    for k in range(cells):
        part_ref[k] = results[k]


def x_last_kernel(
    cells, layer, places, part_ref, lower_turned_ref, packed_ref, _, out_ref, held, sems
):
    slots = part_ref.shape[-1]
    half = slots // 2
    upper, same, opposite = pack_masks(slots)
    one, zero, mid = F32(1.0), F32(0.0), F32(0.5)
    top_scale = jnp.where(same, mid, jnp.where(upper, one, zero))
    low_scale = jnp.where(opposite, mid, jnp.where(upper, zero, one))
    same_scale = jnp.where(same, one, zero)
    opposite_scale = jnp.where(opposite, one, zero)
    extras = packed_ref[len(places) * cells * half :].astype(F32)
    pairs = -(-cells // 2)
    copies = []
    for n, c in enumerate(places):
        group = range(c * cells, (c + 1) * cells)
        halves = []
        for k in range(cells):
            start = (n * cells + k) * half
            packed = packed_ref[start : start + half].astype(F32)
            extra = extras[n * pairs + k // 2 : n * pairs + k // 2 + 1]
            top, low = packed * top_scale, packed * low_scale
            if k % 2 == 0:
                top += extra * opposite_scale
            else:
                low += extra * same_scale
            halves.append(jnp.concatenate([top, low], axis=0).astype(BF))
        turned = [lower_turned_ref[k] for k in group]
        inner = [(dot(t, h) + dot_nt(t, h)).astype(BF) for t, h in zip(turned, halves)]
        results = [dot_nt(i, t) for i, t in zip(inner, turned)]
        for k, result in enumerate(results):
            held[n * cells + k] = (part_ref[c * cells + k] + result).astype(BF)
        copies.append(
            pltpu.make_async_copy(
                held.at[pl.ds(n * cells, cells)],
                out_ref.at[layer, pl.ds(c * cells, cells)],
                sems.at[n],
            )
        )
        copies[n].start()
    for copy in copies:
        copy.wait()


def call(kernel, grid, in_specs, out_specs, out_shape, flops, moved, aliases=None, vmem=24, scratch=()):
    return pl.pallas_call(
        kernel,
        grid=grid,
        in_specs=in_specs,
        out_specs=out_specs,
        out_shape=out_shape,
        scratch_shapes=scratch,
        input_output_aliases=aliases or {},
        compiler_params=pltpu.CompilerParams(vmem_limit_bytes=vmem * MIB),
        cost_estimate=pl.CostEstimate(flops=flops, bytes_accessed=moved, transcendentals=0),
    )


def in_hbm(x):
    return pltpu.with_memory_space_constraint(x, pltpu.HBM)


def body(
    cell_matrix,
    x_coupling,
    y_coupling,
    cell_interp,
    cell_skel,
    cell_rank,
    x_face_interp,
    x_face_skel,
    x_face_rank,
    y_face_interp,
    y_face_skel,
    y_face_rank,
):
    nx, nj, rows, slots = cell_interp.shape
    half = rows // 2
    fslots = x_face_interp.shape[-1]
    cells = next(n for n in (8, 4, 2, 1) if nj % n == 0 and nj > n)
    chunks = nj // cells
    unit = 2 * nx * nj * slots * slots * slots
    smem = pl.BlockSpec(memory_space=pltpu.SMEM)
    shape = jax.ShapeDtypeStruct

    hbm = pl.BlockSpec(memory_space=pltpu.HBM)
    vmem = pl.BlockSpec(memory_space=pltpu.VMEM)
    top = call(
        functools.partial(top_kernel, cells),
        (),
        [hbm, hbm, hbm],
        vmem,
        shape((nj, half, slots), BF),
        0,
        4 * nj * half * slots,
        vmem=8,
        scratch=[
            pltpu.SMEM((nx, nj), jnp.int32),
            pltpu.VMEM((nj, slots), jnp.int32),
            pltpu.VMEM((nj, half, slots), BF),
            pltpu.SemaphoreType.DMA((2,)),
            pltpu.SemaphoreType.DMA((chunks,)),
        ],
    )(in_hbm(cell_rank), in_hbm(cell_skel), in_hbm(cell_interp))
    top_in = passed_along(top, "gx", -1)


    def pack_rows(count):
        extra = count * -(-cells // 2)
        return count * cells * slots // 2 + -(-extra // 16) * 16

    near = max(nx - 2, 0)

    def down(*dims):
        zeros = (0,) * len(dims)
        return pl.BlockSpec((1, cells) + dims, lambda i, c: (nx - 1 - i, chunks - 1 - c) + zeros)

    def down_x(*dims):
        zeros = (0,) * len(dims)

        def place(i, c):
            return (jnp.minimum(nx - 1 - i, near), jnp.where(i == 0, chunks - 1, chunks - 1 - c)) + zeros

        return pl.BlockSpec((1, cells) + dims, place)

    def whole(*dims):
        return pl.BlockSpec(dims, lambda i, c: (0,) * len(dims))

    def from_last(*dims):
        return pl.BlockSpec(
            (cells,) + dims, lambda i, c: (jnp.where(i == 0, chunks - 1 - c, 0),) + (0,) * len(dims)
        )

    x_out, y_out, packed, packed_last, edge, corner, last_turned, last_schur = call(
        functools.partial(main_kernel, cells, nx, chunks),
        (nx, chunks),
        [
            smem, down(slots), down(rows, slots), down(rows, rows),
            smem, down_x(fslots), down_x(rows, fslots), down_x(half),
            smem, down(fslots), down(rows, fslots), down(half),
        ],
        [
            down_x(fslots, fslots),
            down(fslots, fslots),
            whole(pack_rows(chunks - 1), slots),
            whole(pack_rows(1), slots),
            whole(nx, 2, slots, half),
            whole(nx, 2, slots, half),
            from_last(slots, half),
            from_last(slots, slots),
        ],
        [
            shape((nx, nj, fslots, fslots), BF),
            shape((nx, nj, fslots, fslots), BF),
            shape((pack_rows(chunks - 1), slots), BF),
            shape((pack_rows(1), slots), BF),
            shape((nx, 2, slots, half), BF),
            shape((nx, 2, slots, half), BF),
            shape((nj, slots, half), BF),
            shape((nj, slots, slots), BF),
        ],
        20 * unit,
        nx * nj * (rows * rows + 3 * rows * slots + 3 * slots * slots) * 2,
        vmem=32,
        scratch=[
            pltpu.VMEM((nj, slots, half), BF),
            pltpu.VMEM((nj, slots, slots), BF),
            pltpu.VMEM((chunks, cells, slots), F32),
        ],
    )(
        cell_rank, in_hbm(cell_skel), in_hbm(cell_interp), in_hbm(cell_matrix),
        x_face_rank, in_hbm(x_face_skel), in_hbm(x_face_interp), in_hbm(x_coupling),
        y_face_rank, in_hbm(y_face_skel), in_hbm(y_face_interp), in_hbm(y_coupling),
    )
    edge_in = passed_along(edge, "yz", -1)
    packed_in = passed_along(packed, "gx", -1)
    packed_last_in = passed_along(packed_last, "gx", -1)
    face_bytes = nj * (4 * rows * slots + 4 * slots * slots) * 2

    last = nx - 1
    tail = nj - 1
    group = tail // cells

    def last_block(*dims):
        return pl.BlockSpec((1, cells) + dims, lambda c: (last, c) + (0,) * len(dims))

    def plain(*dims):
        return pl.BlockSpec((cells,) + dims, lambda c: (c,) + (0,) * len(dims))

    part, lower_turned = call(
        functools.partial(x_part_kernel, cells, last),
        (chunks,),
        [
            smem,
            last_block(fslots),
            last_block(rows, fslots),
            last_block(half),
            plain(slots, half),
            plain(slots, slots),
            plain(half, slots),
        ],
        [plain(fslots, fslots), plain(fslots, slots)],
        [
            shape((nj, fslots, fslots), F32),
            shape((nj, fslots, slots), BF),
        ],
        8 * unit // nx,
        face_bytes,
    )(x_face_rank, x_face_skel, x_face_interp, x_coupling, last_turned, last_schur, top_in)

    edge_in, part = lax.optimization_barrier((edge_in, part))
    y_out = call(
        functools.partial(y_edge_kernel, nx, tail),
        (1,),
        [
            smem,
            pl.BlockSpec((nx, cells, fslots), lambda i: (0, group, 0)),
            pl.BlockSpec((nx, 1, rows, fslots), lambda i: (0, tail, 0, 0)),
            pl.BlockSpec((nx, cells, half), lambda i: (0, group, 0)),
            pl.BlockSpec((nx, 2, slots, half), lambda i: (0, 0, 0, 0)),
            pl.BlockSpec((nx, 2, slots, half), lambda i: (0, 0, 0, 0)),
            pl.BlockSpec(memory_space=pl.ANY),
        ],
        pl.BlockSpec((nx, 1, fslots, fslots), lambda i: (0, tail, 0, 0)),
        shape((nx, nj, fslots, fslots), BF),
        8 * unit // nj,
        nx * face_bytes // nj,
        {6: 0},
    )(y_face_rank, y_face_skel, in_hbm(y_face_interp), y_coupling, corner, edge_in, y_out)

    for places, arrived in (
        (range(chunks - 1), packed_in),
        (range(chunks - 1, chunks), packed_last_in),
    ):
        count = len(places)
        x_out = call(
            functools.partial(x_last_kernel, cells, last, places),
            (),
            [vmem, vmem, vmem, hbm],
            hbm,
            shape((nx, nj, fslots, fslots), BF),
            3 * unit // nx * count // chunks,
            nj * slots * slots * 11 * count // chunks,
            {3: 0},
            scratch=[
                pltpu.VMEM((count * cells, fslots, fslots), BF),
                pltpu.SemaphoreType.DMA((count,)),
            ],
        )(part, lower_turned, arrived, x_out)
    return (x_out, y_out)


def solution(mesh):
    return jax.shard_map(
        body,
        mesh=mesh,
        in_specs=(
            P("gx", "yz", None, None),
            P("gx", "yz", None),
            P("gx", "yz", None),
            P("gx", "yz", None, None),
            P("gx", "yz", None),
            P("gx", "yz"),
            P("gx", "yz", None, None),
            P("gx", "yz", None),
            P("gx", "yz"),
            P("gx", "yz", None, None),
            P("gx", "yz", None),
            P("gx", "yz"),
        ),
        out_specs=(P("gx", "yz", None, None), P("gx", "yz", None, None)),
        check_vma=False,
    )
```

```python
import functools

import jax
import jax.numpy as jnp
from jax import lax
from jax.experimental import pallas as pl
from jax.experimental.pallas import tpu as pltpu
from jax.sharding import PartitionSpec as P

BF = jnp.bfloat16
F32 = jnp.float32
MIB = 1024 * 1024


def passed_along(x, axis, by):
    devices = lax.axis_size(axis)
    pairs = [(i, i + by) for i in range(devices) if 0 <= i + by < devices]
    return lax.ppermute(x, axis, pairs)


def dot_nt(a, b):
    return lax.dot_general(a, b, (((1,), (1,)), ((), ())), preferred_element_type=F32)


def dot(a, b):
    return lax.dot_general(a, b, (((1,), (0,)), ((), ())), preferred_element_type=F32)


def marks_of(skel_row, rank, interp):
    rows, slots = interp.shape
    live = lax.broadcasted_iota(jnp.int32, (1, slots), 1) < rank
    picked_row = jnp.where(live, skel_row, -1).astype(F32).astype(BF)
    row = lax.broadcasted_iota(jnp.int32, (rows, slots), 0).astype(F32).astype(BF)
    live_row = jnp.where(live, F32(1.0), F32(0.0)).astype(BF)
    return row == picked_row, interp * live_row


def kept_cleared(turned):
    most = jnp.max(turned, axis=0, keepdims=True)
    least = jnp.where(most.astype(F32) == 1.0, F32(1.0), F32(-2.0)).astype(BF)
    return jnp.where(turned >= least, turned, BF(0.0))


def marked_of(skel_row, rank, interp):
    hit, live = marks_of(skel_row, rank, interp)
    return jnp.where(hit, BF(1.0), live)


def bases_of(cells, layer, first, rank_ref, skel, interp_ref):
    marked = [
        marked_of(skel[k : k + 1], rank_ref[layer, first + k], interp_ref[0, k])
        for k in range(cells)
    ]
    return [kept_cleared(t) for t in [jnp.transpose(m) for m in marked]]


def scaled(turned, conduct):
    return turned * -conduct


def face_of(left, link, link_t, right):
    upper = jnp.concatenate([left, link], axis=1)
    lower = jnp.concatenate([link_t, right], axis=1)
    return jnp.concatenate([upper, lower], axis=0)


def project(turned, matrices):
    inner = [dot(t, m).astype(BF) for t, m in zip(turned, matrices)]
    return [dot_nt(i, t) for i, t in zip(inner, turned)]


def top_kernel(cells, rank_hbm, skel_hbm, interp_hbm, out_ref, rank_ref, skel_ref, held, small_sems, sems):
    count, half, _ = out_ref.shape
    small = [
        pltpu.make_async_copy(rank_hbm, rank_ref, small_sems.at[0]),
        pltpu.make_async_copy(skel_hbm.at[0], skel_ref, small_sems.at[1]),
    ]
    copies = []
    for c in range(count // cells):
        group = pl.ds(c * cells, cells)
        copies.append(
            pltpu.make_async_copy(
                interp_hbm.at[0, group, pl.ds(0, half)], held.at[group], sems.at[c]
            )
        )
    for copy in small + copies:
        copy.start()
    for copy in small:
        copy.wait()
    for c in range(count // cells):
        copies[c].wait()
        for k in range(c * cells, (c + 1) * cells):
            out_ref[k] = marked_of(skel_ref[k : k + 1], rank_ref[0, k], held[k])


def pack_masks(size):
    half = size // 2
    row = lax.broadcasted_iota(jnp.int32, (half, size), 0)
    lane = lax.broadcasted_iota(jnp.int32, (half, size), 1)
    ahead = lane - row
    upper = (ahead >= 0) & (ahead < half)
    return upper, ahead == 0, ahead == half


def main_kernel(
    cells, layers, chunks,
    rank_ref, skel_ref, interp_ref, matrix_ref,
    x_rank_ref, x_skel_ref, x_interp_ref, x_coup_ref,
    y_rank_ref, y_skel_ref, y_interp_ref, y_coup_ref,
    x_out_ref, y_out_ref, packed_ref, packed_last_ref, edge_ref, corner_ref, last_turned_ref, last_schur_ref,
    store_turned, store_schur, store_extra, x_coup_held, y_coup_held,
):
    layer = layers - 1 - pl.program_id(0)
    chunk = chunks - 1 - pl.program_id(1)
    first = chunk * cells
    slots = skel_ref.shape[-1]
    half = slots // 2
    top = interp_ref.shape[2] // 2

    rows = pl.ds(pl.multiple_of(first, cells), cells)

    @pl.when((pl.program_id(0) == 0) & (pl.program_id(1) == 0))
    def _():
        x_coup_held[...] = x_coup_ref[...].astype(F32)
        y_coup_held[...] = y_coup_ref[...].astype(F32)

    turned = bases_of(cells, layer, first, rank_ref, skel_ref[layer, rows], interp_ref)
    schurs = project(turned, [matrix_ref[0, k] for k in range(cells)])
    schurs = [s.astype(BF) for s in schurs]

    def faces(out_ref, f_rank_ref, f_skel_ref, f_interp_ref, coup_held, rights):
        found = bases_of(cells, layer, first, f_rank_ref, f_skel_ref[layer, rows], f_interp_ref)
        conducts = coup_held[layer, rows].astype(BF)
        matrices = []
        for k in range(cells):
            right_turned, right = rights[k]
            conduct = conducts[k : k + 1]
            lower = turned[k][:, top:]
            link = dot_nt(scaled(lower, conduct), right_turned).astype(BF)
            link_t = dot_nt(scaled(right_turned, conduct), lower).astype(BF)
            matrices.append(face_of(schurs[k], link, link_t, right))
        results = project(found, matrices)
        for k in range(cells):
            out_ref[0, k] = results[k].astype(BF)

    def stored(place):
        return store_turned[place], store_schur[place]

    after = jnp.minimum(first + cells, store_schur.shape[0] - 1)
    rights = [(turned[k][:, :top], schurs[k]) for k in range(1, cells)]
    faces(y_out_ref, y_rank_ref, y_skel_ref, y_interp_ref, y_coup_held, rights + [stored(after)])

    @pl.when(layer < layers - 1)
    def _():
        rights = [stored(first + k) for k in range(cells)]
        faces(x_out_ref, x_rank_ref, x_skel_ref, x_interp_ref, x_coup_held, rights)

    for k in range(cells):
        store_turned[first + k] = turned[k][:, :top]
        store_schur[first + k] = schurs[k]

    @pl.when(layer == layers - 1)
    def _():
        for k in range(cells):
            last_turned_ref[first + k] = turned[k][:, top:]
            last_schur_ref[first + k] = schurs[k]

    @pl.when(layer == 0)
    def _():
        upper, same, opposite = pack_masks(slots)

        def put(packed_ref, start):
            for k in range(cells):
                above, below = schurs[k][:half].astype(F32), schurs[k][half:].astype(F32)
                place = pl.ds(pl.multiple_of(start + k * half, half), half)
                packed_ref[place] = jnp.where(upper, above, below).astype(BF)

        @pl.when(chunk < chunks - 1)
        def _():
            put(packed_ref, chunk * (cells * half))

        @pl.when(chunk == chunks - 1)
        def _():
            put(packed_last_ref, 0)

        for p in range(0, cells, 2):
            extra = jnp.where(opposite, schurs[p][:half].astype(F32), F32(0.0))
            if p + 1 < cells:
                extra += jnp.where(same, schurs[p + 1][half:].astype(F32), F32(0.0))
            store_extra[chunk, p // 2 : p // 2 + 1] = jnp.sum(extra, axis=0, keepdims=True)

        @pl.when(chunk == 0)
        def _():
            pairs = -(-cells // 2)
            for ref, places in ((packed_ref, range(chunks - 1)), (packed_last_ref, [chunks - 1])):
                start = len(places) * cells * half
                rows = [store_extra[c, :pairs] for c in places]
                pad = ref.shape[0] - start - pairs * len(places)
                if pad:
                    rows.append(jnp.zeros((pad, slots), F32))
                ref[start:] = jnp.concatenate(rows, axis=0).astype(BF)

    @pl.when(chunk == 0)
    def _():
        edge_ref[layer, 0] = turned[0][:, :top]
        edge_ref[layer, 1] = schurs[0]

    @pl.when(chunk == chunks - 1)
    def _():
        corner_ref[layer, 0] = turned[cells - 1][:, top:]
        corner_ref[layer, 1] = schurs[cells - 1]


def y_edge_kernel(layers, place, rank_ref, skel_ref, interp_ref, coup_ref, corner_ref, edge_ref, _, out_ref):
    row = place % skel_ref.shape[1]
    marked = [
        marked_of(skel_ref[i, row : row + 1], rank_ref[i, place], interp_ref[i, 0])
        for i in range(layers)
    ]
    found = [kept_cleared(jnp.transpose(m)) for m in marked]
    matrices = []
    for i in range(layers):
        conduct = coup_ref[i, row : row + 1]
        link = dot_nt(scaled(corner_ref[i, 0], conduct), edge_ref[i, 0]).astype(BF)
        link_t = dot_nt(scaled(edge_ref[i, 0], conduct), corner_ref[i, 0]).astype(BF)
        matrices.append(face_of(corner_ref[i, 1], link, link_t, edge_ref[i, 1]))
    results = project(found, matrices)
    for i in range(layers):
        out_ref[i, 0] = results[i].astype(BF)


def x_part_kernel(
    cells, layer, rank_ref, skel_ref, interp_ref, coup_ref, turned_ref, schur_ref, top_ref,
    part_ref, lower_turned_ref,
):
    half = top_ref.shape[-2]
    faces = bases_of(cells, layer, pl.program_id(0) * cells, rank_ref, skel_ref[0], interp_ref)
    for k in range(cells):
        lower_turned_ref[k] = faces[k][:, half:]
    tops = [kept_cleared(t) for t in [jnp.transpose(top_ref[k]) for k in range(cells)]]
    matrices = []
    for k in range(cells):
        conduct = coup_ref[0, k : k + 1]
        link = dot_nt(scaled(turned_ref[k], conduct), tops[k]).astype(BF)
        link_t = dot_nt(scaled(tops[k], conduct), turned_ref[k]).astype(BF)
        matrices.append(face_of(schur_ref[k], link, link_t, jnp.zeros_like(link)))
    results = project(faces, matrices)
    for k in range(cells):
        part_ref[k] = results[k]


def x_last_kernel(
    cells, layer, places, part_ref, lower_turned_ref, packed_ref, _, out_ref, held, sems
):
    slots = part_ref.shape[-1]
    half = slots // 2
    upper, same, opposite = pack_masks(slots)
    one, zero, mid = F32(1.0), F32(0.0), F32(0.5)
    top_scale = jnp.where(same, mid, jnp.where(upper, one, zero))
    low_scale = jnp.where(opposite, mid, jnp.where(upper, zero, one))
    same_scale = jnp.where(same, one, zero)
    opposite_scale = jnp.where(opposite, one, zero)
    extras = packed_ref[len(places) * cells * half :].astype(F32)
    pairs = -(-cells // 2)
    copies = []
    for n, c in enumerate(places):
        group = range(c * cells, (c + 1) * cells)
        schurs = []
        for k in range(cells):
            start = (n * cells + k) * half
            packed = packed_ref[start : start + half].astype(F32)
            extra = extras[n * pairs + k // 2 : n * pairs + k // 2 + 1]
            top, low = packed * top_scale, packed * low_scale
            if k % 2 == 0:
                top += extra * opposite_scale
            else:
                low += extra * same_scale
            tri = jnp.concatenate([top, low], axis=0).astype(BF)
            schurs.append(tri + jnp.transpose(tri))
        results = project([lower_turned_ref[k] for k in group], schurs)
        for k, result in enumerate(results):
            held[n * cells + k] = (part_ref[c * cells + k] + result).astype(BF)
        copies.append(
            pltpu.make_async_copy(
                held.at[pl.ds(n * cells, cells)],
                out_ref.at[layer, pl.ds(c * cells, cells)],
                sems.at[n],
            )
        )
        copies[n].start()
    for copy in copies:
        copy.wait()


def call(kernel, grid, in_specs, out_specs, out_shape, flops, moved, aliases=None, vmem=24, scratch=()):
    return pl.pallas_call(
        kernel,
        grid=grid,
        in_specs=in_specs,
        out_specs=out_specs,
        out_shape=out_shape,
        scratch_shapes=scratch,
        input_output_aliases=aliases or {},
        compiler_params=pltpu.CompilerParams(vmem_limit_bytes=vmem * MIB),
        cost_estimate=pl.CostEstimate(flops=flops, bytes_accessed=moved, transcendentals=0),
    )


def in_hbm(x):
    return pltpu.with_memory_space_constraint(x, pltpu.HBM)


def body(
    cell_matrix,
    x_coupling,
    y_coupling,
    cell_interp,
    cell_skel,
    cell_rank,
    x_face_interp,
    x_face_skel,
    x_face_rank,
    y_face_interp,
    y_face_skel,
    y_face_rank,
):
    nx, nj, rows, slots = cell_interp.shape
    half = rows // 2
    fslots = x_face_interp.shape[-1]
    cells = next(n for n in (8, 4, 2, 1) if nj % n == 0 and nj > n)
    chunks = nj // cells
    unit = 2 * nx * nj * slots * slots * slots
    smem = pl.BlockSpec(memory_space=pltpu.SMEM)
    shape = jax.ShapeDtypeStruct

    hbm = pl.BlockSpec(memory_space=pltpu.HBM)
    vmem = pl.BlockSpec(memory_space=pltpu.VMEM)
    top = call(
        functools.partial(top_kernel, cells),
        (),
        [hbm, hbm, hbm],
        vmem,
        shape((nj, half, slots), BF),
        0,
        4 * nj * half * slots,
        vmem=8,
        scratch=[
            pltpu.SMEM((nx, nj), jnp.int32),
            pltpu.VMEM((nj, slots), jnp.int32),
            pltpu.VMEM((nj, half, slots), BF),
            pltpu.SemaphoreType.DMA((2,)),
            pltpu.SemaphoreType.DMA((chunks,)),
        ],
    )(in_hbm(cell_rank), in_hbm(cell_skel), in_hbm(cell_interp))
    top_in = passed_along(top, "gx", -1)


    def pack_rows(count):
        extra = count * -(-cells // 2)
        return count * cells * slots // 2 + -(-extra // 16) * 16

    near = max(nx - 2, 0)

    def down(*dims):
        zeros = (0,) * len(dims)
        return pl.BlockSpec((1, cells) + dims, lambda i, c: (nx - 1 - i, chunks - 1 - c) + zeros)

    def down_x(*dims):
        zeros = (0,) * len(dims)

        def place(i, c):
            return (jnp.minimum(nx - 1 - i, near), jnp.where(i == 0, chunks - 1, chunks - 1 - c)) + zeros

        return pl.BlockSpec((1, cells) + dims, place)

    x_out, y_out, packed, packed_last, edge, corner, last_turned, last_schur = call(
        functools.partial(main_kernel, cells, nx, chunks),
        (nx, chunks),
        [
            smem, vmem, down(rows, slots), down(rows, rows),
            smem, vmem, down_x(rows, fslots), vmem,
            smem, vmem, down(rows, fslots), vmem,
        ],
        [
            down_x(fslots, fslots),
            down(fslots, fslots),
            vmem, vmem, vmem, vmem, vmem, vmem,
        ],
        [
            shape((nx, nj, fslots, fslots), BF),
            shape((nx, nj, fslots, fslots), BF),
            shape((pack_rows(chunks - 1), slots), BF),
            shape((pack_rows(1), slots), BF),
            shape((nx, 2, slots, half), BF),
            shape((nx, 2, slots, half), BF),
            shape((nj, slots, half), BF),
            shape((nj, slots, slots), BF),
        ],
        20 * unit,
        nx * nj * (rows * rows + 3 * rows * slots + 3 * slots * slots) * 2,
        vmem=32,
        scratch=[
            pltpu.VMEM((nj, slots, half), BF),
            pltpu.VMEM((nj, slots, slots), BF),
            pltpu.VMEM((chunks, cells, slots), F32),
            pltpu.VMEM((nx, nj, half), F32),
            pltpu.VMEM((nx, nj, half), F32),
        ],
    )(
        cell_rank, cell_skel, in_hbm(cell_interp), in_hbm(cell_matrix),
        x_face_rank, x_face_skel, in_hbm(x_face_interp), x_coupling,
        y_face_rank, y_face_skel, in_hbm(y_face_interp), y_coupling,
    )
    edge_in = passed_along(edge, "yz", -1)
    packed_in = passed_along(packed, "gx", -1)
    packed_last_in = passed_along(packed_last, "gx", -1)
    face_bytes = nj * (4 * rows * slots + 4 * slots * slots) * 2

    last = nx - 1
    tail = nj - 1
    group = tail // cells

    def last_block(*dims):
        return pl.BlockSpec((1, cells) + dims, lambda c: (last, c) + (0,) * len(dims))

    def plain(*dims):
        return pl.BlockSpec((cells,) + dims, lambda c: (c,) + (0,) * len(dims))

    part, lower_turned = call(
        functools.partial(x_part_kernel, cells, last),
        (chunks,),
        [
            smem,
            last_block(fslots),
            last_block(rows, fslots),
            last_block(half),
            plain(slots, half),
            plain(slots, slots),
            plain(half, slots),
        ],
        [plain(fslots, fslots), plain(fslots, slots)],
        [
            shape((nj, fslots, fslots), F32),
            shape((nj, fslots, slots), BF),
        ],
        8 * unit // nx,
        face_bytes,
    )(x_face_rank, x_face_skel, x_face_interp, x_coupling, last_turned, last_schur, top_in)

    edge_in, part = lax.optimization_barrier((edge_in, part))
    y_out = call(
        functools.partial(y_edge_kernel, nx, tail),
        (1,),
        [
            smem,
            pl.BlockSpec((nx, cells, fslots), lambda i: (0, group, 0)),
            pl.BlockSpec((nx, 1, rows, fslots), lambda i: (0, tail, 0, 0)),
            pl.BlockSpec((nx, cells, half), lambda i: (0, group, 0)),
            pl.BlockSpec((nx, 2, slots, half), lambda i: (0, 0, 0, 0)),
            pl.BlockSpec((nx, 2, slots, half), lambda i: (0, 0, 0, 0)),
            pl.BlockSpec(memory_space=pl.ANY),
        ],
        pl.BlockSpec((nx, 1, fslots, fslots), lambda i: (0, tail, 0, 0)),
        shape((nx, nj, fslots, fslots), BF),
        8 * unit // nj,
        nx * face_bytes // nj,
        {6: 0},
    )(y_face_rank, y_face_skel, in_hbm(y_face_interp), y_coupling, corner, edge_in, y_out)

    for places, arrived in (
        (range(chunks - 1), packed_in),
        (range(chunks - 1, chunks), packed_last_in),
    ):
        count = len(places)
        x_out = call(
            functools.partial(x_last_kernel, cells, last, places),
            (),
            [vmem, vmem, vmem, hbm],
            hbm,
            shape((nx, nj, fslots, fslots), BF),
            3 * unit // nx * count // chunks,
            nj * slots * slots * 11 * count // chunks,
            {3: 0},
            scratch=[
                pltpu.VMEM((count * cells, fslots, fslots), BF),
                pltpu.SemaphoreType.DMA((count,)),
            ],
        )(part, lower_turned, arrived, x_out)
    return (x_out, y_out)


def solution(mesh):
    return jax.shard_map(
        body,
        mesh=mesh,
        in_specs=(
            P("gx", "yz", None, None),
            P("gx", "yz", None),
            P("gx", "yz", None),
            P("gx", "yz", None, None),
            P("gx", "yz", None),
            P("gx", "yz"),
            P("gx", "yz", None, None),
            P("gx", "yz", None),
            P("gx", "yz"),
            P("gx", "yz", None, None),
            P("gx", "yz", None),
            P("gx", "yz"),
        ),
        out_specs=(P("gx", "yz", None, None), P("gx", "yz", None, None)),
        check_vma=False,
    )
```

```python
import functools

import jax
import jax.numpy as jnp
from jax import lax
from jax.experimental import pallas as pl
from jax.experimental.pallas import tpu as pltpu
from jax.sharding import PartitionSpec as P

BF = jnp.bfloat16
F32 = jnp.float32
MIB = 1024 * 1024


def passed_along(x, axis, by):
    devices = lax.axis_size(axis)
    pairs = [(i, i + by) for i in range(devices) if 0 <= i + by < devices]
    return lax.ppermute(x, axis, pairs)


def dot_nt(a, b):
    return lax.dot_general(a, b, (((1,), (1,)), ((), ())), preferred_element_type=F32)


def dot(a, b):
    return lax.dot_general(a, b, (((1,), (0,)), ((), ())), preferred_element_type=F32)


def marked_of(skel_row, rank, interp):
    rows, slots = interp.shape
    live = lax.broadcasted_iota(jnp.int32, (1, slots), 1) < rank
    picked_row = jnp.where(live, skel_row, -1).astype(F32).astype(BF)
    row = lax.broadcasted_iota(jnp.int32, (rows, slots), 0).astype(F32).astype(BF)
    live_row = jnp.where(live, F32(1.0), F32(0.0)).astype(BF)
    return jnp.where(row == picked_row, BF(1.0), interp * live_row)


def kept_cleared(turned):
    most = jnp.max(turned, axis=0, keepdims=True)
    least = jnp.where(most.astype(F32) == 1.0, F32(1.0), F32(-2.0)).astype(BF)
    return jnp.where(turned >= least, turned, BF(0.0))


def bases_of(cells, layer, first, rank_ref, skel_ref, interp_of):
    marked = [
        marked_of(skel_ref[layer, pl.ds(first + k, 1)], rank_ref[layer, first + k], interp_of(k))
        for k in range(cells)
    ]
    return [kept_cleared(t) for t in [jnp.transpose(m) for m in marked]]


def scaled(turned, conduct):
    return turned * -conduct.astype(BF)


def face_of(left, link, link_t, right):
    upper = jnp.concatenate([left, link], axis=1)
    lower = jnp.concatenate([link_t, right], axis=1)
    return jnp.concatenate([upper, lower], axis=0)


def joined(lower, conduct, right_turned, left, right):
    link = dot_nt(scaled(lower, conduct), right_turned).astype(BF)
    link_t = dot_nt(scaled(right_turned, conduct), lower).astype(BF)
    return face_of(left, link, link_t, right)


def project(turned, matrices):
    inner = [dot(t, m).astype(BF) for t, m in zip(turned, matrices)]
    return [dot_nt(i, t) for i, t in zip(inner, turned)]


def pack_masks(size):
    half = size // 2
    row = lax.broadcasted_iota(jnp.int32, (half, size), 0)
    lane = lax.broadcasted_iota(jnp.int32, (half, size), 1)
    ahead = lane - row
    upper = (ahead >= 0) & (ahead < half)
    return upper, ahead == 0, ahead == half


def top_kernel(cells, rank_hbm, skel_hbm, interp_hbm, out_ref, rank_ref, skel_ref, held, small_sems, sems):
    count, half, _ = out_ref.shape
    small = [
        pltpu.make_async_copy(rank_hbm, rank_ref, small_sems.at[0]),
        pltpu.make_async_copy(skel_hbm, skel_ref, small_sems.at[1]),
    ]

    def fetch(c):
        group = pl.ds(c * cells, cells)
        return pltpu.make_async_copy(
            interp_hbm.at[0, group, pl.ds(0, half)], held.at[group], sems.at[c]
        )

    for copy in small:
        copy.start()
    for c in range(count // cells):
        fetch(c).start()
    for copy in small:
        copy.wait()

    def step(c, _):
        fetch(c).wait()
        for k in range(cells):
            place = c * cells + k
            out_ref[place] = marked_of(skel_ref[0, pl.ds(place, 1)], rank_ref[0, place], held[place])
        return 0

    lax.fori_loop(0, count // cells, step, 0)


def main_kernel(
    cells, layers, chunks, late,
    rank_ref, skel_ref, interp_ref, matrix_ref,
    x_rank_ref, x_skel_ref, x_interp_ref, x_coup_ref,
    y_rank_ref, y_skel_ref, y_interp_ref, y_coup_ref,
    x_out_ref, y_out_ref, packed_ref, packed_late_ref, edge_ref, corner_ref, last_turned_ref, last_schur_ref,
    store_turned, store_schur, store_extra, x_coup_held, y_coup_held,
):
    layer = layers - 1 - pl.program_id(0)
    chunk = chunks - 1 - pl.program_id(1)
    first = chunk * cells
    slots = skel_ref.shape[-1]
    half = slots // 2
    pairs = -(-cells // 2)
    top = interp_ref.shape[2] // 2

    @pl.when((pl.program_id(0) == 0) & (pl.program_id(1) == 0))
    def _():
        x_coup_held[...] = x_coup_ref[...].astype(F32)
        y_coup_held[...] = y_coup_ref[...].astype(F32)

    turned = bases_of(cells, layer, first, rank_ref, skel_ref, lambda k: interp_ref[0, k])
    schurs = project(turned, [matrix_ref[0, k] for k in range(cells)])
    schurs = [s.astype(BF) for s in schurs]

    def faces(out_ref, f_rank_ref, f_skel_ref, f_interp_ref, coup_held, rights):
        found = bases_of(cells, layer, first, f_rank_ref, f_skel_ref, lambda k: f_interp_ref[0, k])
        matrices = [
            joined(
                turned[k][:, top:], coup_held[layer, pl.ds(first + k, 1)], rights[k][0], schurs[k], rights[k][1]
            )
            for k in range(cells)
        ]
        results = project(found, matrices)
        for k in range(cells):
            out_ref[0, k] = results[k].astype(BF)

    def stored(place):
        return store_turned[place], store_schur[place]

    after = jnp.minimum(first + cells, store_schur.shape[0] - 1)
    rights = [(turned[k][:, :top], schurs[k]) for k in range(1, cells)]
    faces(y_out_ref, y_rank_ref, y_skel_ref, y_interp_ref, y_coup_held, rights + [stored(after)])

    @pl.when(layer < layers - 1)
    def _():
        rights = [stored(first + k) for k in range(cells)]
        faces(x_out_ref, x_rank_ref, x_skel_ref, x_interp_ref, x_coup_held, rights)

    for k in range(cells):
        store_turned[first + k] = turned[k][:, :top]
        store_schur[first + k] = schurs[k]

    @pl.when(layer == layers - 1)
    def _():
        for k in range(cells):
            last_turned_ref[first + k] = turned[k][:, top:]
            last_schur_ref[first + k] = schurs[k]

    @pl.when(layer == 0)
    def _():
        upper, same, opposite = pack_masks(slots)
        packs = []
        for k in range(cells):
            above, below = schurs[k][:half].astype(F32), schurs[k][half:].astype(F32)
            packs.append(jnp.where(upper, above, below).astype(BF))

        def put(ref, start):
            for k in range(cells):
                ref[pl.ds(pl.multiple_of(start + k * half, half), half)] = packs[k]

        @pl.when(chunk < chunks - late)
        def _():
            put(packed_ref, chunk * (cells * half))

        @pl.when(chunk >= chunks - late)
        def _():
            put(packed_late_ref, (chunk - (chunks - late)) * (cells * half))

        for p in range(0, cells, 2):
            extra = jnp.where(opposite, schurs[p][:half].astype(F32), F32(0.0))
            if p + 1 < cells:
                extra += jnp.where(same, schurs[p + 1][half:].astype(F32), F32(0.0))
            store_extra[chunk, p // 2 : p // 2 + 1] = jnp.sum(extra, axis=0, keepdims=True)

        @pl.when(chunk == 0)
        def _():
            for ref, places in ((packed_ref, range(chunks - late)), (packed_late_ref, range(chunks - late, chunks))):
                start = len(places) * cells * half
                rows = [store_extra[c, :pairs] for c in places]
                pad = ref.shape[0] - start - pairs * len(places)
                if pad:
                    rows.append(jnp.zeros((pad, slots), F32))
                ref[start:] = jnp.concatenate(rows, axis=0).astype(BF)

    @pl.when(chunk == 0)
    def _():
        edge_ref[layer, 0] = turned[0][:, :top]
        edge_ref[layer, 1] = schurs[0]

    @pl.when(chunk == chunks - 1)
    def _():
        corner_ref[layer, 0] = turned[cells - 1][:, top:]
        corner_ref[layer, 1] = schurs[cells - 1]


def y_edge_kernel(layers, place, rank_ref, skel_ref, interp_ref, coup_ref, corner_ref, edge_ref, _, out_ref):
    marked = [
        marked_of(skel_ref[i, place : place + 1], rank_ref[i, place], interp_ref[i, 0])
        for i in range(layers)
    ]
    found = [kept_cleared(jnp.transpose(m)) for m in marked]
    matrices = [
        joined(corner_ref[i, 0], coup_ref[i, place : place + 1], edge_ref[i, 0], corner_ref[i, 1], edge_ref[i, 1])
        for i in range(layers)
    ]
    results = project(found, matrices)
    for i in range(layers):
        out_ref[i, 0] = results[i].astype(BF)


def x_part_kernel(
    cells, layer, rank_ref, skel_ref, interp_ref, coup_ref, turned_ref, schur_ref, top_ref,
    part_ref, lower_ref, coup_held,
):
    first = pl.program_id(0) * cells
    half = top_ref.shape[-2]

    @pl.when(pl.program_id(0) == 0)
    def _():
        coup_held[...] = coup_ref[...].astype(F32)

    faces = bases_of(cells, layer, first, rank_ref, skel_ref, lambda k: interp_ref[0, k])
    for k in range(cells):
        lower_ref[first + k] = faces[k][:, half:]
    tops = [kept_cleared(t) for t in [jnp.transpose(top_ref[first + k]) for k in range(cells)]]
    nothing = jnp.zeros(schur_ref.shape[1:], BF)
    matrices = [
        joined(
            turned_ref[first + k], coup_held[layer, pl.ds(first + k, 1)], tops[k], schur_ref[first + k], nothing
        )
        for k in range(cells)
    ]
    results = project(faces, matrices)
    for k in range(cells):
        part_ref[first + k] = results[k]


def x_last_kernel(
    cells, layer, begin, end, part_ref, lower_ref, packed_ref, _, out_ref, held, extra_ref, sems
):
    slots = part_ref.shape[-1]
    half = slots // 2
    pairs = -(-cells // 2)
    upper, same, opposite = pack_masks(slots)
    one, zero, mid = F32(1.0), F32(0.0), F32(0.5)
    top_scale = jnp.where(same, mid, jnp.where(upper, one, zero))
    low_scale = jnp.where(opposite, mid, jnp.where(upper, zero, one))
    same_scale = jnp.where(same, one, zero)
    opposite_scale = jnp.where(opposite, one, zero)
    extra_ref[...] = packed_ref[(end - begin) * cells * half :].astype(F32)

    def out_copy(n):
        return pltpu.make_async_copy(
            held.at[pl.ds(n * cells, cells)],
            out_ref.at[layer, pl.ds((begin + n) * cells, cells)],
            sems.at[n],
        )

    def step(n, _):
        schurs = []
        for k in range(cells):
            start = pl.multiple_of((n * cells + k) * half, half)
            packed = packed_ref[pl.ds(start, half)].astype(F32)
            extra = extra_ref[pl.ds(n * pairs + k // 2, 1)]
            top, low = packed * top_scale, packed * low_scale
            if k % 2 == 0:
                top += extra * opposite_scale
            else:
                low += extra * same_scale
            tri = jnp.concatenate([top, low], axis=0).astype(BF)
            schurs.append(tri + jnp.transpose(tri))
        places = [(begin + n) * cells + k for k in range(cells)]
        results = project([lower_ref[k] for k in places], schurs)
        for k in range(cells):
            held[n * cells + k] = (part_ref[places[k]] + results[k]).astype(BF)
        out_copy(n).start()
        return 0

    lax.fori_loop(0, end - begin, step, 0)
    for n in range(end - begin):
        out_copy(n).wait()


def call(kernel, grid, in_specs, out_specs, out_shape, flops, moved, aliases=None, vmem=24, scratch=()):
    return pl.pallas_call(
        kernel,
        grid=grid,
        in_specs=in_specs,
        out_specs=out_specs,
        out_shape=out_shape,
        scratch_shapes=scratch,
        input_output_aliases=aliases or {},
        compiler_params=pltpu.CompilerParams(vmem_limit_bytes=vmem * MIB),
        cost_estimate=pl.CostEstimate(flops=flops, bytes_accessed=moved, transcendentals=0),
    )


def in_hbm(x):
    return pltpu.with_memory_space_constraint(x, pltpu.HBM)


def body(
    cell_matrix,
    x_coupling,
    y_coupling,
    cell_interp,
    cell_skel,
    cell_rank,
    x_face_interp,
    x_face_skel,
    x_face_rank,
    y_face_interp,
    y_face_skel,
    y_face_rank,
):
    nx, nj, rows, slots = cell_interp.shape
    half = rows // 2
    fslots = x_face_interp.shape[-1]
    cells = next(n for n in (4, 2, 1) if nj % n == 0 and nj > n)
    chunks = nj // cells
    late = max(1, chunks // 4)
    early = chunks - late
    last = nx - 1
    tail = nj - 1
    unit = 2 * nx * nj * slots * slots * slots
    face_bytes = nj * (4 * rows * slots + 4 * slots * slots) * 2
    smem = pl.BlockSpec(memory_space=pltpu.SMEM)
    hbm = pl.BlockSpec(memory_space=pltpu.HBM)
    vmem = pl.BlockSpec(memory_space=pltpu.VMEM)
    shape = jax.ShapeDtypeStruct
    faces_shape = shape((nx, nj, fslots, fslots), BF)

    top = call(
        functools.partial(top_kernel, cells),
        (),
        [hbm, hbm, hbm],
        vmem,
        shape((nj, half, slots), BF),
        0,
        4 * nj * half * slots,
        vmem=8,
        scratch=[
            pltpu.SMEM((nx, nj), jnp.int32),
            pltpu.VMEM((nx, nj, slots), jnp.int32),
            pltpu.VMEM((nj, half, slots), BF),
            pltpu.SemaphoreType.DMA((2,)),
            pltpu.SemaphoreType.DMA((chunks,)),
        ],
    )(in_hbm(cell_rank), in_hbm(cell_skel), in_hbm(cell_interp))
    top_in = passed_along(top, "gx", -1)

    def pack_rows(count):
        extra = count * -(-cells // 2)
        return count * cells * slots // 2 + -(-extra // 16) * 16

    near = max(nx - 2, 0)

    def down(*dims):
        zeros = (0,) * len(dims)
        return pl.BlockSpec((1, cells) + dims, lambda i, c: (nx - 1 - i, chunks - 1 - c) + zeros)

    def down_x(*dims):
        zeros = (0,) * len(dims)

        def place(i, c):
            return (jnp.minimum(nx - 1 - i, near), jnp.where(i == 0, chunks - 1, chunks - 1 - c)) + zeros

        return pl.BlockSpec((1, cells) + dims, place)

    x_out, y_out, packed, packed_late, edge, corner, last_turned, last_schur = call(
        functools.partial(main_kernel, cells, nx, chunks, late),
        (nx, chunks),
        [
            smem, vmem, down(rows, slots), down(rows, rows),
            smem, vmem, down_x(rows, fslots), vmem,
            smem, vmem, down(rows, fslots), vmem,
        ],
        [down_x(fslots, fslots), down(fslots, fslots), vmem, vmem, vmem, vmem, vmem, vmem],
        [
            faces_shape,
            faces_shape,
            shape((pack_rows(early), slots), BF),
            shape((pack_rows(late), slots), BF),
            shape((nx, 2, slots, half), BF),
            shape((nx, 2, slots, half), BF),
            shape((nj, slots, half), BF),
            shape((nj, slots, slots), BF),
        ],
        20 * unit,
        nx * nj * (rows * rows + 3 * rows * slots + 3 * slots * slots) * 2,
        vmem=32,
        scratch=[
            pltpu.VMEM((nj, slots, half), BF),
            pltpu.VMEM((nj, slots, slots), BF),
            pltpu.VMEM((chunks, 8 * -(-cells // 16), slots), F32),
            pltpu.VMEM((nx, nj, half), F32),
            pltpu.VMEM((nx, nj, half), F32),
        ],
    )(
        cell_rank, cell_skel, in_hbm(cell_interp), in_hbm(cell_matrix),
        x_face_rank, x_face_skel, in_hbm(x_face_interp), x_coupling,
        y_face_rank, y_face_skel, in_hbm(y_face_interp), y_coupling,
    )
    edge_in = passed_along(edge, "yz", -1)
    packed_in = passed_along(packed, "gx", -1)
    packed_late_in = passed_along(packed_late, "gx", -1)

    part, lower = call(
        functools.partial(x_part_kernel, cells, last),
        (chunks,),
        [
            smem, vmem, pl.BlockSpec((1, cells, rows, fslots), lambda c: (last, c, 0, 0)), vmem,
            vmem, vmem, vmem,
        ],
        [vmem, vmem],
        [shape((nj, fslots, fslots), F32), shape((nj, fslots, slots), BF)],
        8 * unit // nx,
        face_bytes,
        scratch=[pltpu.VMEM((nx, nj, half), F32)],
    )(x_face_rank, x_face_skel, in_hbm(x_face_interp), x_coupling, last_turned, last_schur, top_in)

    edge_in, part = lax.optimization_barrier((edge_in, part))
    y_out = call(
        functools.partial(y_edge_kernel, nx, tail),
        (1,),
        [
            smem, vmem, pl.BlockSpec((nx, 1, rows, fslots), lambda i: (0, tail, 0, 0)), vmem,
            vmem, vmem, pl.BlockSpec(memory_space=pl.ANY),
        ],
        pl.BlockSpec((nx, 1, fslots, fslots), lambda i: (0, tail, 0, 0)),
        faces_shape,
        8 * unit // nj,
        nx * face_bytes // nj,
        {6: 0},
    )(y_face_rank, y_face_skel, in_hbm(y_face_interp), y_coupling, corner, edge_in, y_out)

    for begin, end, arrived in ((0, early, packed_in), (early, chunks, packed_late_in)):
        count = end - begin
        x_out = call(
            functools.partial(x_last_kernel, cells, last, begin, end),
            (),
            [vmem, vmem, vmem, hbm],
            hbm,
            faces_shape,
            3 * unit // nx * count // chunks,
            nj * slots * slots * 11 * count // chunks,
            {3: 0},
            scratch=[
                pltpu.VMEM((count * cells, fslots, fslots), BF),
                pltpu.VMEM((pack_rows(count) - count * cells * slots // 2, slots), F32),
                pltpu.SemaphoreType.DMA((count,)),
            ],
        )(part, lower, arrived, x_out)
    return (x_out, y_out)


def solution(mesh):
    return jax.shard_map(
        body,
        mesh=mesh,
        in_specs=(
            P("gx", "yz", None, None),
            P("gx", "yz", None),
            P("gx", "yz", None),
            P("gx", "yz", None, None),
            P("gx", "yz", None),
            P("gx", "yz"),
            P("gx", "yz", None, None),
            P("gx", "yz", None),
            P("gx", "yz"),
            P("gx", "yz", None, None),
            P("gx", "yz", None),
            P("gx", "yz"),
        ),
        out_specs=(P("gx", "yz", None, None), P("gx", "yz", None, None)),
        check_vma=False,
    )
```

```python
import functools

import jax
import jax.numpy as jnp
from jax import lax
from jax.experimental import pallas as pl
from jax.experimental.pallas import tpu as pltpu
from jax.sharding import PartitionSpec as P

BF = jnp.bfloat16
F32 = jnp.float32
MIB = 1024 * 1024


def passed_along(x, axis, by):
    devices = lax.axis_size(axis)
    pairs = [(i, i + by) for i in range(devices) if 0 <= i + by < devices]
    return lax.ppermute(x, axis, pairs)


def dot_nt(a, b):
    return lax.dot_general(a, b, (((1,), (1,)), ((), ())), preferred_element_type=F32)


def dot(a, b):
    return lax.dot_general(a, b, (((1,), (0,)), ((), ())), preferred_element_type=F32)


def marks_of(skel_row, rank, interp):
    rows, slots = interp.shape
    live = lax.broadcasted_iota(jnp.int32, (1, slots), 1) < rank
    picked_row = jnp.where(live, skel_row, -1).astype(F32).astype(BF)
    row = lax.broadcasted_iota(jnp.int32, (rows, slots), 0).astype(F32).astype(BF)
    live_row = jnp.where(live, F32(1.0), F32(0.0)).astype(BF)
    return row == picked_row, interp * live_row


def kept_cleared(turned):
    most = jnp.max(turned, axis=0, keepdims=True)
    least = jnp.where(most.astype(F32) == 1.0, F32(1.0), F32(-2.0)).astype(BF)
    return jnp.where(turned >= least, turned, BF(0.0))


def marked_of(skel_row, rank, interp):
    hit, live = marks_of(skel_row, rank, interp)
    return jnp.where(hit, BF(1.0), live)


def bases_of(cells, layer, first, rank_ref, skel, interp_ref):
    marked = [
        marked_of(skel[k : k + 1], rank_ref[layer, first + k], interp_ref[0, k])
        for k in range(cells)
    ]
    return [kept_cleared(t) for t in [jnp.transpose(m) for m in marked]]


def scaled(turned, conduct):
    return turned * -conduct


def face_of(left, link, link_t, right):
    upper = jnp.concatenate([left, link], axis=1)
    lower = jnp.concatenate([link_t, right], axis=1)
    return jnp.concatenate([upper, lower], axis=0)


def project(turned, matrices):
    inner = [dot(t, m).astype(BF) for t, m in zip(turned, matrices)]
    return [dot_nt(i, t) for i, t in zip(inner, turned)]


def top_kernel(cells, rank_hbm, skel_hbm, interp_hbm, out_ref, rank_ref, skel_ref, held, small_sems, sems):
    count, half, _ = out_ref.shape
    small = [
        pltpu.make_async_copy(skel_hbm.at[0], skel_ref, small_sems.at[0]),
        pltpu.make_async_copy(rank_hbm, rank_ref, small_sems.at[1]),
    ]
    copies = []
    for c in range(count // cells):
        group = pl.ds(c * cells, cells)
        copies.append(
            pltpu.make_async_copy(
                interp_hbm.at[0, group, pl.ds(0, half)], held.at[group], sems.at[c]
            )
        )
    for copy in small + copies:
        copy.start()
    for copy in small:
        copy.wait()
    for c in range(count // cells):
        copies[c].wait()
        for k in range(c * cells, (c + 1) * cells):
            out_ref[k] = marked_of(skel_ref[k : k + 1], rank_ref[0, k], held[k])


def pack_masks(size):
    half = size // 2
    row = lax.broadcasted_iota(jnp.int32, (half, size), 0)
    lane = lax.broadcasted_iota(jnp.int32, (half, size), 1)
    ahead = lane - row
    upper = (ahead >= 0) & (ahead < half)
    return upper, ahead == 0, ahead == half


def main_kernel(
    cells, layers, chunks,
    rank_ref, skel_ref, interp_ref, matrix_ref,
    x_rank_ref, x_skel_ref, x_interp_ref, x_coup_ref,
    y_rank_ref, y_skel_ref, y_interp_ref, y_coup_ref,
    x_out_ref, y_out_ref, packed_ref, packed_last_ref, edge_ref, corner_ref, last_turned_ref, last_schur_ref,
    store_turned, store_schur, store_extra, x_coup_held, y_coup_held,
):
    layer = layers - 1 - pl.program_id(0)
    chunk = chunks - 1 - pl.program_id(1)
    first = chunk * cells
    slots = skel_ref.shape[-1]
    half = slots // 2
    top = interp_ref.shape[2] // 2

    rows = pl.ds(pl.multiple_of(first, cells), cells)

    @pl.when((pl.program_id(0) == 0) & (pl.program_id(1) == 0))
    def _():
        x_coup_held[...] = x_coup_ref[...].astype(F32)
        y_coup_held[...] = y_coup_ref[...].astype(F32)

    turned = bases_of(cells, layer, first, rank_ref, skel_ref[layer, rows], interp_ref)
    schurs = project(turned, [matrix_ref[0, k] for k in range(cells)])
    schurs = [s.astype(BF) for s in schurs]

    def bases_and_matrices(f_rank_ref, f_skel_ref, f_interp_ref, coup_held, rights):
        found = bases_of(cells, layer, first, f_rank_ref, f_skel_ref[layer, rows], f_interp_ref)
        conducts = coup_held[layer, rows].astype(BF)
        matrices = []
        for k in range(cells):
            right_turned, right = rights[k]
            conduct = conducts[k : k + 1]
            lower = turned[k][:, top:]
            link = dot_nt(scaled(lower, conduct), right_turned).astype(BF)
            link_t = dot_nt(scaled(right_turned, conduct), lower).astype(BF)
            matrices.append(face_of(schurs[k], link, link_t, right))
        return found, matrices

    def stored(place):
        return store_turned[place], store_schur[place]

    def y_faces():
        after = jnp.minimum(first + cells, store_schur.shape[0] - 1)
        rights = [(turned[k][:, :top], schurs[k]) for k in range(1, cells)] + [stored(after)]
        return bases_and_matrices(y_rank_ref, y_skel_ref, y_interp_ref, y_coup_held, rights)

    @pl.when(layer == layers - 1)
    def _():
        for k, result in enumerate(project(*y_faces())):
            y_out_ref[0, k] = result.astype(BF)

    @pl.when(layer < layers - 1)
    def _():
        rights = [stored(first + k) for k in range(cells)]
        x_found, x_matrices = bases_and_matrices(x_rank_ref, x_skel_ref, x_interp_ref, x_coup_held, rights)
        y_found, y_matrices = y_faces()
        results = project(x_found + y_found, x_matrices + y_matrices)
        for k in range(cells):
            x_out_ref[0, k] = results[k].astype(BF)
            y_out_ref[0, k] = results[cells + k].astype(BF)

    for k in range(cells):
        store_turned[first + k] = turned[k][:, :top]
        store_schur[first + k] = schurs[k]

    @pl.when(layer == layers - 1)
    def _():
        for k in range(cells):
            last_turned_ref[first + k] = turned[k][:, top:]
            last_schur_ref[first + k] = schurs[k]

    @pl.when(layer == 0)
    def _():
        upper, same, opposite = pack_masks(slots)

        def put(packed_ref, start):
            for k in range(cells):
                above, below = schurs[k][:half].astype(F32), schurs[k][half:].astype(F32)
                place = pl.ds(pl.multiple_of(start + k * half, half), half)
                packed_ref[place] = jnp.where(upper, above, below).astype(BF)

        @pl.when(chunk < chunks - 1)
        def _():
            put(packed_ref, chunk * (cells * half))

        @pl.when(chunk == chunks - 1)
        def _():
            put(packed_last_ref, 0)

        for p in range(0, cells, 2):
            extra = jnp.where(opposite, schurs[p][:half].astype(F32), F32(0.0))
            if p + 1 < cells:
                extra += jnp.where(same, schurs[p + 1][half:].astype(F32), F32(0.0))
            store_extra[chunk, p // 2 : p // 2 + 1] = jnp.sum(extra, axis=0, keepdims=True)

        @pl.when(chunk == 0)
        def _():
            pairs = -(-cells // 2)
            for ref, places in ((packed_ref, range(chunks - 1)), (packed_last_ref, [chunks - 1])):
                start = len(places) * cells * half
                rows = [store_extra[c, :pairs] for c in places]
                pad = ref.shape[0] - start - pairs * len(places)
                if pad:
                    rows.append(jnp.zeros((pad, slots), F32))
                ref[start:] = jnp.concatenate(rows, axis=0).astype(BF)

    @pl.when(chunk == 0)
    def _():
        edge_ref[layer, 0] = turned[0][:, :top]
        edge_ref[layer, 1] = schurs[0]

    @pl.when(chunk == chunks - 1)
    def _():
        corner_ref[layer, 0] = turned[cells - 1][:, top:]
        corner_ref[layer, 1] = schurs[cells - 1]


def y_edge_kernel(layers, place, rank_ref, skel_ref, interp_ref, coup_ref, corner_ref, edge_ref, _, out_ref):
    row = place % skel_ref.shape[1]
    marked = [
        marked_of(skel_ref[i, row : row + 1], rank_ref[i, place], interp_ref[i, 0])
        for i in range(layers)
    ]
    found = [kept_cleared(jnp.transpose(m)) for m in marked]
    matrices = []
    for i in range(layers):
        conduct = coup_ref[i, row : row + 1]
        link = dot_nt(scaled(corner_ref[i, 0], conduct), edge_ref[i, 0]).astype(BF)
        link_t = dot_nt(scaled(edge_ref[i, 0], conduct), corner_ref[i, 0]).astype(BF)
        matrices.append(face_of(corner_ref[i, 1], link, link_t, edge_ref[i, 1]))
    results = project(found, matrices)
    for i in range(layers):
        out_ref[i, 0] = results[i].astype(BF)


def x_part_kernel(
    cells, layer, rank_ref, skel_ref, interp_ref, coup_ref, turned_ref, schur_ref, top_ref,
    part_ref, lower_turned_ref,
):
    count, slots, half = turned_ref.shape
    nothing = jnp.zeros((slots, slots), BF)
    for first in range(0, count, cells):
        group = range(first, first + cells)
        skel = skel_ref[layer, first : first + cells]
        marked = [
            marked_of(skel[k - first : k - first + 1], rank_ref[layer, k], interp_ref[layer, k]) for k in group
        ]
        faces = [kept_cleared(t) for t in [jnp.transpose(m) for m in marked]]
        for k in group:
            lower_turned_ref[k] = faces[k - first][:, half:]
        tops = [kept_cleared(t) for t in [jnp.transpose(top_ref[k]) for k in group]]
        matrices = []
        for k, top in zip(group, tops):
            conduct = coup_ref[layer, k : k + 1]
            link = dot_nt(scaled(turned_ref[k], conduct), top).astype(BF)
            link_t = dot_nt(scaled(top, conduct), turned_ref[k]).astype(BF)
            matrices.append(face_of(schur_ref[k], link, link_t, nothing))
        for k, result in zip(group, project(faces, matrices)):
            part_ref[k] = result


def x_last_kernel(
    cells, layer, places, part_ref, lower_turned_ref, packed_ref, _, out_ref, held, sems
):
    slots = part_ref.shape[-1]
    half = slots // 2
    upper, same, opposite = pack_masks(slots)
    one, zero, mid = F32(1.0), F32(0.0), F32(0.5)
    top_scale = jnp.where(same, mid, jnp.where(upper, one, zero))
    low_scale = jnp.where(opposite, mid, jnp.where(upper, zero, one))
    same_scale = jnp.where(same, one, zero)
    opposite_scale = jnp.where(opposite, one, zero)
    extras = packed_ref[len(places) * cells * half :].astype(F32)
    pairs = -(-cells // 2)
    copies = []
    for n, c in enumerate(places):
        group = range(c * cells, (c + 1) * cells)
        schurs = []
        for k in range(cells):
            start = (n * cells + k) * half
            packed = packed_ref[start : start + half].astype(F32)
            extra = extras[n * pairs + k // 2 : n * pairs + k // 2 + 1]
            top, low = packed * top_scale, packed * low_scale
            if k % 2 == 0:
                top += extra * opposite_scale
            else:
                low += extra * same_scale
            tri = jnp.concatenate([top, low], axis=0).astype(BF)
            schurs.append(tri + jnp.transpose(tri))
        results = project([lower_turned_ref[k] for k in group], schurs)
        for k, result in enumerate(results):
            held[n * cells + k] = (part_ref[c * cells + k] + result).astype(BF)
        copies.append(
            pltpu.make_async_copy(
                held.at[pl.ds(n * cells, cells)],
                out_ref.at[layer, pl.ds(c * cells, cells)],
                sems.at[n],
            )
        )
        copies[n].start()
    for copy in copies:
        copy.wait()


def call(kernel, grid, in_specs, out_specs, out_shape, flops, moved, aliases=None, vmem=24, scratch=()):
    return pl.pallas_call(
        kernel,
        grid=grid,
        in_specs=in_specs,
        out_specs=out_specs,
        out_shape=out_shape,
        scratch_shapes=scratch,
        input_output_aliases=aliases or {},
        compiler_params=pltpu.CompilerParams(vmem_limit_bytes=vmem * MIB),
        cost_estimate=pl.CostEstimate(flops=flops, bytes_accessed=moved, transcendentals=0),
    )


def in_hbm(x):
    return pltpu.with_memory_space_constraint(x, pltpu.HBM)


def body(
    cell_matrix,
    x_coupling,
    y_coupling,
    cell_interp,
    cell_skel,
    cell_rank,
    x_face_interp,
    x_face_skel,
    x_face_rank,
    y_face_interp,
    y_face_skel,
    y_face_rank,
):
    nx, nj, rows, slots = cell_interp.shape
    half = rows // 2
    fslots = x_face_interp.shape[-1]
    cells = next(n for n in (8, 4, 2, 1) if nj % n == 0 and nj > n)
    chunks = nj // cells
    face_bytes = nj * (4 * rows * slots + 4 * slots * slots) * 2
    unit = 2 * nx * nj * slots * slots * slots
    smem = pl.BlockSpec(memory_space=pltpu.SMEM)
    shape = jax.ShapeDtypeStruct

    hbm = pl.BlockSpec(memory_space=pltpu.HBM)
    vmem = pl.BlockSpec(memory_space=pltpu.VMEM)
    fine = next(n for n in (4, 2, 1) if nj % n == 0)
    top = call(
        functools.partial(top_kernel, fine),
        (),
        [hbm, hbm, hbm],
        vmem,
        shape((nj, half, slots), BF),
        0,
        4 * nj * half * slots,
        vmem=8,
        scratch=[
            pltpu.SMEM((nx, nj), jnp.int32),
            pltpu.VMEM((nj, slots), jnp.int32),
            pltpu.VMEM((nj, half, slots), BF),
            pltpu.SemaphoreType.DMA((2,)),
            pltpu.SemaphoreType.DMA((nj // fine,)),
        ],
    )(in_hbm(cell_rank), in_hbm(cell_skel), in_hbm(cell_interp))
    (
        top, cell_rank, cell_skel, x_coupling, y_coupling, x_face_skel, x_face_rank, y_face_skel, y_face_rank
    ) = lax.optimization_barrier(
        (top, cell_rank, cell_skel, x_coupling, y_coupling, x_face_skel, x_face_rank, y_face_skel, y_face_rank)
    )
    top_in = passed_along(top, "gx", -1)

    def pack_rows(count):
        extra = count * -(-cells // 2)
        return count * cells * slots // 2 + -(-extra // 16) * 16

    near = max(nx - 2, 0)

    def down(*dims):
        zeros = (0,) * len(dims)
        return pl.BlockSpec((1, cells) + dims, lambda i, c: (nx - 1 - i, chunks - 1 - c) + zeros)

    def down_x(*dims):
        zeros = (0,) * len(dims)

        def place(i, c):
            return (jnp.minimum(nx - 1 - i, near), jnp.where(i == 0, chunks - 1, chunks - 1 - c)) + zeros

        return pl.BlockSpec((1, cells) + dims, place)

    x_out, y_out, packed, packed_last, edge, corner, last_turned, last_schur = call(
        functools.partial(main_kernel, cells, nx, chunks),
        (nx, chunks),
        [
            smem, vmem, down(rows, slots), down(rows, rows),
            smem, vmem, down_x(rows, fslots), vmem,
            smem, vmem, down(rows, fslots), vmem,
        ],
        [
            down_x(fslots, fslots),
            down(fslots, fslots),
            vmem, vmem, vmem, vmem, vmem, vmem,
        ],
        [
            shape((nx, nj, fslots, fslots), BF),
            shape((nx, nj, fslots, fslots), BF),
            shape((pack_rows(chunks - 1), slots), BF),
            shape((pack_rows(1), slots), BF),
            shape((nx, 2, slots, half), BF),
            shape((nx, 2, slots, half), BF),
            shape((nj, slots, half), BF),
            shape((nj, slots, slots), BF),
        ],
        20 * unit,
        nx * nj * (rows * rows + 3 * rows * slots + 3 * slots * slots) * 2,
        vmem=32,
        scratch=[
            pltpu.VMEM((nj, slots, half), BF),
            pltpu.VMEM((nj, slots, slots), BF),
            pltpu.VMEM((chunks, cells, slots), F32),
            pltpu.VMEM((nx, nj, half), F32),
            pltpu.VMEM((nx, nj, half), F32),
        ],
    )(
        cell_rank, cell_skel, in_hbm(cell_interp), in_hbm(cell_matrix),
        x_face_rank, x_face_skel, in_hbm(x_face_interp), x_coupling,
        y_face_rank, y_face_skel, in_hbm(y_face_interp), y_coupling,
    )
    edge_in = passed_along(edge, "yz", -1)
    packed_in = passed_along(packed, "gx", -1)
    packed_last_in = passed_along(packed_last, "gx", -1)

    last = nx - 1
    tail = nj - 1
    group = tail // cells

    part, lower_turned = call(
        functools.partial(x_part_kernel, cells, last),
        (),
        [smem, vmem, vmem, vmem, vmem, vmem, vmem],
        [vmem, vmem],
        [shape((nj, fslots, fslots), F32), shape((nj, fslots, slots), BF)],
        8 * unit // nx,
        face_bytes,
        vmem=16,
    )(x_face_rank, x_face_skel, x_face_interp, x_coupling, last_turned, last_schur, top_in)

    edge_in, part = lax.optimization_barrier((edge_in, part))
    y_out = call(
        functools.partial(y_edge_kernel, nx, tail),
        (1,),
        [
            smem,
            pl.BlockSpec((nx, cells, fslots), lambda i: (0, group, 0)),
            pl.BlockSpec((nx, 1, rows, fslots), lambda i: (0, tail, 0, 0)),
            pl.BlockSpec((nx, cells, half), lambda i: (0, group, 0)),
            pl.BlockSpec((nx, 2, slots, half), lambda i: (0, 0, 0, 0)),
            pl.BlockSpec((nx, 2, slots, half), lambda i: (0, 0, 0, 0)),
            pl.BlockSpec(memory_space=pl.ANY),
        ],
        pl.BlockSpec((nx, 1, fslots, fslots), lambda i: (0, tail, 0, 0)),
        shape((nx, nj, fslots, fslots), BF),
        8 * unit // nj,
        nx * face_bytes // nj,
        {6: 0},
    )(y_face_rank, y_face_skel, in_hbm(y_face_interp), y_coupling, corner, edge_in, y_out)

    for places, arrived in (
        (range(chunks - 1), packed_in),
        (range(chunks - 1, chunks), packed_last_in),
    ):
        count = len(places)
        x_out = call(
            functools.partial(x_last_kernel, cells, last, places),
            (),
            [vmem, vmem, vmem, hbm],
            hbm,
            shape((nx, nj, fslots, fslots), BF),
            3 * unit // nx * count // chunks,
            nj * slots * slots * 11 * count // chunks,
            {3: 0},
            scratch=[
                pltpu.VMEM((count * cells, fslots, fslots), BF),
                pltpu.SemaphoreType.DMA((count,)),
            ],
        )(part, lower_turned, arrived, x_out)
    return (x_out, y_out)


def solution(mesh):
    return jax.shard_map(
        body,
        mesh=mesh,
        in_specs=(
            P("gx", "yz", None, None),
            P("gx", "yz", None),
            P("gx", "yz", None),
            P("gx", "yz", None, None),
            P("gx", "yz", None),
            P("gx", "yz"),
            P("gx", "yz", None, None),
            P("gx", "yz", None),
            P("gx", "yz"),
            P("gx", "yz", None, None),
            P("gx", "yz", None),
            P("gx", "yz"),
        ),
        out_specs=(P("gx", "yz", None, None), P("gx", "yz", None, None)),
        check_vma=False,
    )
```

```python
import functools

import jax
import jax.numpy as jnp
from jax import lax
from jax.experimental import pallas as pl
from jax.experimental.pallas import tpu as pltpu
from jax.sharding import PartitionSpec as P

BF = jnp.bfloat16
F32 = jnp.float32
MIB = 1024 * 1024


def passed_along(x, axis, by):
    devices = lax.axis_size(axis)
    pairs = [(i, i + by) for i in range(devices) if 0 <= i + by < devices]
    return lax.ppermute(x, axis, pairs)


def dot_nt(a, b):
    return lax.dot_general(a, b, (((1,), (1,)), ((), ())), preferred_element_type=F32)


def dot(a, b):
    return lax.dot_general(a, b, (((1,), (0,)), ((), ())), preferred_element_type=F32)


def marks_of(skel_row, rank, interp):
    rows, slots = interp.shape
    live = lax.broadcasted_iota(jnp.int32, (1, slots), 1) < rank
    picked_row = jnp.where(live, skel_row, -1).astype(F32).astype(BF)
    row = lax.broadcasted_iota(jnp.int32, (rows, slots), 0).astype(F32).astype(BF)
    live_row = jnp.where(live, F32(1.0), F32(0.0)).astype(BF)
    return row == picked_row, interp * live_row


def kept_cleared(turned):
    most = jnp.max(turned, axis=0, keepdims=True)
    least = jnp.where(most.astype(F32) == 1.0, F32(1.0), F32(-2.0)).astype(BF)
    return jnp.where(turned >= least, turned, BF(0.0))


def marked_of(skel_row, rank, interp):
    hit, live = marks_of(skel_row, rank, interp)
    return jnp.where(hit, BF(1.0), live)


def bases_of(cells, layer, first, rank_ref, skel, interp_ref):
    marked = [
        marked_of(skel[k : k + 1], rank_ref[layer, first + k], interp_ref[0, k])
        for k in range(cells)
    ]
    return [kept_cleared(t) for t in [jnp.transpose(m) for m in marked]]


def scaled(turned, conduct):
    return turned * -conduct


def face_of(left, link, link_t, right):
    upper = jnp.concatenate([left, link], axis=1)
    lower = jnp.concatenate([link_t, right], axis=1)
    return jnp.concatenate([upper, lower], axis=0)


def project(turned, matrices):
    inner = [dot(t, m).astype(BF) for t, m in zip(turned, matrices)]
    return [dot_nt(i, t) for i, t in zip(inner, turned)]


def top_kernel(cells, rank_hbm, skel_hbm, interp_hbm, out_ref, rank_ref, skel_ref, held, small_sems, sems):
    count, half, _ = out_ref.shape
    small = [
        pltpu.make_async_copy(rank_hbm, rank_ref, small_sems.at[0]),
        pltpu.make_async_copy(skel_hbm.at[0], skel_ref, small_sems.at[1]),
    ]
    copies = []
    for c in range(count // cells):
        group = pl.ds(c * cells, cells)
        copies.append(
            pltpu.make_async_copy(
                interp_hbm.at[0, group, pl.ds(0, half)], held.at[group], sems.at[c]
            )
        )
    for copy in small + copies:
        copy.start()
    for copy in small:
        copy.wait()
    for c in range(count // cells):
        copies[c].wait()
        for k in range(c * cells, (c + 1) * cells):
            out_ref[k] = marked_of(skel_ref[k : k + 1], rank_ref[0, k], held[k])


def pack_masks(size):
    half = size // 2
    row = lax.broadcasted_iota(jnp.int32, (half, size), 0)
    lane = lax.broadcasted_iota(jnp.int32, (half, size), 1)
    ahead = lane - row
    upper = (ahead >= 0) & (ahead < half)
    return upper, ahead == 0, ahead == half


def main_kernel(
    cells, layers, chunks,
    rank_ref, skel_ref, interp_ref, matrix_ref,
    x_rank_ref, x_skel_ref, x_interp_ref, x_coup_ref,
    y_rank_ref, y_skel_ref, y_interp_ref, y_coup_ref,
    x_out_ref, y_out_ref, packed_ref, packed_last_ref, edge_ref, corner_ref, last_turned_ref, last_schur_ref,
    store_turned, store_schur, store_extra, x_coup_held, y_coup_held,
):
    layer = layers - 1 - pl.program_id(0)
    chunk = chunks - 1 - pl.program_id(1)
    first = chunk * cells
    slots = skel_ref.shape[-1]
    half = slots // 2
    top = interp_ref.shape[2] // 2

    rows = pl.ds(pl.multiple_of(first, cells), cells)

    @pl.when((pl.program_id(0) == 0) & (pl.program_id(1) == 0))
    def _():
        x_coup_held[...] = x_coup_ref[...].astype(F32)
        y_coup_held[...] = y_coup_ref[...].astype(F32)

    turned = bases_of(cells, layer, first, rank_ref, skel_ref[layer, rows], interp_ref)
    schurs = project(turned, [matrix_ref[0, k] for k in range(cells)])
    schurs = [s.astype(BF) for s in schurs]

    def faces(out_ref, f_rank_ref, f_skel_ref, f_interp_ref, coup_held, rights):
        found = bases_of(cells, layer, first, f_rank_ref, f_skel_ref[layer, rows], f_interp_ref)
        conducts = coup_held[layer, rows].astype(BF)
        matrices = []
        for k in range(cells):
            right_turned, right = rights[k]
            conduct = conducts[k : k + 1]
            lower = turned[k][:, top:]
            link = dot_nt(scaled(lower, conduct), right_turned).astype(BF)
            link_t = dot_nt(scaled(right_turned, conduct), lower).astype(BF)
            matrices.append(face_of(schurs[k], link, link_t, right))
        results = project(found, matrices)
        for k in range(cells):
            out_ref[0, k] = results[k].astype(BF)

    def stored(place):
        return store_turned[place], store_schur[place]

    after = jnp.minimum(first + cells, store_schur.shape[0] - 1)
    rights = [(turned[k][:, :top], schurs[k]) for k in range(1, cells)]
    faces(y_out_ref, y_rank_ref, y_skel_ref, y_interp_ref, y_coup_held, rights + [stored(after)])

    @pl.when(layer < layers - 1)
    def _():
        rights = [stored(first + k) for k in range(cells)]
        faces(x_out_ref, x_rank_ref, x_skel_ref, x_interp_ref, x_coup_held, rights)

    for k in range(cells):
        store_turned[first + k] = turned[k][:, :top]
        store_schur[first + k] = schurs[k]

    @pl.when(layer == layers - 1)
    def _():
        for k in range(cells):
            last_turned_ref[first + k] = turned[k][:, top:]
            last_schur_ref[first + k] = schurs[k]

    @pl.when(layer == 0)
    def _():
        upper, same, opposite = pack_masks(slots)

        def put(packed_ref, start):
            for k in range(cells):
                above, below = schurs[k][:half].astype(F32), schurs[k][half:].astype(F32)
                place = pl.ds(pl.multiple_of(start + k * half, half), half)
                packed_ref[place] = jnp.where(upper, above, below).astype(BF)

        @pl.when(chunk < chunks - 1)
        def _():
            put(packed_ref, chunk * (cells * half))

        @pl.when(chunk == chunks - 1)
        def _():
            put(packed_last_ref, 0)

        for p in range(0, cells, 2):
            extra = jnp.where(opposite, schurs[p][:half].astype(F32), F32(0.0))
            if p + 1 < cells:
                extra += jnp.where(same, schurs[p + 1][half:].astype(F32), F32(0.0))
            store_extra[chunk, p // 2 : p // 2 + 1] = jnp.sum(extra, axis=0, keepdims=True)

        @pl.when(chunk == 0)
        def _():
            pairs = -(-cells // 2)
            for ref, places in ((packed_ref, range(chunks - 1)), (packed_last_ref, [chunks - 1])):
                start = len(places) * cells * half
                rows = [store_extra[c, :pairs] for c in places]
                pad = ref.shape[0] - start - pairs * len(places)
                if pad:
                    rows.append(jnp.zeros((pad, slots), F32))
                ref[start:] = jnp.concatenate(rows, axis=0).astype(BF)

    @pl.when(chunk == 0)
    def _():
        edge_ref[layer, 0] = turned[0][:, :top]
        edge_ref[layer, 1] = schurs[0]

    @pl.when(chunk == chunks - 1)
    def _():
        corner_ref[layer, 0] = turned[cells - 1][:, top:]
        corner_ref[layer, 1] = schurs[cells - 1]


def y_edge_kernel(layers, place, rank_ref, skel_ref, interp_ref, coup_ref, corner_ref, edge_ref, _, out_ref):
    row = place % skel_ref.shape[1]
    marked = [
        marked_of(skel_ref[i, row : row + 1], rank_ref[i, place], interp_ref[i, 0])
        for i in range(layers)
    ]
    found = [kept_cleared(jnp.transpose(m)) for m in marked]
    matrices = []
    for i in range(layers):
        conduct = coup_ref[i, row : row + 1]
        link = dot_nt(scaled(corner_ref[i, 0], conduct), edge_ref[i, 0]).astype(BF)
        link_t = dot_nt(scaled(edge_ref[i, 0], conduct), corner_ref[i, 0]).astype(BF)
        matrices.append(face_of(corner_ref[i, 1], link, link_t, edge_ref[i, 1]))
    results = project(found, matrices)
    for i in range(layers):
        out_ref[i, 0] = results[i].astype(BF)


def x_part_kernel(
    cells, layer, rank_ref, skel_ref, interp_ref, coup_ref, turned_ref, schur_ref, top_ref,
    part_ref, lower_turned_ref,
):
    count, slots, half = turned_ref.shape
    nothing = jnp.zeros((slots, slots), BF)
    for first in range(0, count, cells):
        group = range(first, first + cells)
        skel = skel_ref[layer, first : first + cells]
        marked = [
            marked_of(skel[k - first : k - first + 1], rank_ref[layer, k], interp_ref[layer, k]) for k in group
        ]
        faces = [kept_cleared(t) for t in [jnp.transpose(m) for m in marked]]
        for k in group:
            lower_turned_ref[k] = faces[k - first][:, half:]
        tops = [kept_cleared(t) for t in [jnp.transpose(top_ref[k]) for k in group]]
        matrices = []
        for k, top in zip(group, tops):
            conduct = coup_ref[layer, k : k + 1]
            link = dot_nt(scaled(turned_ref[k], conduct), top).astype(BF)
            link_t = dot_nt(scaled(top, conduct), turned_ref[k]).astype(BF)
            matrices.append(face_of(schur_ref[k], link, link_t, nothing))
        for k, result in zip(group, project(faces, matrices)):
            part_ref[k] = result


def x_last_kernel(
    cells, layer, places, part_ref, lower_turned_ref, packed_ref, _, out_ref, held, sems
):
    slots = part_ref.shape[-1]
    half = slots // 2
    upper, same, opposite = pack_masks(slots)
    one, zero, mid = F32(1.0), F32(0.0), F32(0.5)
    top_scale = jnp.where(same, mid, jnp.where(upper, one, zero))
    low_scale = jnp.where(opposite, mid, jnp.where(upper, zero, one))
    same_scale = jnp.where(same, one, zero)
    opposite_scale = jnp.where(opposite, one, zero)
    extras = packed_ref[len(places) * cells * half :].astype(F32)
    pairs = -(-cells // 2)
    copies = []
    for n, c in enumerate(places):
        group = range(c * cells, (c + 1) * cells)
        schurs = []
        for k in range(cells):
            start = (n * cells + k) * half
            packed = packed_ref[start : start + half].astype(F32)
            extra = extras[n * pairs + k // 2 : n * pairs + k // 2 + 1]
            top, low = packed * top_scale, packed * low_scale
            if k % 2 == 0:
                top += extra * opposite_scale
            else:
                low += extra * same_scale
            tri = jnp.concatenate([top, low], axis=0).astype(BF)
            schurs.append(tri + jnp.transpose(tri))
        results = project([lower_turned_ref[k] for k in group], schurs)
        part_cells = max(1, cells // 2)
        for start in range(0, cells, part_cells):
            for k in range(start, start + part_cells):
                held[n * cells + k] = (part_ref[c * cells + k] + results[k]).astype(BF)
            copy = pltpu.make_async_copy(
                held.at[pl.ds(n * cells + start, part_cells)],
                out_ref.at[layer, pl.ds(c * cells + start, part_cells)],
                sems.at[n, start // part_cells],
            )
            copy.start()
            copies.append(copy)
    for copy in copies:
        copy.wait()


def call(kernel, grid, in_specs, out_specs, out_shape, flops, moved, aliases=None, vmem=24, scratch=()):
    return pl.pallas_call(
        kernel,
        grid=grid,
        in_specs=in_specs,
        out_specs=out_specs,
        out_shape=out_shape,
        scratch_shapes=scratch,
        input_output_aliases=aliases or {},
        compiler_params=pltpu.CompilerParams(vmem_limit_bytes=vmem * MIB),
        cost_estimate=pl.CostEstimate(flops=flops, bytes_accessed=moved, transcendentals=0),
    )


def in_hbm(x):
    return pltpu.with_memory_space_constraint(x, pltpu.HBM)


def body(
    cell_matrix,
    x_coupling,
    y_coupling,
    cell_interp,
    cell_skel,
    cell_rank,
    x_face_interp,
    x_face_skel,
    x_face_rank,
    y_face_interp,
    y_face_skel,
    y_face_rank,
):
    nx, nj, rows, slots = cell_interp.shape
    half = rows // 2
    fslots = x_face_interp.shape[-1]
    cells = next(n for n in (8, 4, 2, 1) if nj % n == 0 and nj > n)
    chunks = nj // cells
    unit = 2 * nx * nj * slots * slots * slots
    smem = pl.BlockSpec(memory_space=pltpu.SMEM)
    shape = jax.ShapeDtypeStruct

    hbm = pl.BlockSpec(memory_space=pltpu.HBM)
    vmem = pl.BlockSpec(memory_space=pltpu.VMEM)
    large = next(n for n in (16, 8, 4, 2, 1) if nj % n == 0)
    top = call(
        functools.partial(top_kernel, large),
        (),
        [hbm, hbm, hbm],
        vmem,
        shape((nj, half, slots), BF),
        0,
        4 * nj * half * slots,
        vmem=8,
        scratch=[
            pltpu.SMEM((nx, nj), jnp.int32),
            pltpu.VMEM((nj, slots), jnp.int32),
            pltpu.VMEM((nj, half, slots), BF),
            pltpu.SemaphoreType.DMA((2,)),
            pltpu.SemaphoreType.DMA((nj // large,)),
        ],
    )(in_hbm(cell_rank), in_hbm(cell_skel), in_hbm(cell_interp))
    top_in = passed_along(top, "gx", -1)


    def pack_rows(count):
        extra = count * -(-cells // 2)
        return count * cells * slots // 2 + -(-extra // 16) * 16

    near = max(nx - 2, 0)

    def down(*dims):
        zeros = (0,) * len(dims)
        return pl.BlockSpec((1, cells) + dims, lambda i, c: (nx - 1 - i, chunks - 1 - c) + zeros)

    def down_x(*dims):
        zeros = (0,) * len(dims)

        def place(i, c):
            return (jnp.minimum(nx - 1 - i, near), jnp.where(i == 0, chunks - 1, chunks - 1 - c)) + zeros

        return pl.BlockSpec((1, cells) + dims, place)

    x_out, y_out, packed, packed_last, edge, corner, last_turned, last_schur = call(
        functools.partial(main_kernel, cells, nx, chunks),
        (nx, chunks),
        [
            smem, vmem, down(rows, slots), down(rows, rows),
            smem, vmem, down_x(rows, fslots), vmem,
            smem, vmem, down(rows, fslots), vmem,
        ],
        [
            down_x(fslots, fslots),
            down(fslots, fslots),
            vmem, vmem, vmem, vmem, vmem, vmem,
        ],
        [
            shape((nx, nj, fslots, fslots), BF),
            shape((nx, nj, fslots, fslots), BF),
            shape((pack_rows(chunks - 1), slots), BF),
            shape((pack_rows(1), slots), BF),
            shape((nx, 2, slots, half), BF),
            shape((nx, 2, slots, half), BF),
            shape((nj, slots, half), BF),
            shape((nj, slots, slots), BF),
        ],
        20 * unit,
        nx * nj * (rows * rows + 3 * rows * slots + 3 * slots * slots) * 2,
        vmem=32,
        scratch=[
            pltpu.VMEM((nj, slots, half), BF),
            pltpu.VMEM((nj, slots, slots), BF),
            pltpu.VMEM((chunks, cells, slots), F32),
            pltpu.VMEM((nx, nj, half), F32),
            pltpu.VMEM((nx, nj, half), F32),
        ],
    )(
        cell_rank, cell_skel, in_hbm(cell_interp), in_hbm(cell_matrix),
        x_face_rank, x_face_skel, in_hbm(x_face_interp), x_coupling,
        y_face_rank, y_face_skel, in_hbm(y_face_interp), y_coupling,
    )
    edge_in = passed_along(edge, "yz", -1)
    packed_in = passed_along(packed, "gx", -1)
    packed_last_in = passed_along(packed_last, "gx", -1)
    face_bytes = nj * (4 * rows * slots + 4 * slots * slots) * 2

    last = nx - 1
    tail = nj - 1
    group = tail // cells

    part, lower_turned = call(
        functools.partial(x_part_kernel, cells, last),
        (),
        [smem, vmem, vmem, vmem, vmem, vmem, vmem],
        [vmem, vmem],
        [shape((nj, fslots, fslots), F32), shape((nj, fslots, slots), BF)],
        8 * unit // nx,
        face_bytes,
        vmem=16,
    )(x_face_rank, x_face_skel, x_face_interp, x_coupling, last_turned, last_schur, top_in)

    edge_in, part = lax.optimization_barrier((edge_in, part))
    y_out = call(
        functools.partial(y_edge_kernel, nx, tail),
        (1,),
        [
            smem,
            pl.BlockSpec((nx, cells, fslots), lambda i: (0, group, 0)),
            pl.BlockSpec((nx, 1, rows, fslots), lambda i: (0, tail, 0, 0)),
            pl.BlockSpec((nx, cells, half), lambda i: (0, group, 0)),
            pl.BlockSpec((nx, 2, slots, half), lambda i: (0, 0, 0, 0)),
            pl.BlockSpec((nx, 2, slots, half), lambda i: (0, 0, 0, 0)),
            pl.BlockSpec(memory_space=pl.ANY),
        ],
        pl.BlockSpec((nx, 1, fslots, fslots), lambda i: (0, tail, 0, 0)),
        shape((nx, nj, fslots, fslots), BF),
        8 * unit // nj,
        nx * face_bytes // nj,
        {6: 0},
    )(y_face_rank, y_face_skel, in_hbm(y_face_interp), y_coupling, corner, edge_in, y_out)

    for places, arrived in (
        (range(chunks - 1), packed_in),
        (range(chunks - 1, chunks), packed_last_in),
    ):
        count = len(places)
        x_out = call(
            functools.partial(x_last_kernel, cells, last, places),
            (),
            [vmem, vmem, vmem, hbm],
            hbm,
            shape((nx, nj, fslots, fslots), BF),
            3 * unit // nx * count // chunks,
            nj * slots * slots * 11 * count // chunks,
            {3: 0},
            scratch=[
                pltpu.VMEM((count * cells, fslots, fslots), BF),
                pltpu.SemaphoreType.DMA((count, 2)),
            ],
        )(part, lower_turned, arrived, x_out)
    return (x_out, y_out)


def solution(mesh):
    return jax.shard_map(
        body,
        mesh=mesh,
        in_specs=(
            P("gx", "yz", None, None),
            P("gx", "yz", None),
            P("gx", "yz", None),
            P("gx", "yz", None, None),
            P("gx", "yz", None),
            P("gx", "yz"),
            P("gx", "yz", None, None),
            P("gx", "yz", None),
            P("gx", "yz"),
            P("gx", "yz", None, None),
            P("gx", "yz", None),
            P("gx", "yz"),
        ),
        out_specs=(P("gx", "yz", None, None), P("gx", "yz", None, None)),
        check_vma=False,
    )
```

```python
import functools

import jax
import jax.numpy as jnp
from jax import lax
from jax.experimental import pallas as pl
from jax.experimental.pallas import tpu as pltpu
from jax.sharding import PartitionSpec as P

BF = jnp.bfloat16
F32 = jnp.float32
MIB = 1024 * 1024


def passed_along(x, axis, by):
    devices = lax.axis_size(axis)
    pairs = [(i, i + by) for i in range(devices) if 0 <= i + by < devices]
    return lax.ppermute(x, axis, pairs)


def dot_nt(a, b):
    return lax.dot_general(a, b, (((1,), (1,)), ((), ())), preferred_element_type=F32)


def dot(a, b):
    return lax.dot_general(a, b, (((1,), (0,)), ((), ())), preferred_element_type=F32)


def marks_of(skel_row, rank, interp):
    rows, slots = interp.shape
    live = lax.broadcasted_iota(jnp.int32, (1, slots), 1) < rank
    picked_row = jnp.where(live, skel_row, -1).astype(F32).astype(BF)
    row = lax.broadcasted_iota(jnp.int32, (rows, slots), 0).astype(F32).astype(BF)
    live_row = jnp.where(live, F32(1.0), F32(0.0)).astype(BF)
    return row == picked_row, interp * live_row


def kept_cleared(turned):
    most = jnp.max(turned, axis=0, keepdims=True)
    least = jnp.where(most.astype(F32) == 1.0, F32(1.0), F32(-2.0)).astype(BF)
    return jnp.where(turned >= least, turned, BF(0.0))


def marked_of(skel_row, rank, interp):
    hit, live = marks_of(skel_row, rank, interp)
    return jnp.where(hit, BF(1.0), live)


def bases_of(cells, layer, first, rank_ref, skel, interp_ref):
    marked = [
        marked_of(skel[k : k + 1], rank_ref[layer, first + k], interp_ref[0, k])
        for k in range(cells)
    ]
    return [kept_cleared(t) for t in [jnp.transpose(m) for m in marked]]


def scaled(turned, conduct):
    return turned * -conduct


def face_of(left, link, link_t, right):
    upper = jnp.concatenate([left, link], axis=1)
    lower = jnp.concatenate([link_t, right], axis=1)
    return jnp.concatenate([upper, lower], axis=0)


def project(turned, matrices):
    inner = [dot(t, m).astype(BF) for t, m in zip(turned, matrices)]
    return [dot_nt(i, t) for i, t in zip(inner, turned)]


def top_kernel(cells, rank_hbm, skel_hbm, interp_hbm, out_ref, rank_ref, skel_ref, held, small_sems, sems):
    count, half, _ = out_ref.shape
    small = [
        pltpu.make_async_copy(rank_hbm, rank_ref, small_sems.at[0]),
        pltpu.make_async_copy(skel_hbm.at[0], skel_ref, small_sems.at[1]),
    ]
    copies = []
    for c in range(count // cells):
        group = pl.ds(c * cells, cells)
        copies.append(
            pltpu.make_async_copy(
                interp_hbm.at[0, group, pl.ds(0, half)], held.at[group], sems.at[c]
            )
        )
    for copy in small + copies:
        copy.start()
    for copy in small:
        copy.wait()
    for c in range(count // cells):
        copies[c].wait()
        for k in range(c * cells, (c + 1) * cells):
            out_ref[k] = marked_of(skel_ref[k : k + 1], rank_ref[0, k], held[k])


def pack_masks(size):
    half = size // 2
    row = lax.broadcasted_iota(jnp.int32, (half, size), 0)
    lane = lax.broadcasted_iota(jnp.int32, (half, size), 1)
    ahead = lane - row
    upper = (ahead >= 0) & (ahead < half)
    return upper, ahead == 0, ahead == half


def main_kernel(
    cells, layers, chunks,
    rank_ref, skel_ref, interp_ref, matrix_ref,
    x_rank_ref, x_skel_ref, x_interp_ref, x_coup_ref,
    y_rank_ref, y_skel_ref, y_interp_ref, y_coup_ref,
    x_out_ref, y_out_ref, packed_ref, packed_last_ref, edge_ref, corner_ref, last_turned_ref, last_schur_ref,
    store_turned, store_schur, store_extra,
):
    layer = layers - 1 - pl.program_id(0)
    chunk = chunks - 1 - pl.program_id(1)
    first = chunk * cells
    slots = skel_ref.shape[-1]
    half = slots // 2
    top = interp_ref.shape[2] // 2

    turned = bases_of(cells, layer, first, rank_ref, skel_ref[0], interp_ref)
    schurs = project(turned, [matrix_ref[0, k] for k in range(cells)])
    schurs = [s.astype(BF) for s in schurs]

    def faces(out_ref, f_rank_ref, f_skel_ref, f_interp_ref, coup_ref, rights):
        found = bases_of(cells, layer, first, f_rank_ref, f_skel_ref[0], f_interp_ref)
        matrices = []
        for k in range(cells):
            right_turned, right = rights[k]
            conduct = coup_ref[0, k : k + 1]
            lower = turned[k][:, top:]
            link = dot_nt(scaled(lower, conduct), right_turned).astype(BF)
            link_t = dot_nt(scaled(right_turned, conduct), lower).astype(BF)
            matrices.append(face_of(schurs[k], link, link_t, right))
        results = project(found, matrices)
        for k in range(cells):
            out_ref[0, k] = results[k].astype(BF)

    def stored(place):
        return store_turned[place], store_schur[place]

    after = jnp.minimum(first + cells, store_schur.shape[0] - 1)
    rights = [(turned[k][:, :top], schurs[k]) for k in range(1, cells)]
    faces(y_out_ref, y_rank_ref, y_skel_ref, y_interp_ref, y_coup_ref, rights + [stored(after)])

    @pl.when(layer < layers - 1)
    def _():
        rights = [stored(first + k) for k in range(cells)]
        faces(x_out_ref, x_rank_ref, x_skel_ref, x_interp_ref, x_coup_ref, rights)

    for k in range(cells):
        store_turned[first + k] = turned[k][:, :top]
        store_schur[first + k] = schurs[k]

    @pl.when(layer == layers - 1)
    def _():
        for k in range(cells):
            last_turned_ref[first + k] = turned[k][:, top:]
            last_schur_ref[first + k] = schurs[k]

    @pl.when(layer == 0)
    def _():
        upper, same, opposite = pack_masks(slots)

        def put(packed_ref, start):
            for k in range(cells):
                above, below = schurs[k][:half].astype(F32), schurs[k][half:].astype(F32)
                place = pl.ds(pl.multiple_of(start + k * half, half), half)
                packed_ref[place] = jnp.where(upper, above, below).astype(BF)

        @pl.when(chunk < chunks - 1)
        def _():
            put(packed_ref, chunk * (cells * half))

        @pl.when(chunk == chunks - 1)
        def _():
            put(packed_last_ref, 0)

        for p in range(0, cells, 2):
            extra = jnp.where(opposite, schurs[p][:half].astype(F32), F32(0.0))
            if p + 1 < cells:
                extra += jnp.where(same, schurs[p + 1][half:].astype(F32), F32(0.0))
            store_extra[chunk, p // 2 : p // 2 + 1] = jnp.sum(extra, axis=0, keepdims=True)

        @pl.when(chunk == 0)
        def _():
            pairs = -(-cells // 2)
            for ref, places in ((packed_ref, range(chunks - 1)), (packed_last_ref, [chunks - 1])):
                start = len(places) * cells * half
                rows = [store_extra[c, :pairs] for c in places]
                pad = ref.shape[0] - start - pairs * len(places)
                if pad:
                    rows.append(jnp.zeros((pad, slots), F32))
                ref[start:] = jnp.concatenate(rows, axis=0).astype(BF)

    @pl.when(chunk == 0)
    def _():
        edge_ref[layer, 0] = turned[0][:, :top]
        edge_ref[layer, 1] = schurs[0]

    @pl.when(chunk == chunks - 1)
    def _():
        corner_ref[layer, 0] = turned[cells - 1][:, top:]
        corner_ref[layer, 1] = schurs[cells - 1]


def y_edge_kernel(layers, place, rank_ref, skel_ref, interp_ref, coup_ref, corner_ref, edge_ref, _, out_ref):
    row = place % skel_ref.shape[1]
    marked = [
        marked_of(skel_ref[i, row : row + 1], rank_ref[i, place], interp_ref[i, 0])
        for i in range(layers)
    ]
    found = [kept_cleared(jnp.transpose(m)) for m in marked]
    matrices = []
    for i in range(layers):
        conduct = coup_ref[i, row : row + 1]
        link = dot_nt(scaled(corner_ref[i, 0], conduct), edge_ref[i, 0]).astype(BF)
        link_t = dot_nt(scaled(edge_ref[i, 0], conduct), corner_ref[i, 0]).astype(BF)
        matrices.append(face_of(corner_ref[i, 1], link, link_t, edge_ref[i, 1]))
    results = project(found, matrices)
    for i in range(layers):
        out_ref[i, 0] = results[i].astype(BF)


def x_part_kernel(
    cells, layer, rank_ref, skel_ref, interp_ref, coup_ref, turned_ref, schur_ref, top_ref,
    part_ref, lower_ref, lower_turned_ref,
):
    count, slots, half = turned_ref.shape
    nothing = jnp.zeros((slots, slots), BF)
    for first in range(0, count, cells):
        group = range(first, first + cells)
        skel = skel_ref[layer, first : first + cells]
        marked = [
            marked_of(skel[k - first : k - first + 1], rank_ref[layer, k], interp_ref[layer, k]) for k in group
        ]
        faces = [kept_cleared(t) for t in [jnp.transpose(m) for m in marked]]
        for k in group:
            lower_turned_ref[k] = faces[k - first][:, half:]
            lower_ref[k] = jnp.transpose(faces[k - first][:, half:])
        tops = [kept_cleared(t) for t in [jnp.transpose(top_ref[k]) for k in group]]
        matrices = []
        for k, top in zip(group, tops):
            conduct = coup_ref[layer, k : k + 1]
            link = dot_nt(scaled(turned_ref[k], conduct), top).astype(BF)
            link_t = dot_nt(scaled(top, conduct), turned_ref[k]).astype(BF)
            matrices.append(face_of(schur_ref[k], link, link_t, nothing))
        for k, result in zip(group, project(faces, matrices)):
            part_ref[k] = result


def x_last_kernel(
    cells, layer, places, part_ref, lower_ref, lower_turned_ref, packed_ref, _, out_ref, held, sems
):
    slots = part_ref.shape[-1]
    half = slots // 2
    upper, same, opposite = pack_masks(slots)
    one, zero, mid = F32(1.0), F32(0.0), F32(0.5)
    top_scale = jnp.where(same, mid, jnp.where(upper, one, zero))
    low_scale = jnp.where(opposite, mid, jnp.where(upper, zero, one))
    same_scale = jnp.where(same, one, zero)
    opposite_scale = jnp.where(opposite, one, zero)
    extras = packed_ref[len(places) * cells * half :].astype(F32)
    pairs = -(-cells // 2)
    copies = []
    for n, c in enumerate(places):
        group = range(c * cells, (c + 1) * cells)
        schurs = []
        for k in range(cells):
            start = (n * cells + k) * half
            packed = packed_ref[start : start + half].astype(F32)
            extra = extras[n * pairs + k // 2 : n * pairs + k // 2 + 1]
            top, low = packed * top_scale, packed * low_scale
            if k % 2 == 0:
                top += extra * opposite_scale
            else:
                low += extra * same_scale
            tri = jnp.concatenate([top, low], axis=0).astype(BF)
            schurs.append(tri + jnp.transpose(tri))
        inner = [dot(lower_turned_ref[k], h).astype(BF) for k, h in zip(group, schurs)]
        results = [dot(i, lower_ref[k]) for k, i in zip(group, inner)]
        part_cells = max(1, cells // 2)
        for start in range(0, cells, part_cells):
            for k in range(start, start + part_cells):
                held[n * cells + k] = (part_ref[c * cells + k] + results[k]).astype(BF)
            copy = pltpu.make_async_copy(
                held.at[pl.ds(n * cells + start, part_cells)],
                out_ref.at[layer, pl.ds(c * cells + start, part_cells)],
                sems.at[n, start // part_cells],
            )
            copy.start()
            copies.append(copy)
    for copy in copies:
        copy.wait()


def call(kernel, grid, in_specs, out_specs, out_shape, flops, moved, aliases=None, vmem=24, scratch=()):
    return pl.pallas_call(
        kernel,
        grid=grid,
        in_specs=in_specs,
        out_specs=out_specs,
        out_shape=out_shape,
        scratch_shapes=scratch,
        input_output_aliases=aliases or {},
        compiler_params=pltpu.CompilerParams(vmem_limit_bytes=vmem * MIB),
        cost_estimate=pl.CostEstimate(flops=flops, bytes_accessed=moved, transcendentals=0),
    )


def in_hbm(x):
    return pltpu.with_memory_space_constraint(x, pltpu.HBM)


def body(
    cell_matrix,
    x_coupling,
    y_coupling,
    cell_interp,
    cell_skel,
    cell_rank,
    x_face_interp,
    x_face_skel,
    x_face_rank,
    y_face_interp,
    y_face_skel,
    y_face_rank,
):
    nx, nj, rows, slots = cell_interp.shape
    half = rows // 2
    fslots = x_face_interp.shape[-1]
    cells = next(n for n in (8, 4, 2, 1) if nj % n == 0 and nj > n)
    chunks = nj // cells
    unit = 2 * nx * nj * slots * slots * slots
    smem = pl.BlockSpec(memory_space=pltpu.SMEM)
    shape = jax.ShapeDtypeStruct

    hbm = pl.BlockSpec(memory_space=pltpu.HBM)
    vmem = pl.BlockSpec(memory_space=pltpu.VMEM)
    top = call(
        functools.partial(top_kernel, cells),
        (),
        [hbm, hbm, hbm],
        vmem,
        shape((nj, half, slots), BF),
        0,
        4 * nj * half * slots,
        vmem=8,
        scratch=[
            pltpu.SMEM((nx, nj), jnp.int32),
            pltpu.VMEM((nj, slots), jnp.int32),
            pltpu.VMEM((nj, half, slots), BF),
            pltpu.SemaphoreType.DMA((2,)),
            pltpu.SemaphoreType.DMA((chunks,)),
        ],
    )(in_hbm(cell_rank), in_hbm(cell_skel), in_hbm(cell_interp))
    top_in = passed_along(top, "gx", -1)


    def pack_rows(count):
        extra = count * -(-cells // 2)
        return count * cells * slots // 2 + -(-extra // 16) * 16

    near = max(nx - 2, 0)

    def down(*dims):
        zeros = (0,) * len(dims)
        return pl.BlockSpec((1, cells) + dims, lambda i, c: (nx - 1 - i, chunks - 1 - c) + zeros)

    def down_x(*dims):
        zeros = (0,) * len(dims)

        def place(i, c):
            return (jnp.minimum(nx - 1 - i, near), jnp.where(i == 0, chunks - 1, chunks - 1 - c)) + zeros

        return pl.BlockSpec((1, cells) + dims, place)

    x_out, y_out, packed, packed_last, edge, corner, last_turned, last_schur = call(
        functools.partial(main_kernel, cells, nx, chunks),
        (nx, chunks),
        [
            smem, down(slots), down(rows, slots), down(rows, rows),
            smem, down_x(fslots), down_x(rows, fslots), down_x(half),
            smem, down(fslots), down(rows, fslots), down(half),
        ],
        [
            down_x(fslots, fslots),
            down(fslots, fslots),
            vmem, vmem, vmem, vmem, vmem, vmem,
        ],
        [
            shape((nx, nj, fslots, fslots), BF),
            shape((nx, nj, fslots, fslots), BF),
            shape((pack_rows(chunks - 1), slots), BF),
            shape((pack_rows(1), slots), BF),
            shape((nx, 2, slots, half), BF),
            shape((nx, 2, slots, half), BF),
            shape((nj, slots, half), BF),
            shape((nj, slots, slots), BF),
        ],
        20 * unit,
        nx * nj * (rows * rows + 3 * rows * slots + 3 * slots * slots) * 2,
        vmem=32,
        scratch=[
            pltpu.VMEM((nj, slots, half), BF),
            pltpu.VMEM((nj, slots, slots), BF),
            pltpu.VMEM((chunks, cells, slots), F32),
        ],
    )(
        cell_rank, in_hbm(cell_skel), in_hbm(cell_interp), in_hbm(cell_matrix),
        x_face_rank, in_hbm(x_face_skel), in_hbm(x_face_interp), in_hbm(x_coupling),
        y_face_rank, in_hbm(y_face_skel), in_hbm(y_face_interp), in_hbm(y_coupling),
    )
    edge_in = passed_along(edge, "yz", -1)
    packed_in = passed_along(packed, "gx", -1)
    packed_last_in = passed_along(packed_last, "gx", -1)
    face_bytes = nj * (4 * rows * slots + 4 * slots * slots) * 2

    last = nx - 1
    tail = nj - 1
    group = tail // cells

    part, lower, lower_turned = call(
        functools.partial(x_part_kernel, cells, last),
        (),
        [smem, vmem, vmem, vmem, vmem, vmem, vmem],
        [vmem, vmem, vmem],
        [
            shape((nj, fslots, fslots), F32),
            shape((nj, slots, fslots), BF),
            shape((nj, fslots, slots), BF),
        ],
        8 * unit // nx,
        face_bytes,
        vmem=16,
    )(x_face_rank, x_face_skel, x_face_interp, x_coupling, last_turned, last_schur, top_in)

    edge_in, part = lax.optimization_barrier((edge_in, part))
    y_out = call(
        functools.partial(y_edge_kernel, nx, tail),
        (1,),
        [
            smem,
            pl.BlockSpec((nx, cells, fslots), lambda i: (0, group, 0)),
            pl.BlockSpec((nx, 1, rows, fslots), lambda i: (0, tail, 0, 0)),
            pl.BlockSpec((nx, cells, half), lambda i: (0, group, 0)),
            pl.BlockSpec((nx, 2, slots, half), lambda i: (0, 0, 0, 0)),
            pl.BlockSpec((nx, 2, slots, half), lambda i: (0, 0, 0, 0)),
            pl.BlockSpec(memory_space=pl.ANY),
        ],
        pl.BlockSpec((nx, 1, fslots, fslots), lambda i: (0, tail, 0, 0)),
        shape((nx, nj, fslots, fslots), BF),
        8 * unit // nj,
        nx * face_bytes // nj,
        {6: 0},
    )(y_face_rank, y_face_skel, in_hbm(y_face_interp), y_coupling, corner, edge_in, y_out)

    for places, arrived in (
        (range(chunks - 1), packed_in),
        (range(chunks - 1, chunks), packed_last_in),
    ):
        count = len(places)
        x_out = call(
            functools.partial(x_last_kernel, cells, last, places),
            (),
            [vmem, vmem, vmem, vmem, hbm],
            hbm,
            shape((nx, nj, fslots, fslots), BF),
            3 * unit // nx * count // chunks,
            nj * slots * slots * 11 * count // chunks,
            {4: 0},
            scratch=[
                pltpu.VMEM((count * cells, fslots, fslots), BF),
                pltpu.SemaphoreType.DMA((count, 2)),
            ],
        )(part, lower, lower_turned, arrived, x_out)
    return (x_out, y_out)


def solution(mesh):
    return jax.shard_map(
        body,
        mesh=mesh,
        in_specs=(
            P("gx", "yz", None, None),
            P("gx", "yz", None),
            P("gx", "yz", None),
            P("gx", "yz", None, None),
            P("gx", "yz", None),
            P("gx", "yz"),
            P("gx", "yz", None, None),
            P("gx", "yz", None),
            P("gx", "yz"),
            P("gx", "yz", None, None),
            P("gx", "yz", None),
            P("gx", "yz"),
        ),
        out_specs=(P("gx", "yz", None, None), P("gx", "yz", None, None)),
        check_vma=False,
    )
```

```python
import functools

import jax
import jax.numpy as jnp
from jax import lax
from jax.experimental import pallas as pl
from jax.experimental.pallas import tpu as pltpu
from jax.sharding import PartitionSpec as P

BF = jnp.bfloat16
F32 = jnp.float32
MIB = 1024 * 1024


def passed_along(x, axis, by):
    devices = lax.axis_size(axis)
    pairs = [(i, i + by) for i in range(devices) if 0 <= i + by < devices]
    return lax.ppermute(x, axis, pairs)


def dot_nt(a, b):
    return lax.dot_general(a, b, (((1,), (1,)), ((), ())), preferred_element_type=F32)


def dot(a, b):
    return lax.dot_general(a, b, (((1,), (0,)), ((), ())), preferred_element_type=F32)


def marks_of(skel_row, rank, interp):
    rows, slots = interp.shape
    live = lax.broadcasted_iota(jnp.int32, (1, slots), 1) < rank
    picked_row = jnp.where(live, skel_row, -1).astype(F32).astype(BF)
    row = lax.broadcasted_iota(jnp.int32, (rows, slots), 0).astype(F32).astype(BF)
    live_row = jnp.where(live, F32(1.0), F32(0.0)).astype(BF)
    return row == picked_row, interp * live_row


def kept_cleared(turned):
    most = jnp.max(turned, axis=0, keepdims=True)
    least = jnp.where(most.astype(F32) == 1.0, F32(1.0), F32(-2.0)).astype(BF)
    return jnp.where(turned >= least, turned, BF(0.0))


def marked_of(skel_row, rank, interp):
    hit, live = marks_of(skel_row, rank, interp)
    return jnp.where(hit, BF(1.0), live)


def bases_of(cells, layer, first, rank_ref, skel, interp_ref):
    marked = [
        marked_of(skel[k : k + 1], rank_ref[layer, first + k], interp_ref[0, k])
        for k in range(cells)
    ]
    return [kept_cleared(t) for t in [jnp.transpose(m) for m in marked]]


def scaled(turned, conduct):
    return turned * -conduct


def face_of(left, link, link_t, right):
    upper = jnp.concatenate([left, link], axis=1)
    lower = jnp.concatenate([link_t, right], axis=1)
    return jnp.concatenate([upper, lower], axis=0)


def project(turned, matrices):
    inner = [dot(t, m).astype(BF) for t, m in zip(turned, matrices)]
    return [dot_nt(i, t) for i, t in zip(inner, turned)]


def top_kernel(cells, rank_hbm, skel_hbm, interp_hbm, out_ref, rank_ref, skel_ref, held, small_sems, sems):
    count, half, _ = out_ref.shape
    small = [
        pltpu.make_async_copy(rank_hbm, rank_ref, small_sems.at[0]),
        pltpu.make_async_copy(skel_hbm.at[0], skel_ref, small_sems.at[1]),
    ]
    copies = []
    for c in range(count // cells):
        group = pl.ds(c * cells, cells)
        copies.append(
            pltpu.make_async_copy(
                interp_hbm.at[0, group, pl.ds(0, half)], held.at[group], sems.at[c]
            )
        )
    for copy in small + copies:
        copy.start()
    for copy in small:
        copy.wait()
    for c in range(count // cells):
        copies[c].wait()
        for k in range(c * cells, (c + 1) * cells):
            out_ref[k] = marked_of(skel_ref[k : k + 1], rank_ref[0, k], held[k])


def pack_masks(size):
    half = size // 2
    row = lax.broadcasted_iota(jnp.int32, (half, size), 0)
    lane = lax.broadcasted_iota(jnp.int32, (half, size), 1)
    ahead = lane - row
    upper = (ahead >= 0) & (ahead < half)
    return upper, ahead == 0, ahead == half


def main_kernel(
    cells, layers, chunks,
    rank_ref, skel_ref, interp_ref, matrix_ref,
    x_rank_ref, x_skel_ref, x_interp_ref, x_coup_ref,
    y_rank_ref, y_skel_ref, y_interp_ref, y_coup_ref,
    x_out_ref, y_out_ref, packed_ref, packed_last_ref, edge_ref, corner_ref, last_turned_ref, last_schur_ref,
    store_turned, store_schur, store_extra,
):
    layer = layers - 1 - pl.program_id(0)
    chunk = chunks - 1 - pl.program_id(1)
    first = chunk * cells
    slots = skel_ref.shape[-1]
    half = slots // 2
    top = interp_ref.shape[2] // 2

    turned = bases_of(cells, layer, first, rank_ref, skel_ref[0], interp_ref)
    schurs = project(turned, [matrix_ref[0, k] for k in range(cells)])
    schurs = [s.astype(BF) for s in schurs]

    def faces(out_ref, f_rank_ref, f_skel_ref, f_interp_ref, coup_ref, rights):
        found = bases_of(cells, layer, first, f_rank_ref, f_skel_ref[0], f_interp_ref)
        matrices = []
        for k in range(cells):
            right_turned, right = rights[k]
            conduct = coup_ref[0, k : k + 1]
            lower = turned[k][:, top:]
            link = dot_nt(scaled(lower, conduct), right_turned).astype(BF)
            link_t = dot_nt(scaled(right_turned, conduct), lower).astype(BF)
            matrices.append(face_of(schurs[k], link, link_t, right))
        results = project(found, matrices)
        for k in range(cells):
            out_ref[0, k] = results[k].astype(BF)

    def stored(place):
        return store_turned[place], store_schur[place]

    after = jnp.minimum(first + cells, store_schur.shape[0] - 1)
    rights = [(turned[k][:, :top], schurs[k]) for k in range(1, cells)]
    faces(y_out_ref, y_rank_ref, y_skel_ref, y_interp_ref, y_coup_ref, rights + [stored(after)])

    @pl.when(layer < layers - 1)
    def _():
        rights = [stored(first + k) for k in range(cells)]
        faces(x_out_ref, x_rank_ref, x_skel_ref, x_interp_ref, x_coup_ref, rights)

    for k in range(cells):
        store_turned[first + k] = turned[k][:, :top]
        store_schur[first + k] = schurs[k]

    @pl.when(layer == layers - 1)
    def _():
        for k in range(cells):
            last_turned_ref[first + k] = turned[k][:, top:]
            last_schur_ref[first + k] = schurs[k]

    @pl.when(layer == 0)
    def _():
        upper, same, opposite = pack_masks(slots)

        def put(packed_ref, start):
            for k in range(cells):
                above, below = schurs[k][:half].astype(F32), schurs[k][half:].astype(F32)
                place = pl.ds(pl.multiple_of(start + k * half, half), half)
                packed_ref[place] = jnp.where(upper, above, below).astype(BF)

        @pl.when(chunk < chunks - 1)
        def _():
            put(packed_ref, chunk * (cells * half))

        @pl.when(chunk == chunks - 1)
        def _():
            put(packed_last_ref, 0)

        for p in range(0, cells, 2):
            extra = jnp.where(opposite, schurs[p][:half].astype(F32), F32(0.0))
            if p + 1 < cells:
                extra += jnp.where(same, schurs[p + 1][half:].astype(F32), F32(0.0))
            store_extra[chunk, p // 2 : p // 2 + 1] = jnp.sum(extra, axis=0, keepdims=True)

        @pl.when(chunk == 0)
        def _():
            pairs = -(-cells // 2)
            for ref, places in ((packed_ref, range(chunks - 1)), (packed_last_ref, [chunks - 1])):
                start = len(places) * cells * half
                rows = [store_extra[c, :pairs] for c in places]
                pad = ref.shape[0] - start - pairs * len(places)
                if pad:
                    rows.append(jnp.zeros((pad, slots), F32))
                ref[start:] = jnp.concatenate(rows, axis=0).astype(BF)

    @pl.when(chunk == 0)
    def _():
        edge_ref[layer, 0] = turned[0][:, :top]
        edge_ref[layer, 1] = schurs[0]

    @pl.when(chunk == chunks - 1)
    def _():
        corner_ref[layer, 0] = turned[cells - 1][:, top:]
        corner_ref[layer, 1] = schurs[cells - 1]


def y_edge_kernel(layers, place, rank_ref, skel_ref, interp_ref, coup_ref, corner_ref, edge_ref, _, out_ref):
    row = place % skel_ref.shape[1]
    marked = [
        marked_of(skel_ref[i, row : row + 1], rank_ref[i, place], interp_ref[i, 0])
        for i in range(layers)
    ]
    found = [kept_cleared(jnp.transpose(m)) for m in marked]
    matrices = []
    for i in range(layers):
        conduct = coup_ref[i, row : row + 1]
        link = dot_nt(scaled(corner_ref[i, 0], conduct), edge_ref[i, 0]).astype(BF)
        link_t = dot_nt(scaled(edge_ref[i, 0], conduct), corner_ref[i, 0]).astype(BF)
        matrices.append(face_of(corner_ref[i, 1], link, link_t, edge_ref[i, 1]))
    results = project(found, matrices)
    for i in range(layers):
        out_ref[i, 0] = results[i].astype(BF)


def x_part_kernel(
    cells, layer, rank_ref, skel_ref, interp_ref, coup_ref, turned_ref, schur_ref, top_ref,
    part_ref, lower_ref, lower_turned_ref,
):
    count, slots, half = turned_ref.shape
    nothing = jnp.zeros((slots, slots), BF)
    for first in range(0, count, cells):
        group = range(first, first + cells)
        skel = skel_ref[layer, first : first + cells]
        marked = [
            marked_of(skel[k - first : k - first + 1], rank_ref[layer, k], interp_ref[layer, k]) for k in group
        ]
        faces = [kept_cleared(t) for t in [jnp.transpose(m) for m in marked]]
        for k in group:
            lower_turned_ref[k] = faces[k - first][:, half:]
            lower_ref[k] = jnp.transpose(faces[k - first][:, half:])
        tops = [kept_cleared(t) for t in [jnp.transpose(top_ref[k]) for k in group]]
        matrices = []
        for k, top in zip(group, tops):
            conduct = coup_ref[layer, k : k + 1]
            link = dot_nt(scaled(turned_ref[k], conduct), top).astype(BF)
            link_t = dot_nt(scaled(top, conduct), turned_ref[k]).astype(BF)
            matrices.append(face_of(schur_ref[k], link, link_t, nothing))
        for k, result in zip(group, project(faces, matrices)):
            part_ref[k] = result


def x_last_kernel(
    cells, layer, places, part_ref, lower_ref, lower_turned_ref, packed_ref, _, out_ref, held, sems
):
    slots = part_ref.shape[-1]
    half = slots // 2
    upper, same, opposite = pack_masks(slots)
    one, zero, mid = F32(1.0), F32(0.0), F32(0.5)
    top_scale = jnp.where(same, mid, jnp.where(upper, one, zero))
    low_scale = jnp.where(opposite, mid, jnp.where(upper, zero, one))
    same_scale = jnp.where(same, one, zero)
    opposite_scale = jnp.where(opposite, one, zero)
    extras = packed_ref[len(places) * cells * half :].astype(F32)
    pairs = -(-cells // 2)
    copies = []
    for n, c in enumerate(places):
        group = range(c * cells, (c + 1) * cells)
        schurs = []
        for k in range(cells):
            start = (n * cells + k) * half
            packed = packed_ref[start : start + half].astype(F32)
            extra = extras[n * pairs + k // 2 : n * pairs + k // 2 + 1]
            top, low = packed * top_scale, packed * low_scale
            if k % 2 == 0:
                top += extra * opposite_scale
            else:
                low += extra * same_scale
            tri = jnp.concatenate([top, low], axis=0).astype(BF)
            schurs.append(tri + jnp.transpose(tri) if k % 2 == 0 else tri)
        inner = []
        for k, h in zip(group, schurs):
            turned = lower_turned_ref[k]
            both = dot(turned, h) if k % 2 == 0 else dot(turned, h) + dot_nt(turned, h)
            inner.append(both.astype(BF))
        results = [dot(i, lower_ref[k]) for k, i in zip(group, inner)]
        part_cells = max(1, cells // 4)
        for start in range(0, cells, part_cells):
            for k in range(start, start + part_cells):
                held[n * cells + k] = (part_ref[c * cells + k] + results[k]).astype(BF)
            copy = pltpu.make_async_copy(
                held.at[pl.ds(n * cells + start, part_cells)],
                out_ref.at[layer, pl.ds(c * cells + start, part_cells)],
                sems.at[n, start // part_cells],
            )
            copy.start()
            copies.append(copy)
    for copy in copies:
        copy.wait()


def call(kernel, grid, in_specs, out_specs, out_shape, flops, moved, aliases=None, vmem=24, scratch=()):
    return pl.pallas_call(
        kernel,
        grid=grid,
        in_specs=in_specs,
        out_specs=out_specs,
        out_shape=out_shape,
        scratch_shapes=scratch,
        input_output_aliases=aliases or {},
        compiler_params=pltpu.CompilerParams(vmem_limit_bytes=vmem * MIB),
        cost_estimate=pl.CostEstimate(flops=flops, bytes_accessed=moved, transcendentals=0),
    )


def in_hbm(x):
    return pltpu.with_memory_space_constraint(x, pltpu.HBM)


def body(
    cell_matrix,
    x_coupling,
    y_coupling,
    cell_interp,
    cell_skel,
    cell_rank,
    x_face_interp,
    x_face_skel,
    x_face_rank,
    y_face_interp,
    y_face_skel,
    y_face_rank,
):
    nx, nj, rows, slots = cell_interp.shape
    half = rows // 2
    fslots = x_face_interp.shape[-1]
    cells = next(n for n in (8, 4, 2, 1) if nj % n == 0 and nj > n)
    chunks = nj // cells
    unit = 2 * nx * nj * slots * slots * slots
    smem = pl.BlockSpec(memory_space=pltpu.SMEM)
    shape = jax.ShapeDtypeStruct

    hbm = pl.BlockSpec(memory_space=pltpu.HBM)
    vmem = pl.BlockSpec(memory_space=pltpu.VMEM)
    top = call(
        functools.partial(top_kernel, cells),
        (),
        [hbm, hbm, hbm],
        vmem,
        shape((nj, half, slots), BF),
        0,
        4 * nj * half * slots,
        vmem=8,
        scratch=[
            pltpu.SMEM((nx, nj), jnp.int32),
            pltpu.VMEM((nj, slots), jnp.int32),
            pltpu.VMEM((nj, half, slots), BF),
            pltpu.SemaphoreType.DMA((2,)),
            pltpu.SemaphoreType.DMA((chunks,)),
        ],
    )(in_hbm(cell_rank), in_hbm(cell_skel), in_hbm(cell_interp))
    top_in = passed_along(top, "gx", -1)


    def pack_rows(count):
        extra = count * -(-cells // 2)
        return count * cells * slots // 2 + -(-extra // 16) * 16

    near = max(nx - 2, 0)

    def down(*dims):
        zeros = (0,) * len(dims)
        return pl.BlockSpec((1, cells) + dims, lambda i, c: (nx - 1 - i, chunks - 1 - c) + zeros)

    def down_x(*dims):
        zeros = (0,) * len(dims)

        def place(i, c):
            return (jnp.minimum(nx - 1 - i, near), jnp.where(i == 0, chunks - 1, chunks - 1 - c)) + zeros

        return pl.BlockSpec((1, cells) + dims, place)

    x_out, y_out, packed, packed_last, edge, corner, last_turned, last_schur = call(
        functools.partial(main_kernel, cells, nx, chunks),
        (nx, chunks),
        [
            smem, down(slots), down(rows, slots), down(rows, rows),
            smem, down_x(fslots), down_x(rows, fslots), down_x(half),
            smem, down(fslots), down(rows, fslots), down(half),
        ],
        [
            down_x(fslots, fslots),
            down(fslots, fslots),
            vmem, vmem, vmem, vmem, vmem, vmem,
        ],
        [
            shape((nx, nj, fslots, fslots), BF),
            shape((nx, nj, fslots, fslots), BF),
            shape((pack_rows(chunks - 1), slots), BF),
            shape((pack_rows(1), slots), BF),
            shape((nx, 2, slots, half), BF),
            shape((nx, 2, slots, half), BF),
            shape((nj, slots, half), BF),
            shape((nj, slots, slots), BF),
        ],
        20 * unit,
        nx * nj * (rows * rows + 3 * rows * slots + 3 * slots * slots) * 2,
        vmem=32,
        scratch=[
            pltpu.VMEM((nj, slots, half), BF),
            pltpu.VMEM((nj, slots, slots), BF),
            pltpu.VMEM((chunks, cells, slots), F32),
        ],
    )(
        cell_rank, in_hbm(cell_skel), in_hbm(cell_interp), in_hbm(cell_matrix),
        x_face_rank, in_hbm(x_face_skel), in_hbm(x_face_interp), in_hbm(x_coupling),
        y_face_rank, in_hbm(y_face_skel), in_hbm(y_face_interp), in_hbm(y_coupling),
    )
    edge_in = passed_along(edge, "yz", -1)
    packed_in = passed_along(packed, "gx", -1)
    packed_last_in = passed_along(packed_last, "gx", -1)
    face_bytes = nj * (4 * rows * slots + 4 * slots * slots) * 2

    last = nx - 1
    tail = nj - 1
    group = tail // cells

    part, lower, lower_turned = call(
        functools.partial(x_part_kernel, cells, last),
        (),
        [smem, vmem, vmem, vmem, vmem, vmem, vmem],
        [vmem, vmem, vmem],
        [
            shape((nj, fslots, fslots), F32),
            shape((nj, slots, fslots), BF),
            shape((nj, fslots, slots), BF),
        ],
        8 * unit // nx,
        face_bytes,
        vmem=16,
    )(x_face_rank, x_face_skel, x_face_interp, x_coupling, last_turned, last_schur, top_in)

    edge_in, part = lax.optimization_barrier((edge_in, part))
    y_out = call(
        functools.partial(y_edge_kernel, nx, tail),
        (1,),
        [
            smem,
            pl.BlockSpec((nx, cells, fslots), lambda i: (0, group, 0)),
            pl.BlockSpec((nx, 1, rows, fslots), lambda i: (0, tail, 0, 0)),
            pl.BlockSpec((nx, cells, half), lambda i: (0, group, 0)),
            pl.BlockSpec((nx, 2, slots, half), lambda i: (0, 0, 0, 0)),
            pl.BlockSpec((nx, 2, slots, half), lambda i: (0, 0, 0, 0)),
            pl.BlockSpec(memory_space=pl.ANY),
        ],
        pl.BlockSpec((nx, 1, fslots, fslots), lambda i: (0, tail, 0, 0)),
        shape((nx, nj, fslots, fslots), BF),
        8 * unit // nj,
        nx * face_bytes // nj,
        {6: 0},
    )(y_face_rank, y_face_skel, in_hbm(y_face_interp), y_coupling, corner, edge_in, y_out)

    for places, arrived in (
        (range(chunks - 1), packed_in),
        (range(chunks - 1, chunks), packed_last_in),
    ):
        count = len(places)
        x_out = call(
            functools.partial(x_last_kernel, cells, last, places),
            (),
            [vmem, vmem, vmem, vmem, hbm],
            hbm,
            shape((nx, nj, fslots, fslots), BF),
            3 * unit // nx * count // chunks,
            nj * slots * slots * 11 * count // chunks,
            {4: 0},
            scratch=[
                pltpu.VMEM((count * cells, fslots, fslots), BF),
                pltpu.SemaphoreType.DMA((count, 4)),
            ],
        )(part, lower, lower_turned, arrived, x_out)
    return (x_out, y_out)


def solution(mesh):
    return jax.shard_map(
        body,
        mesh=mesh,
        in_specs=(
            P("gx", "yz", None, None),
            P("gx", "yz", None),
            P("gx", "yz", None),
            P("gx", "yz", None, None),
            P("gx", "yz", None),
            P("gx", "yz"),
            P("gx", "yz", None, None),
            P("gx", "yz", None),
            P("gx", "yz"),
            P("gx", "yz", None, None),
            P("gx", "yz", None),
            P("gx", "yz"),
        ),
        out_specs=(P("gx", "yz", None, None), P("gx", "yz", None, None)),
        check_vma=False,
    )
```

```python
import functools

import jax
import jax.numpy as jnp
from jax import lax
from jax.experimental import pallas as pl
from jax.experimental.pallas import tpu as pltpu
from jax.sharding import PartitionSpec as P

BF = jnp.bfloat16
F32 = jnp.float32
MIB = 1024 * 1024


def passed_along(x, axis, by):
    devices = lax.axis_size(axis)
    pairs = [(i, i + by) for i in range(devices) if 0 <= i + by < devices]
    return lax.ppermute(x, axis, pairs)


def dot_nt(a, b):
    return lax.dot_general(a, b, (((1,), (1,)), ((), ())), preferred_element_type=F32)


def dot(a, b):
    return lax.dot_general(a, b, (((1,), (0,)), ((), ())), preferred_element_type=F32)


def marks_of(skel_row, rank, interp):
    rows, slots = interp.shape
    live = lax.broadcasted_iota(jnp.int32, (1, slots), 1) < rank
    picked_row = jnp.where(live, skel_row, -1).astype(F32).astype(BF)
    row = lax.broadcasted_iota(jnp.int32, (rows, slots), 0).astype(F32).astype(BF)
    live_row = jnp.where(live, F32(1.0), F32(0.0)).astype(BF)
    return row == picked_row, interp * live_row


def kept_cleared(turned):
    most = jnp.max(turned, axis=0, keepdims=True)
    least = jnp.where(most.astype(F32) == 1.0, F32(1.0), F32(-2.0)).astype(BF)
    return jnp.where(turned >= least, turned, BF(0.0))


def marked_of(skel_row, rank, interp):
    hit, live = marks_of(skel_row, rank, interp)
    return jnp.where(hit, BF(1.0), live)


def bases_of(cells, layer, first, rank_ref, skel, interp_ref):
    marked = [
        marked_of(skel[k : k + 1], rank_ref[layer, first + k], interp_ref[0, k])
        for k in range(cells)
    ]
    return [kept_cleared(t) for t in [jnp.transpose(m) for m in marked]]


def scaled(turned, conduct):
    return turned * -conduct


def face_of(left, link, link_t, right):
    upper = jnp.concatenate([left, link], axis=1)
    lower = jnp.concatenate([link_t, right], axis=1)
    return jnp.concatenate([upper, lower], axis=0)


def project(turned, matrices):
    inner = [dot(t, m).astype(BF) for t, m in zip(turned, matrices)]
    return [dot_nt(i, t) for i, t in zip(inner, turned)]


def top_kernel(cells, rank_hbm, skel_hbm, interp_hbm, out_ref, rank_ref, skel_ref, held, small_sems, sems):
    count, half, _ = out_ref.shape
    small = [
        pltpu.make_async_copy(rank_hbm, rank_ref, small_sems.at[0]),
        pltpu.make_async_copy(skel_hbm.at[0], skel_ref, small_sems.at[1]),
    ]
    copies = []
    for c in range(count // cells):
        group = pl.ds(c * cells, cells)
        copies.append(
            pltpu.make_async_copy(
                interp_hbm.at[0, group, pl.ds(0, half)], held.at[group], sems.at[c]
            )
        )
    for copy in small + copies:
        copy.start()
    for copy in small:
        copy.wait()
    slots = skel_ref.shape[-1]
    ranks = jnp.transpose(jnp.broadcast_to(rank_ref[0:1].astype(F32), (slots, count)))
    live = lax.broadcasted_iota(jnp.int32, (count, slots), 1).astype(F32) < ranks
    picked = jnp.where(live, skel_ref[...].astype(F32), F32(-1.0))
    lives = jnp.where(live, F32(1.0), F32(0.0))
    row = lax.broadcasted_iota(jnp.int32, (half, slots), 0).astype(F32).astype(BF)
    for c in range(count // cells):
        copies[c].wait()
        for k in range(c * cells, (c + 1) * cells):
            interp = held[k] * lives[k : k + 1].astype(BF)
            out_ref[k] = jnp.where(row == picked[k : k + 1].astype(BF), BF(1.0), interp)


def pack_masks(size):
    half = size // 2
    row = lax.broadcasted_iota(jnp.int32, (half, size), 0)
    lane = lax.broadcasted_iota(jnp.int32, (half, size), 1)
    ahead = lane - row
    upper = (ahead >= 0) & (ahead < half)
    return upper, ahead == 0, ahead == half


def main_kernel(
    cells, layers, chunks,
    rank_ref, skel_ref, interp_ref, matrix_ref,
    x_rank_ref, x_skel_ref, x_interp_ref, x_coup_ref,
    y_rank_ref, y_skel_ref, y_interp_ref, y_coup_ref,
    x_out_ref, y_out_ref, packed_ref, packed_last_ref, edge_ref, corner_ref, last_turned_ref, last_schur_ref,
    store_turned, store_schur, store_extra,
):
    layer = layers - 1 - pl.program_id(0)
    chunk = chunks - 1 - pl.program_id(1)
    first = chunk * cells
    slots = skel_ref.shape[-1]
    half = slots // 2
    top = interp_ref.shape[2] // 2

    turned = bases_of(cells, layer, first, rank_ref, skel_ref[0], interp_ref)
    schurs = project(turned, [matrix_ref[0, k] for k in range(cells)])
    schurs = [s.astype(BF) for s in schurs]

    def faces(out_ref, f_rank_ref, f_skel_ref, f_interp_ref, coup_ref, rights):
        found = bases_of(cells, layer, first, f_rank_ref, f_skel_ref[0], f_interp_ref)
        matrices = []
        for k in range(cells):
            right_turned, right = rights[k]
            conduct = coup_ref[0, k : k + 1]
            lower = turned[k][:, top:]
            link = dot_nt(scaled(lower, conduct), right_turned).astype(BF)
            link_t = dot_nt(scaled(right_turned, conduct), lower).astype(BF)
            matrices.append(face_of(schurs[k], link, link_t, right))
        results = project(found, matrices)
        for k in range(cells):
            out_ref[0, k] = results[k].astype(BF)

    def stored(place):
        return store_turned[place], store_schur[place]

    after = jnp.minimum(first + cells, store_schur.shape[0] - 1)
    rights = [(turned[k][:, :top], schurs[k]) for k in range(1, cells)]
    faces(y_out_ref, y_rank_ref, y_skel_ref, y_interp_ref, y_coup_ref, rights + [stored(after)])

    @pl.when(layer < layers - 1)
    def _():
        rights = [stored(first + k) for k in range(cells)]
        faces(x_out_ref, x_rank_ref, x_skel_ref, x_interp_ref, x_coup_ref, rights)

    for k in range(cells):
        store_turned[first + k] = turned[k][:, :top]
        store_schur[first + k] = schurs[k]

    @pl.when(layer == layers - 1)
    def _():
        for k in range(cells):
            last_turned_ref[first + k] = turned[k][:, top:]
            last_schur_ref[first + k] = schurs[k]

    @pl.when(layer == 0)
    def _():
        upper, same, opposite = pack_masks(slots)

        def put(packed_ref, start):
            for k in range(cells):
                above, below = schurs[k][:half].astype(F32), schurs[k][half:].astype(F32)
                place = pl.ds(pl.multiple_of(start + k * half, half), half)
                packed_ref[place] = jnp.where(upper, above, below).astype(BF)

        @pl.when(chunk < chunks - 1)
        def _():
            put(packed_ref, chunk * (cells * half))

        @pl.when(chunk == chunks - 1)
        def _():
            put(packed_last_ref, 0)

        for p in range(0, cells, 2):
            extra = jnp.where(opposite, schurs[p][:half].astype(F32), F32(0.0))
            if p + 1 < cells:
                extra += jnp.where(same, schurs[p + 1][half:].astype(F32), F32(0.0))
            store_extra[chunk, p // 2 : p // 2 + 1] = jnp.sum(extra, axis=0, keepdims=True)

        @pl.when(chunk == 0)
        def _():
            pairs = -(-cells // 2)
            for ref, places in ((packed_ref, range(chunks - 1)), (packed_last_ref, [chunks - 1])):
                start = len(places) * cells * half
                rows = [store_extra[c, :pairs] for c in places]
                pad = ref.shape[0] - start - pairs * len(places)
                if pad:
                    rows.append(jnp.zeros((pad, slots), F32))
                ref[start:] = jnp.concatenate(rows, axis=0).astype(BF)

    @pl.when(chunk == 0)
    def _():
        edge_ref[layer, 0] = turned[0][:, :top]
        edge_ref[layer, 1] = schurs[0]

    @pl.when(chunk == chunks - 1)
    def _():
        corner_ref[layer, 0] = turned[cells - 1][:, top:]
        corner_ref[layer, 1] = schurs[cells - 1]


def y_edge_kernel(layers, place, rank_ref, skel_ref, interp_ref, coup_ref, corner_ref, edge_ref, _, out_ref):
    row = place % skel_ref.shape[1]
    marked = [
        marked_of(skel_ref[i, row : row + 1], rank_ref[i, place], interp_ref[i, 0])
        for i in range(layers)
    ]
    found = [kept_cleared(jnp.transpose(m)) for m in marked]
    matrices = []
    for i in range(layers):
        conduct = coup_ref[i, row : row + 1]
        link = dot_nt(scaled(corner_ref[i, 0], conduct), edge_ref[i, 0]).astype(BF)
        link_t = dot_nt(scaled(edge_ref[i, 0], conduct), corner_ref[i, 0]).astype(BF)
        matrices.append(face_of(corner_ref[i, 1], link, link_t, edge_ref[i, 1]))
    results = project(found, matrices)
    for i in range(layers):
        out_ref[i, 0] = results[i].astype(BF)


def x_part_kernel(
    cells, layer, rank_ref, skel_ref, interp_ref, coup_ref, turned_ref, schur_ref, top_ref,
    part_ref, lower_ref, lower_turned_ref,
):
    count, slots, half = turned_ref.shape
    nothing = jnp.zeros((slots, slots), BF)
    for first in range(0, count, cells):
        group = range(first, first + cells)
        skel = skel_ref[layer, first : first + cells]
        marked = [
            marked_of(skel[k - first : k - first + 1], rank_ref[layer, k], interp_ref[layer, k]) for k in group
        ]
        faces = [kept_cleared(t) for t in [jnp.transpose(m) for m in marked]]
        for k in group:
            lower_turned_ref[k] = faces[k - first][:, half:]
            lower_ref[k] = jnp.transpose(faces[k - first][:, half:])
        tops = [kept_cleared(t) for t in [jnp.transpose(top_ref[k]) for k in group]]
        matrices = []
        for k, top in zip(group, tops):
            conduct = coup_ref[layer, k : k + 1]
            link = dot_nt(scaled(turned_ref[k], conduct), top).astype(BF)
            link_t = dot_nt(scaled(top, conduct), turned_ref[k]).astype(BF)
            matrices.append(face_of(schur_ref[k], link, link_t, nothing))
        for k, result in zip(group, project(faces, matrices)):
            part_ref[k] = result


def x_last_kernel(
    cells, layer, places, part_ref, lower_ref, lower_turned_ref, packed_ref, _, out_ref, held, sems
):
    slots = part_ref.shape[-1]
    half = slots // 2
    upper, same, opposite = pack_masks(slots)
    one, zero, mid = F32(1.0), F32(0.0), F32(0.5)
    top_scale = jnp.where(same, mid, jnp.where(upper, one, zero))
    low_scale = jnp.where(opposite, mid, jnp.where(upper, zero, one))
    same_scale = jnp.where(same, one, zero)
    opposite_scale = jnp.where(opposite, one, zero)
    extras = packed_ref[len(places) * cells * half :].astype(F32)
    pairs = -(-cells // 2)
    copies = []
    for n, c in enumerate(places):
        group = range(c * cells, (c + 1) * cells)
        schurs = []
        for k in range(cells):
            start = (n * cells + k) * half
            packed = packed_ref[start : start + half].astype(F32)
            extra = extras[n * pairs + k // 2 : n * pairs + k // 2 + 1]
            top, low = packed * top_scale, packed * low_scale
            if k % 2 == 0:
                top += extra * opposite_scale
            else:
                low += extra * same_scale
            tri = jnp.concatenate([top, low], axis=0).astype(BF)
            schurs.append(tri + jnp.transpose(tri))
        inner = [dot(lower_turned_ref[k], h).astype(BF) for k, h in zip(group, schurs)]
        results = [dot(i, lower_ref[k]) for k, i in zip(group, inner)]
        part_cells = max(1, cells // 2)
        for start in range(0, cells, part_cells):
            for k in range(start, start + part_cells):
                held[n * cells + k] = (part_ref[c * cells + k] + results[k]).astype(BF)
            copy = pltpu.make_async_copy(
                held.at[pl.ds(n * cells + start, part_cells)],
                out_ref.at[layer, pl.ds(c * cells + start, part_cells)],
                sems.at[n, start // part_cells],
            )
            copy.start()
            copies.append(copy)
    for copy in copies:
        copy.wait()


def call(kernel, grid, in_specs, out_specs, out_shape, flops, moved, aliases=None, vmem=24, scratch=()):
    return pl.pallas_call(
        kernel,
        grid=grid,
        in_specs=in_specs,
        out_specs=out_specs,
        out_shape=out_shape,
        scratch_shapes=scratch,
        input_output_aliases=aliases or {},
        compiler_params=pltpu.CompilerParams(vmem_limit_bytes=vmem * MIB),
        cost_estimate=pl.CostEstimate(flops=flops, bytes_accessed=moved, transcendentals=0),
    )


def in_hbm(x):
    return pltpu.with_memory_space_constraint(x, pltpu.HBM)


def body(
    cell_matrix,
    x_coupling,
    y_coupling,
    cell_interp,
    cell_skel,
    cell_rank,
    x_face_interp,
    x_face_skel,
    x_face_rank,
    y_face_interp,
    y_face_skel,
    y_face_rank,
):
    nx, nj, rows, slots = cell_interp.shape
    half = rows // 2
    fslots = x_face_interp.shape[-1]
    cells = next(n for n in (8, 4, 2, 1) if nj % n == 0 and nj > n)
    chunks = nj // cells
    unit = 2 * nx * nj * slots * slots * slots
    smem = pl.BlockSpec(memory_space=pltpu.SMEM)
    shape = jax.ShapeDtypeStruct

    hbm = pl.BlockSpec(memory_space=pltpu.HBM)
    vmem = pl.BlockSpec(memory_space=pltpu.VMEM)
    top = call(
        functools.partial(top_kernel, cells),
        (),
        [hbm, hbm, hbm],
        vmem,
        shape((nj, half, slots), BF),
        0,
        4 * nj * half * slots,
        vmem=8,
        scratch=[
            pltpu.VMEM((nx, nj), jnp.int32),
            pltpu.VMEM((nj, slots), jnp.int32),
            pltpu.VMEM((nj, half, slots), BF),
            pltpu.SemaphoreType.DMA((2,)),
            pltpu.SemaphoreType.DMA((chunks,)),
        ],
    )(in_hbm(cell_rank), in_hbm(cell_skel), in_hbm(cell_interp))
    top_in = passed_along(top, "gx", -1)


    def pack_rows(count):
        extra = count * -(-cells // 2)
        return count * cells * slots // 2 + -(-extra // 16) * 16

    near = max(nx - 2, 0)

    def down(*dims):
        zeros = (0,) * len(dims)
        return pl.BlockSpec((1, cells) + dims, lambda i, c: (nx - 1 - i, chunks - 1 - c) + zeros)

    def down_x(*dims):
        zeros = (0,) * len(dims)

        def place(i, c):
            return (jnp.minimum(nx - 1 - i, near), jnp.where(i == 0, chunks - 1, chunks - 1 - c)) + zeros

        return pl.BlockSpec((1, cells) + dims, place)

    x_out, y_out, packed, packed_last, edge, corner, last_turned, last_schur = call(
        functools.partial(main_kernel, cells, nx, chunks),
        (nx, chunks),
        [
            smem, down(slots), down(rows, slots), down(rows, rows),
            smem, down_x(fslots), down_x(rows, fslots), down_x(half),
            smem, down(fslots), down(rows, fslots), down(half),
        ],
        [
            down_x(fslots, fslots),
            down(fslots, fslots),
            vmem, vmem, vmem, vmem, vmem, vmem,
        ],
        [
            shape((nx, nj, fslots, fslots), BF),
            shape((nx, nj, fslots, fslots), BF),
            shape((pack_rows(chunks - 1), slots), BF),
            shape((pack_rows(1), slots), BF),
            shape((nx, 2, slots, half), BF),
            shape((nx, 2, slots, half), BF),
            shape((nj, slots, half), BF),
            shape((nj, slots, slots), BF),
        ],
        20 * unit,
        nx * nj * (rows * rows + 3 * rows * slots + 3 * slots * slots) * 2,
        vmem=32,
        scratch=[
            pltpu.VMEM((nj, slots, half), BF),
            pltpu.VMEM((nj, slots, slots), BF),
            pltpu.VMEM((chunks, cells, slots), F32),
        ],
    )(
        cell_rank, in_hbm(cell_skel), in_hbm(cell_interp), in_hbm(cell_matrix),
        x_face_rank, in_hbm(x_face_skel), in_hbm(x_face_interp), in_hbm(x_coupling),
        y_face_rank, in_hbm(y_face_skel), in_hbm(y_face_interp), in_hbm(y_coupling),
    )
    edge_in = passed_along(edge, "yz", -1)
    packed_in = passed_along(packed, "gx", -1)
    packed_last_in = passed_along(packed_last, "gx", -1)
    face_bytes = nj * (4 * rows * slots + 4 * slots * slots) * 2

    last = nx - 1
    tail = nj - 1
    group = tail // cells

    part, lower, lower_turned = call(
        functools.partial(x_part_kernel, cells, last),
        (),
        [smem, vmem, vmem, vmem, vmem, vmem, vmem],
        [vmem, vmem, vmem],
        [
            shape((nj, fslots, fslots), F32),
            shape((nj, slots, fslots), BF),
            shape((nj, fslots, slots), BF),
        ],
        8 * unit // nx,
        face_bytes,
        vmem=16,
    )(x_face_rank, x_face_skel, x_face_interp, x_coupling, last_turned, last_schur, top_in)

    edge_in, part = lax.optimization_barrier((edge_in, part))
    y_out = call(
        functools.partial(y_edge_kernel, nx, tail),
        (1,),
        [
            smem,
            pl.BlockSpec((nx, cells, fslots), lambda i: (0, group, 0)),
            pl.BlockSpec((nx, 1, rows, fslots), lambda i: (0, tail, 0, 0)),
            pl.BlockSpec((nx, cells, half), lambda i: (0, group, 0)),
            pl.BlockSpec((nx, 2, slots, half), lambda i: (0, 0, 0, 0)),
            pl.BlockSpec((nx, 2, slots, half), lambda i: (0, 0, 0, 0)),
            pl.BlockSpec(memory_space=pl.ANY),
        ],
        pl.BlockSpec((nx, 1, fslots, fslots), lambda i: (0, tail, 0, 0)),
        shape((nx, nj, fslots, fslots), BF),
        8 * unit // nj,
        nx * face_bytes // nj,
        {6: 0},
    )(y_face_rank, y_face_skel, in_hbm(y_face_interp), y_coupling, corner, edge_in, y_out)

    for places, arrived in (
        (range(chunks - 1), packed_in),
        (range(chunks - 1, chunks), packed_last_in),
    ):
        count = len(places)
        x_out = call(
            functools.partial(x_last_kernel, cells, last, places),
            (),
            [vmem, vmem, vmem, vmem, hbm],
            hbm,
            shape((nx, nj, fslots, fslots), BF),
            3 * unit // nx * count // chunks,
            nj * slots * slots * 11 * count // chunks,
            {4: 0},
            scratch=[
                pltpu.VMEM((count * cells, fslots, fslots), BF),
                pltpu.SemaphoreType.DMA((count, 2)),
            ],
        )(part, lower, lower_turned, arrived, x_out)
    return (x_out, y_out)


def solution(mesh):
    return jax.shard_map(
        body,
        mesh=mesh,
        in_specs=(
            P("gx", "yz", None, None),
            P("gx", "yz", None),
            P("gx", "yz", None),
            P("gx", "yz", None, None),
            P("gx", "yz", None),
            P("gx", "yz"),
            P("gx", "yz", None, None),
            P("gx", "yz", None),
            P("gx", "yz"),
            P("gx", "yz", None, None),
            P("gx", "yz", None),
            P("gx", "yz"),
        ),
        out_specs=(P("gx", "yz", None, None), P("gx", "yz", None, None)),
        check_vma=False,
    )
```

```python
import functools

import jax
import jax.numpy as jnp
from jax import lax
from jax.experimental import pallas as pl
from jax.experimental.pallas import tpu as pltpu
from jax.sharding import PartitionSpec as P

BF = jnp.bfloat16
F32 = jnp.float32
MIB = 1024 * 1024


def passed_along(x, axis, by):
    devices = lax.axis_size(axis)
    pairs = [(i, i + by) for i in range(devices) if 0 <= i + by < devices]
    return lax.ppermute(x, axis, pairs)


def dot_nt(a, b):
    return lax.dot_general(a, b, (((1,), (1,)), ((), ())), preferred_element_type=F32)


def dot(a, b):
    return lax.dot_general(a, b, (((1,), (0,)), ((), ())), preferred_element_type=F32)


def kept_cleared(turned):
    most = jnp.max(turned, axis=0, keepdims=True)
    least = jnp.where(most.astype(F32) == 1.0, F32(1.0), F32(-2.0)).astype(BF)
    return jnp.where(turned >= least, turned, BF(0.0))


def marked_with(skel_row, live, interp):
    rows, slots = interp.shape
    picked_row = jnp.where(live, skel_row, -1).astype(F32).astype(BF)
    row = lax.broadcasted_iota(jnp.int32, (rows, slots), 0).astype(F32).astype(BF)
    live_row = jnp.where(live, F32(1.0), F32(0.0)).astype(BF)
    return jnp.where(row == picked_row, BF(1.0), interp * live_row)


def marked_of(skel_row, rank, interp):
    return marked_with(skel_row, lax.broadcasted_iota(jnp.int32, skel_row.shape, 1) < rank, interp)


def bases_of(cells, layer, first, rank_ref, skel, interp_ref):
    marked = [
        marked_of(skel[k : k + 1], rank_ref[layer, first + k], interp_ref[0, k])
        for k in range(cells)
    ]
    return [kept_cleared(t) for t in [jnp.transpose(m) for m in marked]]


def scaled(turned, conduct):
    return turned * -conduct


def face_of(left, link, link_t, right):
    upper = jnp.concatenate([left, link], axis=1)
    lower = jnp.concatenate([link_t, right], axis=1)
    return jnp.concatenate([upper, lower], axis=0)


def project(turned, matrices):
    inner = [dot(t, m).astype(BF) for t, m in zip(turned, matrices)]
    return [dot_nt(i, t) for i, t in zip(inner, turned)]


def pack_masks(size):
    half = size // 2
    row = lax.broadcasted_iota(jnp.int32, (half, size), 0)
    lane = lax.broadcasted_iota(jnp.int32, (half, size), 1)
    ahead = lane - row
    upper = (ahead >= 0) & (ahead < half)
    return upper, ahead == 0, ahead == half


def main_kernel(
    cells, layers, chunks,
    rank_ref, skel_ref, interp_ref, matrix_ref,
    x_rank_ref, x_skel_ref, x_interp_ref, x_coup_ref,
    y_rank_ref, y_skel_ref, y_interp_ref, y_coup_ref,
    x_out_ref, y_out_ref, packed_ref, packed_last_ref, edge_ref, corner_ref, last_turned_ref, last_schur_ref,
    store_turned, store_schur, store_extra,
):
    layer = layers - 1 - pl.program_id(0)
    chunk = chunks - 1 - pl.program_id(1)
    first = chunk * cells
    slots = skel_ref.shape[-1]
    half = slots // 2
    top = interp_ref.shape[2] // 2

    turned = bases_of(cells, layer, first, rank_ref, skel_ref[0], interp_ref)
    schurs = project(turned, [matrix_ref[0, k] for k in range(cells)])
    schurs = [s.astype(BF) for s in schurs]

    def faces(out_ref, f_rank_ref, f_skel_ref, f_interp_ref, coup_ref, rights):
        found = bases_of(cells, layer, first, f_rank_ref, f_skel_ref[0], f_interp_ref)
        matrices = []
        for k in range(cells):
            right_turned, right = rights[k]
            conduct = coup_ref[0, k : k + 1]
            lower = turned[k][:, top:]
            link = dot_nt(scaled(lower, conduct), right_turned).astype(BF)
            link_t = dot_nt(scaled(right_turned, conduct), lower).astype(BF)
            matrices.append(face_of(schurs[k], link, link_t, right))
        results = project(found, matrices)
        for k in range(cells):
            out_ref[0, k] = results[k].astype(BF)

    def stored(place):
        return store_turned[place], store_schur[place]

    after = jnp.minimum(first + cells, store_schur.shape[0] - 1)
    rights = [(turned[k][:, :top], schurs[k]) for k in range(1, cells)]
    faces(y_out_ref, y_rank_ref, y_skel_ref, y_interp_ref, y_coup_ref, rights + [stored(after)])

    @pl.when(layer < layers - 1)
    def _():
        rights = [stored(first + k) for k in range(cells)]
        faces(x_out_ref, x_rank_ref, x_skel_ref, x_interp_ref, x_coup_ref, rights)

    for k in range(cells):
        store_turned[first + k] = turned[k][:, :top]
        store_schur[first + k] = schurs[k]

    @pl.when(layer == layers - 1)
    def _():
        for k in range(cells):
            last_turned_ref[first + k] = turned[k][:, top:]
            last_schur_ref[first + k] = schurs[k]

    @pl.when(layer == 0)
    def _():
        upper, same, opposite = pack_masks(slots)

        def put(packed_ref, start):
            for k in range(cells):
                above, below = schurs[k][:half].astype(F32), schurs[k][half:].astype(F32)
                place = pl.ds(pl.multiple_of(start + k * half, half), half)
                packed_ref[place] = jnp.where(upper, above, below).astype(BF)

        @pl.when(chunk < chunks - 1)
        def _():
            put(packed_ref, chunk * (cells * half))

        @pl.when(chunk == chunks - 1)
        def _():
            put(packed_last_ref, 0)

        for p in range(0, cells, 2):
            extra = jnp.where(opposite, schurs[p][:half].astype(F32), F32(0.0))
            if p + 1 < cells:
                extra += jnp.where(same, schurs[p + 1][half:].astype(F32), F32(0.0))
            store_extra[chunk, p // 2 : p // 2 + 1] = jnp.sum(extra, axis=0, keepdims=True)

        @pl.when(chunk == 0)
        def _():
            pairs = -(-cells // 2)
            for ref, places in ((packed_ref, range(chunks - 1)), (packed_last_ref, [chunks - 1])):
                start = len(places) * cells * half
                rows = [store_extra[c, :pairs] for c in places]
                pad = ref.shape[0] - start - pairs * len(places)
                if pad:
                    rows.append(jnp.zeros((pad, slots), F32))
                ref[start:] = jnp.concatenate(rows, axis=0).astype(BF)

    @pl.when(chunk == 0)
    def _():
        edge_ref[layer, 0] = turned[0][:, :top]
        edge_ref[layer, 1] = schurs[0]

    @pl.when(chunk == chunks - 1)
    def _():
        corner_ref[layer, 0] = turned[cells - 1][:, top:]
        corner_ref[layer, 1] = schurs[cells - 1]


def y_edge_kernel(layers, place, rank_ref, skel_ref, interp_ref, coup_ref, corner_ref, edge_ref, _, out_ref):
    row = place % skel_ref.shape[1]
    marked = [
        marked_of(skel_ref[i, row : row + 1], rank_ref[i, place], interp_ref[i, 0])
        for i in range(layers)
    ]
    found = [kept_cleared(jnp.transpose(m)) for m in marked]
    matrices = []
    for i in range(layers):
        conduct = coup_ref[i, row : row + 1]
        link = dot_nt(scaled(corner_ref[i, 0], conduct), edge_ref[i, 0]).astype(BF)
        link_t = dot_nt(scaled(edge_ref[i, 0], conduct), corner_ref[i, 0]).astype(BF)
        matrices.append(face_of(corner_ref[i, 1], link, link_t, edge_ref[i, 1]))
    results = project(found, matrices)
    for i in range(layers):
        out_ref[i, 0] = results[i].astype(BF)


def x_part_kernel(
    cells, layer, rank_ref, skel_ref, interp_ref, coup_ref, turned_ref, schur_ref, top_ref, picks_ref,
    part_ref, lower_ref, lower_turned_ref,
):
    count, slots, half = turned_ref.shape
    nothing = jnp.zeros((slots, slots), BF)
    for first in range(0, count, cells):
        group = range(first, first + cells)
        skel = skel_ref[layer, first : first + cells]
        marked = [
            marked_of(skel[k - first : k - first + 1], rank_ref[layer, k], interp_ref[layer, k]) for k in group
        ]
        faces = [kept_cleared(t) for t in [jnp.transpose(m) for m in marked]]
        for k in group:
            lower_turned_ref[k] = faces[k - first][:, half:]
            lower_ref[k] = jnp.transpose(faces[k - first][:, half:])
        tops = []
        for k in group:
            picks = picks_ref[k : k + 1]
            tops.append(kept_cleared(jnp.transpose(marked_with(picks - 1, picks > 0, top_ref[k]))))
        matrices = []
        for k, top in zip(group, tops):
            conduct = coup_ref[layer, k : k + 1]
            link = dot_nt(scaled(turned_ref[k], conduct), top).astype(BF)
            link_t = dot_nt(scaled(top, conduct), turned_ref[k]).astype(BF)
            matrices.append(face_of(schur_ref[k], link, link_t, nothing))
        for k, result in zip(group, project(faces, matrices)):
            part_ref[k] = result


def x_last_kernel(
    cells, layer, places, part_ref, lower_ref, lower_turned_ref, packed_ref, _, out_ref, held, sems
):
    slots = part_ref.shape[-1]
    half = slots // 2
    upper, same, opposite = pack_masks(slots)
    one, zero, mid = F32(1.0), F32(0.0), F32(0.5)
    top_scale = jnp.where(same, mid, jnp.where(upper, one, zero))
    low_scale = jnp.where(opposite, mid, jnp.where(upper, zero, one))
    same_scale = jnp.where(same, one, zero)
    opposite_scale = jnp.where(opposite, one, zero)
    extras = packed_ref[len(places) * cells * half :].astype(F32)
    pairs = -(-cells // 2)
    copies = []
    for n, c in enumerate(places):
        group = range(c * cells, (c + 1) * cells)
        schurs = []
        for k in range(cells):
            start = (n * cells + k) * half
            packed = packed_ref[start : start + half].astype(F32)
            extra = extras[n * pairs + k // 2 : n * pairs + k // 2 + 1]
            top, low = packed * top_scale, packed * low_scale
            if k % 2 == 0:
                top += extra * opposite_scale
            else:
                low += extra * same_scale
            tri = jnp.concatenate([top, low], axis=0).astype(BF)
            schurs.append(tri + jnp.transpose(tri))
        inner = [dot(lower_turned_ref[k], h).astype(BF) for k, h in zip(group, schurs)]
        results = [dot(i, lower_ref[k]) for k, i in zip(group, inner)]
        part_cells = max(1, cells // 2)
        for start in range(0, cells, part_cells):
            for k in range(start, start + part_cells):
                held[n * cells + k] = (part_ref[c * cells + k] + results[k]).astype(BF)
            copy = pltpu.make_async_copy(
                held.at[pl.ds(n * cells + start, part_cells)],
                out_ref.at[layer, pl.ds(c * cells + start, part_cells)],
                sems.at[n, start // part_cells],
            )
            copy.start()
            copies.append(copy)
    for copy in copies:
        copy.wait()


def call(kernel, grid, in_specs, out_specs, out_shape, flops, moved, aliases=None, vmem=24, scratch=()):
    return pl.pallas_call(
        kernel,
        grid=grid,
        in_specs=in_specs,
        out_specs=out_specs,
        out_shape=out_shape,
        scratch_shapes=scratch,
        input_output_aliases=aliases or {},
        compiler_params=pltpu.CompilerParams(vmem_limit_bytes=vmem * MIB),
        cost_estimate=pl.CostEstimate(flops=flops, bytes_accessed=moved, transcendentals=0),
    )


def in_hbm(x):
    return pltpu.with_memory_space_constraint(x, pltpu.HBM)


def body(
    cell_matrix,
    x_coupling,
    y_coupling,
    cell_interp,
    cell_skel,
    cell_rank,
    x_face_interp,
    x_face_skel,
    x_face_rank,
    y_face_interp,
    y_face_skel,
    y_face_rank,
):
    nx, nj, rows, slots = cell_interp.shape
    half = rows // 2
    fslots = x_face_interp.shape[-1]
    cells = next(n for n in (8, 4, 2, 1) if nj % n == 0 and nj > n)
    chunks = nj // cells
    unit = 2 * nx * nj * slots * slots * slots
    smem = pl.BlockSpec(memory_space=pltpu.SMEM)
    shape = jax.ShapeDtypeStruct

    hbm = pl.BlockSpec(memory_space=pltpu.HBM)
    vmem = pl.BlockSpec(memory_space=pltpu.VMEM)
    top_in = passed_along(cell_interp[0, :, :half], "gx", -1)
    live = lax.broadcasted_iota(jnp.int32, (nj, slots), 1) < cell_rank[0, :, None]
    gathered = lax.all_gather(jnp.where(live, cell_skel[0] + 1, 0), "gx")
    gathered = jnp.concatenate([gathered, jnp.zeros_like(gathered[:1])], axis=0)
    picks_in = lax.dynamic_index_in_dim(gathered, lax.axis_index("gx") + 1, 0, keepdims=False)

    def pack_rows(count):
        extra = count * -(-cells // 2)
        return count * cells * slots // 2 + -(-extra // 16) * 16

    near = max(nx - 2, 0)

    def down(*dims):
        zeros = (0,) * len(dims)
        return pl.BlockSpec((1, cells) + dims, lambda i, c: (nx - 1 - i, chunks - 1 - c) + zeros)

    def down_x(*dims):
        zeros = (0,) * len(dims)

        def place(i, c):
            return (jnp.minimum(nx - 1 - i, near), jnp.where(i == 0, chunks - 1, chunks - 1 - c)) + zeros

        return pl.BlockSpec((1, cells) + dims, place)

    x_out, y_out, packed, packed_last, edge, corner, last_turned, last_schur = call(
        functools.partial(main_kernel, cells, nx, chunks),
        (nx, chunks),
        [
            smem, down(slots), down(rows, slots), down(rows, rows),
            smem, down_x(fslots), down_x(rows, fslots), down_x(half),
            smem, down(fslots), down(rows, fslots), down(half),
        ],
        [
            down_x(fslots, fslots),
            down(fslots, fslots),
            vmem, vmem, vmem, vmem, vmem, vmem,
        ],
        [
            shape((nx, nj, fslots, fslots), BF),
            shape((nx, nj, fslots, fslots), BF),
            shape((pack_rows(chunks - 1), slots), BF),
            shape((pack_rows(1), slots), BF),
            shape((nx, 2, slots, half), BF),
            shape((nx, 2, slots, half), BF),
            shape((nj, slots, half), BF),
            shape((nj, slots, slots), BF),
        ],
        20 * unit,
        nx * nj * (rows * rows + 3 * rows * slots + 3 * slots * slots) * 2,
        vmem=32,
        scratch=[
            pltpu.VMEM((nj, slots, half), BF),
            pltpu.VMEM((nj, slots, slots), BF),
            pltpu.VMEM((chunks, cells, slots), F32),
        ],
    )(
        cell_rank, in_hbm(cell_skel), in_hbm(cell_interp), in_hbm(cell_matrix),
        x_face_rank, in_hbm(x_face_skel), in_hbm(x_face_interp), in_hbm(x_coupling),
        y_face_rank, in_hbm(y_face_skel), in_hbm(y_face_interp), in_hbm(y_coupling),
    )
    edge_in = passed_along(edge, "yz", -1)
    packed_in = passed_along(packed, "gx", -1)
    packed_last_in = passed_along(packed_last, "gx", -1)
    face_bytes = nj * (4 * rows * slots + 4 * slots * slots) * 2

    last = nx - 1
    tail = nj - 1
    group = tail // cells

    part, lower, lower_turned = call(
        functools.partial(x_part_kernel, cells, last),
        (),
        [smem, vmem, vmem, vmem, vmem, vmem, vmem, vmem],
        [vmem, vmem, vmem],
        [
            shape((nj, fslots, fslots), F32),
            shape((nj, slots, fslots), BF),
            shape((nj, fslots, slots), BF),
        ],
        8 * unit // nx,
        face_bytes,
        vmem=16,
    )(x_face_rank, x_face_skel, x_face_interp, x_coupling, last_turned, last_schur, top_in, picks_in)

    edge_in, part = lax.optimization_barrier((edge_in, part))
    y_out = call(
        functools.partial(y_edge_kernel, nx, tail),
        (1,),
        [
            smem,
            pl.BlockSpec((nx, cells, fslots), lambda i: (0, group, 0)),
            pl.BlockSpec((nx, 1, rows, fslots), lambda i: (0, tail, 0, 0)),
            pl.BlockSpec((nx, cells, half), lambda i: (0, group, 0)),
            pl.BlockSpec((nx, 2, slots, half), lambda i: (0, 0, 0, 0)),
            pl.BlockSpec((nx, 2, slots, half), lambda i: (0, 0, 0, 0)),
            pl.BlockSpec(memory_space=pl.ANY),
        ],
        pl.BlockSpec((nx, 1, fslots, fslots), lambda i: (0, tail, 0, 0)),
        shape((nx, nj, fslots, fslots), BF),
        8 * unit // nj,
        nx * face_bytes // nj,
        {6: 0},
    )(y_face_rank, y_face_skel, in_hbm(y_face_interp), y_coupling, corner, edge_in, y_out)

    for places, arrived in (
        (range(chunks - 1), packed_in),
        (range(chunks - 1, chunks), packed_last_in),
    ):
        count = len(places)
        x_out = call(
            functools.partial(x_last_kernel, cells, last, places),
            (),
            [vmem, vmem, vmem, vmem, hbm],
            hbm,
            shape((nx, nj, fslots, fslots), BF),
            3 * unit // nx * count // chunks,
            nj * slots * slots * 11 * count // chunks,
            {4: 0},
            scratch=[
                pltpu.VMEM((count * cells, fslots, fslots), BF),
                pltpu.SemaphoreType.DMA((count, 2)),
            ],
        )(part, lower, lower_turned, arrived, x_out)
    return (x_out, y_out)


def solution(mesh):
    return jax.shard_map(
        body,
        mesh=mesh,
        in_specs=(
            P("gx", "yz", None, None),
            P("gx", "yz", None),
            P("gx", "yz", None),
            P("gx", "yz", None, None),
            P("gx", "yz", None),
            P("gx", "yz"),
            P("gx", "yz", None, None),
            P("gx", "yz", None),
            P("gx", "yz"),
            P("gx", "yz", None, None),
            P("gx", "yz", None),
            P("gx", "yz"),
        ),
        out_specs=(P("gx", "yz", None, None), P("gx", "yz", None, None)),
        check_vma=False,
    )
```

```python
import functools

import jax
import jax.numpy as jnp
from jax import lax
from jax.experimental import pallas as pl
from jax.experimental.pallas import tpu as pltpu
from jax.sharding import PartitionSpec as P

BF = jnp.bfloat16
F32 = jnp.float32
MIB = 1024 * 1024


def passed_along(x, axis, by):
    devices = lax.axis_size(axis)
    pairs = [(i, i + by) for i in range(devices) if 0 <= i + by < devices]
    return lax.ppermute(x, axis, pairs)


def dot_nt(a, b):
    return lax.dot_general(a, b, (((1,), (1,)), ((), ())), preferred_element_type=F32)


def dot(a, b):
    return lax.dot_general(a, b, (((1,), (0,)), ((), ())), preferred_element_type=F32)


def marks_of(skel_row, rank, interp):
    rows, slots = interp.shape
    live = lax.broadcasted_iota(jnp.int32, (1, slots), 1) < rank
    picked_row = jnp.where(live, skel_row, -1).astype(F32).astype(BF)
    row = lax.broadcasted_iota(jnp.int32, (rows, slots), 0).astype(F32).astype(BF)
    live_row = jnp.where(live, F32(1.0), F32(0.0)).astype(BF)
    return row == picked_row, interp * live_row


def kept_cleared(turned):
    most = jnp.max(turned, axis=0, keepdims=True)
    least = jnp.where(most.astype(F32) == 1.0, F32(1.0), F32(-2.0)).astype(BF)
    return jnp.where(turned >= least, turned, BF(0.0))


def marked_of(skel_row, rank, interp):
    hit, live = marks_of(skel_row, rank, interp)
    return jnp.where(hit, BF(1.0), live)


def bases_of(cells, layer, first, rank_ref, skel, interp_ref):
    marked = [
        marked_of(skel[k : k + 1], rank_ref[layer, first + k], interp_ref[0, k])
        for k in range(cells)
    ]
    return [kept_cleared(t) for t in [jnp.transpose(m) for m in marked]]


def scaled(turned, conduct):
    return turned * -conduct


def face_of(left, link, link_t, right):
    upper = jnp.concatenate([left, link], axis=1)
    lower = jnp.concatenate([link_t, right], axis=1)
    return jnp.concatenate([upper, lower], axis=0)


def project(turned, matrices):
    inner = [dot(t, m).astype(BF) for t, m in zip(turned, matrices)]
    return [dot_nt(i, t) for i, t in zip(inner, turned)]


def top_kernel(cells, rank_hbm, skel_hbm, interp_hbm, out_ref, rank_ref, skel_ref, held, small_sems, sems):
    count, half, _ = out_ref.shape
    small = [
        pltpu.make_async_copy(rank_hbm, rank_ref, small_sems.at[0]),
        pltpu.make_async_copy(skel_hbm.at[0], skel_ref, small_sems.at[1]),
    ]
    copies = []
    for c in range(count // cells):
        group = pl.ds(c * cells, cells)
        copies.append(
            pltpu.make_async_copy(
                interp_hbm.at[0, group, pl.ds(0, half)], held.at[group], sems.at[c]
            )
        )
    for copy in small + copies:
        copy.start()
    for copy in small:
        copy.wait()
    for c in range(count // cells):
        copies[c].wait()
        for k in range(c * cells, (c + 1) * cells):
            out_ref[k] = marked_of(skel_ref[k : k + 1], rank_ref[0, k], held[k])


def pack_masks(size):
    half = size // 2
    row = lax.broadcasted_iota(jnp.int32, (half, size), 0)
    lane = lax.broadcasted_iota(jnp.int32, (half, size), 1)
    ahead = lane - row
    upper = (ahead >= 0) & (ahead < half)
    return upper, ahead == 0, ahead == half


def main_kernel(
    cells, layers, chunks,
    rank_ref, skel_ref, interp_ref, matrix_ref,
    x_rank_ref, x_skel_ref, x_interp_ref, x_coup_ref,
    y_rank_ref, y_skel_ref, y_interp_ref, y_coup_ref,
    x_out_ref, y_out_ref, packed_ref, packed_last_ref, edge_ref, corner_ref, last_turned_ref, last_schur_ref,
    store_turned, store_schur, store_extra,
):
    layer = layers - 1 - pl.program_id(0)
    chunk = chunks - 1 - pl.program_id(1)
    first = chunk * cells
    slots = skel_ref.shape[-1]
    half = slots // 2
    top = interp_ref.shape[2] // 2

    turned = bases_of(cells, layer, first, rank_ref, skel_ref[0], interp_ref)
    schurs = project(turned, [matrix_ref[0, k] for k in range(cells)])
    schurs = [s.astype(BF) for s in schurs]

    def faces(out_ref, f_rank_ref, f_skel_ref, f_interp_ref, coup_ref, rights):
        found = bases_of(cells, layer, first, f_rank_ref, f_skel_ref[0], f_interp_ref)
        matrices = []
        for k in range(cells):
            right_turned, right = rights[k]
            conduct = coup_ref[0, k : k + 1]
            lower = turned[k][:, top:]
            link = dot_nt(scaled(lower, conduct), right_turned).astype(BF)
            link_t = dot_nt(scaled(right_turned, conduct), lower).astype(BF)
            matrices.append(face_of(schurs[k], link, link_t, right))
        results = project(found, matrices)
        for k in range(cells):
            out_ref[0, k] = results[k].astype(BF)

    def stored(place):
        return store_turned[place], store_schur[place]

    after = jnp.minimum(first + cells, store_schur.shape[0] - 1)
    rights = [(turned[k][:, :top], schurs[k]) for k in range(1, cells)]
    faces(y_out_ref, y_rank_ref, y_skel_ref, y_interp_ref, y_coup_ref, rights + [stored(after)])

    @pl.when(layer < layers - 1)
    def _():
        rights = [stored(first + k) for k in range(cells)]
        faces(x_out_ref, x_rank_ref, x_skel_ref, x_interp_ref, x_coup_ref, rights)

    for k in range(cells):
        store_turned[first + k] = turned[k][:, :top]
        store_schur[first + k] = schurs[k]

    @pl.when(layer == layers - 1)
    def _():
        for k in range(cells):
            last_turned_ref[first + k] = turned[k][:, top:]
            last_schur_ref[first + k] = schurs[k]

    @pl.when(layer == 0)
    def _():
        upper, same, opposite = pack_masks(slots)

        def put(packed_ref, start):
            for k in range(cells):
                above, below = schurs[k][:half].astype(F32), schurs[k][half:].astype(F32)
                place = pl.ds(pl.multiple_of(start + k * half, half), half)
                packed_ref[place] = jnp.where(upper, above, below).astype(BF)

        @pl.when(chunk < chunks - 1)
        def _():
            put(packed_ref, chunk * (cells * half))

        @pl.when(chunk == chunks - 1)
        def _():
            put(packed_last_ref, 0)

        for p in range(0, cells, 2):
            extra = jnp.where(opposite, schurs[p][:half].astype(F32), F32(0.0))
            if p + 1 < cells:
                extra += jnp.where(same, schurs[p + 1][half:].astype(F32), F32(0.0))
            store_extra[chunk, p // 2 : p // 2 + 1] = jnp.sum(extra, axis=0, keepdims=True)

        @pl.when(chunk == 0)
        def _():
            pairs = -(-cells // 2)
            start = (chunks - 1) * cells * half
            rows = [store_extra[c, :pairs] for c in range(chunks)]
            pad = packed_ref.shape[0] - start - pairs * chunks
            if pad:
                rows.append(jnp.zeros((pad, slots), F32))
            packed_ref[start:] = jnp.concatenate(rows, axis=0).astype(BF)

    @pl.when(chunk == 0)
    def _():
        edge_ref[layer, 0] = turned[0][:, :top]
        edge_ref[layer, 1] = schurs[0]

    @pl.when(chunk == chunks - 1)
    def _():
        corner_ref[layer, 0] = turned[cells - 1][:, top:]
        corner_ref[layer, 1] = schurs[cells - 1]


def y_edge_kernel(layers, place, rank_ref, skel_ref, interp_ref, coup_ref, corner_ref, edge_ref, _, out_ref):
    row = place % skel_ref.shape[1]
    marked = [
        marked_of(skel_ref[i, row : row + 1], rank_ref[i, place], interp_ref[i, 0])
        for i in range(layers)
    ]
    found = [kept_cleared(jnp.transpose(m)) for m in marked]
    matrices = []
    for i in range(layers):
        conduct = coup_ref[i, row : row + 1]
        link = dot_nt(scaled(corner_ref[i, 0], conduct), edge_ref[i, 0]).astype(BF)
        link_t = dot_nt(scaled(edge_ref[i, 0], conduct), corner_ref[i, 0]).astype(BF)
        matrices.append(face_of(corner_ref[i, 1], link, link_t, edge_ref[i, 1]))
    results = project(found, matrices)
    for i in range(layers):
        out_ref[i, 0] = results[i].astype(BF)


def x_part_kernel(
    cells, layer, rank_ref, skel_ref, interp_ref, coup_ref, turned_ref, schur_ref, top_ref,
    part_ref, lower_ref, lower_turned_ref,
):
    count, slots, half = turned_ref.shape
    nothing = jnp.zeros((slots, slots), BF)
    for first in range(0, count, cells):
        group = range(first, first + cells)
        skel = skel_ref[layer, first : first + cells]
        marked = [
            marked_of(skel[k - first : k - first + 1], rank_ref[layer, k], interp_ref[layer, k]) for k in group
        ]
        faces = [kept_cleared(t) for t in [jnp.transpose(m) for m in marked]]
        for k in group:
            lower_turned_ref[k] = faces[k - first][:, half:]
            lower_ref[k] = jnp.transpose(faces[k - first][:, half:])
        tops = [kept_cleared(t) for t in [jnp.transpose(top_ref[k]) for k in group]]
        matrices = []
        for k, top in zip(group, tops):
            conduct = coup_ref[layer, k : k + 1]
            link = dot_nt(scaled(turned_ref[k], conduct), top).astype(BF)
            link_t = dot_nt(scaled(top, conduct), turned_ref[k]).astype(BF)
            matrices.append(face_of(schur_ref[k], link, link_t, nothing))
        for k, result in zip(group, project(faces, matrices)):
            part_ref[k] = result


def x_last_kernel(
    cells, layer, places, part_ref, lower_ref, lower_turned_ref, extra_ref, packed_ref, _, out_ref, held, sems
):
    slots = part_ref.shape[-1]
    half = slots // 2
    upper, same, opposite = pack_masks(slots)
    one, zero, mid = F32(1.0), F32(0.0), F32(0.5)
    top_scale = jnp.where(same, mid, jnp.where(upper, one, zero))
    low_scale = jnp.where(opposite, mid, jnp.where(upper, zero, one))
    same_scale = jnp.where(same, one, zero)
    opposite_scale = jnp.where(opposite, one, zero)
    extras = extra_ref[(part_ref.shape[0] // cells - 1) * cells * half :].astype(F32)
    pairs = -(-cells // 2)
    copies = []
    for n, c in enumerate(places):
        group = range(c * cells, (c + 1) * cells)
        schurs = []
        for k in range(cells):
            start = (n * cells + k) * half
            packed = packed_ref[start : start + half].astype(F32)
            extra = extras[c * pairs + k // 2 : c * pairs + k // 2 + 1]
            top, low = packed * top_scale, packed * low_scale
            if k % 2 == 0:
                top += extra * opposite_scale
            else:
                low += extra * same_scale
            tri = jnp.concatenate([top, low], axis=0).astype(BF)
            schurs.append(tri + jnp.transpose(tri))
        inner = [dot(lower_turned_ref[k], h).astype(BF) for k, h in zip(group, schurs)]
        results = [dot(i, lower_ref[k]) for k, i in zip(group, inner)]
        part_cells = max(1, cells // 2)
        for start in range(0, cells, part_cells):
            for k in range(start, start + part_cells):
                held[n * cells + k] = (part_ref[c * cells + k] + results[k]).astype(BF)
            copy = pltpu.make_async_copy(
                held.at[pl.ds(n * cells + start, part_cells)],
                out_ref.at[layer, pl.ds(c * cells + start, part_cells)],
                sems.at[n, start // part_cells],
            )
            copy.start()
            copies.append(copy)
    for copy in copies:
        copy.wait()


def call(kernel, grid, in_specs, out_specs, out_shape, flops, moved, aliases=None, vmem=24, scratch=()):
    return pl.pallas_call(
        kernel,
        grid=grid,
        in_specs=in_specs,
        out_specs=out_specs,
        out_shape=out_shape,
        scratch_shapes=scratch,
        input_output_aliases=aliases or {},
        compiler_params=pltpu.CompilerParams(vmem_limit_bytes=vmem * MIB),
        cost_estimate=pl.CostEstimate(flops=flops, bytes_accessed=moved, transcendentals=0),
    )


def in_hbm(x):
    return pltpu.with_memory_space_constraint(x, pltpu.HBM)


def body(
    cell_matrix,
    x_coupling,
    y_coupling,
    cell_interp,
    cell_skel,
    cell_rank,
    x_face_interp,
    x_face_skel,
    x_face_rank,
    y_face_interp,
    y_face_skel,
    y_face_rank,
):
    nx, nj, rows, slots = cell_interp.shape
    half = rows // 2
    fslots = x_face_interp.shape[-1]
    cells = next(n for n in (8, 4, 2, 1) if nj % n == 0 and nj > n)
    chunks = nj // cells
    unit = 2 * nx * nj * slots * slots * slots
    smem = pl.BlockSpec(memory_space=pltpu.SMEM)
    shape = jax.ShapeDtypeStruct

    hbm = pl.BlockSpec(memory_space=pltpu.HBM)
    vmem = pl.BlockSpec(memory_space=pltpu.VMEM)
    top = call(
        functools.partial(top_kernel, cells),
        (),
        [hbm, hbm, hbm],
        vmem,
        shape((nj, half, slots), BF),
        0,
        4 * nj * half * slots,
        vmem=8,
        scratch=[
            pltpu.SMEM((nx, nj), jnp.int32),
            pltpu.VMEM((nj, slots), jnp.int32),
            pltpu.VMEM((nj, half, slots), BF),
            pltpu.SemaphoreType.DMA((2,)),
            pltpu.SemaphoreType.DMA((chunks,)),
        ],
    )(in_hbm(cell_rank), in_hbm(cell_skel), in_hbm(cell_interp))
    top_in = passed_along(top, "gx", -1)


    late_rows = cells * slots // 2
    early_rows = (chunks - 1) * late_rows + -(-chunks * -(-cells // 2) // 16) * 16

    near = max(nx - 2, 0)

    def down(*dims):
        zeros = (0,) * len(dims)
        return pl.BlockSpec((1, cells) + dims, lambda i, c: (nx - 1 - i, chunks - 1 - c) + zeros)

    def down_x(*dims):
        zeros = (0,) * len(dims)

        def place(i, c):
            return (jnp.minimum(nx - 1 - i, near), jnp.where(i == 0, chunks - 1, chunks - 1 - c)) + zeros

        return pl.BlockSpec((1, cells) + dims, place)

    x_out, y_out, packed, packed_last, edge, corner, last_turned, last_schur = call(
        functools.partial(main_kernel, cells, nx, chunks),
        (nx, chunks),
        [
            smem, down(slots), down(rows, slots), down(rows, rows),
            smem, down_x(fslots), down_x(rows, fslots), down_x(half),
            smem, down(fslots), down(rows, fslots), down(half),
        ],
        [
            down_x(fslots, fslots),
            down(fslots, fslots),
            vmem, vmem, vmem, vmem, vmem, vmem,
        ],
        [
            shape((nx, nj, fslots, fslots), BF),
            shape((nx, nj, fslots, fslots), BF),
            shape((early_rows, slots), BF),
            shape((late_rows, slots), BF),
            shape((nx, 2, slots, half), BF),
            shape((nx, 2, slots, half), BF),
            shape((nj, slots, half), BF),
            shape((nj, slots, slots), BF),
        ],
        20 * unit,
        nx * nj * (rows * rows + 3 * rows * slots + 3 * slots * slots) * 2,
        vmem=32,
        scratch=[
            pltpu.VMEM((nj, slots, half), BF),
            pltpu.VMEM((nj, slots, slots), BF),
            pltpu.VMEM((chunks, cells, slots), F32),
        ],
    )(
        cell_rank, in_hbm(cell_skel), in_hbm(cell_interp), in_hbm(cell_matrix),
        x_face_rank, in_hbm(x_face_skel), in_hbm(x_face_interp), in_hbm(x_coupling),
        y_face_rank, in_hbm(y_face_skel), in_hbm(y_face_interp), in_hbm(y_coupling),
    )
    edge_in = passed_along(edge, "yz", -1)
    packed_in = passed_along(packed, "gx", -1)
    packed_last_in = passed_along(packed_last, "gx", -1)
    face_bytes = nj * (4 * rows * slots + 4 * slots * slots) * 2

    last = nx - 1
    tail = nj - 1
    group = tail // cells

    part, lower, lower_turned = call(
        functools.partial(x_part_kernel, cells, last),
        (),
        [smem, vmem, vmem, vmem, vmem, vmem, vmem],
        [vmem, vmem, vmem],
        [
            shape((nj, fslots, fslots), F32),
            shape((nj, slots, fslots), BF),
            shape((nj, fslots, slots), BF),
        ],
        8 * unit // nx,
        face_bytes,
        vmem=16,
    )(x_face_rank, x_face_skel, x_face_interp, x_coupling, last_turned, last_schur, top_in)

    edge_in, part = lax.optimization_barrier((edge_in, part))
    y_out = call(
        functools.partial(y_edge_kernel, nx, tail),
        (1,),
        [
            smem,
            pl.BlockSpec((nx, cells, fslots), lambda i: (0, group, 0)),
            pl.BlockSpec((nx, 1, rows, fslots), lambda i: (0, tail, 0, 0)),
            pl.BlockSpec((nx, cells, half), lambda i: (0, group, 0)),
            pl.BlockSpec((nx, 2, slots, half), lambda i: (0, 0, 0, 0)),
            pl.BlockSpec((nx, 2, slots, half), lambda i: (0, 0, 0, 0)),
            pl.BlockSpec(memory_space=pl.ANY),
        ],
        pl.BlockSpec((nx, 1, fslots, fslots), lambda i: (0, tail, 0, 0)),
        shape((nx, nj, fslots, fslots), BF),
        8 * unit // nj,
        nx * face_bytes // nj,
        {6: 0},
    )(y_face_rank, y_face_skel, in_hbm(y_face_interp), y_coupling, corner, edge_in, y_out)

    for places, arrived in (
        (range(chunks - 1), packed_in),
        (range(chunks - 1, chunks), packed_last_in),
    ):
        count = len(places)
        x_out = call(
            functools.partial(x_last_kernel, cells, last, places),
            (),
            [vmem, vmem, vmem, vmem, vmem, hbm],
            hbm,
            shape((nx, nj, fslots, fslots), BF),
            3 * unit // nx * count // chunks,
            nj * slots * slots * 11 * count // chunks,
            {5: 0},
            scratch=[
                pltpu.VMEM((count * cells, fslots, fslots), BF),
                pltpu.SemaphoreType.DMA((count, 2)),
            ],
        )(part, lower, lower_turned, packed_in, arrived, x_out)
    return (x_out, y_out)


def solution(mesh):
    return jax.shard_map(
        body,
        mesh=mesh,
        in_specs=(
            P("gx", "yz", None, None),
            P("gx", "yz", None),
            P("gx", "yz", None),
            P("gx", "yz", None, None),
            P("gx", "yz", None),
            P("gx", "yz"),
            P("gx", "yz", None, None),
            P("gx", "yz", None),
            P("gx", "yz"),
            P("gx", "yz", None, None),
            P("gx", "yz", None),
            P("gx", "yz"),
        ),
        out_specs=(P("gx", "yz", None, None), P("gx", "yz", None, None)),
        check_vma=False,
    )
```

```python
import functools

import jax
import jax.numpy as jnp
from jax import lax
from jax.experimental import pallas as pl
from jax.experimental.pallas import tpu as pltpu
from jax.sharding import PartitionSpec as P

BF = jnp.bfloat16
F32 = jnp.float32
MIB = 1024 * 1024


def passed_along(x, axis, by):
    devices = lax.axis_size(axis)
    pairs = [(i, i + by) for i in range(devices) if 0 <= i + by < devices]
    return lax.ppermute(x, axis, pairs)


def dot_nt(a, b):
    return lax.dot_general(a, b, (((1,), (1,)), ((), ())), preferred_element_type=F32)


def dot(a, b):
    return lax.dot_general(a, b, (((1,), (0,)), ((), ())), preferred_element_type=F32)


def marks_of(skel_row, rank, interp):
    rows, slots = interp.shape
    live = lax.broadcasted_iota(jnp.int32, (1, slots), 1) < rank
    picked_row = jnp.where(live, skel_row, -1).astype(F32).astype(BF)
    row = lax.broadcasted_iota(jnp.int32, (rows, slots), 0).astype(F32).astype(BF)
    live_row = jnp.where(live, F32(1.0), F32(0.0)).astype(BF)
    return row == picked_row, interp * live_row


def kept_cleared(turned):
    most = jnp.max(turned, axis=0, keepdims=True)
    least = jnp.where(most.astype(F32) == 1.0, F32(1.0), F32(-2.0)).astype(BF)
    return jnp.where(turned >= least, turned, BF(0.0))


def marked_of(skel_row, rank, interp):
    hit, live = marks_of(skel_row, rank, interp)
    return jnp.where(hit, BF(1.0), live)


def bases_of(cells, layer, first, rank_ref, skel, interp_ref):
    marked = [
        marked_of(skel[k : k + 1], rank_ref[layer, first + k], interp_ref[0, k])
        for k in range(cells)
    ]
    return [kept_cleared(t) for t in [jnp.transpose(m) for m in marked]]


def scaled(turned, conduct):
    return turned * -conduct


def face_of(left, link, link_t, right):
    upper = jnp.concatenate([left, link], axis=1)
    lower = jnp.concatenate([link_t, right], axis=1)
    return jnp.concatenate([upper, lower], axis=0)


def project(turned, matrices):
    inner = [dot(t, m).astype(BF) for t, m in zip(turned, matrices)]
    return [dot_nt(i, t) for i, t in zip(inner, turned)]


def top_kernel(cells, rank_hbm, skel_hbm, interp_hbm, out_ref, rank_ref, skel_ref, held, small_sems, sems):
    count, half, _ = out_ref.shape
    small = [
        pltpu.make_async_copy(rank_hbm, rank_ref, small_sems.at[0]),
        pltpu.make_async_copy(skel_hbm.at[0], skel_ref, small_sems.at[1]),
    ]
    copies = []
    for c in range(count // cells):
        group = pl.ds(c * cells, cells)
        copies.append(
            pltpu.make_async_copy(
                interp_hbm.at[0, group, pl.ds(0, half)], held.at[group], sems.at[c]
            )
        )
    for copy in small + copies:
        copy.start()
    for copy in small:
        copy.wait()
    for c in range(count // cells):
        copies[c].wait()
        for k in range(c * cells, (c + 1) * cells):
            out_ref[k] = marked_of(skel_ref[k : k + 1], rank_ref[0, k], held[k])


def pack_masks(size):
    half = size // 2
    row = lax.broadcasted_iota(jnp.int32, (half, size), 0)
    lane = lax.broadcasted_iota(jnp.int32, (half, size), 1)
    ahead = lane - row
    upper = (ahead >= 0) & (ahead < half)
    return upper, ahead == 0, ahead == half


def main_kernel(
    cells, layers, chunks,
    rank_ref, skel_ref, interp_ref, matrix_ref,
    x_rank_ref, x_skel_ref, x_interp_ref, x_coup_ref,
    y_rank_ref, y_skel_ref, y_interp_ref, y_coup_ref,
    x_out_ref, y_out_ref, packed_ref, packed_last_ref, edge_ref, corner_ref, last_turned_ref, last_schur_ref,
    store_turned, store_schur, store_extra,
):
    layer = layers - 1 - pl.program_id(0)
    chunk = chunks - 1 - pl.program_id(1)
    first = chunk * cells
    slots = skel_ref.shape[-1]
    half = slots // 2
    top = interp_ref.shape[2] // 2

    turned = bases_of(cells, layer, first, rank_ref, skel_ref[0], interp_ref)
    schurs = project(turned, [matrix_ref[0, k] for k in range(cells)])
    schurs = [s.astype(BF) for s in schurs]

    def faces(out_ref, f_rank_ref, f_skel_ref, f_interp_ref, coup_ref, rights):
        found = bases_of(cells, layer, first, f_rank_ref, f_skel_ref[0], f_interp_ref)
        matrices = []
        for k in range(cells):
            right_turned, right = rights[k]
            conduct = coup_ref[0, k : k + 1]
            lower = turned[k][:, top:]
            link = dot_nt(scaled(lower, conduct), right_turned).astype(BF)
            link_t = dot_nt(scaled(right_turned, conduct), lower).astype(BF)
            matrices.append(face_of(schurs[k], link, link_t, right))
        results = project(found, matrices)
        for k in range(cells):
            out_ref[0, k] = results[k].astype(BF)

    def stored(place):
        return store_turned[place], store_schur[place]

    after = jnp.minimum(first + cells, store_schur.shape[0] - 1)
    rights = [(turned[k][:, :top], schurs[k]) for k in range(1, cells)]
    faces(y_out_ref, y_rank_ref, y_skel_ref, y_interp_ref, y_coup_ref, rights + [stored(after)])

    @pl.when(layer < layers - 1)
    def _():
        rights = [stored(first + k) for k in range(cells)]
        faces(x_out_ref, x_rank_ref, x_skel_ref, x_interp_ref, x_coup_ref, rights)

    for k in range(cells):
        store_turned[first + k] = turned[k][:, :top]
        store_schur[first + k] = schurs[k]

    @pl.when(layer == layers - 1)
    def _():
        for k in range(cells):
            last_turned_ref[first + k] = turned[k][:, top:]
            last_schur_ref[first + k] = schurs[k]

    @pl.when(layer == 0)
    def _():
        upper, same, opposite = pack_masks(slots)

        def put(packed_ref, start):
            for k in range(cells):
                above, below = schurs[k][:half].astype(F32), schurs[k][half:].astype(F32)
                place = pl.ds(pl.multiple_of(start + k * half, half), half)
                packed_ref[place] = jnp.where(upper, above, below).astype(BF)

        @pl.when(chunk < chunks - 1)
        def _():
            put(packed_ref, chunk * (cells * half))

        @pl.when(chunk == chunks - 1)
        def _():
            put(packed_last_ref, 0)

        for p in range(0, cells, 2):
            extra = jnp.where(opposite, schurs[p][:half].astype(F32), F32(0.0))
            if p + 1 < cells:
                extra += jnp.where(same, schurs[p + 1][half:].astype(F32), F32(0.0))
            store_extra[chunk, p // 2 : p // 2 + 1] = jnp.sum(extra, axis=0, keepdims=True)

        @pl.when(chunk == 0)
        def _():
            pairs = -(-cells // 2)
            start = (chunks - 1) * cells * half
            rows = [store_extra[c, :pairs] for c in range(chunks)]
            pad = packed_ref.shape[0] - start - pairs * chunks
            if pad:
                rows.append(jnp.zeros((pad, slots), F32))
            packed_ref[start:] = jnp.concatenate(rows, axis=0).astype(BF)

    @pl.when(chunk == 0)
    def _():
        edge_ref[layer, 0] = turned[0][:, :top]
        edge_ref[layer, 1] = schurs[0]

    @pl.when(chunk == chunks - 1)
    def _():
        corner_ref[layer, 0] = turned[cells - 1][:, top:]
        corner_ref[layer, 1] = schurs[cells - 1]


def y_edge_kernel(layers, place, rank_ref, skel_ref, interp_ref, coup_ref, corner_ref, edge_ref, _, out_ref):
    row = place % skel_ref.shape[1]
    marked = [
        marked_of(skel_ref[i, row : row + 1], rank_ref[i, place], interp_ref[i, 0])
        for i in range(layers)
    ]
    found = [kept_cleared(jnp.transpose(m)) for m in marked]
    matrices = []
    for i in range(layers):
        conduct = coup_ref[i, row : row + 1]
        link = dot_nt(scaled(corner_ref[i, 0], conduct), edge_ref[i, 0]).astype(BF)
        link_t = dot_nt(scaled(edge_ref[i, 0], conduct), corner_ref[i, 0]).astype(BF)
        matrices.append(face_of(corner_ref[i, 1], link, link_t, edge_ref[i, 1]))
    results = project(found, matrices)
    for i in range(layers):
        out_ref[i, 0] = results[i].astype(BF)


def x_part_kernel(
    cells, layer, rank_ref, skel_ref, interp_ref, coup_ref, turned_ref, schur_ref, top_ref,
    part_ref, lower_ref, lower_turned_ref,
):
    count, slots, half = turned_ref.shape
    nothing = jnp.zeros((slots, slots), BF)
    for first in range(0, count, cells):
        group = range(first, first + cells)
        skel = skel_ref[layer, first : first + cells]
        marked = [
            marked_of(skel[k - first : k - first + 1], rank_ref[layer, k], interp_ref[layer, k]) for k in group
        ]
        faces = [kept_cleared(t) for t in [jnp.transpose(m) for m in marked]]
        for k in group:
            lower_turned_ref[k] = faces[k - first][:, half:]
            lower_ref[k] = jnp.transpose(faces[k - first][:, half:])
        tops = [kept_cleared(t) for t in [jnp.transpose(top_ref[k]) for k in group]]
        matrices = []
        for k, top in zip(group, tops):
            conduct = coup_ref[layer, k : k + 1]
            link = dot_nt(scaled(turned_ref[k], conduct), top).astype(BF)
            link_t = dot_nt(scaled(top, conduct), turned_ref[k]).astype(BF)
            matrices.append(face_of(schur_ref[k], link, link_t, nothing))
        for k, result in zip(group, project(faces, matrices)):
            part_ref[k] = result


def unpack_scale(row, lane, half):
    ahead = lane - jnp.where(row < half, row, row - half)
    inside = (ahead >= 0) & (ahead < half)
    one, zero, mid = F32(1.0), F32(0.0), F32(0.5)
    first = jnp.where(ahead == 0, mid, jnp.where(inside, one, zero))
    second = jnp.where(ahead == half, mid, jnp.where(inside, zero, one))
    return jnp.where(row < half, first, second).astype(BF)


def x_last_kernel(
    cells, layer, places, part_ref, lower_ref, lower_turned_ref, extra_ref, packed_ref, _, out_ref, held, sems
):
    slots = part_ref.shape[-1]
    half = slots // 2
    row = lax.broadcasted_iota(jnp.int32, (slots, slots), 0)
    lane = lax.broadcasted_iota(jnp.int32, (slots, slots), 1)
    direct = unpack_scale(row, lane, half)
    mirrored = unpack_scale(lane, row, half)
    apart = jnp.where(jnp.abs(row - lane) == half, F32(1.0), F32(0.0)).astype(BF)
    left = lane < half
    extras = extra_ref[(part_ref.shape[0] // cells - 1) * cells * half :].astype(F32)
    rolled = pltpu.roll(extras, half, 1)
    left_row = lax.broadcasted_iota(jnp.int32, extras.shape, 1) < half
    extra_pair = (
        jnp.where(left_row, rolled, extras).astype(BF).astype(F32),
        jnp.where(left_row, extras, rolled).astype(BF).astype(F32),
    )
    pairs = -(-cells // 2)
    copies = []
    for n, c in enumerate(places):
        group = range(c * cells, (c + 1) * cells)
        schurs = []
        for k in range(0, cells, 2):
            start = (n * cells + k) * half
            if k + 1 < cells:
                stacked = packed_ref[start : start + slots]
            else:
                stacked = jnp.concatenate([packed_ref[start : start + half]] * 2, axis=0)
            turned = jnp.transpose(stacked)
            swapped = jnp.concatenate([turned[:, half:], turned[:, :half]], axis=1)
            wide = (jnp.where(left, turned, swapped), jnp.where(left, swapped, turned))
            for member in range(min(2, cells - k)):
                block = stacked[member * half : (member + 1) * half]
                double = jnp.concatenate([block, block], axis=0)
                extra = extra_pair[member][c * pairs + k // 2 : c * pairs + k // 2 + 1].astype(BF)
                schurs.append(double * direct + wide[member] * mirrored + extra * apart)
        inner = [dot(lower_turned_ref[k], h).astype(BF) for k, h in zip(group, schurs)]
        results = [dot(i, lower_ref[k]) for k, i in zip(group, inner)]
        part_cells = max(1, cells // 2)
        for start in range(0, cells, part_cells):
            for k in range(start, start + part_cells):
                held[n * cells + k] = (part_ref[c * cells + k] + results[k]).astype(BF)
            copy = pltpu.make_async_copy(
                held.at[pl.ds(n * cells + start, part_cells)],
                out_ref.at[layer, pl.ds(c * cells + start, part_cells)],
                sems.at[n, start // part_cells],
            )
            copy.start()
            copies.append(copy)
    for copy in copies:
        copy.wait()


def call(kernel, grid, in_specs, out_specs, out_shape, flops, moved, aliases=None, vmem=24, scratch=()):
    return pl.pallas_call(
        kernel,
        grid=grid,
        in_specs=in_specs,
        out_specs=out_specs,
        out_shape=out_shape,
        scratch_shapes=scratch,
        input_output_aliases=aliases or {},
        compiler_params=pltpu.CompilerParams(vmem_limit_bytes=vmem * MIB),
        cost_estimate=pl.CostEstimate(flops=flops, bytes_accessed=moved, transcendentals=0),
    )


def in_hbm(x):
    return pltpu.with_memory_space_constraint(x, pltpu.HBM)


def body(
    cell_matrix,
    x_coupling,
    y_coupling,
    cell_interp,
    cell_skel,
    cell_rank,
    x_face_interp,
    x_face_skel,
    x_face_rank,
    y_face_interp,
    y_face_skel,
    y_face_rank,
):
    nx, nj, rows, slots = cell_interp.shape
    half = rows // 2
    fslots = x_face_interp.shape[-1]
    cells = next(n for n in (8, 4, 2, 1) if nj % n == 0 and nj > n)
    chunks = nj // cells
    unit = 2 * nx * nj * slots * slots * slots
    smem = pl.BlockSpec(memory_space=pltpu.SMEM)
    shape = jax.ShapeDtypeStruct

    hbm = pl.BlockSpec(memory_space=pltpu.HBM)
    vmem = pl.BlockSpec(memory_space=pltpu.VMEM)
    top = call(
        functools.partial(top_kernel, cells),
        (),
        [hbm, hbm, hbm],
        vmem,
        shape((nj, half, slots), BF),
        0,
        4 * nj * half * slots,
        vmem=8,
        scratch=[
            pltpu.SMEM((nx, nj), jnp.int32),
            pltpu.VMEM((nj, slots), jnp.int32),
            pltpu.VMEM((nj, half, slots), BF),
            pltpu.SemaphoreType.DMA((2,)),
            pltpu.SemaphoreType.DMA((chunks,)),
        ],
    )(in_hbm(cell_rank), in_hbm(cell_skel), in_hbm(cell_interp))
    top_in = passed_along(top, "gx", -1)


    late_rows = cells * slots // 2
    early_rows = (chunks - 1) * late_rows + -(-chunks * -(-cells // 2) // 16) * 16

    near = max(nx - 2, 0)

    def down(*dims):
        zeros = (0,) * len(dims)
        return pl.BlockSpec((1, cells) + dims, lambda i, c: (nx - 1 - i, chunks - 1 - c) + zeros)

    def down_x(*dims):
        zeros = (0,) * len(dims)

        def place(i, c):
            return (jnp.minimum(nx - 1 - i, near), jnp.where(i == 0, chunks - 1, chunks - 1 - c)) + zeros

        return pl.BlockSpec((1, cells) + dims, place)

    x_out, y_out, packed, packed_last, edge, corner, last_turned, last_schur = call(
        functools.partial(main_kernel, cells, nx, chunks),
        (nx, chunks),
        [
            smem, down(slots), down(rows, slots), down(rows, rows),
            smem, down_x(fslots), down_x(rows, fslots), down_x(half),
            smem, down(fslots), down(rows, fslots), down(half),
        ],
        [
            down_x(fslots, fslots),
            down(fslots, fslots),
            vmem, vmem, vmem, vmem, vmem, vmem,
        ],
        [
            shape((nx, nj, fslots, fslots), BF),
            shape((nx, nj, fslots, fslots), BF),
            shape((early_rows, slots), BF),
            shape((late_rows, slots), BF),
            shape((nx, 2, slots, half), BF),
            shape((nx, 2, slots, half), BF),
            shape((nj, slots, half), BF),
            shape((nj, slots, slots), BF),
        ],
        20 * unit,
        nx * nj * (rows * rows + 3 * rows * slots + 3 * slots * slots) * 2,
        vmem=32,
        scratch=[
            pltpu.VMEM((nj, slots, half), BF),
            pltpu.VMEM((nj, slots, slots), BF),
            pltpu.VMEM((chunks, cells, slots), F32),
        ],
    )(
        cell_rank, in_hbm(cell_skel), in_hbm(cell_interp), in_hbm(cell_matrix),
        x_face_rank, in_hbm(x_face_skel), in_hbm(x_face_interp), in_hbm(x_coupling),
        y_face_rank, in_hbm(y_face_skel), in_hbm(y_face_interp), in_hbm(y_coupling),
    )
    edge_in = passed_along(edge, "yz", -1)
    packed_in = passed_along(packed, "gx", -1)
    packed_last_in = passed_along(packed_last, "gx", -1)
    face_bytes = nj * (4 * rows * slots + 4 * slots * slots) * 2

    last = nx - 1
    tail = nj - 1
    group = tail // cells

    part, lower, lower_turned = call(
        functools.partial(x_part_kernel, cells, last),
        (),
        [smem, vmem, vmem, vmem, vmem, vmem, vmem],
        [vmem, vmem, vmem],
        [
            shape((nj, fslots, fslots), F32),
            shape((nj, slots, fslots), BF),
            shape((nj, fslots, slots), BF),
        ],
        8 * unit // nx,
        face_bytes,
        vmem=16,
    )(x_face_rank, x_face_skel, x_face_interp, x_coupling, last_turned, last_schur, top_in)

    edge_in, part = lax.optimization_barrier((edge_in, part))
    y_out = call(
        functools.partial(y_edge_kernel, nx, tail),
        (1,),
        [
            smem,
            pl.BlockSpec((nx, cells, fslots), lambda i: (0, group, 0)),
            pl.BlockSpec((nx, 1, rows, fslots), lambda i: (0, tail, 0, 0)),
            pl.BlockSpec((nx, cells, half), lambda i: (0, group, 0)),
            pl.BlockSpec((nx, 2, slots, half), lambda i: (0, 0, 0, 0)),
            pl.BlockSpec((nx, 2, slots, half), lambda i: (0, 0, 0, 0)),
            pl.BlockSpec(memory_space=pl.ANY),
        ],
        pl.BlockSpec((nx, 1, fslots, fslots), lambda i: (0, tail, 0, 0)),
        shape((nx, nj, fslots, fslots), BF),
        8 * unit // nj,
        nx * face_bytes // nj,
        {6: 0},
    )(y_face_rank, y_face_skel, in_hbm(y_face_interp), y_coupling, corner, edge_in, y_out)

    for places, arrived in (
        (range(chunks - 1), packed_in),
        (range(chunks - 1, chunks), packed_last_in),
    ):
        count = len(places)
        x_out = call(
            functools.partial(x_last_kernel, cells, last, places),
            (),
            [vmem, vmem, vmem, vmem, vmem, hbm],
            hbm,
            shape((nx, nj, fslots, fslots), BF),
            3 * unit // nx * count // chunks,
            nj * slots * slots * 11 * count // chunks,
            {5: 0},
            scratch=[
                pltpu.VMEM((count * cells, fslots, fslots), BF),
                pltpu.SemaphoreType.DMA((count, 2)),
            ],
        )(part, lower, lower_turned, packed_in, arrived, x_out)
    return (x_out, y_out)


def solution(mesh):
    return jax.shard_map(
        body,
        mesh=mesh,
        in_specs=(
            P("gx", "yz", None, None),
            P("gx", "yz", None),
            P("gx", "yz", None),
            P("gx", "yz", None, None),
            P("gx", "yz", None),
            P("gx", "yz"),
            P("gx", "yz", None, None),
            P("gx", "yz", None),
            P("gx", "yz"),
            P("gx", "yz", None, None),
            P("gx", "yz", None),
            P("gx", "yz"),
        ),
        out_specs=(P("gx", "yz", None, None), P("gx", "yz", None, None)),
        check_vma=False,
    )
```

```python
import functools

import jax
import jax.numpy as jnp
from jax import lax
from jax.experimental import pallas as pl
from jax.experimental.pallas import tpu as pltpu
from jax.sharding import PartitionSpec as P

BF = jnp.bfloat16
F32 = jnp.float32
MIB = 1024 * 1024


def passed_along(x, axis, by):
    devices = lax.axis_size(axis)
    pairs = [(i, i + by) for i in range(devices) if 0 <= i + by < devices]
    return lax.ppermute(x, axis, pairs)


def dot_nt(a, b):
    return lax.dot_general(a, b, (((1,), (1,)), ((), ())), preferred_element_type=F32)


def dot(a, b):
    return lax.dot_general(a, b, (((1,), (0,)), ((), ())), preferred_element_type=F32)


def marks_of(skel_row, rank, interp):
    rows, slots = interp.shape
    live = lax.broadcasted_iota(jnp.int32, (1, slots), 1) < rank
    picked_row = jnp.where(live, skel_row, -1).astype(F32).astype(BF)
    row = lax.broadcasted_iota(jnp.int32, (rows, slots), 0).astype(F32).astype(BF)
    live_row = jnp.where(live, F32(1.0), F32(0.0)).astype(BF)
    return row == picked_row, interp * live_row


def kept_cleared(turned):
    most = jnp.max(turned, axis=0, keepdims=True)
    least = jnp.where(most.astype(F32) == 1.0, F32(1.0), F32(-2.0)).astype(BF)
    return jnp.where(turned >= least, turned, BF(0.0))


def marked_of(skel_row, rank, interp):
    hit, live = marks_of(skel_row, rank, interp)
    return jnp.where(hit, BF(1.0), live)


def bases_of(cells, layer, first, rank_ref, skel, interp_ref):
    marked = [
        marked_of(skel[k : k + 1], rank_ref[layer, first + k], interp_ref[0, k])
        for k in range(cells)
    ]
    return [kept_cleared(t) for t in [jnp.transpose(m) for m in marked]]


def scaled(turned, conduct):
    return turned * -conduct


def face_of(left, link, link_t, right):
    upper = jnp.concatenate([left, link], axis=1)
    lower = jnp.concatenate([link_t, right], axis=1)
    return jnp.concatenate([upper, lower], axis=0)


def project(turned, matrices):
    inner = [dot(t, m).astype(BF) for t, m in zip(turned, matrices)]
    return [dot_nt(i, t) for i, t in zip(inner, turned)]


def top_kernel(rank_hbm, skel_hbm, interp_hbm, out_ref, rank_ref, skel_ref, held, small_sems, sems):
    count, half, _ = out_ref.shape
    small = [
        pltpu.make_async_copy(rank_hbm, rank_ref, small_sems.at[0]),
        pltpu.make_async_copy(skel_hbm.at[0], skel_ref, small_sems.at[1]),
    ]
    bounds = [0, count // 2, count // 4 * 3, count // 8 * 7, count]
    groups = [(begin, end) for begin, end in zip(bounds, bounds[1:]) if begin < end]
    copies = []
    for n, (begin, end) in enumerate(groups):
        group = pl.ds(begin, end - begin)
        copies.append(
            pltpu.make_async_copy(
                interp_hbm.at[0, group, pl.ds(0, half)], held.at[group], sems.at[n]
            )
        )
    for copy in copies + small:
        copy.start()
    for copy in small:
        copy.wait()
    for copy, (begin, end) in zip(copies, groups):
        copy.wait()
        for k in range(begin, end):
            out_ref[k] = marked_of(skel_ref[k : k + 1], rank_ref[0, k], held[k])


def pack_masks(size):
    half = size // 2
    row = lax.broadcasted_iota(jnp.int32, (half, size), 0)
    lane = lax.broadcasted_iota(jnp.int32, (half, size), 1)
    ahead = lane - row
    upper = (ahead >= 0) & (ahead < half)
    return upper, ahead == 0, ahead == half


def main_kernel(
    cells, layers, chunks,
    rank_ref, skel_ref, interp_ref, matrix_ref,
    x_rank_ref, x_skel_ref, x_interp_ref, x_coup_ref,
    y_rank_ref, y_skel_ref, y_interp_ref, y_coup_ref,
    x_out_ref, y_out_ref, packed_ref, packed_last_ref, edge_ref, corner_ref, last_turned_ref, last_schur_ref,
    store_turned, store_schur, store_extra,
):
    layer = layers - 1 - pl.program_id(0)
    chunk = chunks - 1 - pl.program_id(1)
    first = chunk * cells
    slots = skel_ref.shape[-1]
    half = slots // 2
    top = interp_ref.shape[2] // 2

    turned = bases_of(cells, layer, first, rank_ref, skel_ref[0], interp_ref)
    schurs = project(turned, [matrix_ref[0, k] for k in range(cells)])
    schurs = [s.astype(BF) for s in schurs]

    def faces(out_ref, f_rank_ref, f_skel_ref, f_interp_ref, coup_ref, rights):
        found = bases_of(cells, layer, first, f_rank_ref, f_skel_ref[0], f_interp_ref)
        matrices = []
        for k in range(cells):
            right_turned, right = rights[k]
            conduct = coup_ref[0, k : k + 1]
            lower = turned[k][:, top:]
            link = dot_nt(scaled(lower, conduct), right_turned).astype(BF)
            link_t = dot_nt(scaled(right_turned, conduct), lower).astype(BF)
            matrices.append(face_of(schurs[k], link, link_t, right))
        results = project(found, matrices)
        for k in range(cells):
            out_ref[0, k] = results[k].astype(BF)

    def stored(place):
        return store_turned[place], store_schur[place]

    after = jnp.minimum(first + cells, store_schur.shape[0] - 1)
    rights = [(turned[k][:, :top], schurs[k]) for k in range(1, cells)]
    faces(y_out_ref, y_rank_ref, y_skel_ref, y_interp_ref, y_coup_ref, rights + [stored(after)])

    @pl.when(layer < layers - 1)
    def _():
        rights = [stored(first + k) for k in range(cells)]
        faces(x_out_ref, x_rank_ref, x_skel_ref, x_interp_ref, x_coup_ref, rights)

    for k in range(cells):
        store_turned[first + k] = turned[k][:, :top]
        store_schur[first + k] = schurs[k]

    @pl.when(layer == layers - 1)
    def _():
        for k in range(cells):
            last_turned_ref[first + k] = turned[k][:, top:]
            last_schur_ref[first + k] = schurs[k]

    @pl.when(layer == 0)
    def _():
        upper, same, opposite = pack_masks(slots)

        def put(packed_ref, start):
            for k in range(cells):
                above, below = schurs[k][:half].astype(F32), schurs[k][half:].astype(F32)
                place = pl.ds(pl.multiple_of(start + k * half, half), half)
                packed_ref[place] = jnp.where(upper, above, below).astype(BF)

        @pl.when(chunk < chunks - 1)
        def _():
            put(packed_ref, chunk * (cells * half))

        @pl.when(chunk == chunks - 1)
        def _():
            put(packed_last_ref, 0)

        for p in range(0, cells, 2):
            extra = jnp.where(opposite, schurs[p][:half].astype(F32), F32(0.0))
            if p + 1 < cells:
                extra += jnp.where(same, schurs[p + 1][half:].astype(F32), F32(0.0))
            store_extra[chunk, p // 2 : p // 2 + 1] = jnp.sum(extra, axis=0, keepdims=True)

        @pl.when(chunk == 0)
        def _():
            pairs = -(-cells // 2)
            start = (chunks - 1) * cells * half
            rows = [store_extra[c, :pairs] for c in range(chunks)]
            pad = packed_ref.shape[0] - start - pairs * chunks
            if pad:
                rows.append(jnp.zeros((pad, slots), F32))
            packed_ref[start:] = jnp.concatenate(rows, axis=0).astype(BF)

    @pl.when(chunk == 0)
    def _():
        edge_ref[layer, 0] = turned[0][:, :top]
        edge_ref[layer, 1] = schurs[0]

    @pl.when(chunk == chunks - 1)
    def _():
        corner_ref[layer, 0] = turned[cells - 1][:, top:]
        corner_ref[layer, 1] = schurs[cells - 1]


def y_edge_kernel(layers, place, rank_ref, skel_ref, interp_ref, coup_ref, corner_ref, edge_ref, _, out_ref):
    row = place % skel_ref.shape[1]
    marked = [
        marked_of(skel_ref[i, row : row + 1], rank_ref[i, place], interp_ref[i, 0])
        for i in range(layers)
    ]
    found = [kept_cleared(jnp.transpose(m)) for m in marked]
    matrices = []
    for i in range(layers):
        conduct = coup_ref[i, row : row + 1]
        link = dot_nt(scaled(corner_ref[i, 0], conduct), edge_ref[i, 0]).astype(BF)
        link_t = dot_nt(scaled(edge_ref[i, 0], conduct), corner_ref[i, 0]).astype(BF)
        matrices.append(face_of(corner_ref[i, 1], link, link_t, edge_ref[i, 1]))
    results = project(found, matrices)
    for i in range(layers):
        out_ref[i, 0] = results[i].astype(BF)


def x_part_kernel(
    cells, layer, rank_ref, skel_ref, interp_ref, coup_ref, turned_ref, schur_ref, top_ref,
    part_ref, lower_ref, lower_turned_ref,
):
    count, slots, half = turned_ref.shape
    nothing = jnp.zeros((slots, slots), BF)
    for first in range(0, count, cells):
        group = range(first, first + cells)
        skel = skel_ref[layer, first : first + cells]
        marked = [
            marked_of(skel[k - first : k - first + 1], rank_ref[layer, k], interp_ref[layer, k]) for k in group
        ]
        faces = [kept_cleared(t) for t in [jnp.transpose(m) for m in marked]]
        for k in group:
            lower_turned_ref[k] = faces[k - first][:, half:]
            lower_ref[k] = jnp.transpose(faces[k - first][:, half:])
        tops = [kept_cleared(t) for t in [jnp.transpose(top_ref[k]) for k in group]]
        matrices = []
        for k, top in zip(group, tops):
            conduct = coup_ref[layer, k : k + 1]
            link = dot_nt(scaled(turned_ref[k], conduct), top).astype(BF)
            link_t = dot_nt(scaled(top, conduct), turned_ref[k]).astype(BF)
            matrices.append(face_of(schur_ref[k], link, link_t, nothing))
        for k, result in zip(group, project(faces, matrices)):
            part_ref[k] = result


def x_last_kernel(
    cells, layer, places, part_ref, lower_ref, lower_turned_ref, extra_ref, packed_ref, _, out_ref, held, sems
):
    slots = part_ref.shape[-1]
    half = slots // 2
    upper, same, opposite = pack_masks(slots)
    one, zero, mid = F32(1.0), F32(0.0), F32(0.5)
    top_scale = jnp.where(same, mid, jnp.where(upper, one, zero))
    low_scale = jnp.where(opposite, mid, jnp.where(upper, zero, one))
    same_scale = jnp.where(same, one, zero)
    opposite_scale = jnp.where(opposite, one, zero)
    extras = extra_ref[(part_ref.shape[0] // cells - 1) * cells * half :].astype(F32)
    pairs = -(-cells // 2)
    copies = []
    for n, c in enumerate(places):
        group = range(c * cells, (c + 1) * cells)
        schurs = []
        for k in range(cells):
            start = (n * cells + k) * half
            packed = packed_ref[start : start + half].astype(F32)
            extra = extras[c * pairs + k // 2 : c * pairs + k // 2 + 1]
            top, low = packed * top_scale, packed * low_scale
            if k % 2 == 0:
                top += extra * opposite_scale
            else:
                low += extra * same_scale
            tri = jnp.concatenate([top, low], axis=0).astype(BF)
            schurs.append(tri + jnp.transpose(tri))
        inner = [dot(lower_turned_ref[k], h).astype(BF) for k, h in zip(group, schurs)]
        results = [dot(i, lower_ref[k]) for k, i in zip(group, inner)]
        part_cells = max(1, cells // 2)
        for start in range(0, cells, part_cells):
            for k in range(start, start + part_cells):
                held[n * cells + k] = (part_ref[c * cells + k] + results[k]).astype(BF)
            copy = pltpu.make_async_copy(
                held.at[pl.ds(n * cells + start, part_cells)],
                out_ref.at[layer, pl.ds(c * cells + start, part_cells)],
                sems.at[n, start // part_cells],
            )
            copy.start()
            copies.append(copy)
    for copy in copies:
        copy.wait()


def call(kernel, grid, in_specs, out_specs, out_shape, flops, moved, aliases=None, vmem=24, scratch=()):
    return pl.pallas_call(
        kernel,
        grid=grid,
        in_specs=in_specs,
        out_specs=out_specs,
        out_shape=out_shape,
        scratch_shapes=scratch,
        input_output_aliases=aliases or {},
        compiler_params=pltpu.CompilerParams(vmem_limit_bytes=vmem * MIB),
        cost_estimate=pl.CostEstimate(flops=flops, bytes_accessed=moved, transcendentals=0),
    )


def in_hbm(x):
    return pltpu.with_memory_space_constraint(x, pltpu.HBM)


def body(
    cell_matrix,
    x_coupling,
    y_coupling,
    cell_interp,
    cell_skel,
    cell_rank,
    x_face_interp,
    x_face_skel,
    x_face_rank,
    y_face_interp,
    y_face_skel,
    y_face_rank,
):
    nx, nj, rows, slots = cell_interp.shape
    half = rows // 2
    fslots = x_face_interp.shape[-1]
    cells = next(n for n in (8, 4, 2, 1) if nj % n == 0 and nj > n)
    chunks = nj // cells
    unit = 2 * nx * nj * slots * slots * slots
    smem = pl.BlockSpec(memory_space=pltpu.SMEM)
    shape = jax.ShapeDtypeStruct

    hbm = pl.BlockSpec(memory_space=pltpu.HBM)
    vmem = pl.BlockSpec(memory_space=pltpu.VMEM)
    top = call(
        top_kernel,
        (),
        [hbm, hbm, hbm],
        vmem,
        shape((nj, half, slots), BF),
        0,
        4 * nj * half * slots,
        vmem=8,
        scratch=[
            pltpu.SMEM((nx, nj), jnp.int32),
            pltpu.VMEM((nj, slots), jnp.int32),
            pltpu.VMEM((nj, half, slots), BF),
            pltpu.SemaphoreType.DMA((2,)),
            pltpu.SemaphoreType.DMA((4,)),
        ],
    )(in_hbm(cell_rank), in_hbm(cell_skel), in_hbm(cell_interp))
    top_in = passed_along(top, "gx", -1)


    late_rows = cells * slots // 2
    early_rows = (chunks - 1) * late_rows + -(-chunks * -(-cells // 2) // 16) * 16

    near = max(nx - 2, 0)

    def down(*dims):
        zeros = (0,) * len(dims)
        return pl.BlockSpec((1, cells) + dims, lambda i, c: (nx - 1 - i, chunks - 1 - c) + zeros)

    def down_x(*dims):
        zeros = (0,) * len(dims)

        def place(i, c):
            return (jnp.minimum(nx - 1 - i, near), jnp.where(i == 0, chunks - 1, chunks - 1 - c)) + zeros

        return pl.BlockSpec((1, cells) + dims, place)

    x_out, y_out, packed, packed_last, edge, corner, last_turned, last_schur = call(
        functools.partial(main_kernel, cells, nx, chunks),
        (nx, chunks),
        [
            smem, down(slots), down(rows, slots), down(rows, rows),
            smem, down_x(fslots), down_x(rows, fslots), down_x(half),
            smem, down(fslots), down(rows, fslots), down(half),
        ],
        [
            down_x(fslots, fslots),
            down(fslots, fslots),
            vmem, vmem, vmem, vmem, vmem, vmem,
        ],
        [
            shape((nx, nj, fslots, fslots), BF),
            shape((nx, nj, fslots, fslots), BF),
            shape((early_rows, slots), BF),
            shape((late_rows, slots), BF),
            shape((nx, 2, slots, half), BF),
            shape((nx, 2, slots, half), BF),
            shape((nj, slots, half), BF),
            shape((nj, slots, slots), BF),
        ],
        20 * unit,
        nx * nj * (rows * rows + 3 * rows * slots + 3 * slots * slots) * 2,
        vmem=32,
        scratch=[
            pltpu.VMEM((nj, slots, half), BF),
            pltpu.VMEM((nj, slots, slots), BF),
            pltpu.VMEM((chunks, cells, slots), F32),
        ],
    )(
        cell_rank, in_hbm(cell_skel), in_hbm(cell_interp), in_hbm(cell_matrix),
        x_face_rank, in_hbm(x_face_skel), in_hbm(x_face_interp), in_hbm(x_coupling),
        y_face_rank, in_hbm(y_face_skel), in_hbm(y_face_interp), in_hbm(y_coupling),
    )
    edge_in = passed_along(edge, "yz", -1)
    packed_in = passed_along(packed, "gx", -1)
    packed_last_in = passed_along(packed_last, "gx", -1)
    face_bytes = nj * (4 * rows * slots + 4 * slots * slots) * 2

    last = nx - 1
    tail = nj - 1
    group = tail // cells

    part, lower, lower_turned = call(
        functools.partial(x_part_kernel, cells, last),
        (),
        [smem, vmem, vmem, vmem, vmem, vmem, vmem],
        [vmem, vmem, vmem],
        [
            shape((nj, fslots, fslots), F32),
            shape((nj, slots, fslots), BF),
            shape((nj, fslots, slots), BF),
        ],
        8 * unit // nx,
        face_bytes,
        vmem=16,
    )(x_face_rank, x_face_skel, x_face_interp, x_coupling, last_turned, last_schur, top_in)

    edge_in, part = lax.optimization_barrier((edge_in, part))
    y_out = call(
        functools.partial(y_edge_kernel, nx, tail),
        (1,),
        [
            smem,
            pl.BlockSpec((nx, cells, fslots), lambda i: (0, group, 0)),
            pl.BlockSpec((nx, 1, rows, fslots), lambda i: (0, tail, 0, 0)),
            pl.BlockSpec((nx, cells, half), lambda i: (0, group, 0)),
            pl.BlockSpec((nx, 2, slots, half), lambda i: (0, 0, 0, 0)),
            pl.BlockSpec((nx, 2, slots, half), lambda i: (0, 0, 0, 0)),
            pl.BlockSpec(memory_space=pl.ANY),
        ],
        pl.BlockSpec((nx, 1, fslots, fslots), lambda i: (0, tail, 0, 0)),
        shape((nx, nj, fslots, fslots), BF),
        8 * unit // nj,
        nx * face_bytes // nj,
        {6: 0},
    )(y_face_rank, y_face_skel, in_hbm(y_face_interp), y_coupling, corner, edge_in, y_out)

    for places, arrived in (
        (range(chunks - 1), packed_in),
        (range(chunks - 1, chunks), packed_last_in),
    ):
        count = len(places)
        x_out = call(
            functools.partial(x_last_kernel, cells, last, places),
            (),
            [vmem, vmem, vmem, vmem, vmem, hbm],
            hbm,
            shape((nx, nj, fslots, fslots), BF),
            3 * unit // nx * count // chunks,
            nj * slots * slots * 11 * count // chunks,
            {5: 0},
            scratch=[
                pltpu.VMEM((count * cells, fslots, fslots), BF),
                pltpu.SemaphoreType.DMA((count, 2)),
            ],
        )(part, lower, lower_turned, packed_in, arrived, x_out)
    return (x_out, y_out)


def solution(mesh):
    return jax.shard_map(
        body,
        mesh=mesh,
        in_specs=(
            P("gx", "yz", None, None),
            P("gx", "yz", None),
            P("gx", "yz", None),
            P("gx", "yz", None, None),
            P("gx", "yz", None),
            P("gx", "yz"),
            P("gx", "yz", None, None),
            P("gx", "yz", None),
            P("gx", "yz"),
            P("gx", "yz", None, None),
            P("gx", "yz", None),
            P("gx", "yz"),
        ),
        out_specs=(P("gx", "yz", None, None), P("gx", "yz", None, None)),
        check_vma=False,
    )
```

```python
import functools

import jax
import jax.numpy as jnp
from jax import lax
from jax.experimental import pallas as pl
from jax.experimental.pallas import tpu as pltpu
from jax.sharding import PartitionSpec as P

BF = jnp.bfloat16
F32 = jnp.float32
MIB = 1024 * 1024


def passed_along(x, axis, by):
    devices = lax.axis_size(axis)
    pairs = [(i, i + by) for i in range(devices) if 0 <= i + by < devices]
    return lax.ppermute(x, axis, pairs)


def passed_round(x, axis):
    devices = lax.axis_size(axis)
    return lax.ppermute(x, axis, [(i, (i - 1) % devices) for i in range(devices)])


def dot_nt(a, b):
    return lax.dot_general(a, b, (((1,), (1,)), ((), ())), preferred_element_type=F32)


def dot(a, b):
    return lax.dot_general(a, b, (((1,), (0,)), ((), ())), preferred_element_type=F32)


def marks_of(skel_row, rank, interp):
    rows, slots = interp.shape
    live = lax.broadcasted_iota(jnp.int32, (1, slots), 1) < rank
    picked_row = jnp.where(live, skel_row, -1).astype(F32).astype(BF)
    row = lax.broadcasted_iota(jnp.int32, (rows, slots), 0).astype(F32).astype(BF)
    live_row = jnp.where(live, F32(1.0), F32(0.0)).astype(BF)
    return row == picked_row, interp * live_row


def kept_cleared(turned):
    most = jnp.max(turned, axis=0, keepdims=True)
    least = jnp.where(most.astype(F32) == 1.0, F32(1.0), F32(-2.0)).astype(BF)
    return jnp.where(turned >= least, turned, BF(0.0))


def marked_of(skel_row, rank, interp):
    hit, live = marks_of(skel_row, rank, interp)
    return jnp.where(hit, BF(1.0), live)


def bases_of(cells, layer, first, rank_ref, skel, interp_ref):
    marked = [
        marked_of(skel[k : k + 1], rank_ref[layer, first + k], interp_ref[0, k])
        for k in range(cells)
    ]
    return [kept_cleared(t) for t in [jnp.transpose(m) for m in marked]]


def scaled(turned, conduct):
    return turned * -conduct


def face_of(left, link, link_t, right):
    upper = jnp.concatenate([left, link], axis=1)
    lower = jnp.concatenate([link_t, right], axis=1)
    return jnp.concatenate([upper, lower], axis=0)


def project(turned, matrices):
    inner = [dot(t, m).astype(BF) for t, m in zip(turned, matrices)]
    return [dot_nt(i, t) for i, t in zip(inner, turned)]


def top_kernel(cells, rank_hbm, skel_hbm, interp_hbm, out_ref, rank_ref, skel_ref, held, small_sems, sems):
    count, half, _ = out_ref.shape
    small = [
        pltpu.make_async_copy(rank_hbm, rank_ref, small_sems.at[0]),
        pltpu.make_async_copy(skel_hbm.at[0], skel_ref, small_sems.at[1]),
    ]
    copies = []
    for c in range(count // cells):
        group = pl.ds(c * cells, cells)
        copies.append(
            pltpu.make_async_copy(
                interp_hbm.at[0, group, pl.ds(0, half)], held.at[group], sems.at[c]
            )
        )
    for copy in small + copies:
        copy.start()
    for copy in small:
        copy.wait()
    for c in range(count // cells):
        copies[c].wait()
        for k in range(c * cells, (c + 1) * cells):
            out_ref[k] = marked_of(skel_ref[k : k + 1], rank_ref[0, k], held[k])


def pack_masks(size):
    half = size // 2
    row = lax.broadcasted_iota(jnp.int32, (half, size), 0)
    lane = lax.broadcasted_iota(jnp.int32, (half, size), 1)
    ahead = lane - row
    upper = (ahead >= 0) & (ahead < half)
    return upper, ahead == 0, ahead == half


def main_kernel(
    cells, layers, chunks,
    rank_ref, skel_ref, interp_ref, matrix_ref,
    x_rank_ref, x_skel_ref, x_interp_ref, x_coup_ref,
    y_rank_ref, y_skel_ref, y_interp_ref, y_coup_ref,
    x_out_ref, y_out_ref, packed_ref, packed_last_ref, edge_ref, corner_ref, last_turned_ref, last_schur_ref,
    store_turned, store_schur, store_extra,
):
    layer = layers - 1 - pl.program_id(0)
    chunk = chunks - 1 - pl.program_id(1)
    first = chunk * cells
    slots = skel_ref.shape[-1]
    half = slots // 2
    top = interp_ref.shape[2] // 2

    turned = bases_of(cells, layer, first, rank_ref, skel_ref[0], interp_ref)
    schurs = project(turned, [matrix_ref[0, k] for k in range(cells)])
    schurs = [s.astype(BF) for s in schurs]

    def faces(out_ref, f_rank_ref, f_skel_ref, f_interp_ref, coup_ref, rights):
        found = bases_of(cells, layer, first, f_rank_ref, f_skel_ref[0], f_interp_ref)
        matrices = []
        for k in range(cells):
            right_turned, right = rights[k]
            conduct = coup_ref[0, k : k + 1]
            lower = turned[k][:, top:]
            link = dot_nt(scaled(lower, conduct), right_turned).astype(BF)
            link_t = dot_nt(scaled(right_turned, conduct), lower).astype(BF)
            matrices.append(face_of(schurs[k], link, link_t, right))
        results = project(found, matrices)
        for k in range(cells):
            out_ref[0, k] = results[k].astype(BF)

    def stored(place):
        return store_turned[place], store_schur[place]

    after = jnp.minimum(first + cells, store_schur.shape[0] - 1)
    rights = [(turned[k][:, :top], schurs[k]) for k in range(1, cells)]
    faces(y_out_ref, y_rank_ref, y_skel_ref, y_interp_ref, y_coup_ref, rights + [stored(after)])

    @pl.when(layer < layers - 1)
    def _():
        rights = [stored(first + k) for k in range(cells)]
        faces(x_out_ref, x_rank_ref, x_skel_ref, x_interp_ref, x_coup_ref, rights)

    for k in range(cells):
        store_turned[first + k] = turned[k][:, :top]
        store_schur[first + k] = schurs[k]

    @pl.when(layer == layers - 1)
    def _():
        for k in range(cells):
            last_turned_ref[first + k] = turned[k][:, top:]
            last_schur_ref[first + k] = schurs[k]

    @pl.when(layer == 0)
    def _():
        upper, same, opposite = pack_masks(slots)

        def put(packed_ref, start):
            for k in range(cells):
                above, below = schurs[k][:half].astype(F32), schurs[k][half:].astype(F32)
                place = pl.ds(pl.multiple_of(start + k * half, half), half)
                packed_ref[place] = jnp.where(upper, above, below).astype(BF)

        @pl.when(chunk < chunks - 1)
        def _():
            put(packed_ref, chunk * (cells * half))

        @pl.when(chunk == chunks - 1)
        def _():
            put(packed_last_ref, 0)

        for p in range(0, cells, 2):
            extra = jnp.where(opposite, schurs[p][:half].astype(F32), F32(0.0))
            if p + 1 < cells:
                extra += jnp.where(same, schurs[p + 1][half:].astype(F32), F32(0.0))
            store_extra[chunk, p // 2 : p // 2 + 1] = jnp.sum(extra, axis=0, keepdims=True)

        @pl.when(chunk == 0)
        def _():
            pairs = -(-cells // 2)
            start = (chunks - 1) * cells * half
            rows = [store_extra[c, :pairs] for c in range(chunks)]
            pad = packed_ref.shape[0] - start - pairs * chunks
            if pad:
                rows.append(jnp.zeros((pad, slots), F32))
            packed_ref[start:] = jnp.concatenate(rows, axis=0).astype(BF)

    @pl.when(chunk == 0)
    def _():
        edge_ref[layer, 0] = turned[0][:, :top]
        edge_ref[layer, 1] = schurs[0]

    @pl.when(chunk == chunks - 1)
    def _():
        corner_ref[layer, 0] = turned[cells - 1][:, top:]
        corner_ref[layer, 1] = schurs[cells - 1]


def y_edge_kernel(layers, place, rank_ref, skel_ref, interp_ref, coup_ref, corner_ref, edge_ref, _, out_ref):
    row = place % skel_ref.shape[1]
    marked = [
        marked_of(skel_ref[i, row : row + 1], rank_ref[i, place], interp_ref[i, 0])
        for i in range(layers)
    ]
    found = [kept_cleared(jnp.transpose(m)) for m in marked]
    matrices = []
    for i in range(layers):
        conduct = coup_ref[i, row : row + 1]
        link = dot_nt(scaled(corner_ref[i, 0], conduct), edge_ref[i, 0]).astype(BF)
        link_t = dot_nt(scaled(edge_ref[i, 0], conduct), corner_ref[i, 0]).astype(BF)
        matrices.append(face_of(corner_ref[i, 1], link, link_t, edge_ref[i, 1]))
    results = project(found, matrices)
    for i in range(layers):
        out_ref[i, 0] = results[i].astype(BF)


def x_part_kernel(
    cells, layer, inner_ref, rank_ref, skel_ref, interp_ref, coup_ref, turned_ref, schur_ref, top_ref,
    part_ref, lower_ref, lower_turned_ref,
):
    count, slots, half = turned_ref.shape
    nothing = jnp.zeros((slots, slots), BF)
    inner = jnp.where(jnp.full((1, slots), inner_ref[0]) > 0, F32(1.0), F32(0.0)).astype(BF)
    for first in range(0, count, cells):
        group = range(first, first + cells)
        skel = skel_ref[layer, first : first + cells]
        marked = [
            marked_of(skel[k - first : k - first + 1], rank_ref[layer, k], interp_ref[layer, k]) for k in group
        ]
        faces = [kept_cleared(t) for t in [jnp.transpose(m) for m in marked]]
        for k in group:
            lower = faces[k - first][:, half:] * inner
            lower_turned_ref[k] = lower
            lower_ref[k] = jnp.transpose(lower)
        tops = [kept_cleared(t) * inner for t in [jnp.transpose(top_ref[k]) for k in group]]
        matrices = []
        for k, top in zip(group, tops):
            conduct = coup_ref[layer, k : k + 1]
            link = dot_nt(scaled(turned_ref[k], conduct), top).astype(BF)
            link_t = dot_nt(scaled(top, conduct), turned_ref[k]).astype(BF)
            matrices.append(face_of(schur_ref[k], link, link_t, nothing))
        for k, result in zip(group, project(faces, matrices)):
            part_ref[k] = result


def x_last_kernel(
    cells, layer, places, part_ref, lower_ref, lower_turned_ref, extra_ref, packed_ref, _, out_ref, held, sems
):
    slots = part_ref.shape[-1]
    half = slots // 2
    upper, same, opposite = pack_masks(slots)
    one, zero, mid = F32(1.0), F32(0.0), F32(0.5)
    top_scale = jnp.where(same, mid, jnp.where(upper, one, zero))
    low_scale = jnp.where(opposite, mid, jnp.where(upper, zero, one))
    same_scale = jnp.where(same, one, zero)
    opposite_scale = jnp.where(opposite, one, zero)
    extras = extra_ref[(part_ref.shape[0] // cells - 1) * cells * half :].astype(F32)
    pairs = -(-cells // 2)
    copies = []
    for n, c in enumerate(places):
        group = range(c * cells, (c + 1) * cells)
        schurs = []
        for k in range(cells):
            start = (n * cells + k) * half
            packed = packed_ref[start : start + half].astype(F32)
            extra = extras[c * pairs + k // 2 : c * pairs + k // 2 + 1]
            top, low = packed * top_scale, packed * low_scale
            if k % 2 == 0:
                top += extra * opposite_scale
            else:
                low += extra * same_scale
            tri = jnp.concatenate([top, low], axis=0).astype(BF)
            schurs.append(tri + jnp.transpose(tri))
        inner = [dot(lower_turned_ref[k], h).astype(BF) for k, h in zip(group, schurs)]
        results = [dot(i, lower_ref[k]) for k, i in zip(group, inner)]
        part_cells = max(1, cells // 2)
        for start in range(0, cells, part_cells):
            for k in range(start, start + part_cells):
                held[n * cells + k] = (part_ref[c * cells + k] + results[k]).astype(BF)
            copy = pltpu.make_async_copy(
                held.at[pl.ds(n * cells + start, part_cells)],
                out_ref.at[layer, pl.ds(c * cells + start, part_cells)],
                sems.at[n, start // part_cells],
            )
            copy.start()
            copies.append(copy)
    for copy in copies:
        copy.wait()


def call(kernel, grid, in_specs, out_specs, out_shape, flops, moved, aliases=None, vmem=24, scratch=()):
    return pl.pallas_call(
        kernel,
        grid=grid,
        in_specs=in_specs,
        out_specs=out_specs,
        out_shape=out_shape,
        scratch_shapes=scratch,
        input_output_aliases=aliases or {},
        compiler_params=pltpu.CompilerParams(vmem_limit_bytes=vmem * MIB),
        cost_estimate=pl.CostEstimate(flops=flops, bytes_accessed=moved, transcendentals=0),
    )


def in_hbm(x):
    return pltpu.with_memory_space_constraint(x, pltpu.HBM)


def body(
    cell_matrix,
    x_coupling,
    y_coupling,
    cell_interp,
    cell_skel,
    cell_rank,
    x_face_interp,
    x_face_skel,
    x_face_rank,
    y_face_interp,
    y_face_skel,
    y_face_rank,
):
    nx, nj, rows, slots = cell_interp.shape
    half = rows // 2
    fslots = x_face_interp.shape[-1]
    cells = next(n for n in (8, 4, 2, 1) if nj % n == 0 and nj > n)
    chunks = nj // cells
    unit = 2 * nx * nj * slots * slots * slots
    smem = pl.BlockSpec(memory_space=pltpu.SMEM)
    shape = jax.ShapeDtypeStruct

    hbm = pl.BlockSpec(memory_space=pltpu.HBM)
    vmem = pl.BlockSpec(memory_space=pltpu.VMEM)
    top = call(
        functools.partial(top_kernel, cells),
        (),
        [hbm, hbm, hbm],
        vmem,
        shape((nj, half, slots), BF),
        0,
        4 * nj * half * slots,
        vmem=8,
        scratch=[
            pltpu.SMEM((nx, nj), jnp.int32),
            pltpu.VMEM((nj, slots), jnp.int32),
            pltpu.VMEM((nj, half, slots), BF),
            pltpu.SemaphoreType.DMA((2,)),
            pltpu.SemaphoreType.DMA((chunks,)),
        ],
    )(in_hbm(cell_rank), in_hbm(cell_skel), in_hbm(cell_interp))
    top_in = passed_round(top, "gx")


    late_rows = cells * slots // 2
    early_rows = (chunks - 1) * late_rows + -(-chunks * -(-cells // 2) // 16) * 16

    near = max(nx - 2, 0)

    def down(*dims):
        zeros = (0,) * len(dims)
        return pl.BlockSpec((1, cells) + dims, lambda i, c: (nx - 1 - i, chunks - 1 - c) + zeros)

    def down_x(*dims):
        zeros = (0,) * len(dims)

        def place(i, c):
            return (jnp.minimum(nx - 1 - i, near), jnp.where(i == 0, chunks - 1, chunks - 1 - c)) + zeros

        return pl.BlockSpec((1, cells) + dims, place)

    x_out, y_out, packed, packed_last, edge, corner, last_turned, last_schur = call(
        functools.partial(main_kernel, cells, nx, chunks),
        (nx, chunks),
        [
            smem, down(slots), down(rows, slots), down(rows, rows),
            smem, down_x(fslots), down_x(rows, fslots), down_x(half),
            smem, down(fslots), down(rows, fslots), down(half),
        ],
        [
            down_x(fslots, fslots),
            down(fslots, fslots),
            vmem, vmem, vmem, vmem, vmem, vmem,
        ],
        [
            shape((nx, nj, fslots, fslots), BF),
            shape((nx, nj, fslots, fslots), BF),
            shape((early_rows, slots), BF),
            shape((late_rows, slots), BF),
            shape((nx, 2, slots, half), BF),
            shape((nx, 2, slots, half), BF),
            shape((nj, slots, half), BF),
            shape((nj, slots, slots), BF),
        ],
        20 * unit,
        nx * nj * (rows * rows + 3 * rows * slots + 3 * slots * slots) * 2,
        vmem=32,
        scratch=[
            pltpu.VMEM((nj, slots, half), BF),
            pltpu.VMEM((nj, slots, slots), BF),
            pltpu.VMEM((chunks, cells, slots), F32),
        ],
    )(
        cell_rank, in_hbm(cell_skel), in_hbm(cell_interp), in_hbm(cell_matrix),
        x_face_rank, in_hbm(x_face_skel), in_hbm(x_face_interp), in_hbm(x_coupling),
        y_face_rank, in_hbm(y_face_skel), in_hbm(y_face_interp), in_hbm(y_coupling),
    )
    edge_in = passed_along(edge, "yz", -1)
    packed_in = passed_round(packed, "gx")
    packed_last_in = passed_round(packed_last, "gx")
    face_bytes = nj * (4 * rows * slots + 4 * slots * slots) * 2

    last = nx - 1
    tail = nj - 1
    group = tail // cells

    inner = (lax.axis_index("gx") + 1 < lax.axis_size("gx")).astype(jnp.int32).reshape(1)
    part, lower, lower_turned = call(
        functools.partial(x_part_kernel, cells, last),
        (),
        [smem, smem, vmem, vmem, vmem, vmem, vmem, vmem],
        [vmem, vmem, vmem],
        [
            shape((nj, fslots, fslots), F32),
            shape((nj, slots, fslots), BF),
            shape((nj, fslots, slots), BF),
        ],
        8 * unit // nx,
        face_bytes,
        vmem=16,
    )(inner, x_face_rank, x_face_skel, x_face_interp, x_coupling, last_turned, last_schur, top_in)

    edge_in, part = lax.optimization_barrier((edge_in, part))
    y_out = call(
        functools.partial(y_edge_kernel, nx, tail),
        (1,),
        [
            smem,
            pl.BlockSpec((nx, cells, fslots), lambda i: (0, group, 0)),
            pl.BlockSpec((nx, 1, rows, fslots), lambda i: (0, tail, 0, 0)),
            pl.BlockSpec((nx, cells, half), lambda i: (0, group, 0)),
            pl.BlockSpec((nx, 2, slots, half), lambda i: (0, 0, 0, 0)),
            pl.BlockSpec((nx, 2, slots, half), lambda i: (0, 0, 0, 0)),
            pl.BlockSpec(memory_space=pl.ANY),
        ],
        pl.BlockSpec((nx, 1, fslots, fslots), lambda i: (0, tail, 0, 0)),
        shape((nx, nj, fslots, fslots), BF),
        8 * unit // nj,
        nx * face_bytes // nj,
        {6: 0},
    )(y_face_rank, y_face_skel, in_hbm(y_face_interp), y_coupling, corner, edge_in, y_out)

    for places, arrived in (
        (range(chunks - 1), packed_in),
        (range(chunks - 1, chunks), packed_last_in),
    ):
        count = len(places)
        x_out = call(
            functools.partial(x_last_kernel, cells, last, places),
            (),
            [vmem, vmem, vmem, vmem, vmem, hbm],
            hbm,
            shape((nx, nj, fslots, fslots), BF),
            3 * unit // nx * count // chunks,
            nj * slots * slots * 11 * count // chunks,
            {5: 0},
            scratch=[
                pltpu.VMEM((count * cells, fslots, fslots), BF),
                pltpu.SemaphoreType.DMA((count, 2)),
            ],
        )(part, lower, lower_turned, packed_in, arrived, x_out)
    return (x_out, y_out)


def solution(mesh):
    return jax.shard_map(
        body,
        mesh=mesh,
        in_specs=(
            P("gx", "yz", None, None),
            P("gx", "yz", None),
            P("gx", "yz", None),
            P("gx", "yz", None, None),
            P("gx", "yz", None),
            P("gx", "yz"),
            P("gx", "yz", None, None),
            P("gx", "yz", None),
            P("gx", "yz"),
            P("gx", "yz", None, None),
            P("gx", "yz", None),
            P("gx", "yz"),
        ),
        out_specs=(P("gx", "yz", None, None), P("gx", "yz", None, None)),
        check_vma=False,
    )
```

```python
import functools

import jax
import jax.numpy as jnp
from jax import lax
from jax.experimental import pallas as pl
from jax.experimental.pallas import tpu as pltpu
from jax.sharding import PartitionSpec as P

BF = jnp.bfloat16
F32 = jnp.float32
MIB = 1024 * 1024


def passed_along(x, axis, by):
    devices = lax.axis_size(axis)
    pairs = [(i, i + by) for i in range(devices) if 0 <= i + by < devices]
    return lax.ppermute(x, axis, pairs)


def passed_round(x, axis):
    devices = lax.axis_size(axis)
    return lax.ppermute(x, axis, [(i, (i - 1) % devices) for i in range(devices)])


def dot_nt(a, b):
    return lax.dot_general(a, b, (((1,), (1,)), ((), ())), preferred_element_type=F32)


def dot(a, b):
    return lax.dot_general(a, b, (((1,), (0,)), ((), ())), preferred_element_type=F32)


def marks_of(skel_row, rank, interp):
    rows, slots = interp.shape
    live = lax.broadcasted_iota(jnp.int32, (1, slots), 1) < rank
    picked_row = jnp.where(live, skel_row, -1).astype(F32).astype(BF)
    row = lax.broadcasted_iota(jnp.int32, (rows, slots), 0).astype(F32).astype(BF)
    live_row = jnp.where(live, F32(1.0), F32(0.0)).astype(BF)
    return row == picked_row, interp * live_row


def kept_cleared(turned):
    most = jnp.max(turned, axis=0, keepdims=True)
    least = jnp.where(most.astype(F32) == 1.0, F32(1.0), F32(-2.0)).astype(BF)
    return jnp.where(turned >= least, turned, BF(0.0))


def marked_of(skel_row, rank, interp):
    hit, live = marks_of(skel_row, rank, interp)
    return jnp.where(hit, BF(1.0), live)


def bases_of(cells, layer, first, rank_ref, skel, interp_ref):
    marked = [
        marked_of(skel[k : k + 1], rank_ref[layer, first + k], interp_ref[0, k])
        for k in range(cells)
    ]
    return [kept_cleared(t) for t in [jnp.transpose(m) for m in marked]]


def scaled(turned, conduct):
    return turned * -conduct


def face_of(left, link, link_t, right):
    upper = jnp.concatenate([left, link], axis=1)
    lower = jnp.concatenate([link_t, right], axis=1)
    return jnp.concatenate([upper, lower], axis=0)


def project(turned, matrices):
    inner = [dot(t, m).astype(BF) for t, m in zip(turned, matrices)]
    return [dot_nt(i, t) for i, t in zip(inner, turned)]


def top_kernel(cells, rank_hbm, skel_hbm, interp_hbm, out_ref, rank_ref, skel_ref, held, small_sems, sems):
    count, half, _ = out_ref.shape
    small = [
        pltpu.make_async_copy(rank_hbm, rank_ref, small_sems.at[0]),
        pltpu.make_async_copy(skel_hbm.at[0], skel_ref, small_sems.at[1]),
    ]
    copies = []
    for c in range(count // cells):
        group = pl.ds(c * cells, cells)
        copies.append(
            pltpu.make_async_copy(
                interp_hbm.at[0, group, pl.ds(0, half)], held.at[group], sems.at[c]
            )
        )
    for copy in small + copies:
        copy.start()
    for copy in small:
        copy.wait()
    for c in range(count // cells):
        copies[c].wait()
        for k in range(c * cells, (c + 1) * cells):
            out_ref[k] = marked_of(skel_ref[k : k + 1], rank_ref[0, k], held[k])


def pack_masks(size):
    half = size // 2
    row = lax.broadcasted_iota(jnp.int32, (half, size), 0)
    lane = lax.broadcasted_iota(jnp.int32, (half, size), 1)
    ahead = lane - row
    upper = (ahead >= 0) & (ahead < half)
    return upper, ahead == 0, ahead == half


def main_kernel(
    cells, layers, chunks,
    rank_ref, skel_ref, interp_ref, matrix_ref,
    x_rank_ref, x_skel_ref, x_interp_ref, x_coup_ref,
    y_rank_ref, y_skel_ref, y_interp_ref, y_coup_ref,
    x_out_ref, y_out_ref, packed_ref, packed_last_ref, edge_ref, corner_ref, last_turned_ref, last_schur_ref,
    store_turned, store_schur, store_extra,
):
    layer = layers - 1 - pl.program_id(0)
    chunk = chunks - 1 - pl.program_id(1)
    first = chunk * cells
    slots = skel_ref.shape[-1]
    half = slots // 2
    top = interp_ref.shape[2] // 2

    turned = bases_of(cells, layer, first, rank_ref, skel_ref[0], interp_ref)
    schurs = project(turned, [matrix_ref[0, k] for k in range(cells)])
    schurs = [s.astype(BF) for s in schurs]

    def faces(out_ref, f_rank_ref, f_skel_ref, f_interp_ref, coup_ref, rights):
        found = bases_of(cells, layer, first, f_rank_ref, f_skel_ref[0], f_interp_ref)
        matrices = []
        for k in range(cells):
            right_turned, right = rights[k]
            conduct = coup_ref[0, k : k + 1]
            lower = turned[k][:, top:]
            link = dot_nt(scaled(lower, conduct), right_turned).astype(BF)
            link_t = dot_nt(scaled(right_turned, conduct), lower).astype(BF)
            matrices.append(face_of(schurs[k], link, link_t, right))
        results = project(found, matrices)
        for k in range(cells):
            out_ref[0, k] = results[k].astype(BF)

    def stored(place):
        return store_turned[place], store_schur[place]

    after = jnp.minimum(first + cells, store_schur.shape[0] - 1)
    rights = [(turned[k][:, :top], schurs[k]) for k in range(1, cells)]
    faces(y_out_ref, y_rank_ref, y_skel_ref, y_interp_ref, y_coup_ref, rights + [stored(after)])

    @pl.when(layer < layers - 1)
    def _():
        rights = [stored(first + k) for k in range(cells)]
        faces(x_out_ref, x_rank_ref, x_skel_ref, x_interp_ref, x_coup_ref, rights)

    for k in range(cells):
        store_turned[first + k] = turned[k][:, :top]
        store_schur[first + k] = schurs[k]

    @pl.when(layer == layers - 1)
    def _():
        for k in range(cells):
            last_turned_ref[first + k] = turned[k][:, top:]
            last_schur_ref[first + k] = schurs[k]

    @pl.when(layer == 0)
    def _():
        upper, same, opposite = pack_masks(slots)

        def put(packed_ref, start):
            for k in range(cells):
                above, below = schurs[k][:half].astype(F32), schurs[k][half:].astype(F32)
                place = pl.ds(pl.multiple_of(start + k * half, half), half)
                packed_ref[place] = jnp.where(upper, above, below).astype(BF)

        @pl.when(chunk < chunks - 1)
        def _():
            put(packed_ref, chunk * (cells * half))

        @pl.when(chunk == chunks - 1)
        def _():
            put(packed_last_ref, 0)

        for p in range(0, cells, 2):
            extra = jnp.where(opposite, schurs[p][:half].astype(F32), F32(0.0))
            if p + 1 < cells:
                extra += jnp.where(same, schurs[p + 1][half:].astype(F32), F32(0.0))
            store_extra[chunk, p // 2 : p // 2 + 1] = jnp.sum(extra, axis=0, keepdims=True)

        @pl.when(chunk == 0)
        def _():
            pairs = -(-cells // 2)
            start = (chunks - 1) * cells * half
            rows = [store_extra[c, :pairs] for c in range(chunks)]
            pad = packed_ref.shape[0] - start - pairs * chunks
            if pad:
                rows.append(jnp.zeros((pad, slots), F32))
            packed_ref[start:] = jnp.concatenate(rows, axis=0).astype(BF)

    @pl.when(chunk == 0)
    def _():
        edge_ref[layer, 0] = turned[0][:, :top]
        edge_ref[layer, 1] = schurs[0]

    @pl.when(chunk == chunks - 1)
    def _():
        corner_ref[layer, 0] = turned[cells - 1][:, top:]
        corner_ref[layer, 1] = schurs[cells - 1]


def y_edge_kernel(layers, place, rank_ref, skel_ref, interp_ref, coup_ref, corner_ref, edge_ref, _, out_ref):
    row = place % skel_ref.shape[1]
    marked = [
        marked_of(skel_ref[i, row : row + 1], rank_ref[i, place], interp_ref[i, 0])
        for i in range(layers)
    ]
    found = [kept_cleared(jnp.transpose(m)) for m in marked]
    matrices = []
    for i in range(layers):
        conduct = coup_ref[i, row : row + 1]
        link = dot_nt(scaled(corner_ref[i, 0], conduct), edge_ref[i, 0]).astype(BF)
        link_t = dot_nt(scaled(edge_ref[i, 0], conduct), corner_ref[i, 0]).astype(BF)
        matrices.append(face_of(corner_ref[i, 1], link, link_t, edge_ref[i, 1]))
    results = project(found, matrices)
    for i in range(layers):
        out_ref[i, 0] = results[i].astype(BF)


def x_part_kernel(
    cells, layer, inner_ref, rank_ref, skel_hbm, interp_hbm, coup_hbm, turned_ref, schur_ref, top_ref,
    part_ref, lower_ref, lower_turned_ref, skel_ref, interp_ref, coup_ref, small_sems, sems,
):
    count, slots, half = turned_ref.shape
    small = [
        pltpu.make_async_copy(skel_hbm.at[layer], skel_ref, small_sems.at[0]),
        pltpu.make_async_copy(coup_hbm.at[layer], coup_ref, small_sems.at[1]),
    ]
    fetches = []
    for n in range(count // cells):
        places = pl.ds(n * cells, cells)
        fetches.append(
            pltpu.make_async_copy(interp_hbm.at[layer, places], interp_ref.at[places], sems.at[n])
        )
    for copy in small + fetches:
        copy.start()
    for copy in small:
        copy.wait()
    nothing = jnp.zeros((slots, slots), BF)
    inner = jnp.where(jnp.full((1, slots), inner_ref[0]) > 0, F32(1.0), F32(0.0)).astype(BF)
    for first in range(0, count, cells):
        group = range(first, first + cells)
        fetches[first // cells].wait()
        skel = skel_ref[first : first + cells]
        marked = [
            marked_of(skel[k - first : k - first + 1], rank_ref[layer, k], interp_ref[k]) for k in group
        ]
        faces = [kept_cleared(t) for t in [jnp.transpose(m) for m in marked]]
        for k in group:
            lower = faces[k - first][:, half:] * inner
            lower_turned_ref[k] = lower
            lower_ref[k] = jnp.transpose(lower)
        tops = [kept_cleared(t) * inner for t in [jnp.transpose(top_ref[k]) for k in group]]
        matrices = []
        for k, top in zip(group, tops):
            conduct = coup_ref[k : k + 1]
            link = dot_nt(scaled(turned_ref[k], conduct), top).astype(BF)
            link_t = dot_nt(scaled(top, conduct), turned_ref[k]).astype(BF)
            matrices.append(face_of(schur_ref[k], link, link_t, nothing))
        for k, result in zip(group, project(faces, matrices)):
            part_ref[k] = result


def x_last_kernel(
    cells, layer, places, part_ref, lower_ref, lower_turned_ref, extra_ref, packed_ref, _, out_ref, held, sems
):
    slots = part_ref.shape[-1]
    half = slots // 2
    upper, same, opposite = pack_masks(slots)
    one, zero, mid = F32(1.0), F32(0.0), F32(0.5)
    top_scale = jnp.where(same, mid, jnp.where(upper, one, zero))
    low_scale = jnp.where(opposite, mid, jnp.where(upper, zero, one))
    same_scale = jnp.where(same, one, zero)
    opposite_scale = jnp.where(opposite, one, zero)
    extras = extra_ref[(part_ref.shape[0] // cells - 1) * cells * half :].astype(F32)
    pairs = -(-cells // 2)
    copies = []
    for n, c in enumerate(places):
        group = range(c * cells, (c + 1) * cells)
        schurs = []
        for k in range(cells):
            start = (n * cells + k) * half
            packed = packed_ref[start : start + half].astype(F32)
            extra = extras[c * pairs + k // 2 : c * pairs + k // 2 + 1]
            top, low = packed * top_scale, packed * low_scale
            if k % 2 == 0:
                top += extra * opposite_scale
            else:
                low += extra * same_scale
            tri = jnp.concatenate([top, low], axis=0).astype(BF)
            schurs.append(tri + jnp.transpose(tri))
        inner = [dot(lower_turned_ref[k], h).astype(BF) for k, h in zip(group, schurs)]
        results = [dot(i, lower_ref[k]) for k, i in zip(group, inner)]
        part_cells = max(1, cells // 2)
        for start in range(0, cells, part_cells):
            for k in range(start, start + part_cells):
                held[n * cells + k] = (part_ref[c * cells + k] + results[k]).astype(BF)
            copy = pltpu.make_async_copy(
                held.at[pl.ds(n * cells + start, part_cells)],
                out_ref.at[layer, pl.ds(c * cells + start, part_cells)],
                sems.at[n, start // part_cells],
            )
            copy.start()
            copies.append(copy)
    for copy in copies:
        copy.wait()


def call(kernel, grid, in_specs, out_specs, out_shape, flops, moved, aliases=None, vmem=24, scratch=()):
    return pl.pallas_call(
        kernel,
        grid=grid,
        in_specs=in_specs,
        out_specs=out_specs,
        out_shape=out_shape,
        scratch_shapes=scratch,
        input_output_aliases=aliases or {},
        compiler_params=pltpu.CompilerParams(vmem_limit_bytes=vmem * MIB),
        cost_estimate=pl.CostEstimate(flops=flops, bytes_accessed=moved, transcendentals=0),
    )


def in_hbm(x):
    return pltpu.with_memory_space_constraint(x, pltpu.HBM)


def in_vmem(x):
    return pltpu.with_memory_space_constraint(x, pltpu.VMEM)


def body(
    cell_matrix,
    x_coupling,
    y_coupling,
    cell_interp,
    cell_skel,
    cell_rank,
    x_face_interp,
    x_face_skel,
    x_face_rank,
    y_face_interp,
    y_face_skel,
    y_face_rank,
):
    nx, nj, rows, slots = cell_interp.shape
    half = rows // 2
    fslots = x_face_interp.shape[-1]
    cells = next(n for n in (8, 4, 2, 1) if nj % n == 0 and nj > n)
    chunks = nj // cells
    unit = 2 * nx * nj * slots * slots * slots
    smem = pl.BlockSpec(memory_space=pltpu.SMEM)
    shape = jax.ShapeDtypeStruct

    hbm = pl.BlockSpec(memory_space=pltpu.HBM)
    vmem = pl.BlockSpec(memory_space=pltpu.VMEM)
    top = call(
        functools.partial(top_kernel, cells),
        (),
        [hbm, hbm, hbm],
        vmem,
        shape((nj, half, slots), BF),
        0,
        4 * nj * half * slots,
        vmem=8,
        scratch=[
            pltpu.SMEM((nx, nj), jnp.int32),
            pltpu.VMEM((nj, slots), jnp.int32),
            pltpu.VMEM((nj, half, slots), BF),
            pltpu.SemaphoreType.DMA((2,)),
            pltpu.SemaphoreType.DMA((chunks,)),
        ],
    )(in_hbm(cell_rank), in_hbm(cell_skel), in_hbm(cell_interp))
    top_in = passed_round(in_vmem(top), "gx")


    late_rows = cells * slots // 2
    early_rows = (chunks - 1) * late_rows + -(-chunks * -(-cells // 2) // 16) * 16

    near = max(nx - 2, 0)

    def down(*dims):
        zeros = (0,) * len(dims)
        return pl.BlockSpec((1, cells) + dims, lambda i, c: (nx - 1 - i, chunks - 1 - c) + zeros)

    def down_x(*dims):
        zeros = (0,) * len(dims)

        def place(i, c):
            return (jnp.minimum(nx - 1 - i, near), jnp.where(i == 0, chunks - 1, chunks - 1 - c)) + zeros

        return pl.BlockSpec((1, cells) + dims, place)

    x_out, y_out, packed, packed_last, edge, corner, last_turned, last_schur = call(
        functools.partial(main_kernel, cells, nx, chunks),
        (nx, chunks),
        [
            smem, down(slots), down(rows, slots), down(rows, rows),
            smem, down_x(fslots), down_x(rows, fslots), down_x(half),
            smem, down(fslots), down(rows, fslots), down(half),
        ],
        [
            down_x(fslots, fslots),
            down(fslots, fslots),
            vmem, vmem, vmem, pl.BlockSpec((nx, 2, slots, half), lambda i, c: (0, 0, 0, 0)), vmem, vmem,
        ],
        [
            shape((nx, nj, fslots, fslots), BF),
            shape((nx, nj, fslots, fslots), BF),
            shape((early_rows, slots), BF),
            shape((late_rows, slots), BF),
            shape((nx, 2, slots, half), BF),
            shape((nx, 2, slots, half), BF),
            shape((nj, slots, half), BF),
            shape((nj, slots, slots), BF),
        ],
        20 * unit,
        nx * nj * (rows * rows + 3 * rows * slots + 3 * slots * slots) * 2,
        vmem=32,
        scratch=[
            pltpu.VMEM((nj, slots, half), BF),
            pltpu.VMEM((nj, slots, slots), BF),
            pltpu.VMEM((chunks, cells, slots), F32),
        ],
    )(
        cell_rank, in_hbm(cell_skel), in_hbm(cell_interp), in_hbm(cell_matrix),
        x_face_rank, in_hbm(x_face_skel), in_hbm(x_face_interp), in_hbm(x_coupling),
        y_face_rank, in_hbm(y_face_skel), in_hbm(y_face_interp), in_hbm(y_coupling),
    )
    edge_in = passed_along(edge, "yz", -1)
    packed_in = passed_round(packed, "gx")
    packed_last_in = in_vmem(passed_round(packed_last, "gx"))
    face_bytes = nj * (4 * rows * slots + 4 * slots * slots) * 2

    last = nx - 1
    tail = nj - 1
    group = tail // cells

    inner = (lax.axis_index("gx") + 1 < lax.axis_size("gx")).astype(jnp.int32).reshape(1)
    part, lower, lower_turned = call(
        functools.partial(x_part_kernel, cells, last),
        (),
        [smem, smem, hbm, hbm, hbm, vmem, vmem, vmem],
        [vmem, vmem, vmem],
        [
            shape((nj, fslots, fslots), F32),
            shape((nj, slots, fslots), BF),
            shape((nj, fslots, slots), BF),
        ],
        8 * unit // nx,
        face_bytes,
        vmem=16,
        scratch=[
            pltpu.VMEM((nj, slots), jnp.int32),
            pltpu.VMEM((nj, rows, fslots), BF),
            pltpu.VMEM((nj, half), BF),
            pltpu.SemaphoreType.DMA((2,)),
            pltpu.SemaphoreType.DMA((chunks,)),
        ],
    )(inner, x_face_rank, in_hbm(x_face_skel), in_hbm(x_face_interp), in_hbm(x_coupling), last_turned, last_schur, top_in)

    edge_in, part = lax.optimization_barrier((edge_in, part))
    y_out = call(
        functools.partial(y_edge_kernel, nx, tail),
        (1,),
        [
            smem,
            pl.BlockSpec((nx, cells, fslots), lambda i: (0, group, 0)),
            pl.BlockSpec((nx, 1, rows, fslots), lambda i: (0, tail, 0, 0)),
            pl.BlockSpec((nx, cells, half), lambda i: (0, group, 0)),
            pl.BlockSpec((nx, 2, slots, half), lambda i: (0, 0, 0, 0)),
            pl.BlockSpec((nx, 2, slots, half), lambda i: (0, 0, 0, 0)),
            pl.BlockSpec(memory_space=pl.ANY),
        ],
        pl.BlockSpec((nx, 1, fslots, fslots), lambda i: (0, tail, 0, 0)),
        shape((nx, nj, fslots, fslots), BF),
        8 * unit // nj,
        nx * face_bytes // nj,
        {6: 0},
    )(y_face_rank, y_face_skel, in_hbm(y_face_interp), y_coupling, corner, edge_in, y_out)

    for places, arrived in (
        (range(chunks - 1), packed_in),
        (range(chunks - 1, chunks), packed_last_in),
    ):
        count = len(places)
        x_out = call(
            functools.partial(x_last_kernel, cells, last, places),
            (),
            [vmem, vmem, vmem, vmem, vmem, hbm],
            hbm,
            shape((nx, nj, fslots, fslots), BF),
            3 * unit // nx * count // chunks,
            nj * slots * slots * 11 * count // chunks,
            {5: 0},
            scratch=[
                pltpu.VMEM((count * cells, fslots, fslots), BF),
                pltpu.SemaphoreType.DMA((count, 2)),
            ],
        )(part, lower, lower_turned, packed_in, arrived, x_out)
    return (x_out, y_out)


def solution(mesh):
    return jax.shard_map(
        body,
        mesh=mesh,
        in_specs=(
            P("gx", "yz", None, None),
            P("gx", "yz", None),
            P("gx", "yz", None),
            P("gx", "yz", None, None),
            P("gx", "yz", None),
            P("gx", "yz"),
            P("gx", "yz", None, None),
            P("gx", "yz", None),
            P("gx", "yz"),
            P("gx", "yz", None, None),
            P("gx", "yz", None),
            P("gx", "yz"),
        ),
        out_specs=(P("gx", "yz", None, None), P("gx", "yz", None, None)),
        check_vma=False,
    )
```

```python
import functools

import jax
import jax.numpy as jnp
from jax import lax
from jax.experimental import pallas as pl
from jax.experimental.pallas import tpu as pltpu
from jax.sharding import PartitionSpec as P

BF = jnp.bfloat16
F32 = jnp.float32
MIB = 1024 * 1024


def passed_along(x, axis, by):
    devices = lax.axis_size(axis)
    pairs = [(i, i + by) for i in range(devices) if 0 <= i + by < devices]
    return lax.ppermute(x, axis, pairs)


def dot_nt(a, b):
    return lax.dot_general(a, b, (((1,), (1,)), ((), ())), preferred_element_type=F32)


def dot(a, b):
    return lax.dot_general(a, b, (((1,), (0,)), ((), ())), preferred_element_type=F32)


def marks_of(skel_row, rank, interp):
    rows, slots = interp.shape
    live = lax.broadcasted_iota(jnp.int32, (1, slots), 1) < rank
    picked_row = jnp.where(live, skel_row, -1).astype(F32).astype(BF)
    row = lax.broadcasted_iota(jnp.int32, (rows, slots), 0).astype(F32).astype(BF)
    live_row = jnp.where(live, F32(1.0), F32(0.0)).astype(BF)
    return row == picked_row, interp * live_row


def kept_cleared(turned):
    most = jnp.max(turned, axis=0, keepdims=True)
    least = jnp.where(most.astype(F32) == 1.0, F32(1.0), F32(-2.0)).astype(BF)
    return jnp.where(turned >= least, turned, BF(0.0))


def marked_of(skel_row, rank, interp):
    hit, live = marks_of(skel_row, rank, interp)
    return jnp.where(hit, BF(1.0), live)


def bases_of(cells, layer, first, rank_ref, skel, interp_ref):
    marked = [
        marked_of(skel[k : k + 1], rank_ref[layer, first + k], interp_ref[0, k])
        for k in range(cells)
    ]
    return [kept_cleared(t) for t in [jnp.transpose(m) for m in marked]]


def scaled(turned, conduct):
    return turned * -conduct


def face_of(left, link, link_t, right):
    upper = jnp.concatenate([left, link], axis=1)
    lower = jnp.concatenate([link_t, right], axis=1)
    return jnp.concatenate([upper, lower], axis=0)


def project(turned, matrices):
    inner = [dot(t, m).astype(BF) for t, m in zip(turned, matrices)]
    return [dot_nt(i, t) for i, t in zip(inner, turned)]


def top_kernel(cells, rank_hbm, skel_hbm, interp_hbm, out_ref, rank_ref, skel_ref, held, small_sems, sems):
    count, half, _ = out_ref.shape
    small = [
        pltpu.make_async_copy(rank_hbm, rank_ref, small_sems.at[0]),
        pltpu.make_async_copy(skel_hbm.at[0], skel_ref, small_sems.at[1]),
    ]
    copies = []
    for c in range(count // cells):
        group = pl.ds(c * cells, cells)
        copies.append(
            pltpu.make_async_copy(
                interp_hbm.at[0, group, pl.ds(0, half)], held.at[group], sems.at[c]
            )
        )
    for copy in small + copies:
        copy.start()
    for copy in small:
        copy.wait()
    for c in range(count // cells):
        copies[c].wait()
        for k in range(c * cells, (c + 1) * cells):
            out_ref[k] = marked_of(skel_ref[k : k + 1], rank_ref[0, k], held[k])


def pack_masks(size):
    half = size // 2
    row = lax.broadcasted_iota(jnp.int32, (half, size), 0)
    lane = lax.broadcasted_iota(jnp.int32, (half, size), 1)
    ahead = lane - row
    upper = (ahead >= 0) & (ahead < half)
    return upper, ahead == 0, ahead == half


def main_kernel(
    cells, layers, chunks,
    rank_ref, skel_ref, interp_ref, matrix_ref,
    x_rank_ref, x_skel_ref, x_interp_ref, x_coup_ref,
    y_rank_ref, y_skel_ref, y_interp_ref, y_coup_ref,
    x_out_ref, y_out_ref, packed_ref, packed_last_ref, edge_ref, corner_ref, last_turned_ref, last_schur_ref,
    store_turned, store_schur, store_extra,
):
    layer = layers - 1 - pl.program_id(0)
    chunk = chunks - 1 - pl.program_id(1)
    first = chunk * cells
    slots = skel_ref.shape[-1]
    half = slots // 2
    top = interp_ref.shape[2] // 2

    turned = bases_of(cells, layer, first, rank_ref, skel_ref[0], interp_ref)
    schurs = project(turned, [matrix_ref[0, k] for k in range(cells)])
    schurs = [s.astype(BF) for s in schurs]

    def faces(out_ref, f_rank_ref, f_skel_ref, f_interp_ref, coup_ref, rights):
        found = bases_of(cells, layer, first, f_rank_ref, f_skel_ref[0], f_interp_ref)
        matrices = []
        for k in range(cells):
            right_turned, right = rights[k]
            conduct = coup_ref[0, k : k + 1]
            lower = turned[k][:, top:]
            link = dot_nt(scaled(lower, conduct), right_turned).astype(BF)
            link_t = dot_nt(scaled(right_turned, conduct), lower).astype(BF)
            matrices.append(face_of(schurs[k], link, link_t, right))
        results = project(found, matrices)
        for k in range(cells):
            out_ref[0, k] = results[k].astype(BF)

    def stored(place):
        return store_turned[place], store_schur[place]

    after = jnp.minimum(first + cells, store_schur.shape[0] - 1)
    rights = [(turned[k][:, :top], schurs[k]) for k in range(1, cells)]
    faces(y_out_ref, y_rank_ref, y_skel_ref, y_interp_ref, y_coup_ref, rights + [stored(after)])

    @pl.when(layer < layers - 1)
    def _():
        rights = [stored(first + k) for k in range(cells)]
        faces(x_out_ref, x_rank_ref, x_skel_ref, x_interp_ref, x_coup_ref, rights)

    for k in range(cells):
        store_turned[first + k] = turned[k][:, :top]
        store_schur[first + k] = schurs[k]

    @pl.when(layer == layers - 1)
    def _():
        for k in range(cells):
            last_turned_ref[first + k] = turned[k][:, top:]
            last_schur_ref[first + k] = schurs[k]

    @pl.when(layer == 0)
    def _():
        upper, same, opposite = pack_masks(slots)

        def put(packed_ref, start):
            for k in range(cells):
                above, below = schurs[k][:half].astype(F32), schurs[k][half:].astype(F32)
                place = pl.ds(pl.multiple_of(start + k * half, half), half)
                packed_ref[place] = jnp.where(upper, above, below).astype(BF)

        @pl.when(chunk < chunks - 1)
        def _():
            put(packed_ref, chunk * (cells * half))

        @pl.when(chunk == chunks - 1)
        def _():
            put(packed_last_ref, 0)

        for p in range(0, cells, 2):
            extra = jnp.where(opposite, schurs[p][:half].astype(F32), F32(0.0))
            if p + 1 < cells:
                extra += jnp.where(same, schurs[p + 1][half:].astype(F32), F32(0.0))
            store_extra[chunk, p // 2 : p // 2 + 1] = jnp.sum(extra, axis=0, keepdims=True)

        @pl.when(chunk == 0)
        def _():
            pairs = -(-cells // 2)
            start = (chunks - 1) * cells * half
            rows = [store_extra[c, :pairs] for c in range(chunks)]
            pad = packed_ref.shape[0] - start - pairs * chunks
            if pad:
                rows.append(jnp.zeros((pad, slots), F32))
            packed_ref[start:] = jnp.concatenate(rows, axis=0).astype(BF)

    @pl.when(chunk == 0)
    def _():
        edge_ref[layer, 0] = turned[0][:, :top]
        edge_ref[layer, 1] = schurs[0]

    @pl.when(chunk == chunks - 1)
    def _():
        corner_ref[layer, 0] = turned[cells - 1][:, top:]
        corner_ref[layer, 1] = schurs[cells - 1]


def y_edge_kernel(layers, place, rank_ref, skel_ref, interp_ref, coup_ref, corner_ref, edge_ref, _, out_ref):
    row = place % skel_ref.shape[1]
    marked = [
        marked_of(skel_ref[i, row : row + 1], rank_ref[i, place], interp_ref[i, 0])
        for i in range(layers)
    ]
    found = [kept_cleared(jnp.transpose(m)) for m in marked]
    matrices = []
    for i in range(layers):
        conduct = coup_ref[i, row : row + 1]
        link = dot_nt(scaled(corner_ref[i, 0], conduct), edge_ref[i, 0]).astype(BF)
        link_t = dot_nt(scaled(edge_ref[i, 0], conduct), corner_ref[i, 0]).astype(BF)
        matrices.append(face_of(corner_ref[i, 1], link, link_t, edge_ref[i, 1]))
    results = project(found, matrices)
    for i in range(layers):
        out_ref[i, 0] = results[i].astype(BF)


def x_part_kernel(
    cells, layer, rank_ref, skel_ref, interp_ref, coup_ref, turned_ref, schur_ref, top_ref,
    part_ref, lower_ref, lower_turned_ref,
):
    count, slots, half = turned_ref.shape
    nothing = jnp.zeros((slots, slots), BF)
    for first in range(0, count, cells):
        group = range(first, first + cells)
        skel = skel_ref[layer, first : first + cells]
        marked = [
            marked_of(skel[k - first : k - first + 1], rank_ref[layer, k], interp_ref[layer, k]) for k in group
        ]
        faces = [kept_cleared(t) for t in [jnp.transpose(m) for m in marked]]
        for k in group:
            lower_turned_ref[k] = faces[k - first][:, half:]
            lower_ref[k] = jnp.transpose(faces[k - first][:, half:])
        tops = [kept_cleared(t) for t in [jnp.transpose(top_ref[k]) for k in group]]
        matrices = []
        for k, top in zip(group, tops):
            conduct = coup_ref[layer, k : k + 1]
            link = dot_nt(scaled(turned_ref[k], conduct), top).astype(BF)
            link_t = dot_nt(scaled(top, conduct), turned_ref[k]).astype(BF)
            matrices.append(face_of(schur_ref[k], link, link_t, nothing))
        for k, result in zip(group, project(faces, matrices)):
            part_ref[k] = result


def x_last_kernel(
    cells, layer, places, extra_start, part_ref, lower_ref, lower_turned_ref, extra_ref, packed_ref, _,
    out_ref, held, sems,
):
    slots = part_ref.shape[-1]
    half = slots // 2
    upper, same, opposite = pack_masks(slots)
    one, zero, mid = F32(1.0), F32(0.0), F32(0.5)
    top_scale = jnp.where(same, mid, jnp.where(upper, one, zero))
    low_scale = jnp.where(opposite, mid, jnp.where(upper, zero, one))
    same_scale = jnp.where(same, one, zero)
    opposite_scale = jnp.where(opposite, one, zero)
    extras = extra_ref[extra_start:].astype(F32)
    pairs = -(-cells // 2)
    copies = []
    for n, c in enumerate(places):
        group = range(c * cells, (c + 1) * cells)
        schurs = []
        for k in range(cells):
            start = (n * cells + k) * half
            packed = packed_ref[start : start + half].astype(F32)
            extra = extras[c * pairs + k // 2 : c * pairs + k // 2 + 1]
            top, low = packed * top_scale, packed * low_scale
            if k % 2 == 0:
                top += extra * opposite_scale
            else:
                low += extra * same_scale
            tri = jnp.concatenate([top, low], axis=0).astype(BF)
            schurs.append(tri + jnp.transpose(tri))
        inner = [dot(lower_turned_ref[k], h).astype(BF) for k, h in zip(group, schurs)]
        results = [dot(i, lower_ref[k]) for k, i in zip(group, inner)]
        part_cells = cells
        for start in range(0, cells, part_cells):
            for k in range(start, start + part_cells):
                held[n * cells + k] = (part_ref[c * cells + k] + results[k]).astype(BF)
            copy = pltpu.make_async_copy(
                held.at[pl.ds(n * cells + start, part_cells)],
                out_ref.at[layer, pl.ds(c * cells + start, part_cells)],
                sems.at[n, start // part_cells],
            )
            copy.start()
            copies.append(copy)
    for copy in copies:
        copy.wait()


def call(kernel, grid, in_specs, out_specs, out_shape, flops, moved, aliases=None, vmem=24, scratch=()):
    return pl.pallas_call(
        kernel,
        grid=grid,
        in_specs=in_specs,
        out_specs=out_specs,
        out_shape=out_shape,
        scratch_shapes=scratch,
        input_output_aliases=aliases or {},
        compiler_params=pltpu.CompilerParams(vmem_limit_bytes=vmem * MIB),
        cost_estimate=pl.CostEstimate(flops=flops, bytes_accessed=moved, transcendentals=0),
    )


def in_hbm(x):
    return pltpu.with_memory_space_constraint(x, pltpu.HBM)


def body(
    cell_matrix,
    x_coupling,
    y_coupling,
    cell_interp,
    cell_skel,
    cell_rank,
    x_face_interp,
    x_face_skel,
    x_face_rank,
    y_face_interp,
    y_face_skel,
    y_face_rank,
):
    nx, nj, rows, slots = cell_interp.shape
    half = rows // 2
    fslots = x_face_interp.shape[-1]
    cells = next(n for n in (8, 4, 2, 1) if nj % n == 0 and nj > n)
    chunks = nj // cells
    unit = 2 * nx * nj * slots * slots * slots
    smem = pl.BlockSpec(memory_space=pltpu.SMEM)
    shape = jax.ShapeDtypeStruct

    hbm = pl.BlockSpec(memory_space=pltpu.HBM)
    vmem = pl.BlockSpec(memory_space=pltpu.VMEM)
    top = call(
        functools.partial(top_kernel, cells),
        (),
        [hbm, hbm, hbm],
        vmem,
        shape((nj, half, slots), BF),
        0,
        4 * nj * half * slots,
        vmem=8,
        scratch=[
            pltpu.SMEM((nx, nj), jnp.int32),
            pltpu.VMEM((nj, slots), jnp.int32),
            pltpu.VMEM((nj, half, slots), BF),
            pltpu.SemaphoreType.DMA((2,)),
            pltpu.SemaphoreType.DMA((chunks,)),
        ],
    )(in_hbm(cell_rank), in_hbm(cell_skel), in_hbm(cell_interp))
    top_in = passed_along(top, "gx", -1)


    late_rows = cells * slots // 2
    early_rows = (chunks - 1) * late_rows + -(-chunks * -(-cells // 2) // 16) * 16

    near = max(nx - 2, 0)

    def down(*dims):
        zeros = (0,) * len(dims)
        return pl.BlockSpec((1, cells) + dims, lambda i, c: (nx - 1 - i, chunks - 1 - c) + zeros)

    def down_x(*dims):
        zeros = (0,) * len(dims)

        def place(i, c):
            return (jnp.minimum(nx - 1 - i, near), jnp.where(i == 0, chunks - 1, chunks - 1 - c)) + zeros

        return pl.BlockSpec((1, cells) + dims, place)

    x_out, y_out, packed, packed_last, edge, corner, last_turned, last_schur = call(
        functools.partial(main_kernel, cells, nx, chunks),
        (nx, chunks),
        [
            smem, down(slots), down(rows, slots), down(rows, rows),
            smem, down_x(fslots), down_x(rows, fslots), down_x(half),
            smem, down(fslots), down(rows, fslots), down(half),
        ],
        [
            down_x(fslots, fslots),
            down(fslots, fslots),
            vmem, vmem, vmem, vmem, vmem, vmem,
        ],
        [
            shape((nx, nj, fslots, fslots), BF),
            shape((nx, nj, fslots, fslots), BF),
            shape((early_rows, slots), BF),
            shape((late_rows, slots), BF),
            shape((nx, 2, slots, half), BF),
            shape((nx, 2, slots, half), BF),
            shape((nj, slots, half), BF),
            shape((nj, slots, slots), BF),
        ],
        20 * unit,
        nx * nj * (rows * rows + 3 * rows * slots + 3 * slots * slots) * 2,
        vmem=32,
        scratch=[
            pltpu.VMEM((nj, slots, half), BF),
            pltpu.VMEM((nj, slots, slots), BF),
            pltpu.VMEM((chunks, cells, slots), F32),
        ],
    )(
        cell_rank, in_hbm(cell_skel), in_hbm(cell_interp), in_hbm(cell_matrix),
        x_face_rank, in_hbm(x_face_skel), in_hbm(x_face_interp), in_hbm(x_coupling),
        y_face_rank, in_hbm(y_face_skel), in_hbm(y_face_interp), in_hbm(y_coupling),
    )
    edge_in = passed_along(edge, "yz", -1)
    packed_in = passed_along(packed, "gx", -1)
    packed_last_in = passed_along(packed_last, "gx", -1)
    face_bytes = nj * (4 * rows * slots + 4 * slots * slots) * 2

    last = nx - 1
    tail = nj - 1
    group = tail // cells

    part, lower, lower_turned = call(
        functools.partial(x_part_kernel, cells, last),
        (),
        [smem, vmem, vmem, vmem, vmem, vmem, vmem],
        [vmem, vmem, vmem],
        [
            shape((nj, fslots, fslots), F32),
            shape((nj, slots, fslots), BF),
            shape((nj, fslots, slots), BF),
        ],
        8 * unit // nx,
        face_bytes,
        vmem=16,
    )(x_face_rank, x_face_skel, x_face_interp, x_coupling, last_turned, last_schur, top_in)

    edge_in, part = lax.optimization_barrier((edge_in, part))
    y_out = call(
        functools.partial(y_edge_kernel, nx, tail),
        (1,),
        [
            smem,
            pl.BlockSpec((nx, cells, fslots), lambda i: (0, group, 0)),
            pl.BlockSpec((nx, 1, rows, fslots), lambda i: (0, tail, 0, 0)),
            pl.BlockSpec((nx, cells, half), lambda i: (0, group, 0)),
            pl.BlockSpec((nx, 2, slots, half), lambda i: (0, 0, 0, 0)),
            pl.BlockSpec((nx, 2, slots, half), lambda i: (0, 0, 0, 0)),
            pl.BlockSpec(memory_space=pl.ANY),
        ],
        pl.BlockSpec((nx, 1, fslots, fslots), lambda i: (0, tail, 0, 0)),
        shape((nx, nj, fslots, fslots), BF),
        8 * unit // nj,
        nx * face_bytes // nj,
        {6: 0},
    )(y_face_rank, y_face_skel, in_hbm(y_face_interp), y_coupling, corner, edge_in, y_out)

    few = cells // 2 if cells % 4 == 0 else cells
    late = cells // few
    for places, arrived in (
        (range((chunks - 1) * late), packed_in),
        (range((chunks - 1) * late, chunks * late), packed_last_in),
    ):
        count = len(places)
        x_out = call(
            functools.partial(x_last_kernel, few, last, places, (chunks - 1) * late_rows),
            (),
            [vmem, vmem, vmem, vmem, vmem, hbm],
            hbm,
            shape((nx, nj, fslots, fslots), BF),
            3 * unit // nx * count // (chunks * late),
            nj * slots * slots * 11 * count // (chunks * late),
            {5: 0},
            scratch=[
                pltpu.VMEM((count * few, fslots, fslots), BF),
                pltpu.SemaphoreType.DMA((count, 1)),
            ],
        )(part, lower, lower_turned, packed_in, arrived, x_out)
    return (x_out, y_out)


def solution(mesh):
    return jax.shard_map(
        body,
        mesh=mesh,
        in_specs=(
            P("gx", "yz", None, None),
            P("gx", "yz", None),
            P("gx", "yz", None),
            P("gx", "yz", None, None),
            P("gx", "yz", None),
            P("gx", "yz"),
            P("gx", "yz", None, None),
            P("gx", "yz", None),
            P("gx", "yz"),
            P("gx", "yz", None, None),
            P("gx", "yz", None),
            P("gx", "yz"),
        ),
        out_specs=(P("gx", "yz", None, None), P("gx", "yz", None, None)),
        check_vma=False,
    )
```

```python
import functools

import jax
import jax.numpy as jnp
from jax import lax
from jax.experimental import pallas as pl
from jax.experimental.pallas import tpu as pltpu
from jax.sharding import PartitionSpec as P

BF = jnp.bfloat16
F32 = jnp.float32
MIB = 1024 * 1024


def passed_along(x, axis, by):
    devices = lax.axis_size(axis)
    pairs = [(i, i + by) for i in range(devices) if 0 <= i + by < devices]
    return lax.ppermute(x, axis, pairs)


def dot_nt(a, b):
    return lax.dot_general(a, b, (((1,), (1,)), ((), ())), preferred_element_type=F32)


def dot(a, b):
    return lax.dot_general(a, b, (((1,), (0,)), ((), ())), preferred_element_type=F32)


def marks_of(skel_row, rank, interp):
    rows, slots = interp.shape
    live = lax.broadcasted_iota(jnp.int32, (1, slots), 1) < rank
    picked_row = jnp.where(live, skel_row, -1).astype(F32).astype(BF)
    row = lax.broadcasted_iota(jnp.int32, (rows, slots), 0).astype(F32).astype(BF)
    live_row = jnp.where(live, F32(1.0), F32(0.0)).astype(BF)
    return row == picked_row, interp * live_row


def kept_cleared(turned):
    most = jnp.max(turned, axis=0, keepdims=True)
    least = jnp.where(most.astype(F32) == 1.0, F32(1.0), F32(-2.0)).astype(BF)
    return jnp.where(turned >= least, turned, BF(0.0))


def marked_of(skel_row, rank, interp):
    hit, live = marks_of(skel_row, rank, interp)
    return jnp.where(hit, BF(1.0), live)


def bases_of(cells, layer, first, rank_ref, skel, interp_ref):
    marked = [
        marked_of(skel[k : k + 1], rank_ref[layer, first + k], interp_ref[0, k])
        for k in range(cells)
    ]
    return [kept_cleared(t) for t in [jnp.transpose(m) for m in marked]]


def scaled(turned, conduct):
    return turned * -conduct


def face_of(left, link, link_t, right):
    upper = jnp.concatenate([left, link], axis=1)
    lower = jnp.concatenate([link_t, right], axis=1)
    return jnp.concatenate([upper, lower], axis=0)


def project(turned, matrices):
    inner = [dot(t, m).astype(BF) for t, m in zip(turned, matrices)]
    return [dot_nt(i, t) for i, t in zip(inner, turned)]


def top_kernel(cells, rank_hbm, skel_hbm, interp_hbm, out_ref, rank_ref, skel_ref, held, small_sems, sems):
    count, half, _ = out_ref.shape
    small = [
        pltpu.make_async_copy(rank_hbm, rank_ref, small_sems.at[0]),
        pltpu.make_async_copy(skel_hbm.at[0], skel_ref, small_sems.at[1]),
    ]
    copies = []
    for c in range(count // cells):
        group = pl.ds(c * cells, cells)
        copies.append(
            pltpu.make_async_copy(
                interp_hbm.at[0, group, pl.ds(0, half)], held.at[group], sems.at[c]
            )
        )
    for copy in small + copies:
        copy.start()
    for copy in small:
        copy.wait()
    for c in range(count // cells):
        copies[c].wait()
        for k in range(c * cells, (c + 1) * cells):
            out_ref[k] = marked_of(skel_ref[k : k + 1], rank_ref[0, k], held[k])


def pack_masks(size):
    half = size // 2
    row = lax.broadcasted_iota(jnp.int32, (half, size), 0)
    lane = lax.broadcasted_iota(jnp.int32, (half, size), 1)
    ahead = lane - row
    upper = (ahead >= 0) & (ahead < half)
    return upper, ahead == 0, ahead == half


def main_kernel(
    cells, layers, chunks,
    rank_ref, skel_ref, interp_ref, matrix_ref,
    x_rank_ref, x_skel_ref, x_interp_ref, x_coup_ref,
    y_rank_ref, y_skel_ref, y_interp_ref, y_coup_ref,
    x_out_ref, y_out_ref, packed_ref, packed_last_ref, edge_ref, corner_ref, last_turned_ref, last_schur_ref,
    store_turned, store_schur, store_extra,
):
    layer = layers - 1 - pl.program_id(0)
    chunk = chunks - 1 - pl.program_id(1)
    first = chunk * cells
    slots = skel_ref.shape[-1]
    half = slots // 2
    top = interp_ref.shape[2] // 2

    turned = bases_of(cells, layer, first, rank_ref, skel_ref[0], interp_ref)
    schurs = project(turned, [matrix_ref[0, k] for k in range(cells)])
    schurs = [s.astype(BF) for s in schurs]

    def faces(out_ref, f_rank_ref, f_skel_ref, f_interp_ref, coup_ref, rights):
        found = bases_of(cells, layer, first, f_rank_ref, f_skel_ref[0], f_interp_ref)
        matrices = []
        for k in range(cells):
            right_turned, right = rights[k]
            conduct = coup_ref[0, k : k + 1]
            lower = turned[k][:, top:]
            link = dot_nt(scaled(lower, conduct), right_turned).astype(BF)
            link_t = dot_nt(scaled(right_turned, conduct), lower).astype(BF)
            matrices.append(face_of(schurs[k], link, link_t, right))
        results = project(found, matrices)
        for k in range(cells):
            out_ref[0, k] = results[k].astype(BF)

    def stored(place):
        return store_turned[place], store_schur[place]

    after = jnp.minimum(first + cells, store_schur.shape[0] - 1)
    rights = [(turned[k][:, :top], schurs[k]) for k in range(1, cells)]
    faces(y_out_ref, y_rank_ref, y_skel_ref, y_interp_ref, y_coup_ref, rights + [stored(after)])

    @pl.when(layer < layers - 1)
    def _():
        rights = [stored(first + k) for k in range(cells)]
        faces(x_out_ref, x_rank_ref, x_skel_ref, x_interp_ref, x_coup_ref, rights)

    for k in range(cells):
        store_turned[first + k] = turned[k][:, :top]
        store_schur[first + k] = schurs[k]

    @pl.when(layer == layers - 1)
    def _():
        for k in range(cells):
            last_turned_ref[first + k] = turned[k][:, top:]
            last_schur_ref[first + k] = schurs[k]

    @pl.when(layer == 0)
    def _():
        upper, same, opposite = pack_masks(slots)

        def put(packed_ref, start):
            for k in range(cells):
                above, below = schurs[k][:half].astype(F32), schurs[k][half:].astype(F32)
                place = pl.ds(pl.multiple_of(start + k * half, half), half)
                packed_ref[place] = jnp.where(upper, above, below).astype(BF)

        @pl.when(chunk < chunks - 1)
        def _():
            put(packed_ref, chunk * (cells * half))

        @pl.when(chunk == chunks - 1)
        def _():
            put(packed_last_ref, 0)

        for p in range(0, cells, 2):
            extra = jnp.where(opposite, schurs[p][:half].astype(F32), F32(0.0))
            if p + 1 < cells:
                extra += jnp.where(same, schurs[p + 1][half:].astype(F32), F32(0.0))
            store_extra[chunk, p // 2 : p // 2 + 1] = jnp.sum(extra, axis=0, keepdims=True)

        @pl.when(chunk == 0)
        def _():
            pairs = -(-cells // 2)
            start = (chunks - 1) * cells * half
            rows = [store_extra[c, :pairs] for c in range(chunks)]
            pad = packed_ref.shape[0] - start - pairs * chunks
            if pad:
                rows.append(jnp.zeros((pad, slots), F32))
            packed_ref[start:] = jnp.concatenate(rows, axis=0).astype(BF)

    @pl.when(chunk == 0)
    def _():
        edge_ref[layer, 0] = turned[0][:, :top]
        edge_ref[layer, 1] = schurs[0]

    @pl.when(chunk == chunks - 1)
    def _():
        corner_ref[layer, 0] = turned[cells - 1][:, top:]
        corner_ref[layer, 1] = schurs[cells - 1]


def y_edge_kernel(layers, place, rank_ref, skel_ref, interp_ref, coup_ref, corner_ref, edge_ref, _, out_ref):
    row = place % skel_ref.shape[1]
    marked = [
        marked_of(skel_ref[i, row : row + 1], rank_ref[i, place], interp_ref[i, 0])
        for i in range(layers)
    ]
    found = [kept_cleared(jnp.transpose(m)) for m in marked]
    matrices = []
    for i in range(layers):
        conduct = coup_ref[i, row : row + 1]
        link = dot_nt(scaled(corner_ref[i, 0], conduct), edge_ref[i, 0]).astype(BF)
        link_t = dot_nt(scaled(edge_ref[i, 0], conduct), corner_ref[i, 0]).astype(BF)
        matrices.append(face_of(corner_ref[i, 1], link, link_t, edge_ref[i, 1]))
    results = project(found, matrices)
    for i in range(layers):
        out_ref[i, 0] = results[i].astype(BF)


def x_part_kernel(
    cells, layer, rank_ref, skel_ref, interp_ref, coup_ref, turned_ref, schur_ref, top_ref,
    part_ref, lower_ref, lower_turned_ref,
):
    count, slots, half = turned_ref.shape
    nothing = jnp.zeros((slots, slots), BF)
    for first in range(0, count, cells):
        group = range(first, first + cells)
        skel = skel_ref[layer, first : first + cells]
        marked = [
            marked_of(skel[k - first : k - first + 1], rank_ref[layer, k], interp_ref[layer, k]) for k in group
        ]
        faces = [kept_cleared(t) for t in [jnp.transpose(m) for m in marked]]
        for k in group:
            lower_turned_ref[k] = faces[k - first][:, half:]
            lower_ref[k] = jnp.transpose(faces[k - first][:, half:])
        tops = [kept_cleared(t) for t in [jnp.transpose(top_ref[k]) for k in group]]
        matrices = []
        for k, top in zip(group, tops):
            conduct = coup_ref[layer, k : k + 1]
            link = dot_nt(scaled(turned_ref[k], conduct), top).astype(BF)
            link_t = dot_nt(scaled(top, conduct), turned_ref[k]).astype(BF)
            matrices.append(face_of(schur_ref[k], link, link_t, nothing))
        for k, result in zip(group, project(faces, matrices)):
            part_ref[k] = result


def x_last_kernel(
    cells, layer, begin, extra_start, part_ref, lower_ref, lower_turned_ref, extra_ref, packed_ref, _,
    out_ref, held, sems,
):
    slots = part_ref.shape[-1]
    half = slots // 2
    upper, same, opposite = pack_masks(slots)
    one, zero, mid = F32(1.0), F32(0.0), F32(0.5)
    top_scale = jnp.where(same, mid, jnp.where(upper, one, zero))
    low_scale = jnp.where(opposite, mid, jnp.where(upper, zero, one))
    same_scale = jnp.where(same, one, zero)
    opposite_scale = jnp.where(opposite, one, zero)
    extras = extra_ref[extra_start:].astype(F32)
    copies = []
    group = range(begin, begin + cells)
    schurs = []
    for k in range(cells):
        start = k * half
        packed = packed_ref[start : start + half].astype(F32)
        extra = extras[(begin + k) // 2 : (begin + k) // 2 + 1]
        top, low = packed * top_scale, packed * low_scale
        if k % 2 == 0:
            top += extra * opposite_scale
        else:
            low += extra * same_scale
        tri = jnp.concatenate([top, low], axis=0).astype(BF)
        schurs.append(tri + jnp.transpose(tri))
    inner = [dot(lower_turned_ref[k], h).astype(BF) for k, h in zip(group, schurs)]
    results = [dot(i, lower_ref[k]) for k, i in zip(group, inner)]
    part_cells = max(1, cells // 4)
    for start in range(0, cells, part_cells):
        for k in range(start, start + part_cells):
            held[k] = (part_ref[begin + k] + results[k]).astype(BF)
        copy = pltpu.make_async_copy(
            held.at[pl.ds(start, part_cells)],
            out_ref.at[layer, pl.ds(begin + start, part_cells)],
            sems.at[start // part_cells],
        )
        copy.start()
        copies.append(copy)
    for copy in copies:
        copy.wait()


def call(kernel, grid, in_specs, out_specs, out_shape, flops, moved, aliases=None, vmem=24, scratch=()):
    return pl.pallas_call(
        kernel,
        grid=grid,
        in_specs=in_specs,
        out_specs=out_specs,
        out_shape=out_shape,
        scratch_shapes=scratch,
        input_output_aliases=aliases or {},
        compiler_params=pltpu.CompilerParams(vmem_limit_bytes=vmem * MIB),
        cost_estimate=pl.CostEstimate(flops=flops, bytes_accessed=moved, transcendentals=0),
    )


def in_hbm(x):
    return pltpu.with_memory_space_constraint(x, pltpu.HBM)


def body(
    cell_matrix,
    x_coupling,
    y_coupling,
    cell_interp,
    cell_skel,
    cell_rank,
    x_face_interp,
    x_face_skel,
    x_face_rank,
    y_face_interp,
    y_face_skel,
    y_face_rank,
):
    nx, nj, rows, slots = cell_interp.shape
    half = rows // 2
    fslots = x_face_interp.shape[-1]
    cells = next(n for n in (8, 4, 2, 1) if nj % n == 0 and nj > n)
    chunks = nj // cells
    unit = 2 * nx * nj * slots * slots * slots
    smem = pl.BlockSpec(memory_space=pltpu.SMEM)
    shape = jax.ShapeDtypeStruct

    hbm = pl.BlockSpec(memory_space=pltpu.HBM)
    vmem = pl.BlockSpec(memory_space=pltpu.VMEM)
    top = call(
        functools.partial(top_kernel, cells),
        (),
        [hbm, hbm, hbm],
        vmem,
        shape((nj, half, slots), BF),
        0,
        4 * nj * half * slots,
        vmem=8,
        scratch=[
            pltpu.SMEM((nx, nj), jnp.int32),
            pltpu.VMEM((nj, slots), jnp.int32),
            pltpu.VMEM((nj, half, slots), BF),
            pltpu.SemaphoreType.DMA((2,)),
            pltpu.SemaphoreType.DMA((chunks,)),
        ],
    )(in_hbm(cell_rank), in_hbm(cell_skel), in_hbm(cell_interp))
    top_in = passed_along(top, "gx", -1)


    late_rows = cells * slots // 2
    early_rows = (chunks - 1) * late_rows + -(-chunks * -(-cells // 2) // 16) * 16

    near = max(nx - 2, 0)

    def down(*dims):
        zeros = (0,) * len(dims)
        return pl.BlockSpec((1, cells) + dims, lambda i, c: (nx - 1 - i, chunks - 1 - c) + zeros)

    def down_x(*dims):
        zeros = (0,) * len(dims)

        def place(i, c):
            return (jnp.minimum(nx - 1 - i, near), jnp.where(i == 0, chunks - 1, chunks - 1 - c)) + zeros

        return pl.BlockSpec((1, cells) + dims, place)

    x_out, y_out, packed, packed_last, edge, corner, last_turned, last_schur = call(
        functools.partial(main_kernel, cells, nx, chunks),
        (nx, chunks),
        [
            smem, down(slots), down(rows, slots), down(rows, rows),
            smem, down_x(fslots), down_x(rows, fslots), down_x(half),
            smem, down(fslots), down(rows, fslots), down(half),
        ],
        [
            down_x(fslots, fslots),
            down(fslots, fslots),
            vmem, vmem, vmem, vmem, vmem, vmem,
        ],
        [
            shape((nx, nj, fslots, fslots), BF),
            shape((nx, nj, fslots, fslots), BF),
            shape((early_rows, slots), BF),
            shape((late_rows, slots), BF),
            shape((nx, 2, slots, half), BF),
            shape((nx, 2, slots, half), BF),
            shape((nj, slots, half), BF),
            shape((nj, slots, slots), BF),
        ],
        20 * unit,
        nx * nj * (rows * rows + 3 * rows * slots + 3 * slots * slots) * 2,
        vmem=32,
        scratch=[
            pltpu.VMEM((nj, slots, half), BF),
            pltpu.VMEM((nj, slots, slots), BF),
            pltpu.VMEM((chunks, cells, slots), F32),
        ],
    )(
        cell_rank, in_hbm(cell_skel), in_hbm(cell_interp), in_hbm(cell_matrix),
        x_face_rank, in_hbm(x_face_skel), in_hbm(x_face_interp), in_hbm(x_coupling),
        y_face_rank, in_hbm(y_face_skel), in_hbm(y_face_interp), in_hbm(y_coupling),
    )
    edge_in = passed_along(edge, "yz", -1)
    packed_in = passed_along(packed, "gx", -1)
    packed_last_in = passed_along(packed_last, "gx", -1)
    face_bytes = nj * (4 * rows * slots + 4 * slots * slots) * 2

    last = nx - 1
    tail = nj - 1
    group = tail // cells

    part, lower, lower_turned = call(
        functools.partial(x_part_kernel, cells, last),
        (),
        [smem, vmem, vmem, vmem, vmem, vmem, vmem],
        [vmem, vmem, vmem],
        [
            shape((nj, fslots, fslots), F32),
            shape((nj, slots, fslots), BF),
            shape((nj, fslots, slots), BF),
        ],
        8 * unit // nx,
        face_bytes,
        vmem=16,
    )(x_face_rank, x_face_skel, x_face_interp, x_coupling, last_turned, last_schur, top_in)

    edge_in, part = lax.optimization_barrier((edge_in, part))
    y_out = call(
        functools.partial(y_edge_kernel, nx, tail),
        (1,),
        [
            smem,
            pl.BlockSpec((nx, cells, fslots), lambda i: (0, group, 0)),
            pl.BlockSpec((nx, 1, rows, fslots), lambda i: (0, tail, 0, 0)),
            pl.BlockSpec((nx, cells, half), lambda i: (0, group, 0)),
            pl.BlockSpec((nx, 2, slots, half), lambda i: (0, 0, 0, 0)),
            pl.BlockSpec((nx, 2, slots, half), lambda i: (0, 0, 0, 0)),
            pl.BlockSpec(memory_space=pl.ANY),
        ],
        pl.BlockSpec((nx, 1, fslots, fslots), lambda i: (0, tail, 0, 0)),
        shape((nx, nj, fslots, fslots), BF),
        8 * unit // nj,
        nx * face_bytes // nj,
        {6: 0},
    )(y_face_rank, y_face_skel, in_hbm(y_face_interp), y_coupling, corner, edge_in, y_out)

    early = (chunks - 1) * cells
    for begin, count, arrived in ((0, early, packed_in), (early, cells, packed_last_in)):
        x_out = call(
            functools.partial(x_last_kernel, count, last, begin, (chunks - 1) * late_rows),
            (),
            [vmem, vmem, vmem, vmem, vmem, hbm],
            hbm,
            shape((nx, nj, fslots, fslots), BF),
            3 * unit // nx * count // nj,
            slots * slots * 11 * count,
            {5: 0},
            scratch=[
                pltpu.VMEM((count, fslots, fslots), BF),
                pltpu.SemaphoreType.DMA((8,)),
            ],
        )(part, lower, lower_turned, packed_in, arrived, x_out)
    return (x_out, y_out)


def solution(mesh):
    return jax.shard_map(
        body,
        mesh=mesh,
        in_specs=(
            P("gx", "yz", None, None),
            P("gx", "yz", None),
            P("gx", "yz", None),
            P("gx", "yz", None, None),
            P("gx", "yz", None),
            P("gx", "yz"),
            P("gx", "yz", None, None),
            P("gx", "yz", None),
            P("gx", "yz"),
            P("gx", "yz", None, None),
            P("gx", "yz", None),
            P("gx", "yz"),
        ),
        out_specs=(P("gx", "yz", None, None), P("gx", "yz", None, None)),
        check_vma=False,
    )
```

```python
import functools

import jax
import jax.numpy as jnp
from jax import lax
from jax.experimental import pallas as pl
from jax.experimental.pallas import tpu as pltpu
from jax.sharding import PartitionSpec as P

BF = jnp.bfloat16
F32 = jnp.float32
MIB = 1024 * 1024


def passed_along(x, axis, by):
    devices = lax.axis_size(axis)
    pairs = [(i, i + by) for i in range(devices) if 0 <= i + by < devices]
    return lax.ppermute(x, axis, pairs)


def dot_nt(a, b):
    return lax.dot_general(a, b, (((1,), (1,)), ((), ())), preferred_element_type=F32)


def dot(a, b):
    return lax.dot_general(a, b, (((1,), (0,)), ((), ())), preferred_element_type=F32)


def marks_of(skel_row, rank, interp):
    rows, slots = interp.shape
    live = lax.broadcasted_iota(jnp.int32, (1, slots), 1) < rank
    picked_row = jnp.where(live, skel_row, -1).astype(F32).astype(BF)
    row = lax.broadcasted_iota(jnp.int32, (rows, slots), 0).astype(F32).astype(BF)
    live_row = jnp.where(live, F32(1.0), F32(0.0)).astype(BF)
    return row == picked_row, interp * live_row


def kept_cleared(turned):
    most = jnp.max(turned, axis=0, keepdims=True)
    least = jnp.where(most.astype(F32) == 1.0, F32(1.0), F32(-2.0)).astype(BF)
    return jnp.where(turned >= least, turned, BF(0.0))


def marked_of(skel_row, rank, interp):
    hit, live = marks_of(skel_row, rank, interp)
    return jnp.where(hit, BF(1.0), live)


def bases_of(cells, layer, first, rank_ref, skel, interp_ref):
    marked = [
        marked_of(skel[k : k + 1], rank_ref[layer, first + k], interp_ref[0, k])
        for k in range(cells)
    ]
    return [kept_cleared(t) for t in [jnp.transpose(m) for m in marked]]


def scaled(turned, conduct):
    return turned * -conduct


def face_of(left, link, link_t, right):
    upper = jnp.concatenate([left, link], axis=1)
    lower = jnp.concatenate([link_t, right], axis=1)
    return jnp.concatenate([upper, lower], axis=0)


def project(turned, matrices):
    inner = [dot(t, m).astype(BF) for t, m in zip(turned, matrices)]
    return [dot_nt(i, t) for i, t in zip(inner, turned)]


def top_kernel(cells, rank_hbm, skel_hbm, interp_hbm, out_ref, rank_ref, skel_ref, held, small_sems, sems):
    count, half, _ = out_ref.shape
    small = [
        pltpu.make_async_copy(rank_hbm, rank_ref, small_sems.at[0]),
        pltpu.make_async_copy(skel_hbm.at[0], skel_ref, small_sems.at[1]),
    ]
    copies = []
    for c in range(count // cells):
        group = pl.ds(c * cells, cells)
        copies.append(
            pltpu.make_async_copy(
                interp_hbm.at[0, group, pl.ds(0, half)], held.at[group], sems.at[c]
            )
        )
    for copy in small + copies:
        copy.start()
    for copy in small:
        copy.wait()
    for c in range(count // cells):
        copies[c].wait()
        for k in range(c * cells, (c + 1) * cells):
            out_ref[k] = marked_of(skel_ref[k : k + 1], rank_ref[0, k], held[k])


def pack_masks(size):
    half = size // 2
    row = lax.broadcasted_iota(jnp.int32, (half, size), 0)
    lane = lax.broadcasted_iota(jnp.int32, (half, size), 1)
    ahead = lane - row
    upper = (ahead >= 0) & (ahead < half)
    return upper, ahead == 0, ahead == half


def main_kernel(
    cells, layers, chunks,
    rank_ref, skel_ref, interp_ref, matrix_ref,
    x_rank_ref, x_skel_ref, x_interp_ref, x_coup_ref,
    y_rank_ref, y_skel_ref, y_interp_ref, y_coup_ref,
    x_out_ref, y_out_ref, packed_ref, packed_last_ref, edge_ref, corner_ref, last_turned_ref, last_schur_ref,
    store_turned, store_schur, store_extra,
):
    layer = layers - 1 - pl.program_id(0)
    chunk = chunks - 1 - pl.program_id(1)
    first = chunk * cells
    slots = skel_ref.shape[-1]
    half = slots // 2
    top = interp_ref.shape[2] // 2

    turned = bases_of(cells, layer, first, rank_ref, skel_ref[0], interp_ref)
    schurs = project(turned, [matrix_ref[0, k] for k in range(cells)])
    schurs = [s.astype(BF) for s in schurs]

    def faces(out_ref, f_rank_ref, f_skel_ref, f_interp_ref, coup_ref, rights):
        found = bases_of(cells, layer, first, f_rank_ref, f_skel_ref[0], f_interp_ref)
        matrices = []
        for k in range(cells):
            right_turned, right = rights[k]
            conduct = coup_ref[0, k : k + 1]
            lower = turned[k][:, top:]
            link = dot_nt(scaled(lower, conduct), right_turned).astype(BF)
            link_t = dot_nt(scaled(right_turned, conduct), lower).astype(BF)
            matrices.append(face_of(schurs[k], link, link_t, right))
        results = project(found, matrices)
        for k in range(cells):
            out_ref[0, k] = results[k].astype(BF)

    def stored(place):
        return store_turned[place], store_schur[place]

    after = jnp.minimum(first + cells, store_schur.shape[0] - 1)
    rights = [(turned[k][:, :top], schurs[k]) for k in range(1, cells)]
    faces(y_out_ref, y_rank_ref, y_skel_ref, y_interp_ref, y_coup_ref, rights + [stored(after)])

    @pl.when(layer < layers - 1)
    def _():
        rights = [stored(first + k) for k in range(cells)]
        faces(x_out_ref, x_rank_ref, x_skel_ref, x_interp_ref, x_coup_ref, rights)

    for k in range(cells):
        store_turned[first + k] = turned[k][:, :top]
        store_schur[first + k] = schurs[k]

    @pl.when(layer == layers - 1)
    def _():
        for k in range(cells):
            last_turned_ref[first + k] = turned[k][:, top:]
            last_schur_ref[first + k] = schurs[k]

    @pl.when(layer == 0)
    def _():
        upper, same, opposite = pack_masks(slots)

        def put(packed_ref, start):
            for k in range(cells):
                above, below = schurs[k][:half].astype(F32), schurs[k][half:].astype(F32)
                place = pl.ds(pl.multiple_of(start + k * half, half), half)
                packed_ref[place] = jnp.where(upper, above, below).astype(BF)

        @pl.when(chunk < chunks - 1)
        def _():
            put(packed_ref, chunk * (cells * half))

        @pl.when(chunk == chunks - 1)
        def _():
            put(packed_last_ref, 0)

        for p in range(0, cells, 2):
            extra = jnp.where(opposite, schurs[p][:half].astype(F32), F32(0.0))
            if p + 1 < cells:
                extra += jnp.where(same, schurs[p + 1][half:].astype(F32), F32(0.0))
            store_extra[chunk, p // 2 : p // 2 + 1] = jnp.sum(extra, axis=0, keepdims=True)

        @pl.when(chunk == 0)
        def _():
            pairs = -(-cells // 2)
            start = (chunks - 1) * cells * half
            rows = [store_extra[c, :pairs] for c in range(chunks)]
            pad = packed_ref.shape[0] - start - pairs * chunks
            if pad:
                rows.append(jnp.zeros((pad, slots), F32))
            packed_ref[start:] = jnp.concatenate(rows, axis=0).astype(BF)

    @pl.when(chunk == 0)
    def _():
        edge_ref[layer, 0] = turned[0][:, :top]
        edge_ref[layer, 1] = schurs[0]

    @pl.when(chunk == chunks - 1)
    def _():
        corner_ref[layer, 0] = turned[cells - 1][:, top:]
        corner_ref[layer, 1] = schurs[cells - 1]


def y_edge_kernel(layers, place, rank_ref, skel_ref, interp_ref, coup_ref, corner_ref, edge_ref, _, out_ref):
    row = place % skel_ref.shape[1]
    marked = [
        marked_of(skel_ref[i, row : row + 1], rank_ref[i, place], interp_ref[i, 0])
        for i in range(layers)
    ]
    found = [kept_cleared(jnp.transpose(m)) for m in marked]
    matrices = []
    for i in range(layers):
        conduct = coup_ref[i, row : row + 1]
        link = dot_nt(scaled(corner_ref[i, 0], conduct), edge_ref[i, 0]).astype(BF)
        link_t = dot_nt(scaled(edge_ref[i, 0], conduct), corner_ref[i, 0]).astype(BF)
        matrices.append(face_of(corner_ref[i, 1], link, link_t, edge_ref[i, 1]))
    results = project(found, matrices)
    for i in range(layers):
        out_ref[i, 0] = results[i].astype(BF)


def x_part_kernel(
    cells, layer, rank_ref, skel_ref, interp_ref, coup_ref, turned_ref, schur_ref, top_ref,
    part_ref, lower_ref, lower_turned_ref,
):
    count, slots, half = turned_ref.shape
    nothing = jnp.zeros((slots, slots), BF)
    for first in range(0, count, cells):
        group = range(first, first + cells)
        skel = skel_ref[layer, first : first + cells]
        marked = [
            marked_of(skel[k - first : k - first + 1], rank_ref[layer, k], interp_ref[layer, k]) for k in group
        ]
        faces = [kept_cleared(t) for t in [jnp.transpose(m) for m in marked]]
        for k in group:
            lower_turned_ref[k] = faces[k - first][:, half:]
            lower_ref[k] = jnp.transpose(faces[k - first][:, half:])
        tops = [kept_cleared(t) for t in [jnp.transpose(top_ref[k]) for k in group]]
        matrices = []
        for k, top in zip(group, tops):
            conduct = coup_ref[layer, k : k + 1]
            link = dot_nt(scaled(turned_ref[k], conduct), top).astype(BF)
            link_t = dot_nt(scaled(top, conduct), turned_ref[k]).astype(BF)
            matrices.append(face_of(schur_ref[k], link, link_t, nothing))
        for k, result in zip(group, project(faces, matrices)):
            part_ref[k] = result


def x_last_kernel(
    cells, layer, begin, extra_start, part_ref, lower_ref, lower_turned_ref, extra_ref, packed_ref, _,
    out_ref, held, sems,
):
    slots = part_ref.shape[-1]
    half = slots // 2
    upper, same, opposite = pack_masks(slots)
    one, zero, mid = F32(1.0), F32(0.0), F32(0.5)
    top_scale = jnp.where(same, mid, jnp.where(upper, one, zero))
    low_scale = jnp.where(opposite, mid, jnp.where(upper, zero, one))
    same_scale = jnp.where(same, one, zero)
    opposite_scale = jnp.where(opposite, one, zero)
    extras = extra_ref[extra_start:].astype(F32)
    copies = []
    group = range(begin, begin + cells)
    schurs = []
    for k in range(cells):
        start = k * half
        packed = packed_ref[start : start + half].astype(F32)
        extra = extras[(begin + k) // 2 : (begin + k) // 2 + 1]
        top, low = packed * top_scale, packed * low_scale
        if k % 2 == 0:
            top += extra * opposite_scale
        else:
            low += extra * same_scale
        tri = jnp.concatenate([top, low], axis=0).astype(BF)
        schurs.append(tri + jnp.transpose(tri))
    inner = [dot(lower_turned_ref[k], h).astype(BF) for k, h in zip(group, schurs)]
    results = [dot(i, lower_ref[k]) for k, i in zip(group, inner)]
    part_cells = max(1, cells // 4)
    for start in range(0, cells, part_cells):
        for k in range(start, start + part_cells):
            held[k] = (part_ref[begin + k] + results[k]).astype(BF)
        copy = pltpu.make_async_copy(
            held.at[pl.ds(start, part_cells)],
            out_ref.at[layer, pl.ds(begin + start, part_cells)],
            sems.at[start // part_cells],
        )
        copy.start()
        copies.append(copy)
    for copy in copies:
        copy.wait()


def call(kernel, grid, in_specs, out_specs, out_shape, flops, moved, aliases=None, vmem=24, scratch=()):
    return pl.pallas_call(
        kernel,
        grid=grid,
        in_specs=in_specs,
        out_specs=out_specs,
        out_shape=out_shape,
        scratch_shapes=scratch,
        input_output_aliases=aliases or {},
        compiler_params=pltpu.CompilerParams(vmem_limit_bytes=vmem * MIB),
        cost_estimate=pl.CostEstimate(flops=flops, bytes_accessed=moved, transcendentals=0),
    )


def in_hbm(x):
    return pltpu.with_memory_space_constraint(x, pltpu.HBM)


def body(
    cell_matrix,
    x_coupling,
    y_coupling,
    cell_interp,
    cell_skel,
    cell_rank,
    x_face_interp,
    x_face_skel,
    x_face_rank,
    y_face_interp,
    y_face_skel,
    y_face_rank,
):
    nx, nj, rows, slots = cell_interp.shape
    half = rows // 2
    fslots = x_face_interp.shape[-1]
    cells = next(n for n in (8, 4, 2, 1) if nj % n == 0 and nj > n)
    chunks = nj // cells
    unit = 2 * nx * nj * slots * slots * slots
    smem = pl.BlockSpec(memory_space=pltpu.SMEM)
    shape = jax.ShapeDtypeStruct

    hbm = pl.BlockSpec(memory_space=pltpu.HBM)
    vmem = pl.BlockSpec(memory_space=pltpu.VMEM)
    top = call(
        functools.partial(top_kernel, cells),
        (),
        [hbm, hbm, hbm],
        vmem,
        shape((nj, half, slots), BF),
        0,
        4 * nj * half * slots,
        vmem=8,
        scratch=[
            pltpu.SMEM((nx, nj), jnp.int32),
            pltpu.VMEM((nj, slots), jnp.int32),
            pltpu.VMEM((nj, half, slots), BF),
            pltpu.SemaphoreType.DMA((2,)),
            pltpu.SemaphoreType.DMA((chunks,)),
        ],
    )(in_hbm(cell_rank), in_hbm(cell_skel), in_hbm(cell_interp))
    top_in = passed_along(top, "gx", -1)


    late_rows = cells * slots // 2
    early_rows = (chunks - 1) * late_rows + -(-chunks * -(-cells // 2) // 16) * 16

    near = max(nx - 2, 0)

    def down(*dims):
        zeros = (0,) * len(dims)
        return pl.BlockSpec((1, cells) + dims, lambda i, c: (nx - 1 - i, chunks - 1 - c) + zeros)

    def down_x(*dims):
        zeros = (0,) * len(dims)

        def place(i, c):
            return (jnp.minimum(nx - 1 - i, near), jnp.where(i == 0, chunks - 1, chunks - 1 - c)) + zeros

        return pl.BlockSpec((1, cells) + dims, place)

    x_out, y_out, packed, packed_last, edge, corner, last_turned, last_schur = call(
        functools.partial(main_kernel, cells, nx, chunks),
        (nx, chunks),
        [
            smem, down(slots), down(rows, slots), down(rows, rows),
            smem, down_x(fslots), down_x(rows, fslots), down_x(half),
            smem, down(fslots), down(rows, fslots), down(half),
        ],
        [
            down_x(fslots, fslots),
            down(fslots, fslots),
            vmem, vmem, vmem, vmem, vmem, vmem,
        ],
        [
            shape((nx, nj, fslots, fslots), BF),
            shape((nx, nj, fslots, fslots), BF),
            shape((early_rows, slots), BF),
            shape((late_rows, slots), BF),
            shape((nx, 2, slots, half), BF),
            shape((nx, 2, slots, half), BF),
            shape((nj, slots, half), BF),
            shape((nj, slots, slots), BF),
        ],
        20 * unit,
        nx * nj * (rows * rows + 3 * rows * slots + 3 * slots * slots) * 2,
        vmem=32,
        scratch=[
            pltpu.VMEM((nj, slots, half), BF),
            pltpu.VMEM((nj, slots, slots), BF),
            pltpu.VMEM((chunks, cells, slots), F32),
        ],
    )(
        in_hbm(cell_rank), in_hbm(cell_skel), in_hbm(cell_interp), in_hbm(cell_matrix),
        in_hbm(x_face_rank), in_hbm(x_face_skel), in_hbm(x_face_interp), in_hbm(x_coupling),
        in_hbm(y_face_rank), in_hbm(y_face_skel), in_hbm(y_face_interp), in_hbm(y_coupling),
    )
    edge_in = passed_along(edge, "yz", -1)
    packed_in = passed_along(packed, "gx", -1)
    packed_last_in = passed_along(packed_last, "gx", -1)
    face_bytes = nj * (4 * rows * slots + 4 * slots * slots) * 2

    last = nx - 1
    tail = nj - 1
    group = tail // cells

    part, lower, lower_turned = call(
        functools.partial(x_part_kernel, cells, last),
        (),
        [smem, vmem, vmem, vmem, vmem, vmem, vmem],
        [vmem, vmem, vmem],
        [
            shape((nj, fslots, fslots), F32),
            shape((nj, slots, fslots), BF),
            shape((nj, fslots, slots), BF),
        ],
        8 * unit // nx,
        face_bytes,
        vmem=16,
    )(x_face_rank, x_face_skel, x_face_interp, x_coupling, last_turned, last_schur, top_in)

    edge_in, part = lax.optimization_barrier((edge_in, part))
    y_out = call(
        functools.partial(y_edge_kernel, nx, tail),
        (1,),
        [
            smem,
            pl.BlockSpec((nx, cells, fslots), lambda i: (0, group, 0)),
            pl.BlockSpec((nx, 1, rows, fslots), lambda i: (0, tail, 0, 0)),
            pl.BlockSpec((nx, cells, half), lambda i: (0, group, 0)),
            pl.BlockSpec((nx, 2, slots, half), lambda i: (0, 0, 0, 0)),
            pl.BlockSpec((nx, 2, slots, half), lambda i: (0, 0, 0, 0)),
            pl.BlockSpec(memory_space=pl.ANY),
        ],
        pl.BlockSpec((nx, 1, fslots, fslots), lambda i: (0, tail, 0, 0)),
        shape((nx, nj, fslots, fslots), BF),
        8 * unit // nj,
        nx * face_bytes // nj,
        {6: 0},
    )(y_face_rank, y_face_skel, in_hbm(y_face_interp), y_coupling, corner, edge_in, y_out)

    early = (chunks - 1) * cells
    for begin, count, arrived in ((0, early, packed_in), (early, cells, packed_last_in)):
        x_out = call(
            functools.partial(x_last_kernel, count, last, begin, (chunks - 1) * late_rows),
            (),
            [vmem, vmem, vmem, vmem, vmem, hbm],
            hbm,
            shape((nx, nj, fslots, fslots), BF),
            3 * unit // nx * count // nj,
            slots * slots * 11 * count,
            {5: 0},
            scratch=[
                pltpu.VMEM((count, fslots, fslots), BF),
                pltpu.SemaphoreType.DMA((8,)),
            ],
        )(part, lower, lower_turned, packed_in, arrived, x_out)
    return (x_out, y_out)


def solution(mesh):
    return jax.shard_map(
        body,
        mesh=mesh,
        in_specs=(
            P("gx", "yz", None, None),
            P("gx", "yz", None),
            P("gx", "yz", None),
            P("gx", "yz", None, None),
            P("gx", "yz", None),
            P("gx", "yz"),
            P("gx", "yz", None, None),
            P("gx", "yz", None),
            P("gx", "yz"),
            P("gx", "yz", None, None),
            P("gx", "yz", None),
            P("gx", "yz"),
        ),
        out_specs=(P("gx", "yz", None, None), P("gx", "yz", None, None)),
        check_vma=False,
    )
```
